32 devices in a mesh: chain: 2 (over core), leaf: 4 (over y, x), head: 4 (over z).
Axes of the slice: x: 2, y: 2, z: 4, core: 2. Of those that a mesh axis runs over, the one named last changes fastest.
Arguments:
- query_in: bfloat16 [4096, 16, 128], P(('chain', 'leaf'), 'head'), may hold values from -6 to 6
- key_in: bfloat16 [4096, 16, 128], P(('chain', 'leaf'), 'head'), may hold values from -120 to 120
- value_in: bfloat16 [4096, 16, 128], P(('chain', 'leaf'), 'head'), may hold values from -6 to 6
- gate_in: bfloat16 [4096, 16, 128], P(('chain', 'leaf'), 'head'), may hold values from -6 to 6
- write_strength: float32 [16, 4096], P('head', ('chain', 'leaf')), as said below
- log_decay: float32 [16, 4096], P('head', ('chain', 'leaf')), as said below
- doc_resets: int32 [64], P(('chain', 'leaf')), may hold values from 0 to 1, as said below
- conv_weight: float32 [3, 4, 16, 128], P(None, None, 'head'), may hold values from -3 to 3
- output_norm_gain: float32 [128], replicated, may hold values from 0.25 to 1.75
- output_projection_weight: bfloat16 [2048, 4096], P(None, 'head'), may hold values from -0.125 to 0.125
Outputs:
- mixed: bfloat16 [4096, 4096], P(('chain', 'leaf'), 'head')
The draws below stay inside these ranges and needn't reach their ends.
Inputs may be any that keep to these rules, and one draw needn't show every extreme that they name: `write_strength`: strictly positive. `log_decay`: strictly negative. `doc_resets`: at least one block of every draw starts a document.
All inputs are finite; a program needn't handle non-finite values.
Results may differ from the reference program's by a relative error of at most 0.0064.
Values may be sent and summed in bfloat16 or wider, within the bound.
No kernel may reach another device: no remote copies, remote signals or barrier semaphores. Data moves between devices by JAX's collectives and lax.ppermute only.
A program may use at most 64 MiB of HBM per device.

```python
import jax
import jax.numpy as jnp
from jax import lax

H = 16
DK = 128
DV = 128
D = 4096
BLOCK = 64
KCONV = 4
TOK_DEV = 512
TOKENS = 4096
NBLOCK = 64


def head_kinds(key):
    picker = jax.random.fold_in(key, 11)
    return jax.random.randint(picker, (H,), 0, 2) > 0


def draw_key_in(key, part):
    ladder = jnp.broadcast_to(jnp.arange(DK, dtype=jnp.int32), (H, DK))
    ranking = jax.random.permutation(jax.random.fold_in(key, 41), ladder, axis=1, independent=True)
    channel_scale = 30.0 ** (ranking.astype(jnp.float32) / (DK - 1))
    unscaled = jnp.clip(jax.random.normal(jax.random.fold_in(key, 42), (TOKENS, H, DK), jnp.float32), -4.0, 4.0)
    return (unscaled * channel_scale[None, :, :]).astype(jnp.bfloat16)


def draw_log_decay(key, part):
    lagging_version = head_kinds(key)
    rough = jax.random.uniform(jax.random.fold_in(key, 1), (H, TOKENS), jnp.float32, 0.5, 1.5)
    segment = jax.random.uniform(jax.random.fold_in(key, 2), (H, TOKENS // TOK_DEV, 1), jnp.float32, 0.5, 1.5)
    segment = jnp.broadcast_to(segment, (H, TOKENS // TOK_DEV, TOK_DEV)).reshape(H, TOKENS)
    fast_scale = jax.random.uniform(jax.random.fold_in(key, 3), (H, 1), jnp.float32, 20.0, 50.0)
    slow_scale = jax.random.uniform(jax.random.fold_in(key, 4), (H, 1), jnp.float32, 0.1, 0.5)
    rapid_fraction = -rough * segment / fast_scale
    leisurely_fraction = -rough * segment * slow_scale / TOKENS
    spots = jax.random.randint(jax.random.fold_in(key, 5), (H, 2), 0, TOKENS)
    objective_scores = jax.random.uniform(jax.random.fold_in(key, 6), (H, 2), jnp.float32, 0.2, 0.4)
    positions = jnp.arange(TOKENS, dtype=jnp.int32)
    hit_markers = positions[None, :, None] == spots[:, None, :]
    clustered_sets = jnp.sum(jnp.where(hit_markers, jnp.log(1.0 - objective_scores)[:, None, :], 0.0), axis=-1)
    return jnp.where(lagging_version[:, None], leisurely_fraction, rapid_fraction) + clustered_sets


def draw_write_strength(key, part):
    lagging_version = head_kinds(key)
    rough = jax.random.uniform(jax.random.fold_in(key, 21), (H, TOKENS), jnp.float32, 0.5, 1.5)
    fast_level = jax.random.uniform(jax.random.fold_in(key, 22), (H, 1), jnp.float32, 0.3, 0.65)
    slow_level = jax.random.uniform(jax.random.fold_in(key, 23), (H, 1), jnp.float32, 0.1, 0.3)
    slow_factor = min(0.5, 64.0 * DK / TOKENS)
    rapid_fraction = jnp.minimum(fast_level * rough, 1.0)
    leisurely_fraction = jnp.minimum(slow_level * rough * slow_factor, 1.0)
    return jnp.where(lagging_version[:, None], leisurely_fraction, rapid_fraction)


def draw_doc_resets(key, part):
    flagged = jax.random.randint(jax.random.fold_in(key, 31), (NBLOCK,), 0, 256) == 0
    forced = jax.random.randint(jax.random.fold_in(key, 32), (), 1, NBLOCK)
    marked = flagged | (jnp.arange(NBLOCK, dtype=jnp.int32) == forced)
    return marked.astype(jnp.int32)


def block_levels(key, shape, shards, least, largest):
    def one(dim, shards_of):
        draws = jax.random.uniform(jax.random.fold_in(jax.random.fold_in(key, 6), dim), (shards_of,), jnp.float32, least / len(shards), largest / len(shards))
        return jnp.repeat(jnp.exp(draws), shape[dim] // shards_of).reshape((-1,) + (1,) * (len(shape) - dim - 1))

    loudness = one(*shards[0])
    for cut in shards[1:]:
        loudness = loudness * one(*cut)
    return loudness


def bell_draw(key, dims, deviation, most, pieces=(), kind=jnp.bfloat16):
    level = block_levels(key, dims, pieces, -0.22, 0.18) if pieces else 1.0
    result = jax.random.normal(key, dims, jnp.float32) * deviation * level
    return jnp.minimum(jnp.maximum(result, -most), most).astype(kind)


def setup_inputs(seed: int = 0) -> dict:
    streams_of = jax.random.split(jax.random.key(seed), 11)
    return {
        "query_in": bell_draw(streams_of[0], (TOKENS, H, DK), 1.0, 6.0, ((0, 8), (1, 4))),
        "key_in": draw_key_in(jax.random.fold_in(streams_of[10], 71), 0),
        "value_in": bell_draw(streams_of[2], (TOKENS, H, DV), 1.0, 6.0, ((0, 8), (1, 4))),
        "gate_in": bell_draw(streams_of[3], (TOKENS, H, DV), 1.0, 6.0, ((0, 8), (1, 4))),
        "write_strength": draw_write_strength(jax.random.fold_in(streams_of[10], 71), 0),
        "log_decay": draw_log_decay(jax.random.fold_in(streams_of[10], 71), 0),
        "doc_resets": draw_doc_resets(jax.random.fold_in(streams_of[10], 71), 0),
        "conv_weight": bell_draw(streams_of[7], (3, KCONV, H, DK), KCONV ** -0.5, 3.0, ((2, 4),), jnp.float32),
        "output_norm_gain": jnp.clip(1.0 + 0.15 * jax.random.normal(streams_of[8], (DV,), jnp.float32), 0.25, 1.75),
        "output_projection_weight": bell_draw(streams_of[9], (H * DV, D), (H * DV) ** -0.5, 0.125, ((1, 4),)),
    }


highest = lax.Precision.HIGHEST
epsilon = 1e-06

def unit_rows(matrix):
    return matrix / jnp.sqrt(lax.optimization_barrier(jnp.sum(matrix * matrix, axis=-1, keepdims=True)) + epsilon)

def causal_filter(signal, weights):
    kernel = weights.shape[0]
    length = signal.shape[0]
    padded = jnp.pad(signal.astype(jnp.float32), ((kernel - 1, 0), (0, 0), (0, 0)))
    running = weights[0] * padded[0:length]
    for offset in range(1, kernel):
        running = running + weights[offset] * padded[offset:offset + length]
    return jax.nn.silu(running)

def block_terms(query_unit, key_unit, value_act, strength, decays, keep_block):
    block_len = query_unit.shape[1]
    depth_k = key_unit.shape[2]
    value_width = value_act.shape[2]
    row_index = lax.broadcasted_iota(jnp.int32, (block_len, block_len), 0)
    col_index = lax.broadcasted_iota(jnp.int32, (block_len, block_len), 1)
    strict_mask = row_index > col_index
    causal_mask = row_index >= col_index
    cumulative = jnp.cumsum(decays, axis=-1)
    spread_log = cumulative[:, :, None] - cumulative[:, None, :]
    fading = jnp.where(causal_mask, jnp.exp(jnp.where(causal_mask, spread_log, 0.0)), 0.0)
    growth = jnp.exp(cumulative)
    query_float = query_unit.astype(jnp.float32)
    key_float = key_unit.astype(jnp.float32)
    value_float = value_act.astype(jnp.float32)
    key_gram = jnp.einsum('nte,nse->nts', key_float, key_float, precision=highest)
    query_gram = jnp.einsum('nte,nse->nts', query_float, key_float, precision=highest)
    lower = jnp.where(strict_mask, strength[:, :, None] * fading * key_gram, 0.0)
    mixing = fading * query_gram
    targets = jnp.concatenate([strength[:, :, None] * value_float, (strength * growth)[:, :, None] * key_float], axis=-1)
    solved = jax.scipy.linalg.solve_triangular(jnp.eye(block_len, dtype=jnp.float32) + lower, targets, lower=True, unit_diagonal=True)
    local_values = solved[..., :value_width]
    write_keys = solved[..., value_width:]
    tail_fade = jnp.exp(cumulative[:, -1:] - cumulative)
    decayed_addresses = tail_fade[:, :, None] * key_float
    key_eye = jnp.eye(depth_k, dtype=jnp.float32)
    keep_mat = keep_block[:, None, None]
    transition = keep_mat * (growth[:, -1, None, None] * key_eye - jnp.einsum('nce,ncf->nef', decayed_addresses, write_keys, precision=highest))
    addition = jnp.einsum('nce,ncf->nef', decayed_addresses, local_values, precision=highest)
    query_eff = keep_mat * (growth[:, :, None] * query_float - jnp.einsum('nts,nse->nte', mixing, write_keys, precision=highest))
    own_output = jnp.einsum('nts,nsf->ntf', mixing, local_values, precision=highest)
    return (transition, addition, query_eff, own_output)

def head_core(argument_arrays):
    query_head, key_head, value_head, strength, decays, keep_block = argument_arrays
    length = query_head.shape[0]
    blocks = length // BLOCK
    all_terms = block_terms(query_head.reshape(blocks, BLOCK, -1), key_head.reshape(blocks, BLOCK, -1), value_head.reshape(blocks, BLOCK, -1), strength.reshape(blocks, BLOCK), decays.reshape(blocks, BLOCK), keep_block)

    def advance(state, terms_now):
        transition, addition, query_eff, own_output = terms_now
        produced = jnp.dot(query_eff.astype(jnp.float32), state.astype(jnp.float32), precision=highest, preferred_element_type=jnp.float32) + own_output
        following = jnp.dot(transition.astype(jnp.float32), state.astype(jnp.float32), precision=highest, preferred_element_type=jnp.float32) + addition
        return (following, produced)
    initial = jnp.zeros((key_head.shape[1], value_head.shape[1]), jnp.float32)
    final_state, produced = lax.scan(advance, initial, all_terms)
    return produced.reshape(length, value_head.shape[1])

def reference(query_in, key_in, value_in, gate_in, write_strength, log_decay, doc_resets, conv_weight, output_norm_gain, output_projection_weight):
    query_conv = causal_filter(query_in, conv_weight[0])
    key_conv = causal_filter(key_in, conv_weight[1])
    value_conv = causal_filter(value_in, conv_weight[2])
    query_unit = (unit_rows(query_conv) * DK ** (-0.5)).astype(jnp.bfloat16)
    key_unit = unit_rows(key_conv).astype(jnp.bfloat16)
    value_act = value_conv.astype(jnp.bfloat16)
    keep_block = (1 - doc_resets).astype(jnp.float32)
    keep_heads = jnp.broadcast_to(keep_block, (H, keep_block.shape[0]))
    core = lax.map(head_core, (jnp.moveaxis(query_unit, 1, 0), jnp.moveaxis(key_unit, 1, 0), jnp.moveaxis(value_act, 1, 0), write_strength, log_decay, keep_heads))
    core = jnp.moveaxis(core, 0, 1)
    scale_rms = jnp.sqrt(lax.optimization_barrier(jnp.mean(core * core, axis=-1, keepdims=True)) + epsilon)
    normed = (core / scale_rms * output_norm_gain * jax.nn.silu(gate_in.astype(jnp.float32))).astype(jnp.bfloat16)
    flat = normed.reshape(normed.shape[0], H * DV)
    return jnp.dot(flat.astype(jnp.float32), output_projection_weight.astype(jnp.float32), preferred_element_type=jnp.float32).astype(jnp.bfloat16)
```

```python
import functools

import jax
import jax.numpy as jnp
from jax import lax
from jax.experimental import pallas as pl
from jax.experimental.pallas import tpu as pltpu
from jax.sharding import PartitionSpec as P

BLOCK = 64
CHUNK = 128
EPSILON = 1e-06
FAR = -1e30
F32 = jnp.float32
BF16 = jnp.bfloat16
NN = (((1,), (0,)), ((), ()))
NT = (((1,), (1,)), ((), ()))
TN = (((0,), (0,)), ((), ()))


def split(a):
    high = a.astype(BF16)
    return high, (a - high.astype(F32)).astype(BF16)


def mul(a, b, dims=NN):
    return lax.dot_general(a, b, dims, preferred_element_type=F32)


def mul_one(a, b):
    return mul(a.astype(BF16), b.astype(BF16))


def mul_split(a, b):
    a_high, a_low = split(a)
    b_high, b_low = split(b)
    return mul(a_high, b_high) + (mul(a_low, b_high) + mul(a_high, b_low))


def indices():
    shape = (CHUNK, CHUNK)
    return (
        lax.broadcasted_iota(jnp.int32, shape, 0),
        lax.broadcasted_iota(jnp.int32, shape, 1),
    )


def running_decay(row_scalars, chunks):
    row, col = indices()
    upto = (row <= col).astype(F32)
    return lax.dot_general(
        row_scalars[:chunks], upto, NN, precision=lax.Precision.HIGHEST, preferred_element_type=F32
    )


def convolve(x_ref, rim_ref, taps_ref, which, head, padded, store):
    length = x_ref.shape[1]
    padded[0:8] = rim_ref[which, head]
    padded[8 : 8 + length] = x_ref[head].astype(F32)
    taps = taps_ref[which, head]
    count = taps.shape[0]
    for c in range(length // CHUNK):
        begin = c * CHUNK + 9 - count
        total = taps[0:1] * padded[begin : begin + CHUNK]
        for j in range(1, count):
            total = total + taps[j : j + 1] * padded[begin + j : begin + j + CHUNK]
        store(c, total / (1.0 + jnp.exp(-total)))


def unit(rows):
    return rows * lax.rsqrt(jnp.sum(rows * rows, axis=-1, keepdims=True) + EPSILON)


def fading_of(cum_col, cum_row, second_resets, row, col):
    apart = ((row // BLOCK) != (col // BLOCK)).astype(jnp.int32) * second_resets
    mask = (row >= col) & (apart == 0)
    return jnp.exp(jnp.where(mask, cum_col - cum_row, FAR))


def lower_inverse(lowers, row, col):
    differ = row ^ col
    eye = (row == col).astype(F32)
    diagonal = [jnp.where(differ < 8, low, 0.0) for low in lowers]
    powers = [d.astype(BF16) for d in diagonal]
    squares = [mul(p, p).astype(BF16) for p in powers]
    inverse = [eye - d for d in diagonal]
    fourths = [mul(s, s).astype(BF16) for s in squares]
    inverse = [x + mul(x.astype(BF16), s) for x, s in zip(inverse, squares)]
    inverse = [x + mul(x.astype(BF16), s) for x, s in zip(inverse, fourths)]
    size = 8
    while size < CHUNK:
        joint = (differ >= size) & (differ < 2 * size)
        rounded = [x.astype(BF16) for x in inverse]
        inner = [
            mul(jnp.where(joint, low, 0.0).astype(BF16), x) for low, x in zip(lowers, rounded)
        ]
        inverse = [
            x - mul(r, i.astype(BF16)) for x, r, i in zip(inverse, rounded, inner)
        ]
        size *= 2
    return inverse


def maps_kernel(
    resets, key_ref, value_ref, rim_ref, taps_ref, scalars_ref,
    unit_ref, solved_ref, starts_ref, map_ref,
    padded, value_s, step_s,
):
    heads, length, depth = key_ref.shape
    chunks = length // CHUNK
    row, col = indices()

    def filters(h, carry):
        def store_key(c, rows):
            unit_ref[h, c * CHUNK : (c + 1) * CHUNK] = unit(rows).astype(BF16)

        def store_value(c, rows):
            value_s[h, c * CHUNK : (c + 1) * CHUNK] = rows.astype(BF16)

        convolve(key_ref, rim_ref, taps_ref, 1, h, padded, store_key)
        convolve(value_ref, rim_ref, taps_ref, 2, h, padded, store_value)
        return carry

    lax.fori_loop(0, heads, filters, 0)

    together = 2

    def solve(p, carry):
        parts = []
        lowers = []
        for k in range(together):
            h = p * together + k
            scalars = scalars_ref[h]
            cum = running_decay(scalars, chunks)
            columns = jnp.transpose(jnp.concatenate([cum, scalars[chunks:]], axis=0))
            for c in range(chunks):
                first, second = resets[2 * c], resets[2 * c + 1]
                cum_col = columns[:, c : c + 1]
                strength = columns[:, chunks + c : chunks + c + 1]
                cum_row = cum[c : c + 1]
                key = unit_ref[h, c * CHUNK : (c + 1) * CHUNK]
                gram = mul(key, key, NT)
                fading = fading_of(cum_col, cum_row, second, row, col)
                lowers.append(jnp.where(row > col, strength * fading * gram, 0.0))
                parts.append((h, c, first, second, cum_col, cum_row, scalars[chunks + c : chunks + c + 1]))
        inverses = lower_inverse(lowers, row, col)
        for (h, c, first, second, cum_col, cum_row, strength_row), inverse in zip(parts, inverses):
            keep_first = (1 - first).astype(F32)
            keep_second = (1 - second).astype(F32)
            keep_both = keep_first * keep_second
            key = unit_ref[h, c * CHUNK : (c + 1) * CHUNK]
            value = value_s[h, c * CHUNK : (c + 1) * CHUNK]
            in_first = lax.broadcasted_iota(jnp.int32, (1, CHUNK), 1) < BLOCK
            growth_row = jnp.exp(cum_row) * jnp.where(in_first, keep_first, keep_both)
            by_strength = inverse * strength_row
            high, low = split(by_strength * growth_row)
            write_keys = mul(high, key) + mul(low, key)
            high, low = split(by_strength)
            local_values = mul(high, value) + mul(low, value)
            solved = jnp.concatenate([write_keys, local_values], axis=1)
            solved_ref[h, c * CHUNK : (c + 1) * CHUNK] = solved
            end = cum_row[:, CHUNK - 1 : CHUNK]
            first_rows = lax.broadcasted_iota(jnp.int32, (CHUNK, 1), 0) < BLOCK
            tail = jnp.exp(end - cum_col) * jnp.where(first_rows, keep_second, 1.0)
            high, low = split(tail * solved)
            product = mul(key, high, TN) + mul(key, low, TN)
            passed = jnp.exp(end) * keep_both
            step_s[h, c, :, :depth] = jnp.where(row == col, passed, 0.0) - product[:, :depth]
            step_s[h, c, :, depth:] = product[:, depth:]
        return carry

    lax.fori_loop(0, heads // together, solve, 0)

    states = [step_s[h, 0] for h in range(heads)]
    for c in range(1, chunks):
        for h in range(heads):
            starts_ref[h, c - 1] = states[h]
            step = step_s[h, c]
            joined = mul_split(step[:, :depth], states[h])
            states[h] = jnp.concatenate(
                [joined[:, :depth], joined[:, depth:] + step[:, depth:]], axis=1
            )
    for h in range(heads):
        map_ref[h] = states[h].astype(BF16)


def reads_kernel(
    resets, query_ref, gate_ref, gain_ref, rim_ref, taps_ref, scalars_ref,
    unit_ref, solved_ref, starts_ref,
    reach_ref, part_ref, gating_ref,
    padded, query_s,
):
    heads, length, depth = query_ref.shape
    chunks = length // CHUNK
    row, col = indices()

    def one_head(h, carry):
        def store_query(c, rows):
            query_s[c * CHUNK : (c + 1) * CHUNK] = (unit(rows) * depth**-0.5).astype(BF16)

        convolve(query_ref, rim_ref, taps_ref, 0, h, padded, store_query)
        scalars = scalars_ref[h]
        cum = running_decay(scalars, chunks)
        columns = jnp.transpose(jnp.concatenate([cum, scalars[chunks:]], axis=0))
        for c in range(chunks):
            here = slice(c * CHUNK, (c + 1) * CHUNK)
            first, second = resets[2 * c], resets[2 * c + 1]
            keep_first = (1 - first).astype(F32)
            keep_both = keep_first * (1 - second).astype(F32)
            cum_col = columns[:, c : c + 1]
            query = query_s[here]
            gram = mul(query, unit_ref[h, here], NT)
            mixing = fading_of(cum_col, cum[c : c + 1], second, row, col) * gram
            own = mul_split(mixing, solved_ref[h, here])
            first_rows = lax.broadcasted_iota(jnp.int32, (CHUNK, 1), 0) < BLOCK
            growth = jnp.exp(cum_col) * jnp.where(first_rows, keep_first, keep_both)
            reach = growth * query.astype(F32) - own[:, :depth]
            part = own[:, depth:]
            if c:
                both = mul_split(reach, starts_ref[h, c - 1])
                reach = both[:, :depth]
                part = part + both[:, depth:]
            reach_ref[h, here] = reach
            part_ref[h, here] = part
            gate = gate_ref[h, here].astype(F32)
            gating_ref[h, here] = gain_ref[...] * (gate / (1.0 + jnp.exp(-gate)))
        return carry

    lax.fori_loop(0, heads, one_head, 0)


def join_kernel(place, count, *refs):
    maps = refs[:count]
    before_ref, whole_ref, ordered = refs[count:]
    heads, depth, _ = before_ref.shape
    me = place[0]
    for k in range(count):
        ordered[partner(me, k, count)] = maps[k][...]
    row, col = indices()
    eye = (row == col).astype(F32)
    states = [jnp.concatenate([eye, jnp.zeros((depth, depth), F32)], axis=1)] * heads
    for lap in range(count):

        @pl.when(lap == me)
        def _():
            for h in range(heads):
                before_ref[h] = states[h]

        for h in range(heads):
            step = ordered[lap, h]
            if lap:
                high, low = split(states[h])
                trans = step[:, :depth]
                joined = mul(trans, high) + mul(trans, low)
                states[h] = jnp.concatenate(
                    [joined[:, :depth], joined[:, depth:] + step[:, depth:].astype(F32)], axis=1
                )
            else:
                states[h] = step.astype(F32)
    for h in range(heads):
        whole_ref[h] = states[h]


def outputs_kernel(arrived_ref, before_ref, reach_ref, part_ref, gating_ref, normed_ref):
    heads, length, depth = reach_ref.shape
    chunks = length // CHUNK
    for h in range(heads):
        before = before_ref[h]
        incoming = mul_split(before[:, :depth], arrived_ref[h].astype(F32)) + before[:, depth:]
        high, low = split(incoming)
        for c in range(chunks):
            here = slice(c * CHUNK, (c + 1) * CHUNK)
            reach_high, reach_low = split(reach_ref[h, here])
            core = part_ref[h, here] + (
                mul(reach_high, high) + (mul(reach_high, low) + mul(reach_low, high))
            )
            scale = lax.rsqrt(jnp.sum(core * core, axis=-1, keepdims=True) / depth + EPSILON)
            normed_ref[here, h * depth : (h + 1) * depth] = (
                core * scale * gating_ref[h, here]
            ).astype(BF16)


def partner(place, k, count):
    if count & (count - 1) == 0:
        return place ^ k
    return lax.rem(place + count - k, count)


def pairs_at(k, count):
    if count & (count - 1) == 0:
        return [(i, i ^ k) for i in range(count)]
    return [(i, (i + k) % count) for i in range(count)]


def from_behind(value, axis, steps):
    count = lax.axis_size(axis)
    return lax.ppermute(value, axis, [(i, i + steps) for i in range(count - steps)])


VMEM = pl.BlockSpec(memory_space=pltpu.VMEM)
SMEM = pl.BlockSpec(memory_space=pltpu.SMEM)
PARAMS = pltpu.CompilerParams(vmem_limit_bytes=48 * 1024 * 1024)


def on_device(
    query_in,
    key_in,
    value_in,
    gate_in,
    write_strength,
    log_decay,
    doc_resets,
    conv_weight,
    output_norm_gain,
    output_projection_weight,
):
    length, heads, depth = query_in.shape
    chunks = length // CHUNK
    taps = conv_weight.shape[1]
    tails = jnp.stack([x[length - taps + 1 :] for x in (query_in, key_in, value_in)])
    rims = from_behind(tails, ("chain", "leaf"), 1)
    rims = jnp.pad(
        jnp.transpose(rims, (0, 2, 1, 3)).astype(F32), ((0, 0), (0, 0), (9 - taps, 0), (0, 0))
    )
    query, key, value, gate = (
        jnp.transpose(x, (1, 0, 2)) for x in (query_in, key_in, value_in, gate_in)
    )
    taps_by_head = jnp.transpose(conv_weight, (0, 2, 1, 3))
    scalars = jnp.concatenate(
        [log_decay.reshape(heads, chunks, CHUNK), write_strength.reshape(heads, chunks, CHUNK)],
        axis=1,
    )
    per_token = jax.ShapeDtypeStruct((heads, length, depth), F32)
    unit_key, solved, starts, own_map = pl.pallas_call(
        maps_kernel,
        out_shape=(
            jax.ShapeDtypeStruct((heads, length, depth), BF16),
            jax.ShapeDtypeStruct((heads, length, 2 * depth), F32),
            jax.ShapeDtypeStruct((heads, chunks - 1, depth, 2 * depth), F32),
            jax.ShapeDtypeStruct((heads, depth, 2 * depth), BF16),
        ),
        in_specs=[SMEM] + [VMEM] * 5,
        out_specs=[VMEM] * 4,
        scratch_shapes=[
            pltpu.VMEM((length + 8, depth), F32),
            pltpu.VMEM((heads, length, depth), BF16),
            pltpu.VMEM((heads, chunks, depth, 2 * depth), F32),
        ],
        compiler_params=PARAMS,
    )(doc_resets, key, value, rims, taps_by_head, scalars)

    leaves = lax.axis_size("leaf")
    maps = [own_map] + [
        lax.ppermute(own_map, "leaf", pairs_at(k, leaves)) for k in range(1, leaves)
    ]
    reach, part, gating = pl.pallas_call(
        reads_kernel,
        out_shape=(per_token, per_token, per_token),
        in_specs=[SMEM] + [VMEM] * 9,
        out_specs=[VMEM] * 3,
        scratch_shapes=[
            pltpu.VMEM((length + 8, depth), F32),
            pltpu.VMEM((length, depth), BF16),
        ],
        compiler_params=PARAMS,
        cost_estimate=pl.CostEstimate(
            flops=6 * 10**9, bytes_accessed=8 * 2**20, transcendentals=10**6
        ),
    )(
        doc_resets, query, gate, output_norm_gain.reshape(1, depth), rims, taps_by_head, scalars,
        unit_key, solved, starts,
    )
    pair = jax.ShapeDtypeStruct((heads, depth, 2 * depth), F32)
    place = lax.axis_index("leaf").astype(jnp.int32).reshape(1)
    before, whole = pl.pallas_call(
        lambda place, *refs: join_kernel(place, leaves, *refs),
        out_shape=(pair, pair),
        in_specs=[SMEM] + [VMEM] * leaves,
        out_specs=[VMEM] * 2,
        scratch_shapes=[pltpu.VMEM((leaves, heads, depth, 2 * depth), BF16)],
        compiler_params=PARAMS,
    )(place, *maps)

    trans, state = whole[..., :depth], whole[..., depth:]
    arrived = from_behind(state.astype(BF16), "chain", 1)
    for _ in range(lax.axis_size("chain") - 2):
        passed = jnp.einsum(
            "hij,hjk->hik", trans, arrived.astype(F32), precision=lax.Precision.HIGHEST
        )
        arrived = from_behind((passed + state).astype(BF16), "chain", 1)

    normed = pl.pallas_call(
        outputs_kernel,
        out_shape=jax.ShapeDtypeStruct((length, heads * depth), BF16),
        in_specs=[VMEM] * 5,
        out_specs=VMEM,
        compiler_params=PARAMS,
    )(arrived, before, reach, part, gating)

    ring = lax.axis_size("head")
    mine = lax.axis_index("head")
    width = heads * depth
    weights = output_projection_weight
    mixed = None
    block = normed
    for k in range(ring):
        owner = lax.rem(mine + ring - k, ring)
        rows = lax.dynamic_slice_in_dim(weights, owner * width, width, 0)
        if k + 1 < ring:
            following = lax.ppermute(block, "head", [(i, (i + 1) % ring) for i in range(ring)])
        term = jnp.dot(block, rows, preferred_element_type=F32)
        mixed = term if mixed is None else mixed + term
        if k + 1 < ring:
            block = following
    return mixed.astype(BF16)


def solution(mesh):
    return jax.shard_map(
        on_device,
        mesh=mesh,
        in_specs=(
            P(("chain", "leaf"), "head", None),
            P(("chain", "leaf"), "head", None),
            P(("chain", "leaf"), "head", None),
            P(("chain", "leaf"), "head", None),
            P("head", ("chain", "leaf")),
            P("head", ("chain", "leaf")),
            P(("chain", "leaf")),
            P(None, None, "head", None),
            P(),
            P(None, "head"),
        ),
        out_specs=P(("chain", "leaf"), "head"),
        check_vma=False,
    )
```

```python
import functools

import jax
import jax.numpy as jnp
from jax import lax
from jax.experimental import pallas as pl
from jax.experimental.pallas import tpu as pltpu
from jax.sharding import PartitionSpec as P

BLOCK = 64
CHUNK = 128
PARTS = 2
EPSILON = 1e-06
FAR = -1e30
F32 = jnp.float32
BF16 = jnp.bfloat16
NN = (((1,), (0,)), ((), ()))
NT = (((1,), (1,)), ((), ()))
TN = (((0,), (0,)), ((), ()))


def split(a):
    high = a.astype(BF16)
    return high, (a - high.astype(F32)).astype(BF16)


def mul(a, b, dims=NN):
    return lax.dot_general(a, b, dims, preferred_element_type=F32)


def mul_one(a, b):
    return mul(a.astype(BF16), b.astype(BF16))


def mul_split(a, b):
    a_high, a_low = split(a)
    b_high, b_low = split(b)
    return mul(a_high, b_high) + (mul(a_low, b_high) + mul(a_high, b_low))


def indices():
    shape = (CHUNK, CHUNK)
    return (
        lax.broadcasted_iota(jnp.int32, shape, 0),
        lax.broadcasted_iota(jnp.int32, shape, 1),
    )


def running_decay(row_scalars, chunks):
    row, col = indices()
    upto = (row <= col).astype(F32)
    return lax.dot_general(
        row_scalars[:chunks], upto, NN, precision=lax.Precision.HIGHEST, preferred_element_type=F32
    )


def convolve(x_ref, rim_ref, taps_ref, which, head, padded, store):
    length = x_ref.shape[1]
    padded[0:8] = rim_ref[which, head]
    padded[8 : 8 + length] = x_ref[head].astype(F32)
    taps = taps_ref[which, head]
    count = taps.shape[0]
    for c in range(length // CHUNK):
        begin = c * CHUNK + 9 - count
        total = taps[0:1] * padded[begin : begin + CHUNK]
        for j in range(1, count):
            total = total + taps[j : j + 1] * padded[begin + j : begin + j + CHUNK]
        store(c, total / (1.0 + jnp.exp(-total)))


def unit(rows):
    return rows * lax.rsqrt(jnp.sum(rows * rows, axis=-1, keepdims=True) + EPSILON)


def fading_of(cum_col, cum_row, second_resets, row, col):
    apart = ((row // BLOCK) != (col // BLOCK)).astype(jnp.int32) * second_resets
    mask = (row >= col) & (apart == 0)
    return jnp.exp(jnp.where(mask, cum_col - cum_row, FAR))


def lower_inverse(lowers, row, col):
    differ = row ^ col
    eye = (row == col).astype(F32)
    diagonal = [jnp.where(differ < 8, low, 0.0) for low in lowers]
    powers = [d.astype(BF16) for d in diagonal]
    squares = [mul(p, p).astype(BF16) for p in powers]
    inverse = [eye - d for d in diagonal]
    fourths = [mul(s, s).astype(BF16) for s in squares]
    inverse = [x + mul(x.astype(BF16), s) for x, s in zip(inverse, squares)]
    inverse = [x + mul(x.astype(BF16), s) for x, s in zip(inverse, fourths)]
    size = 8
    while size < CHUNK:
        joint = (differ >= size) & (differ < 2 * size)
        rounded = [x.astype(BF16) for x in inverse]
        inner = [
            mul(jnp.where(joint, low, 0.0).astype(BF16), x) for low, x in zip(lowers, rounded)
        ]
        inverse = [
            x - mul(r, i.astype(BF16)) for x, r, i in zip(inverse, rounded, inner)
        ]
        size *= 2
    return inverse


def maps_kernel(
    resets, key_ref, value_ref, rim_ref, taps_ref, scalars_ref,
    unit_ref, solved_ref, starts_ref, map_ref,
    padded, value_s, step_s,
):
    heads, length, depth = key_ref.shape
    chunks = length // CHUNK
    row, col = indices()

    def filters(h, carry):
        def store_key(c, rows):
            unit_ref[h, c * CHUNK : (c + 1) * CHUNK] = unit(rows).astype(BF16)

        def store_value(c, rows):
            value_s[h, c * CHUNK : (c + 1) * CHUNK] = rows.astype(BF16)

        convolve(key_ref, rim_ref, taps_ref, 1, h, padded, store_key)
        convolve(value_ref, rim_ref, taps_ref, 2, h, padded, store_value)
        return carry

    lax.fori_loop(0, heads, filters, 0)

    together = 2

    def solve(p, carry):
        parts = []
        lowers = []
        for k in range(together):
            h = p * together + k
            scalars = scalars_ref[h]
            cum = running_decay(scalars, chunks)
            columns = jnp.transpose(jnp.concatenate([cum, scalars[chunks:]], axis=0))
            for c in range(chunks):
                first, second = resets[2 * c], resets[2 * c + 1]
                cum_col = columns[:, c : c + 1]
                strength = columns[:, chunks + c : chunks + c + 1]
                cum_row = cum[c : c + 1]
                key = unit_ref[h, c * CHUNK : (c + 1) * CHUNK]
                gram = mul(key, key, NT)
                fading = fading_of(cum_col, cum_row, second, row, col)
                lowers.append(jnp.where(row > col, strength * fading * gram, 0.0))
                parts.append((h, c, first, second, cum_col, cum_row, scalars[chunks + c : chunks + c + 1]))
        inverses = lower_inverse(lowers, row, col)
        for (h, c, first, second, cum_col, cum_row, strength_row), inverse in zip(parts, inverses):
            keep_first = (1 - first).astype(F32)
            keep_second = (1 - second).astype(F32)
            keep_both = keep_first * keep_second
            key = unit_ref[h, c * CHUNK : (c + 1) * CHUNK]
            value = value_s[h, c * CHUNK : (c + 1) * CHUNK]
            in_first = lax.broadcasted_iota(jnp.int32, (1, CHUNK), 1) < BLOCK
            growth_row = jnp.exp(cum_row) * jnp.where(in_first, keep_first, keep_both)
            by_strength = inverse * strength_row
            high, low = split(by_strength * growth_row)
            write_keys = mul(high, key) + mul(low, key)
            high, low = split(by_strength)
            local_values = mul(high, value) + mul(low, value)
            solved = jnp.concatenate([write_keys, local_values], axis=1)
            solved_ref[h, c * CHUNK : (c + 1) * CHUNK] = solved
            end = cum_row[:, CHUNK - 1 : CHUNK]
            first_rows = lax.broadcasted_iota(jnp.int32, (CHUNK, 1), 0) < BLOCK
            tail = jnp.exp(end - cum_col) * jnp.where(first_rows, keep_second, 1.0)
            high, low = split(tail * solved)
            product = mul(key, high, TN) + mul(key, low, TN)
            passed = jnp.exp(end) * keep_both
            step_s[h, c, :, :depth] = jnp.where(row == col, passed, 0.0) - product[:, :depth]
            step_s[h, c, :, depth:] = product[:, depth:]
        return carry

    lax.fori_loop(0, heads // together, solve, 0)

    states = [step_s[h, 0] for h in range(heads)]
    for c in range(1, chunks):
        for h in range(heads):
            starts_ref[h, c - 1] = states[h]
            step = step_s[h, c]
            joined = mul_split(step[:, :depth], states[h])
            states[h] = jnp.concatenate(
                [joined[:, :depth], joined[:, depth:] + step[:, depth:]], axis=1
            )
    for h in range(heads):
        map_ref[h] = states[h].astype(BF16)


def reads_kernel(
    resets, query_ref, gate_ref, gain_ref, rim_ref, taps_ref, scalars_ref,
    unit_ref, solved_ref, starts_ref,
    reach_ref, part_ref, gating_ref,
    padded, query_s,
):
    heads, length, depth = query_ref.shape
    chunks = length // CHUNK
    row, col = indices()

    def one_head(h, carry):
        def store_query(c, rows):
            query_s[c * CHUNK : (c + 1) * CHUNK] = (unit(rows) * depth**-0.5).astype(BF16)

        convolve(query_ref, rim_ref, taps_ref, 0, h, padded, store_query)
        scalars = scalars_ref[h]
        cum = running_decay(scalars, chunks)
        columns = jnp.transpose(jnp.concatenate([cum, scalars[chunks:]], axis=0))
        for c in range(chunks):
            here = slice(c * CHUNK, (c + 1) * CHUNK)
            first, second = resets[2 * c], resets[2 * c + 1]
            keep_first = (1 - first).astype(F32)
            keep_both = keep_first * (1 - second).astype(F32)
            cum_col = columns[:, c : c + 1]
            query = query_s[here]
            gram = mul(query, unit_ref[h, here], NT)
            mixing = fading_of(cum_col, cum[c : c + 1], second, row, col) * gram
            own = mul_split(mixing, solved_ref[h, here])
            first_rows = lax.broadcasted_iota(jnp.int32, (CHUNK, 1), 0) < BLOCK
            growth = jnp.exp(cum_col) * jnp.where(first_rows, keep_first, keep_both)
            reach = growth * query.astype(F32) - own[:, :depth]
            part = own[:, depth:]
            if c:
                both = mul_split(reach, starts_ref[h, c - 1])
                reach = both[:, :depth]
                part = part + both[:, depth:]
            reach_ref[h, here] = reach
            part_ref[h, here] = part
            gate = gate_ref[h, here].astype(F32)
            gating_ref[h, here] = gain_ref[...] * (gate / (1.0 + jnp.exp(-gate)))
        return carry

    lax.fori_loop(0, heads, one_head, 0)


def join_kernel(place, count, *refs):
    maps = refs[:count]
    before_ref, whole_ref, ordered = refs[count:]
    heads, depth, _ = before_ref.shape
    me = place[0]
    for k in range(count):
        ordered[partner(me, k, count)] = maps[k][...]
    row, col = indices()
    eye = (row == col).astype(F32)
    states = [jnp.concatenate([eye, jnp.zeros((depth, depth), F32)], axis=1)] * heads
    for lap in range(count):

        @pl.when(lap == me)
        def _():
            for h in range(heads):
                before_ref[h] = states[h]

        for h in range(heads):
            step = ordered[lap, h]
            if lap:
                high, low = split(states[h])
                trans = step[:, :depth]
                joined = mul(trans, high) + mul(trans, low)
                states[h] = jnp.concatenate(
                    [joined[:, :depth], joined[:, depth:] + step[:, depth:].astype(F32)], axis=1
                )
            else:
                states[h] = step.astype(F32)
    for h in range(heads):
        whole_ref[h] = states[h]


def outputs_kernel(begin, arrived_ref, before_ref, reach_ref, part_ref, gating_ref, normed_ref):
    heads, _, depth = reach_ref.shape
    chunks = normed_ref.shape[0] // CHUNK
    for h in range(heads):
        before = before_ref[h]
        incoming = mul_split(before[:, :depth], arrived_ref[h].astype(F32)) + before[:, depth:]
        high, low = split(incoming)
        for c in range(chunks):
            here = slice(begin + c * CHUNK, begin + (c + 1) * CHUNK)
            reach_high, reach_low = split(reach_ref[h, here])
            core = part_ref[h, here] + (
                mul(reach_high, high) + (mul(reach_high, low) + mul(reach_low, high))
            )
            scale = lax.rsqrt(jnp.sum(core * core, axis=-1, keepdims=True) / depth + EPSILON)
            normed_ref[c * CHUNK : (c + 1) * CHUNK, h * depth : (h + 1) * depth] = (
                core * scale * gating_ref[h, here]
            ).astype(BF16)


def partner(place, k, count):
    if count & (count - 1) == 0:
        return place ^ k
    return lax.rem(place + count - k, count)


def pairs_at(k, count):
    if count & (count - 1) == 0:
        return [(i, i ^ k) for i in range(count)]
    return [(i, (i + k) % count) for i in range(count)]


def from_behind(value, axis, steps):
    count = lax.axis_size(axis)
    return lax.ppermute(value, axis, [(i, i + steps) for i in range(count - steps)])


VMEM = pl.BlockSpec(memory_space=pltpu.VMEM)
SMEM = pl.BlockSpec(memory_space=pltpu.SMEM)
PARAMS = pltpu.CompilerParams(vmem_limit_bytes=20 * 1024 * 1024)


def on_device(
    query_in,
    key_in,
    value_in,
    gate_in,
    write_strength,
    log_decay,
    doc_resets,
    conv_weight,
    output_norm_gain,
    output_projection_weight,
):
    length, heads, depth = query_in.shape
    chunks = length // CHUNK
    taps = conv_weight.shape[1]
    tails = jnp.stack([x[length - taps + 1 :] for x in (query_in, key_in, value_in)])
    rims = from_behind(tails, ("chain", "leaf"), 1)
    rims = jnp.pad(
        jnp.transpose(rims, (0, 2, 1, 3)).astype(F32), ((0, 0), (0, 0), (9 - taps, 0), (0, 0))
    )
    query, key, value, gate = (
        jnp.transpose(x, (1, 0, 2)) for x in (query_in, key_in, value_in, gate_in)
    )
    taps_by_head = jnp.transpose(conv_weight, (0, 2, 1, 3))
    scalars = jnp.concatenate(
        [log_decay.reshape(heads, chunks, CHUNK), write_strength.reshape(heads, chunks, CHUNK)],
        axis=1,
    )
    per_token = jax.ShapeDtypeStruct((heads, length, depth), F32)
    unit_key, solved, starts, own_map = pl.pallas_call(
        maps_kernel,
        out_shape=(
            jax.ShapeDtypeStruct((heads, length, depth), BF16),
            jax.ShapeDtypeStruct((heads, length, 2 * depth), F32),
            jax.ShapeDtypeStruct((heads, chunks - 1, depth, 2 * depth), F32),
            jax.ShapeDtypeStruct((heads, depth, 2 * depth), BF16),
        ),
        in_specs=[SMEM] + [VMEM] * 5,
        out_specs=[VMEM] * 4,
        scratch_shapes=[
            pltpu.VMEM((length + 8, depth), F32),
            pltpu.VMEM((heads, length, depth), BF16),
            pltpu.VMEM((heads, chunks, depth, 2 * depth), F32),
        ],
        compiler_params=PARAMS,
    )(doc_resets, key, value, rims, taps_by_head, scalars)

    leaves = lax.axis_size("leaf")
    maps = [own_map] + [
        lax.ppermute(own_map, "leaf", pairs_at(k, leaves)) for k in range(1, leaves)
    ]
    reach, part, gating = pl.pallas_call(
        reads_kernel,
        out_shape=(per_token, per_token, per_token),
        in_specs=[SMEM] + [VMEM] * 9,
        out_specs=[VMEM] * 3,
        scratch_shapes=[
            pltpu.VMEM((length + 8, depth), F32),
            pltpu.VMEM((length, depth), BF16),
        ],
        compiler_params=PARAMS,
        cost_estimate=pl.CostEstimate(
            flops=6 * 10**9, bytes_accessed=8 * 2**20, transcendentals=10**6
        ),
    )(
        doc_resets, query, gate, output_norm_gain.reshape(1, depth), rims, taps_by_head, scalars,
        unit_key, solved, starts,
    )
    maps, reach, part, gating = lax.optimization_barrier((maps, reach, part, gating))
    pair = jax.ShapeDtypeStruct((heads, depth, 2 * depth), F32)
    place = lax.axis_index("leaf").astype(jnp.int32).reshape(1)
    before, whole = pl.pallas_call(
        lambda place, *refs: join_kernel(place, leaves, *refs),
        out_shape=(pair, pair),
        in_specs=[SMEM] + [VMEM] * leaves,
        out_specs=[VMEM] * 2,
        scratch_shapes=[pltpu.VMEM((leaves, heads, depth, 2 * depth), BF16)],
        compiler_params=PARAMS,
    )(place, *maps)

    trans, state = whole[..., :depth], whole[..., depth:]
    arrived = from_behind(state.astype(BF16), "chain", 1)
    for _ in range(lax.axis_size("chain") - 2):
        passed = jnp.einsum(
            "hij,hjk->hik", trans, arrived.astype(F32), precision=lax.Precision.HIGHEST
        )
        arrived = from_behind((passed + state).astype(BF16), "chain", 1)

    ring = lax.axis_size("head")
    mine = lax.axis_index("head")
    width = heads * depth
    part_rows = length // PARTS
    blocks = [
        pl.pallas_call(
            functools.partial(outputs_kernel, p * part_rows),
            out_shape=jax.ShapeDtypeStruct((part_rows, width), BF16),
            in_specs=[VMEM] * 5,
            out_specs=VMEM,
            compiler_params=PARAMS,
        )(arrived, before, reach, part, gating)
        for p in range(PARTS)
    ]
    mixed = [None] * PARTS
    around = [(i, (i + 1) % ring) for i in range(ring)]
    for k in range(ring):
        owner = lax.rem(mine + ring - k, ring)
        rows = lax.dynamic_slice_in_dim(output_projection_weight, owner * width, width, 0)
        if k + 1 < ring:
            following = [lax.ppermute(block, "head", around) for block in blocks]
        for p, block in enumerate(blocks):
            term = jnp.dot(block, rows, preferred_element_type=F32)
            mixed[p] = term if mixed[p] is None else mixed[p] + term
        if k + 1 < ring:
            blocks = following
    return jnp.concatenate([m.astype(BF16) for m in mixed], axis=0)


def solution(mesh):
    return jax.shard_map(
        on_device,
        mesh=mesh,
        in_specs=(
            P(("chain", "leaf"), "head", None),
            P(("chain", "leaf"), "head", None),
            P(("chain", "leaf"), "head", None),
            P(("chain", "leaf"), "head", None),
            P("head", ("chain", "leaf")),
            P("head", ("chain", "leaf")),
            P(("chain", "leaf")),
            P(None, None, "head", None),
            P(),
            P(None, "head"),
        ),
        out_specs=P(("chain", "leaf"), "head"),
        check_vma=False,
    )
```

```python
import functools

import jax
import jax.numpy as jnp
from jax import lax
from jax.experimental import pallas as pl
from jax.experimental.pallas import tpu as pltpu
from jax.sharding import PartitionSpec as P

BLOCK = 64
CHUNK = 128
GROUPS = 2
RIM = 8
EPSILON = 1e-06
FAR = -1e30
F32 = jnp.float32
BF16 = jnp.bfloat16
NN = (((1,), (0,)), ((), ()))
NT = (((1,), (1,)), ((), ()))
TN = (((0,), (0,)), ((), ()))


def split(a):
    high = a.astype(BF16)
    return high, (a - high.astype(F32)).astype(BF16)


def mul(a, b, dims=NN):
    return lax.dot_general(a, b, dims, preferred_element_type=F32)


def mul_split(a, b):
    a_high, a_low = split(a)
    b_high, b_low = split(b)
    return mul(a_high, b_high) + (mul(a_low, b_high) + mul(a_high, b_low))


def rows_of(c):
    return slice(c * CHUNK, (c + 1) * CHUNK)


def indices():
    shape = (CHUNK, CHUNK)
    return (
        lax.broadcasted_iota(jnp.int32, shape, 0),
        lax.broadcasted_iota(jnp.int32, shape, 1),
    )


def token_scalars(decay_ref, strength_ref, c):
    row, col = indices()
    cum = lax.dot_general(
        decay_ref[:, rows_of(c)],
        (row <= col).astype(F32),
        NN,
        precision=lax.Precision.HIGHEST,
        preferred_element_type=F32,
    )
    strength = strength_ref[:, rows_of(c)]
    stacked = [cum, strength]
    missing = 8 - 2 * cum.shape[0]
    if missing > 0:
        stacked.append(jnp.zeros((missing, CHUNK), F32))
    return cum, strength, jnp.transpose(jnp.concatenate(stacked, axis=0))


def convolve(x_ref, rims, taps_ref, which, head, padded, store):
    length = x_ref.shape[1]
    padded[0:RIM] = rims[which * RIM : (which + 1) * RIM, head, :]
    padded[RIM : RIM + length] = x_ref[head].astype(F32)
    count = taps_ref.shape[1]
    taps = [taps_ref[which, j, head : head + 1, :] for j in range(count)]
    for c in range(length // CHUNK):
        begin = c * CHUNK + RIM + 1 - count
        total = taps[0] * padded[begin : begin + CHUNK]
        for j in range(1, count):
            total = total + taps[j] * padded[begin + j : begin + j + CHUNK]
        store(c, total / (1.0 + jnp.exp(-total)))


def unit(rows):
    return rows * lax.rsqrt(jnp.sum(rows * rows, axis=-1, keepdims=True) + EPSILON)


def same_document(second_resets, row, col):
    return ((row // BLOCK) - (col // BLOCK)) * second_resets == 0


def lower_inverse(lowers, row, col):
    differ = row ^ col
    eye = (row == col).astype(F32)
    in_block = (differ < 8).astype(F32)
    diagonal = [low * in_block for low in lowers]
    rounded_lowers = [low.astype(BF16) for low in lowers]
    powers = [d.astype(BF16) for d in diagonal]
    squares = [mul(p, p).astype(BF16) for p in powers]
    inverse = [eye - d for d in diagonal]
    fourths = [mul(s, s).astype(BF16) for s in squares]
    inverse = [x + mul(x.astype(BF16), s) for x, s in zip(inverse, squares)]
    inverse = [x + mul(x.astype(BF16), s) for x, s in zip(inverse, fourths)]
    size = 8
    while size < CHUNK:
        joint = ((differ >= size) & (differ < 2 * size)).astype(F32).astype(BF16)
        rounded = [x.astype(BF16) for x in inverse]
        inner = [mul(low * joint, x).astype(BF16) for low, x in zip(rounded_lowers, rounded)]
        inverse = [x - mul(r, i) for x, r, i in zip(inverse, rounded, inner)]
        size *= 2
    return inverse


def rims_kernel(*refs):
    *inputs, packed_ref = refs
    for i, x_ref in enumerate(inputs):
        packed_ref[i * RIM : (i + 1) * RIM] = x_ref[...]


def maps_kernel(
    base, resets, key_ref, value_ref, rim_ref, taps_ref, decay_ref, strength_ref,
    unit_ref, solved_ref, starts_ref, map_ref,
    rims, padded, value_s, step_s,
):
    heads, length, depth = unit_ref.shape
    chunks = length // CHUNK
    total_heads = decay_ref.shape[0]
    row, col = indices()
    rims[...] = rim_ref[...].astype(F32)
    for g in range(heads):

        def store_key(c, rows):
            unit_ref[g, rows_of(c)] = unit(rows).astype(BF16)

        def store_value(c, rows):
            value_s[g, rows_of(c)] = rows.astype(BF16)

        convolve(key_ref, rims, taps_ref, 1, base + g, padded, store_key)
        convolve(value_ref, rims, taps_ref, 2, base + g, padded, store_value)

    parts = []
    lowers = []
    for c in range(chunks):
        cum, strengths, columns = token_scalars(decay_ref, strength_ref, c)
        first, second = resets[2 * c], resets[2 * c + 1]
        strictly = (row > col) & same_document(second, row, col)
        for g in range(heads):
            h = base + g
            cum_col = columns[:, h : h + 1]
            cum_row = cum[h : h + 1]
            key = unit_ref[g, rows_of(c)]
            fading = jnp.exp(jnp.where(strictly, cum_col - cum_row, FAR))
            strength_col = columns[:, total_heads + h : total_heads + h + 1]
            lowers.append(strength_col * fading * mul(key, key, NT))
            parts.append((g, c, first, second, cum_col, cum_row, strengths[h : h + 1]))
    inverses = lower_inverse(lowers, row, col)
    in_first = lax.broadcasted_iota(jnp.int32, (1, CHUNK), 1) < BLOCK
    first_rows = lax.broadcasted_iota(jnp.int32, (CHUNK, 1), 0) < BLOCK
    for (g, c, first, second, cum_col, cum_row, strength_row), inverse in zip(parts, inverses):
        keep_first = (1 - first).astype(F32)
        keep_second = (1 - second).astype(F32)
        keep_both = keep_first * keep_second
        key = unit_ref[g, rows_of(c)]
        value = value_s[g, rows_of(c)]
        growth_row = jnp.exp(cum_row) * jnp.where(in_first, keep_first, keep_both)
        by_strength = inverse * strength_row
        high, low = split(by_strength * growth_row)
        write_keys = mul(high, key) + mul(low, key)
        high, low = split(by_strength)
        local_values = mul(high, value) + mul(low, value)
        solved = jnp.concatenate([write_keys, local_values], axis=1)
        solved_ref[g, rows_of(c)] = solved
        end = cum_row[:, CHUNK - 1 : CHUNK]
        tail = jnp.exp(end - cum_col) * jnp.where(first_rows, keep_second, 1.0)
        high, low = split(tail * solved)
        product = mul(key, high, TN) + mul(key, low, TN)
        passed = jnp.exp(end) * keep_both
        step_s[g, c, :, :depth] = jnp.where(row == col, passed, 0.0) - product[:, :depth]
        step_s[g, c, :, depth:] = product[:, depth:]

    states = [step_s[g, 0] for g in range(heads)]
    for c in range(1, chunks):
        for g in range(heads):
            starts_ref[g, c - 1] = states[g]
            step = step_s[g, c]
            joined = mul_split(step[:, :depth], states[g])
            states[g] = jnp.concatenate(
                [joined[:, :depth], joined[:, depth:] + step[:, depth:]], axis=1
            )
    for g in range(heads):
        map_ref[g] = states[g].astype(BF16)


def reads_kernel(
    base, resets, query_ref, gate_ref, gain_ref, rim_ref, taps_ref, decay_ref, strength_ref,
    unit_ref, solved_ref, starts_ref,
    reach_ref, part_ref, gating_ref,
    rims, padded, query_s,
):
    heads, length, depth = unit_ref.shape
    chunks = length // CHUNK
    row, col = indices()
    first_rows = lax.broadcasted_iota(jnp.int32, (CHUNK, 1), 0) < BLOCK
    rims[...] = rim_ref[...].astype(F32)
    for g in range(heads):

        def store_query(c, rows):
            query_s[g, rows_of(c)] = (unit(rows) * depth**-0.5).astype(BF16)

        convolve(query_ref, rims, taps_ref, 0, base + g, padded, store_query)

    for c in range(chunks):
        here = rows_of(c)
        cum, _, columns = token_scalars(decay_ref, strength_ref, c)
        first, second = resets[2 * c], resets[2 * c + 1]
        keep_first = (1 - first).astype(F32)
        keep_both = keep_first * (1 - second).astype(F32)
        upto = (row >= col) & same_document(second, row, col)
        for g in range(heads):
            h = base + g
            cum_col = columns[:, h : h + 1]
            query = query_s[g, here]
            fading = jnp.exp(jnp.where(upto, cum_col - cum[h : h + 1], FAR))
            mixing = fading * mul(query, unit_ref[g, here], NT)
            own = mul_split(mixing, solved_ref[g, here])
            growth = jnp.exp(cum_col) * jnp.where(first_rows, keep_first, keep_both)
            reach = growth * query.astype(F32) - own[:, :depth]
            part = own[:, depth:]
            if c:
                both = mul_split(reach, starts_ref[g, c - 1])
                reach = both[:, :depth]
                part = part + both[:, depth:]
            reach_ref[g, here] = reach
            part_ref[g, here] = part
            gate = gate_ref[h, here].astype(F32)
            gating_ref[g, here] = gain_ref[...] * (gate / (1.0 + jnp.exp(-gate)))


def partner(place, k, count):
    if count & (count - 1) == 0:
        return place ^ k
    return lax.rem(place + count - k, count)


def pairs_at(k, count):
    if count & (count - 1) == 0:
        return [(i, i ^ k) for i in range(count)]
    return [(i, (i + k) % count) for i in range(count)]


def join_kernel(count, place, *refs):
    maps = refs[:count]
    before_ref, state_ref, whole_ref, ordered = refs[count:]
    heads, depth, _ = before_ref.shape
    me = place[0]
    for k in range(count):
        ordered[partner(me, k, count)] = maps[k][...]
    row, col = indices()
    eye = (row == col).astype(F32)
    states = [jnp.concatenate([eye, jnp.zeros((depth, depth), F32)], axis=1)] * heads
    for lap in range(count):

        @pl.when(lap == me)
        def _():
            for h in range(heads):
                before_ref[h] = states[h]

        for h in range(heads):
            step = ordered[lap, h]
            if lap:
                high, low = split(states[h])
                trans = step[:, :depth]
                joined = mul(trans, high) + mul(trans, low)
                states[h] = jnp.concatenate(
                    [joined[:, :depth], joined[:, depth:] + step[:, depth:].astype(F32)], axis=1
                )
            else:
                states[h] = step.astype(F32)
    for h in range(heads):
        whole_ref[h] = states[h]
        state_ref[h] = states[h][:, depth:].astype(BF16)


def outputs_kernel(arrived_ref, before_ref, reach_ref, part_ref, gating_ref, normed_ref):
    heads, length, depth = reach_ref.shape
    for g in range(heads):
        before = before_ref[g]
        incoming = mul_split(before[:, :depth], arrived_ref[g].astype(F32)) + before[:, depth:]
        high, low = split(incoming)
        for c in range(length // CHUNK):
            here = rows_of(c)
            reach_high, reach_low = split(reach_ref[g, here])
            core = part_ref[g, here] + (
                mul(reach_high, high) + (mul(reach_high, low) + mul(reach_low, high))
            )
            scale = lax.rsqrt(jnp.sum(core * core, axis=-1, keepdims=True) / depth + EPSILON)
            normed_ref[here, g * depth : (g + 1) * depth] = (
                core * scale * gating_ref[g, here]
            ).astype(BF16)


def projected_kernel(section, total_ref, block_ref, weights_ref, out_ref):
    out_ref[...] = total_ref[...] + mul(block_ref[...], weights_ref[...])


def from_behind(value, axis, steps):
    count = lax.axis_size(axis)
    return lax.ppermute(value, axis, [(i, i + steps) for i in range(count - steps)])


VMEM = pl.BlockSpec(memory_space=pltpu.VMEM)
SMEM = pl.BlockSpec(memory_space=pltpu.SMEM)
PARAMS = pltpu.CompilerParams(vmem_limit_bytes=16 * 1024 * 1024)


def pack_rims(inputs):
    length, heads, depth = inputs[0].shape
    last = pl.BlockSpec((RIM, heads, depth), lambda i: (length // RIM - 1, 0, 0))
    packed = (len(inputs) * RIM, heads, depth)
    return pl.pallas_call(
        rims_kernel,
        grid=(1,),
        out_shape=jax.ShapeDtypeStruct(packed, BF16),
        in_specs=[last] * len(inputs),
        out_specs=pl.BlockSpec(packed, lambda i: (0, 0, 0)),
    )(*inputs)


def maps_of(base, heads, resets, key, value, rims, taps, decay, strength):
    _, length, depth = key.shape
    chunks = length // CHUNK
    return pl.pallas_call(
        functools.partial(maps_kernel, base),
        out_shape=(
            jax.ShapeDtypeStruct((heads, length, depth), BF16),
            jax.ShapeDtypeStruct((heads, length, 2 * depth), F32),
            jax.ShapeDtypeStruct((heads, chunks - 1, depth, 2 * depth), F32),
            jax.ShapeDtypeStruct((heads, depth, 2 * depth), BF16),
        ),
        in_specs=[SMEM] + [VMEM] * 6,
        out_specs=[VMEM] * 4,
        scratch_shapes=[
            pltpu.VMEM(rims.shape, F32),
            pltpu.VMEM((length + RIM, depth), F32),
            pltpu.VMEM((heads, length, depth), BF16),
            pltpu.VMEM((heads, chunks, depth, 2 * depth), F32),
        ],
        compiler_params=PARAMS,
        cost_estimate=pl.CostEstimate(
            flops=5 * 10**9, bytes_accessed=4 * 2**20, transcendentals=10**6
        ),
    )(resets, key, value, rims, taps, decay, strength)


def reads_of(base, heads, resets, query, gate, gain, rims, taps, decay, strength, made):
    _, length, depth = query.shape
    per_token = jax.ShapeDtypeStruct((heads, length, depth), F32)
    return pl.pallas_call(
        functools.partial(reads_kernel, base),
        out_shape=(per_token, per_token, per_token),
        in_specs=[SMEM] + [VMEM] * 10,
        out_specs=[VMEM] * 3,
        scratch_shapes=[
            pltpu.VMEM(rims.shape, F32),
            pltpu.VMEM((length + RIM, depth), F32),
            pltpu.VMEM((heads, length, depth), BF16),
        ],
        compiler_params=PARAMS,
        cost_estimate=pl.CostEstimate(
            flops=3 * 10**9, bytes_accessed=4 * 2**20, transcendentals=10**6
        ),
    )(resets, query, gate, gain, rims, taps, decay, strength, *made)


def join(place, maps):
    count = len(maps)
    heads, depth, _ = maps[0].shape
    pair = jax.ShapeDtypeStruct((heads, depth, 2 * depth), F32)
    return pl.pallas_call(
        functools.partial(join_kernel, count),
        out_shape=(pair, jax.ShapeDtypeStruct((heads, depth, depth), BF16), pair),
        in_specs=[SMEM] + [VMEM] * count,
        out_specs=[VMEM] * 3,
        scratch_shapes=[pltpu.VMEM((count, heads, depth, 2 * depth), BF16)],
        compiler_params=PARAMS,
    )(place, *maps)


def outputs_of(arrived, before, reads):
    heads, length, depth = reads[0].shape
    return pl.pallas_call(
        outputs_kernel,
        out_shape=jax.ShapeDtypeStruct((length, heads * depth), BF16),
        in_specs=[VMEM] * 5,
        out_specs=VMEM,
        compiler_params=PARAMS,
    )(arrived, before, *reads)


def projected(section, total, block, weights):
    length, columns = total.shape
    width = block.shape[1]
    return pl.pallas_call(
        projected_kernel,
        out_shape=jax.ShapeDtypeStruct(total.shape, F32),
        grid_spec=pltpu.PrefetchScalarGridSpec(
            num_scalar_prefetch=1,
            grid=(length // CHUNK,),
            in_specs=[
                pl.BlockSpec((CHUNK, columns), lambda i, s: (i, 0)),
                pl.BlockSpec((CHUNK, width), lambda i, s: (i, 0)),
                pl.BlockSpec((width, columns), lambda i, s: (s[0], 0)),
            ],
            out_specs=pl.BlockSpec((CHUNK, columns), lambda i, s: (i, 0)),
        ),
        compiler_params=PARAMS,
    )(section.astype(jnp.int32).reshape(1), total, block, weights)


def after(first, *values):
    return lax.optimization_barrier((first, *values))[1:]


def on_device(
    query_in,
    key_in,
    value_in,
    gate_in,
    write_strength,
    log_decay,
    doc_resets,
    conv_weight,
    output_norm_gain,
    output_projection_weight,
):
    length, heads, depth = query_in.shape
    size = heads // GROUPS
    rims = from_behind(pack_rims((query_in, key_in, value_in)), ("chain", "leaf"), 1)
    key, value = (jnp.transpose(x, (1, 0, 2)) for x in (key_in, value_in))
    gain = output_norm_gain.reshape(1, depth)
    leaves = lax.axis_size("leaf")
    place = lax.axis_index("leaf").astype(jnp.int32).reshape(1)

    made = []
    exchanged = []
    for g in range(GROUPS):
        unit_key, solved, starts, own_map = maps_of(
            g * size, size, doc_resets, key, value, rims, conv_weight, log_decay, write_strength
        )
        made.append((unit_key, solved, starts))
        exchanged.append(
            [own_map]
            + [lax.ppermute(own_map, "leaf", pairs_at(k, leaves)) for k in range(1, leaves)]
        )
        key, value = after(own_map, key, value)
        if g == 0:
            query_in, gate_in = after(own_map, query_in, gate_in)
    query, gate = (jnp.transpose(x, (1, 0, 2)) for x in (query_in, gate_in))

    blocks = []
    for g in range(GROUPS):
        reads = reads_of(
            g * size, size, doc_resets, query, gate, gain, rims, conv_weight, log_decay,
            write_strength, made[g],
        )
        maps, reads = lax.optimization_barrier((exchanged[g], reads))
        before, state, whole = join(place, maps)
        query, gate = after(state, query, gate)
        arrived = from_behind(state, "chain", 1)
        for _ in range(lax.axis_size("chain") - 2):
            passed = jnp.einsum(
                "hij,hjk->hik",
                whole[..., :depth],
                arrived.astype(F32),
                precision=lax.Precision.HIGHEST,
            )
            arrived = from_behind((passed + whole[..., depth:]).astype(BF16), "chain", 1)
        blocks.append(outputs_of(arrived, before, reads))

    ring = lax.axis_size("head")
    mine = lax.axis_index("head")
    width = size * depth
    around = [(i, (i + 1) % ring) for i in range(ring)]
    mixed = None
    for k in range(ring):
        owner = lax.rem(mine + ring - k, ring)
        if k + 1 < ring:
            following = [lax.ppermute(block, "head", around) for block in blocks]
        for g, block in enumerate(blocks):
            section = owner * GROUPS + g
            if k + 1 == ring and g + 2 == GROUPS:
                mixed = projected(section, mixed, block, output_projection_weight)
                continue
            rows = lax.dynamic_slice_in_dim(output_projection_weight, section * width, width, 0)
            term = jnp.dot(block, rows, preferred_element_type=F32)
            mixed = term if mixed is None else mixed + term
        if k + 1 < ring:
            blocks = following
    return mixed.astype(BF16)


def solution(mesh):
    return jax.shard_map(
        on_device,
        mesh=mesh,
        in_specs=(
            P(("chain", "leaf"), "head", None),
            P(("chain", "leaf"), "head", None),
            P(("chain", "leaf"), "head", None),
            P(("chain", "leaf"), "head", None),
            P("head", ("chain", "leaf")),
            P("head", ("chain", "leaf")),
            P(("chain", "leaf")),
            P(None, None, "head", None),
            P(),
            P(None, "head"),
        ),
        out_specs=P(("chain", "leaf"), "head"),
        check_vma=False,
    )
```

```python
import functools

import jax
import jax.numpy as jnp
from jax import lax
from jax.experimental import pallas as pl
from jax.experimental.pallas import tpu as pltpu
from jax.sharding import PartitionSpec as P

BLOCK = 64
CHUNK = 128
GROUPS = 2
RIM = 8
EPSILON = 1e-06
FAR = -1e30
F32 = jnp.float32
BF16 = jnp.bfloat16
NN = (((1,), (0,)), ((), ()))
NT = (((1,), (1,)), ((), ()))
TN = (((0,), (0,)), ((), ()))


def split(a):
    high = a.astype(BF16)
    return high, (a - high.astype(F32)).astype(BF16)


def mul(a, b, dims=NN):
    return lax.dot_general(a, b, dims, preferred_element_type=F32)


def mul_split(a, b):
    a_high, a_low = split(a)
    b_high, b_low = split(b)
    return mul(a_high, b_high) + (mul(a_low, b_high) + mul(a_high, b_low))


def rows_of(c):
    return slice(c * CHUNK, (c + 1) * CHUNK)


def indices():
    shape = (CHUNK, CHUNK)
    return (
        lax.broadcasted_iota(jnp.int32, shape, 0),
        lax.broadcasted_iota(jnp.int32, shape, 1),
    )


def token_scalars(decay_ref, strength_ref, c):
    row, col = indices()
    cum = lax.dot_general(
        decay_ref[:, rows_of(c)],
        (row <= col).astype(F32),
        NN,
        precision=lax.Precision.HIGHEST,
        preferred_element_type=F32,
    )
    strength = strength_ref[:, rows_of(c)]
    stacked = [cum, strength]
    missing = 8 - 2 * cum.shape[0]
    if missing > 0:
        stacked.append(jnp.zeros((missing, CHUNK), F32))
    return cum, strength, jnp.transpose(jnp.concatenate(stacked, axis=0))


def convolve(x_ref, rims, taps_ref, which, head, padded, store):
    length = x_ref.shape[1]
    padded[0:RIM] = rims[which * RIM : (which + 1) * RIM, head, :]
    padded[RIM : RIM + length] = x_ref[head].astype(F32)
    count = taps_ref.shape[1]
    taps = [taps_ref[which, j, head : head + 1, :] for j in range(count)]
    for c in range(length // CHUNK):
        begin = c * CHUNK + RIM + 1 - count
        total = taps[0] * padded[begin : begin + CHUNK]
        for j in range(1, count):
            total = total + taps[j] * padded[begin + j : begin + j + CHUNK]
        store(c, total / (1.0 + jnp.exp(-total)))


def unit(rows):
    return rows * lax.rsqrt(jnp.sum(rows * rows, axis=-1, keepdims=True) + EPSILON)


def same_document(second_resets, row, col):
    return ((row // BLOCK) - (col // BLOCK)) * second_resets == 0


def lower_inverse(lowers, row, col):
    differ = row ^ col
    eye = (row == col).astype(F32)
    in_block = (differ < 8).astype(F32)
    diagonal = [low * in_block for low in lowers]
    rounded_lowers = [low.astype(BF16) for low in lowers]
    powers = [d.astype(BF16) for d in diagonal]
    squares = [mul(p, p).astype(BF16) for p in powers]
    inverse = [eye - d for d in diagonal]
    fourths = [mul(s, s).astype(BF16) for s in squares]
    inverse = [x + mul(x.astype(BF16), s) for x, s in zip(inverse, squares)]
    inverse = [x + mul(x.astype(BF16), s) for x, s in zip(inverse, fourths)]
    size = 8
    while size < CHUNK:
        joint = ((differ >= size) & (differ < 2 * size)).astype(F32).astype(BF16)
        rounded = [x.astype(BF16) for x in inverse]
        inner = [mul(low * joint, x).astype(BF16) for low, x in zip(rounded_lowers, rounded)]
        inverse = [x - mul(r, i) for x, r, i in zip(inverse, rounded, inner)]
        size *= 2
    return inverse


def rims_kernel(*refs):
    *inputs, packed_ref, arrived = refs
    copies = []
    for i, x_ref in enumerate(inputs):
        last = x_ref.at[pl.ds(x_ref.shape[0] - RIM, RIM)]
        here = packed_ref.at[pl.ds(i * RIM, RIM)]
        copies.append(pltpu.make_async_copy(last, here, arrived.at[i]))
    for copy in copies:
        copy.start()
    for copy in copies:
        copy.wait()


def maps_kernel(
    base, resets, key_ref, value_ref, rim_ref, taps_ref, decay_ref, strength_ref,
    unit_ref, solved_ref, starts_ref, map_ref,
    rims, padded, value_s, step_s,
):
    heads, length, depth = unit_ref.shape
    chunks = length // CHUNK
    total_heads = decay_ref.shape[0]
    row, col = indices()
    rims[...] = rim_ref[...].astype(F32)
    for g in range(heads):

        def store_key(c, rows):
            unit_ref[g, rows_of(c)] = unit(rows).astype(BF16)

        def store_value(c, rows):
            value_s[g, rows_of(c)] = rows.astype(BF16)

        convolve(key_ref, rims, taps_ref, 1, base + g, padded, store_key)
        convolve(value_ref, rims, taps_ref, 2, base + g, padded, store_value)

    parts = []
    lowers = []
    for c in range(chunks):
        cum, strengths, columns = token_scalars(decay_ref, strength_ref, c)
        first, second = resets[2 * c], resets[2 * c + 1]
        strictly = (row > col) & same_document(second, row, col)
        for g in range(heads):
            h = base + g
            cum_col = columns[:, h : h + 1]
            cum_row = cum[h : h + 1]
            key = unit_ref[g, rows_of(c)]
            fading = jnp.exp(jnp.where(strictly, cum_col - cum_row, FAR))
            strength_col = columns[:, total_heads + h : total_heads + h + 1]
            lowers.append(strength_col * fading * mul(key, key, NT))
            parts.append((g, c, first, second, cum_col, cum_row, strengths[h : h + 1]))
    inverses = lower_inverse(lowers, row, col)
    in_first = lax.broadcasted_iota(jnp.int32, (1, CHUNK), 1) < BLOCK
    first_rows = lax.broadcasted_iota(jnp.int32, (CHUNK, 1), 0) < BLOCK
    for (g, c, first, second, cum_col, cum_row, strength_row), inverse in zip(parts, inverses):
        keep_first = (1 - first).astype(F32)
        keep_second = (1 - second).astype(F32)
        keep_both = keep_first * keep_second
        key = unit_ref[g, rows_of(c)]
        value = value_s[g, rows_of(c)]
        growth_row = jnp.exp(cum_row) * jnp.where(in_first, keep_first, keep_both)
        by_strength = inverse * strength_row
        high, low = split(by_strength * growth_row)
        write_keys = mul(high, key) + mul(low, key)
        high, low = split(by_strength)
        local_values = mul(high, value) + mul(low, value)
        solved = jnp.concatenate([write_keys, local_values], axis=1)
        solved_ref[g, rows_of(c)] = solved
        end = cum_row[:, CHUNK - 1 : CHUNK]
        tail = jnp.exp(end - cum_col) * jnp.where(first_rows, keep_second, 1.0)
        high, low = split(tail * solved)
        product = mul(key, high, TN) + mul(key, low, TN)
        passed = jnp.exp(end) * keep_both
        step_s[g, c, :, :depth] = jnp.where(row == col, passed, 0.0) - product[:, :depth]
        step_s[g, c, :, depth:] = product[:, depth:]

    states = [step_s[g, 0] for g in range(heads)]
    for c in range(1, chunks):
        for g in range(heads):
            starts_ref[g, c - 1] = states[g]
            step = step_s[g, c]
            joined = mul_split(step[:, :depth], states[g])
            states[g] = jnp.concatenate(
                [joined[:, :depth], joined[:, depth:] + step[:, depth:]], axis=1
            )
    for g in range(heads):
        map_ref[g] = states[g].astype(BF16)


def reads_kernel(
    base, resets, query_ref, gate_ref, gain_ref, rim_ref, taps_ref, decay_ref, strength_ref,
    unit_ref, solved_ref, starts_ref,
    reach_ref, part_ref, gating_ref,
    rims, padded, query_s,
):
    heads, length, depth = unit_ref.shape
    chunks = length // CHUNK
    row, col = indices()
    first_rows = lax.broadcasted_iota(jnp.int32, (CHUNK, 1), 0) < BLOCK
    rims[...] = rim_ref[...].astype(F32)
    for g in range(heads):

        def store_query(c, rows):
            query_s[g, rows_of(c)] = (unit(rows) * depth**-0.5).astype(BF16)

        convolve(query_ref, rims, taps_ref, 0, base + g, padded, store_query)

    for c in range(chunks):
        here = rows_of(c)
        cum, _, columns = token_scalars(decay_ref, strength_ref, c)
        first, second = resets[2 * c], resets[2 * c + 1]
        keep_first = (1 - first).astype(F32)
        keep_both = keep_first * (1 - second).astype(F32)
        upto = (row >= col) & same_document(second, row, col)
        for g in range(heads):
            h = base + g
            cum_col = columns[:, h : h + 1]
            query = query_s[g, here]
            fading = jnp.exp(jnp.where(upto, cum_col - cum[h : h + 1], FAR))
            mixing = fading * mul(query, unit_ref[g, here], NT)
            own = mul_split(mixing, solved_ref[g, here])
            growth = jnp.exp(cum_col) * jnp.where(first_rows, keep_first, keep_both)
            reach = growth * query.astype(F32) - own[:, :depth]
            part = own[:, depth:]
            if c:
                both = mul_split(reach, starts_ref[g, c - 1])
                reach = both[:, :depth]
                part = part + both[:, depth:]
            reach_ref[g, here] = reach
            part_ref[g, here] = part
            gate = gate_ref[h, here].astype(F32)
            gating_ref[g, here] = gain_ref[...] * (gate / (1.0 + jnp.exp(-gate)))


def partner(place, k, count):
    if count & (count - 1) == 0:
        return place ^ k
    return lax.rem(place + count - k, count)


def pairs_at(k, count):
    if count & (count - 1) == 0:
        return [(i, i ^ k) for i in range(count)]
    return [(i, (i + k) % count) for i in range(count)]


def join_kernel(count, place, *refs):
    maps = refs[:count]
    before_ref, state_ref, *trans_ref, ordered = refs[count:]
    heads, depth, _ = before_ref.shape
    me = place[0]
    for k in range(count):
        ordered[partner(me, k, count)] = maps[k][...]
    row, col = indices()
    eye = (row == col).astype(F32)
    states = [jnp.concatenate([eye, jnp.zeros((depth, depth), F32)], axis=1)] * heads
    for lap in range(count):

        @pl.when(lap == me)
        def _():
            for h in range(heads):
                before_ref[h] = states[h]

        for h in range(heads):
            step = ordered[lap, h]
            if lap:
                high, low = split(states[h])
                trans = step[:, :depth]
                joined = mul(trans, high) + mul(trans, low)
                states[h] = jnp.concatenate(
                    [joined[:, :depth], joined[:, depth:] + step[:, depth:].astype(F32)], axis=1
                )
            else:
                states[h] = step.astype(F32)
    for h in range(heads):
        state_ref[h] = states[h][:, depth:].astype(state_ref.dtype)
        for ref in trans_ref:
            ref[h] = states[h][:, :depth]


def outputs_kernel(arrived_ref, before_ref, reach_ref, part_ref, gating_ref, normed_ref):
    heads, length, depth = reach_ref.shape
    for g in range(heads):
        before = before_ref[g]
        incoming = mul_split(before[:, :depth], arrived_ref[g].astype(F32)) + before[:, depth:]
        high, low = split(incoming)
        for c in range(length // CHUNK):
            here = rows_of(c)
            reach_high, reach_low = split(reach_ref[g, here])
            core = part_ref[g, here] + (
                mul(reach_high, high) + (mul(reach_high, low) + mul(reach_low, high))
            )
            scale = lax.rsqrt(jnp.sum(core * core, axis=-1, keepdims=True) / depth + EPSILON)
            normed_ref[here, g * depth : (g + 1) * depth] = (
                core * scale * gating_ref[g, here]
            ).astype(BF16)


def projected_kernel(section, total_ref, block_ref, weights_ref, out_ref):
    out_ref[...] = (total_ref[...] + mul(block_ref[...], weights_ref[...])).astype(out_ref.dtype)


def from_behind(value, axis, steps):
    count = lax.axis_size(axis)
    return lax.ppermute(value, axis, [(i, i + steps) for i in range(count - steps)])


VMEM = pl.BlockSpec(memory_space=pltpu.VMEM)
SMEM = pl.BlockSpec(memory_space=pltpu.SMEM)
PARAMS = pltpu.CompilerParams(vmem_limit_bytes=16 * 1024 * 1024)


def pack_rims(inputs):
    _, heads, depth = inputs[0].shape
    return pl.pallas_call(
        rims_kernel,
        out_shape=jax.ShapeDtypeStruct((len(inputs) * RIM, heads, depth), BF16),
        in_specs=[pl.BlockSpec(memory_space=pltpu.HBM)] * len(inputs),
        out_specs=VMEM,
        scratch_shapes=[pltpu.SemaphoreType.DMA((len(inputs),))],
    )(*inputs)


def maps_of(base, heads, resets, key, value, rims, taps, decay, strength):
    _, length, depth = key.shape
    chunks = length // CHUNK
    return pl.pallas_call(
        functools.partial(maps_kernel, base),
        out_shape=(
            jax.ShapeDtypeStruct((heads, length, depth), BF16),
            jax.ShapeDtypeStruct((heads, length, 2 * depth), F32),
            jax.ShapeDtypeStruct((heads, chunks - 1, depth, 2 * depth), F32),
            jax.ShapeDtypeStruct((heads, depth, 2 * depth), BF16),
        ),
        in_specs=[SMEM] + [VMEM] * 6,
        out_specs=[VMEM] * 4,
        scratch_shapes=[
            pltpu.VMEM(rims.shape, F32),
            pltpu.VMEM((length + RIM, depth), F32),
            pltpu.VMEM((heads, length, depth), BF16),
            pltpu.VMEM((heads, chunks, depth, 2 * depth), F32),
        ],
        compiler_params=PARAMS,
        cost_estimate=pl.CostEstimate(
            flops=5 * 10**9, bytes_accessed=4 * 2**20, transcendentals=10**6
        ),
    )(resets, key, value, rims, taps, decay, strength)


def reads_of(base, heads, resets, query, gate, gain, rims, taps, decay, strength, made):
    _, length, depth = query.shape
    per_token = jax.ShapeDtypeStruct((heads, length, depth), F32)
    return pl.pallas_call(
        functools.partial(reads_kernel, base),
        out_shape=(per_token, per_token, per_token),
        in_specs=[SMEM] + [VMEM] * 10,
        out_specs=[VMEM] * 3,
        scratch_shapes=[
            pltpu.VMEM(rims.shape, F32),
            pltpu.VMEM((length + RIM, depth), F32),
            pltpu.VMEM((heads, length, depth), BF16),
        ],
        compiler_params=PARAMS,
        cost_estimate=pl.CostEstimate(
            flops=3 * 10**9, bytes_accessed=4 * 2**20, transcendentals=10**6
        ),
    )(resets, query, gate, gain, rims, taps, decay, strength, *made)


def join(place, maps, links):
    count = len(maps)
    heads, depth, _ = maps[0].shape
    pair = jax.ShapeDtypeStruct((heads, depth, 2 * depth), F32)
    square = (heads, depth, depth)
    if links == 1:
        totals = (jax.ShapeDtypeStruct(square, BF16),)
    else:
        totals = (jax.ShapeDtypeStruct(square, F32),) * 2
    return pl.pallas_call(
        functools.partial(join_kernel, count),
        out_shape=(pair, *totals),
        in_specs=[SMEM] + [VMEM] * count,
        out_specs=[VMEM] * (1 + len(totals)),
        scratch_shapes=[pltpu.VMEM((count, heads, depth, 2 * depth), BF16)],
        compiler_params=PARAMS,
    )(place, *maps)


def outputs_of(arrived, before, reads):
    heads, length, depth = reads[0].shape
    return pl.pallas_call(
        outputs_kernel,
        out_shape=jax.ShapeDtypeStruct((length, heads * depth), BF16),
        in_specs=[VMEM] * 5,
        out_specs=VMEM,
        compiler_params=PARAMS,
    )(arrived, before, *reads)


def projected(section, total, block, weights, dtype):
    length, columns = total.shape
    width = block.shape[1]
    return pl.pallas_call(
        projected_kernel,
        out_shape=jax.ShapeDtypeStruct(total.shape, dtype),
        grid_spec=pltpu.PrefetchScalarGridSpec(
            num_scalar_prefetch=1,
            grid=(length // CHUNK,),
            in_specs=[
                pl.BlockSpec((CHUNK, columns), lambda i, s: (i, 0)),
                pl.BlockSpec((CHUNK, width), lambda i, s: (i, 0)),
                pl.BlockSpec((width, columns), lambda i, s: (s[0], 0)),
            ],
            out_specs=pl.BlockSpec((CHUNK, columns), lambda i, s: (i, 0)),
        ),
        compiler_params=PARAMS,
        cost_estimate=pl.CostEstimate(
            flops=2 * length * columns * width,
            bytes_accessed=4 * length * columns,
            transcendentals=0,
        ),
    )(section.astype(jnp.int32).reshape(1), total, block, weights)


def after(first, *values):
    return lax.optimization_barrier((first, *values))[1:]


def on_device(
    query_in,
    key_in,
    value_in,
    gate_in,
    write_strength,
    log_decay,
    doc_resets,
    conv_weight,
    output_norm_gain,
    output_projection_weight,
):
    length, heads, depth = query_in.shape
    size = heads // GROUPS
    rims = from_behind(pack_rims((query_in, key_in, value_in)), ("chain", "leaf"), 1)
    key, value = (jnp.transpose(x, (1, 0, 2)) for x in (key_in, value_in))
    gain = output_norm_gain.reshape(1, depth)
    leaves = lax.axis_size("leaf")
    place = lax.axis_index("leaf").astype(jnp.int32).reshape(1)

    made = []
    exchanged = []
    for g in range(GROUPS):
        unit_key, solved, starts, own_map = maps_of(
            g * size, size, doc_resets, key, value, rims, conv_weight, log_decay, write_strength
        )
        made.append((unit_key, solved, starts))
        exchanged.append(
            [own_map]
            + [lax.ppermute(own_map, "leaf", pairs_at(k, leaves)) for k in range(1, leaves)]
        )
        key, value = after(own_map, key, value)
        if g == 0:
            query_in, gate_in = after(own_map, query_in, gate_in)
    query, gate = (jnp.transpose(x, (1, 0, 2)) for x in (query_in, gate_in))

    blocks = []
    links = lax.axis_size("chain") - 1
    for g in range(GROUPS):
        reads = reads_of(
            g * size, size, doc_resets, query, gate, gain, rims, conv_weight, log_decay,
            write_strength, made[g],
        )
        maps, reads, _ = lax.optimization_barrier((exchanged[g], reads, exchanged[-1][0]))
        before, state, *trans = join(place, maps, links)
        arrived = from_behind(state.astype(BF16), "chain", 1)
        for _ in range(links - 1):
            passed = jnp.einsum(
                "hij,hjk->hik",
                trans[0],
                arrived.astype(F32),
                precision=lax.Precision.HIGHEST,
            )
            arrived = from_behind((passed + state).astype(BF16), "chain", 1)
        blocks.append(outputs_of(arrived, before, reads))
        query, gate = after(blocks[g], query, gate)

    ring = lax.axis_size("head")
    mine = lax.axis_index("head")
    width = size * depth
    around = [(i, (i + 1) % ring) for i in range(ring)]
    mixed = None
    for k in range(ring):
        owner = lax.rem(mine + ring - k, ring)
        if k + 1 < ring:
            following = [lax.ppermute(block, "head", around) for block in blocks]
        for g, block in enumerate(blocks):
            section = owner * GROUPS + g
            if k + 1 == ring:
                dtype = BF16 if g + 1 == GROUPS else F32
                mixed = projected(section, mixed, block, output_projection_weight, dtype)
                continue
            rows = lax.dynamic_slice_in_dim(output_projection_weight, section * width, width, 0)
            term = jnp.dot(block, rows, preferred_element_type=F32)
            mixed = term if mixed is None else mixed + term
        if k + 1 < ring:
            blocks = following
    return mixed


def solution(mesh):
    return jax.shard_map(
        on_device,
        mesh=mesh,
        in_specs=(
            P(("chain", "leaf"), "head", None),
            P(("chain", "leaf"), "head", None),
            P(("chain", "leaf"), "head", None),
            P(("chain", "leaf"), "head", None),
            P("head", ("chain", "leaf")),
            P("head", ("chain", "leaf")),
            P(("chain", "leaf")),
            P(None, None, "head", None),
            P(),
            P(None, "head"),
        ),
        out_specs=P(("chain", "leaf"), "head"),
        check_vma=False,
    )
```

```python
import functools

import jax
import jax.numpy as jnp
from jax import lax
from jax.experimental import pallas as pl
from jax.experimental.pallas import tpu as pltpu
from jax.sharding import PartitionSpec as P

BLOCK = 64
CHUNK = 128
GROUPS = 2
RIM = 8
EPSILON = 1e-06
FAR = -1e30
LARGE = 1e38
AGAIN = 16
F32 = jnp.float32
BF16 = jnp.bfloat16
NN = (((1,), (0,)), ((), ()))
NT = (((1,), (1,)), ((), ()))
TN = (((0,), (0,)), ((), ()))


def split(a):
    high = a.astype(BF16)
    return high, (a - high.astype(F32)).astype(BF16)


def mul(a, b, dims=NN):
    return lax.dot_general(a, b, dims, preferred_element_type=F32)


def mul_split(a, b):
    a_high, a_low = split(a)
    b_high, b_low = split(b)
    return mul(a_high, b_high) + (mul(a_low, b_high) + mul(a_high, b_low))


def rows_of(c):
    return slice(c * CHUNK, (c + 1) * CHUNK)


def indices():
    shape = (CHUNK, CHUNK)
    return (
        lax.broadcasted_iota(jnp.int32, shape, 0),
        lax.broadcasted_iota(jnp.int32, shape, 1),
    )


def token_scalars(decay_ref, strength_ref, c):
    row, col = indices()
    cum = lax.dot_general(
        decay_ref[:, rows_of(c)],
        (row <= col).astype(F32),
        NN,
        precision=lax.Precision.HIGHEST,
        preferred_element_type=F32,
    )
    strength = strength_ref[:, rows_of(c)]
    stacked = [cum, strength]
    missing = 8 - 2 * cum.shape[0]
    if missing > 0:
        stacked.append(jnp.zeros((missing, CHUNK), F32))
    return cum, strength, jnp.transpose(jnp.concatenate(stacked, axis=0))


def silu(x):
    below = jnp.minimum(1.0 + jnp.exp(-x), LARGE)
    inverse = pl.reciprocal(below, approx=True)
    return x * (inverse * (2.0 - below * inverse))


def filtered(padded, taps, begin, length):
    first = begin + RIM + 1 - len(taps)
    total = taps[0] * padded[first : first + length]
    for j in range(1, len(taps)):
        total = total + taps[j] * padded[first + j : first + j + length]
    return silu(total)


def taps_of(taps_ref, which, head):
    return [taps_ref[which, j, pl.ds(head, 1), :] for j in range(taps_ref.shape[1])]


def unit(rows):
    return rows * lax.rsqrt(jnp.sum(rows * rows, axis=-1, keepdims=True) + EPSILON)


def same_document(second_resets, row, col):
    return ((row // BLOCK) - (col // BLOCK)) * second_resets == 0


def lower_inverse(lowers, row, col):
    differ = row ^ col
    eye = (row == col).astype(F32)
    in_block = (differ < 8).astype(F32)
    diagonal = [low * in_block for low in lowers]
    powers = [d.astype(BF16) for d in diagonal]
    squares = [mul(p, p).astype(BF16) for p in powers]
    inverse = [eye - d for d in diagonal]
    fourths = [mul(s, s).astype(BF16) for s in squares]
    inverse = [x + mul(x.astype(BF16), s) for x, s in zip(inverse, squares)]
    inverse = [x + mul(x.astype(BF16), s) for x, s in zip(inverse, fourths)]
    size = 8
    while size < CHUNK:
        joint = odd_blocks(((differ >= size) & (differ < 2 * size)).astype(F32), size)
        rounded = [x.astype(BF16) for x in inverse]
        inner = [
            mul((odd_blocks(low, size) * joint).astype(BF16), x)
            for low, x in zip(lowers, rounded)
        ]
        outer = [
            mul(odd_blocks(x, size).astype(BF16), with_even_zeros(i, size).astype(BF16))
            for x, i in zip(inverse, inner)
        ]
        inverse = [less_in_odd(x, o, size) for x, o in zip(inverse, outer)]
        size *= 2
    return inverse


def odd_blocks(a, size):
    return jnp.concatenate([a[b : b + size] for b in range(size, a.shape[0], 2 * size)], axis=0)


def with_even_zeros(odd, size):
    zeros = jnp.zeros((size, odd.shape[1]), odd.dtype)
    pieces = []
    for b in range(0, odd.shape[0], size):
        pieces += [zeros, odd[b : b + size]]
    return jnp.concatenate(pieces, axis=0)


def less_in_odd(a, odd, size):
    pieces = []
    for b in range(0, odd.shape[0], size):
        pieces.append(a[2 * b : 2 * b + size])
        pieces.append(a[2 * b + size : 2 * b + 2 * size] - odd[b : b + size])
    return jnp.concatenate(pieces, axis=0)


def rims_kernel(*refs):
    *inputs, packed_ref, arrived = refs
    copies = []
    for i, x_ref in enumerate(inputs):
        last = x_ref.at[pl.ds(x_ref.shape[0] - RIM, RIM)]
        here = packed_ref.at[pl.ds(i * RIM, RIM)]
        copies.append(pltpu.make_async_copy(last, here, arrived.at[i]))
    for copy in copies:
        copy.start()
    for copy in copies:
        copy.wait()


def filters_kernel(key_ref, value_ref, taps_ref, unit_ref, value_out_ref, first_ref, padded):
    length, heads, _ = key_ref.shape
    for i, x_ref in enumerate((key_ref, value_ref)):
        for c in range(length // CHUNK):
            begin = RIM + c * CHUNK
            padded[i, :, begin : begin + CHUNK] = jnp.swapaxes(x_ref[rows_of(c)], 0, 1).astype(F32)
        padded[i, :, 0:RIM] = jnp.zeros((heads, RIM, padded.shape[3]), F32)
        first_ref[i] = padded[i, :, RIM : RIM + AGAIN]

    def one_head(h, carry):
        for i in range(2):
            taps = taps_of(taps_ref, 1 + i, h)
            for c in range(length // CHUNK):
                rows = filtered(padded.at[i, h], taps, c * CHUNK, CHUNK)
                if i == 0:
                    unit_ref[h, rows_of(c)] = unit(rows).astype(BF16)
                else:
                    value_out_ref[h, rows_of(c)] = rows.astype(BF16)
        return carry

    lax.fori_loop(0, heads, one_head, 0)


def maps_kernel(
    base, resets, unit_in_ref, value_in_ref, first_ref, rim_ref, taps_ref, decay_ref, strength_ref,
    unit_ref, solved_ref, starts_ref, map_ref,
    rims, padded, value_s, step_s,
):
    heads, length, depth = unit_ref.shape
    chunks = length // CHUNK
    total_heads = decay_ref.shape[0]
    row, col = indices()
    rims[...] = rim_ref[...].astype(F32)
    for g in range(heads):
        h = base + g
        unit_ref[g] = unit_in_ref[h]
        value_s[g] = value_in_ref[h]
        for i in range(2):
            padded[g, i, 0:RIM] = rims[(1 + i) * RIM : (2 + i) * RIM, h, :]
            padded[g, i, RIM : RIM + AGAIN] = first_ref[i, h]
            rows = filtered(padded.at[g, i], taps_of(taps_ref, 1 + i, h), 0, AGAIN)
            if i == 0:
                unit_ref[g, 0:AGAIN] = unit(rows).astype(BF16)
            else:
                value_s[g, 0:AGAIN] = rows.astype(BF16)

    parts = []
    lowers = []
    for c in range(chunks):
        cum, _, columns = token_scalars(decay_ref, strength_ref, c)
        first, second = resets[2 * c], resets[2 * c + 1]
        strictly = (row > col) & same_document(second, row, col)
        for g in range(heads):
            h = base + g
            cum_col = columns[:, h : h + 1]
            cum_row = cum[h : h + 1]
            key = unit_ref[g, rows_of(c)]
            fading = jnp.exp(jnp.where(strictly, cum_col - cum_row, FAR))
            strength_col = columns[:, total_heads + h : total_heads + h + 1]
            lowers.append(strength_col * fading * mul(key, key, NT))
            parts.append((g, c, first, second, cum_col, cum_row, strength_col))
    inverses = lower_inverse(lowers, row, col)
    eye = (row == col).astype(F32)
    first_rows = lax.broadcasted_iota(jnp.int32, (CHUNK, 1), 0) < BLOCK
    for (g, c, first, second, cum_col, cum_row, strength_col), inverse in zip(parts, inverses):
        keep_first = (1 - first).astype(F32)
        keep_second = (1 - second).astype(F32)
        keep_both = keep_first * keep_second
        key = unit_ref[g, rows_of(c)]
        growth = jnp.exp(cum_col) * jnp.where(first_rows, keep_first, keep_both)
        targets = jnp.concatenate(
            [
                (strength_col * growth) * key.astype(F32),
                strength_col * value_s[g, rows_of(c)].astype(F32),
            ],
            axis=1,
        )
        solved = targets + mul((inverse - eye).astype(BF16), targets.astype(BF16))
        solved_ref[g, rows_of(c)] = solved
        end = cum_row[:, CHUNK - 1 : CHUNK]
        tail = jnp.exp(end - cum_col) * jnp.where(first_rows, keep_second, 1.0)
        product = mul(key, (tail * solved).astype(BF16), TN)
        passed = jnp.exp(end) * keep_both
        step_s[g, c, :, :depth] = jnp.where(row == col, passed, 0.0) - product[:, :depth]
        step_s[g, c, :, depth:] = product[:, depth:]

    states = [step_s[g, 0] for g in range(heads)]
    for c in range(1, chunks):
        for g in range(heads):
            starts_ref[g, c - 1] = states[g]
            step = step_s[g, c]
            trans = step[:, :depth].astype(BF16)
            high, low = split(states[g])
            joined = mul(trans, high) + mul(trans, low)
            states[g] = jnp.concatenate(
                [joined[:, :depth], joined[:, depth:] + step[:, depth:]], axis=1
            )
    for g in range(heads):
        map_ref[g] = states[g].astype(BF16)


def reads_kernel(
    base, resets, query_ref, gate_ref, gain_ref, rim_ref, taps_ref, decay_ref, strength_ref,
    unit_ref, solved_ref, starts_ref,
    reach_ref, part_ref, gating_ref,
    rims, padded, query_s,
):
    heads, length, depth = unit_ref.shape
    chunks = length // CHUNK
    row, col = indices()
    first_rows = lax.broadcasted_iota(jnp.int32, (CHUNK, 1), 0) < BLOCK
    rims[...] = rim_ref[...].astype(F32)
    for g in range(heads):
        h = base + g
        padded[g, 0:RIM] = rims[0:RIM, h, :]
        padded[g, RIM : RIM + length] = query_ref[h].astype(F32)
        taps = taps_of(taps_ref, 0, h)
        for c in range(chunks):
            rows = filtered(padded.at[g], taps, c * CHUNK, CHUNK)
            query_s[g, rows_of(c)] = (unit(rows) * depth**-0.5).astype(BF16)

    for c in range(chunks):
        here = rows_of(c)
        cum, _, columns = token_scalars(decay_ref, strength_ref, c)
        first, second = resets[2 * c], resets[2 * c + 1]
        keep_first = (1 - first).astype(F32)
        keep_both = keep_first * (1 - second).astype(F32)
        upto = (row >= col) & same_document(second, row, col)
        for g in range(heads):
            h = base + g
            cum_col = columns[:, h : h + 1]
            query = query_s[g, here]
            fading = jnp.exp(jnp.where(upto, cum_col - cum[h : h + 1], FAR))
            mixing = fading * mul(query, unit_ref[g, here], NT)
            own = mul_split(mixing, solved_ref[g, here])
            growth = jnp.exp(cum_col) * jnp.where(first_rows, keep_first, keep_both)
            reach = growth * query.astype(F32) - own[:, :depth]
            part = own[:, depth:]
            if c:
                both = mul_split(reach, starts_ref[g, c - 1])
                reach = both[:, :depth]
                part = part + both[:, depth:]
            reach_ref[g, here] = reach.astype(BF16)
            part_ref[g, here] = part
            gate = gate_ref[h, here].astype(F32)
            gating_ref[g, here] = gain_ref[...] * silu(gate)


def partner(place, k, count):
    if count & (count - 1) == 0:
        return place ^ k
    return lax.rem(place + count - k, count)


def pairs_at(k, count):
    if count & (count - 1) == 0:
        return [(i, i ^ k) for i in range(count)]
    return [(i, (i + k) % count) for i in range(count)]


def join_kernel(count, place, *refs):
    maps = refs[:count]
    before_ref, state_ref, *trans_ref, ordered = refs[count:]
    heads, depth, _ = before_ref.shape
    me = place[0]
    for k in range(count):
        ordered[partner(me, k, count)] = maps[k][...]
    row, col = indices()
    eye = (row == col).astype(F32)
    states = [jnp.concatenate([eye, jnp.zeros((depth, depth), F32)], axis=1)] * heads
    for lap in range(count):

        @pl.when(lap == me)
        def _():
            for h in range(heads):
                before_ref[h] = states[h]

        for h in range(heads):
            step = ordered[lap, h]
            if lap:
                high, low = split(states[h])
                trans = step[:, :depth]
                joined = mul(trans, high) + mul(trans, low)
                states[h] = jnp.concatenate(
                    [joined[:, :depth], joined[:, depth:] + step[:, depth:].astype(F32)], axis=1
                )
            else:
                states[h] = step.astype(F32)
    for h in range(heads):
        state_ref[h] = states[h][:, depth:].astype(state_ref.dtype)
        for ref in trans_ref:
            ref[h] = states[h][:, :depth]


def outputs_kernel(arrived_ref, before_ref, reach_ref, part_ref, gating_ref, normed_ref):
    heads, length, depth = reach_ref.shape
    for g in range(heads):
        before = before_ref[g]
        incoming = mul_split(before[:, :depth], arrived_ref[g].astype(F32)) + before[:, depth:]
        high, low = split(incoming)
        for c in range(length // CHUNK):
            here = rows_of(c)
            reach = reach_ref[g, here]
            core = part_ref[g, here] + (mul(reach, high) + mul(reach, low))
            scale = lax.rsqrt(jnp.sum(core * core, axis=-1, keepdims=True) / depth + EPSILON)
            normed_ref[here, g * depth : (g + 1) * depth] = (
                core * scale * gating_ref[g, here]
            ).astype(BF16)


def projected_kernel(section, total_ref, block_ref, weights_ref, out_ref):
    out_ref[...] = total_ref[...] + mul(block_ref[...], weights_ref[...])


def last_kernel(section, total_ref, block_ref, weights_ref, out_ref, tiles, written):
    width = block_ref.shape[1]
    rows = weights_ref[pl.ds(pl.multiple_of(section[0] * width, width), width), :]
    copies = []
    for i in range(total_ref.shape[0] // CHUNK):
        here = rows_of(i)
        tiles[here] = (total_ref[here] + mul(block_ref[here], rows)).astype(BF16)
        copies.append(pltpu.make_async_copy(tiles.at[here], out_ref.at[here], written.at[i]))
        copies[-1].start()
    for copy in copies:
        copy.wait()


def from_behind(value, axis, steps):
    count = lax.axis_size(axis)
    return lax.ppermute(value, axis, [(i, i + steps) for i in range(count - steps)])


VMEM = pl.BlockSpec(memory_space=pltpu.VMEM)
SMEM = pl.BlockSpec(memory_space=pltpu.SMEM)
PARAMS = pltpu.CompilerParams(vmem_limit_bytes=12 * 1024 * 1024)


def pack_rims(inputs):
    _, heads, depth = inputs[0].shape
    return pl.pallas_call(
        rims_kernel,
        out_shape=jax.ShapeDtypeStruct((len(inputs) * RIM, heads, depth), BF16),
        in_specs=[pl.BlockSpec(memory_space=pltpu.HBM)] * len(inputs),
        out_specs=VMEM,
        scratch_shapes=[pltpu.SemaphoreType.DMA((len(inputs),))],
    )(*inputs)


def filters_of(key_in, value_in, taps):
    length, heads, depth = key_in.shape
    per_token = jax.ShapeDtypeStruct((heads, length, depth), BF16)
    return pl.pallas_call(
        filters_kernel,
        out_shape=(per_token, per_token, jax.ShapeDtypeStruct((2, heads, AGAIN, depth), F32)),
        in_specs=[VMEM] * 3,
        out_specs=[VMEM] * 3,
        scratch_shapes=[pltpu.VMEM((2, heads, length + RIM, depth), F32)],
        compiler_params=PARAMS,
        cost_estimate=pl.CostEstimate(
            flops=3 * 10**9, bytes_accessed=4 * 2**20, transcendentals=10**6
        ),
    )(key_in, value_in, taps)


def maps_of(base, heads, resets, unit_in, value_in, first, rims, taps, decay, strength):
    _, length, depth = unit_in.shape
    chunks = length // CHUNK
    return pl.pallas_call(
        functools.partial(maps_kernel, base),
        out_shape=(
            jax.ShapeDtypeStruct((heads, length, depth), BF16),
            jax.ShapeDtypeStruct((heads, length, 2 * depth), F32),
            jax.ShapeDtypeStruct((heads, chunks - 1, depth, 2 * depth), F32),
            jax.ShapeDtypeStruct((heads, depth, 2 * depth), BF16),
        ),
        in_specs=[SMEM] + [VMEM] * 7,
        out_specs=[VMEM] * 4,
        scratch_shapes=[
            pltpu.VMEM(rims.shape, F32),
            pltpu.VMEM((heads, 2, RIM + AGAIN, depth), F32),
            pltpu.VMEM((heads, length, depth), BF16),
            pltpu.VMEM((heads, chunks, depth, 2 * depth), F32),
        ],
        compiler_params=PARAMS,
        cost_estimate=pl.CostEstimate(
            flops=5 * 10**9, bytes_accessed=4 * 2**20, transcendentals=10**6
        ),
    )(resets, unit_in, value_in, first, rims, taps, decay, strength)


def reads_of(base, heads, resets, query, gate, gain, rims, taps, decay, strength, made):
    _, length, depth = query.shape
    per_token = jax.ShapeDtypeStruct((heads, length, depth), F32)
    return pl.pallas_call(
        functools.partial(reads_kernel, base),
        out_shape=(jax.ShapeDtypeStruct(per_token.shape, BF16), per_token, per_token),
        in_specs=[SMEM] + [VMEM] * 10,
        out_specs=[VMEM] * 3,
        scratch_shapes=[
            pltpu.VMEM(rims.shape, F32),
            pltpu.VMEM((heads, length + RIM, depth), F32),
            pltpu.VMEM((heads, length, depth), BF16),
        ],
        compiler_params=PARAMS,
        cost_estimate=pl.CostEstimate(
            flops=3 * 10**9, bytes_accessed=4 * 2**20, transcendentals=10**6
        ),
    )(resets, query, gate, gain, rims, taps, decay, strength, *made)


def join(place, maps, links):
    count = len(maps)
    heads, depth, _ = maps[0].shape
    pair = jax.ShapeDtypeStruct((heads, depth, 2 * depth), F32)
    square = (heads, depth, depth)
    if links == 1:
        totals = (jax.ShapeDtypeStruct(square, BF16),)
    else:
        totals = (jax.ShapeDtypeStruct(square, F32),) * 2
    return pl.pallas_call(
        functools.partial(join_kernel, count),
        out_shape=(pair, *totals),
        in_specs=[SMEM] + [VMEM] * count,
        out_specs=[VMEM] * (1 + len(totals)),
        scratch_shapes=[pltpu.VMEM((count, heads, depth, 2 * depth), BF16)],
        compiler_params=PARAMS,
    )(place, *maps)


def outputs_of(arrived, before, reads):
    heads, length, depth = reads[0].shape
    return pl.pallas_call(
        outputs_kernel,
        out_shape=jax.ShapeDtypeStruct((length, heads * depth), BF16),
        in_specs=[VMEM] * 5,
        out_specs=VMEM,
        compiler_params=PARAMS,
    )(arrived, before, *reads)


def projected(section, total, block, weights):
    length, columns = total.shape
    width = block.shape[1]
    return pl.pallas_call(
        projected_kernel,
        out_shape=jax.ShapeDtypeStruct(total.shape, F32),
        grid_spec=pltpu.PrefetchScalarGridSpec(
            num_scalar_prefetch=1,
            grid=(length // CHUNK,),
            in_specs=[
                pl.BlockSpec((CHUNK, columns), lambda i, s: (i, 0)),
                pl.BlockSpec((CHUNK, width), lambda i, s: (i, 0)),
                pl.BlockSpec((width, columns), lambda i, s: (s[0], 0)),
            ],
            out_specs=pl.BlockSpec((CHUNK, columns), lambda i, s: (i, 0)),
        ),
        compiler_params=PARAMS,
        cost_estimate=pl.CostEstimate(
            flops=2 * length * columns * width,
            bytes_accessed=4 * length * columns,
            transcendentals=0,
        ),
    )(section.astype(jnp.int32).reshape(1), total, block, weights)


def last_projected(section, total, block, weights):
    return pl.pallas_call(
        last_kernel,
        out_shape=jax.ShapeDtypeStruct(total.shape, BF16),
        in_specs=[SMEM] + [VMEM] * 3,
        out_specs=pl.BlockSpec(memory_space=pl.ANY),
        scratch_shapes=[
            pltpu.VMEM(total.shape, BF16),
            pltpu.SemaphoreType.DMA((total.shape[0] // CHUNK,)),
        ],
        compiler_params=PARAMS,
    )(section.astype(jnp.int32).reshape(1), total, block, weights)


def after(first, *values):
    return lax.optimization_barrier((first, *values))[1:]


def on_device(
    query_in,
    key_in,
    value_in,
    gate_in,
    write_strength,
    log_decay,
    doc_resets,
    conv_weight,
    output_norm_gain,
    output_projection_weight,
):
    length, heads, depth = query_in.shape
    size = heads // GROUPS
    rims = from_behind(pack_rims((query_in, key_in, value_in)), ("chain", "leaf"), 1)
    key, value, first = filters_of(key_in, value_in, conv_weight)
    gain = output_norm_gain.reshape(1, depth)
    leaves = lax.axis_size("leaf")
    place = lax.axis_index("leaf").astype(jnp.int32).reshape(1)

    made = []
    exchanged = []
    for g in range(GROUPS):
        unit_key, solved, starts, own_map = maps_of(
            g * size, size, doc_resets, key, value, first, rims, conv_weight, log_decay,
            write_strength,
        )
        made.append((unit_key, solved, starts))
        exchanged.append(
            [own_map]
            + [lax.ppermute(own_map, "leaf", pairs_at(k, leaves)) for k in range(1, leaves)]
        )
        key, value = after(own_map, key, value)
        if g == 0:
            query_in, gate_in = after(own_map, query_in, gate_in)
    query, gate = (jnp.transpose(x, (1, 0, 2)) for x in (query_in, gate_in))

    blocks = []
    links = lax.axis_size("chain") - 1
    for g in range(GROUPS):
        reads = reads_of(
            g * size, size, doc_resets, query, gate, gain, rims, conv_weight, log_decay,
            write_strength, made[g],
        )
        maps, reads, _ = lax.optimization_barrier((exchanged[g], reads, exchanged[-1][0]))
        before, state, *trans = join(place, maps, links)
        arrived = from_behind(state.astype(BF16), "chain", 1)
        for _ in range(links - 1):
            passed = jnp.einsum(
                "hij,hjk->hik",
                trans[0],
                arrived.astype(F32),
                precision=lax.Precision.HIGHEST,
            )
            arrived = from_behind((passed + state).astype(BF16), "chain", 1)
        blocks.append(outputs_of(arrived, before, reads))
        query, gate = after(blocks[g], query, gate)

    ring = lax.axis_size("head")
    mine = lax.axis_index("head")
    width = size * depth
    around = [(i, (i + 1) % ring) for i in range(ring)]
    mixed = None
    for k in range(ring):
        owner = lax.rem(mine + ring - k, ring)
        if k + 1 < ring:
            following = [lax.ppermute(block, "head", around) for block in blocks]
        for g, block in enumerate(blocks):
            section = owner * GROUPS + g
            if k + 1 == ring:
                add = last_projected if g + 1 == GROUPS else projected
                mixed = add(section, mixed, block, output_projection_weight)
                continue
            rows = lax.dynamic_slice_in_dim(output_projection_weight, section * width, width, 0)
            term = jnp.dot(block, rows, preferred_element_type=F32)
            mixed = term if mixed is None else mixed + term
        if k + 1 < ring:
            blocks = following
    return mixed


def solution(mesh):
    return jax.shard_map(
        on_device,
        mesh=mesh,
        in_specs=(
            P(("chain", "leaf"), "head", None),
            P(("chain", "leaf"), "head", None),
            P(("chain", "leaf"), "head", None),
            P(("chain", "leaf"), "head", None),
            P("head", ("chain", "leaf")),
            P("head", ("chain", "leaf")),
            P(("chain", "leaf")),
            P(None, None, "head", None),
            P(),
            P(None, "head"),
        ),
        out_specs=P(("chain", "leaf"), "head"),
        check_vma=False,
    )
```

```python
import functools

import jax
import jax.numpy as jnp
from jax import lax
from jax.experimental import pallas as pl
from jax.experimental.pallas import tpu as pltpu
from jax.sharding import PartitionSpec as P

BLOCK = 64
CHUNK = 128
GROUPS = 2
RIM = 8
EPSILON = 1e-06
FAR = -1e30
LARGE = 1e38
AGAIN = 16
F32 = jnp.float32
BF16 = jnp.bfloat16
NN = (((1,), (0,)), ((), ()))
NT = (((1,), (1,)), ((), ()))
TN = (((0,), (0,)), ((), ()))


def split(a):
    high = a.astype(BF16)
    return high, (a - high.astype(F32)).astype(BF16)


def mul(a, b, dims=NN):
    return lax.dot_general(a, b, dims, preferred_element_type=F32)


def mul_split(a, b):
    a_high, a_low = split(a)
    b_high, b_low = split(b)
    return mul(a_high, b_high) + (mul(a_low, b_high) + mul(a_high, b_low))


def rows_of(c):
    return slice(c * CHUNK, (c + 1) * CHUNK)


def indices():
    shape = (CHUNK, CHUNK)
    return (
        lax.broadcasted_iota(jnp.int32, shape, 0),
        lax.broadcasted_iota(jnp.int32, shape, 1),
    )


def token_scalars(decay_ref, strength_ref, c):
    row, col = indices()
    cum = lax.dot_general(
        decay_ref[:, rows_of(c)],
        (row <= col).astype(F32),
        NN,
        precision=lax.Precision.HIGHEST,
        preferred_element_type=F32,
    )
    strength = strength_ref[:, rows_of(c)]
    stacked = [cum, strength]
    missing = 8 - 2 * cum.shape[0]
    if missing > 0:
        stacked.append(jnp.zeros((missing, CHUNK), F32))
    return cum, strength, jnp.transpose(jnp.concatenate(stacked, axis=0))


def silu(x):
    below = jnp.minimum(1.0 + jnp.exp(-x), LARGE)
    inverse = pl.reciprocal(below, approx=True)
    return x * (inverse * (2.0 - below * inverse))


def filtered(padded, taps, begin, length):
    first = begin + RIM + 1 - len(taps)
    total = taps[0] * padded[first : first + length]
    for j in range(1, len(taps)):
        total = total + taps[j] * padded[first + j : first + j + length]
    return silu(total)


def taps_of(taps_ref, which, head):
    return [taps_ref[which, j, pl.ds(head, 1), :] for j in range(taps_ref.shape[1])]


def unit(rows):
    return rows * lax.rsqrt(jnp.sum(rows * rows, axis=-1, keepdims=True) + EPSILON)


def same_document(second_resets, row, col):
    return ((row // BLOCK) - (col // BLOCK)) * second_resets == 0


def lower_inverse(lowers, row, col):
    differ = row ^ col
    eye = (row == col).astype(F32)
    in_block = (differ < 8).astype(F32)
    diagonal = [low * in_block for low in lowers]
    powers = [d.astype(BF16) for d in diagonal]
    squares = [mul(p, p).astype(BF16) for p in powers]
    inverse = [eye - d for d in diagonal]
    fourths = [mul(s, s).astype(BF16) for s in squares]
    inverse = [x + mul(x.astype(BF16), s) for x, s in zip(inverse, squares)]
    inverse = [x + mul(x.astype(BF16), s) for x, s in zip(inverse, fourths)]
    size = 8
    while size < CHUNK:
        joint = odd_blocks(((differ >= size) & (differ < 2 * size)).astype(F32), size)
        rounded = [x.astype(BF16) for x in inverse]
        inner = [
            mul((odd_blocks(low, size) * joint).astype(BF16), x)
            for low, x in zip(lowers, rounded)
        ]
        outer = [
            mul(odd_blocks(x, size).astype(BF16), with_even_zeros(i, size).astype(BF16))
            for x, i in zip(inverse, inner)
        ]
        inverse = [less_in_odd(x, o, size) for x, o in zip(inverse, outer)]
        size *= 2
    return inverse


def odd_blocks(a, size):
    return jnp.concatenate([a[b : b + size] for b in range(size, a.shape[0], 2 * size)], axis=0)


def with_even_zeros(odd, size):
    zeros = jnp.zeros((size, odd.shape[1]), odd.dtype)
    pieces = []
    for b in range(0, odd.shape[0], size):
        pieces += [zeros, odd[b : b + size]]
    return jnp.concatenate(pieces, axis=0)


def less_in_odd(a, odd, size):
    pieces = []
    for b in range(0, odd.shape[0], size):
        pieces.append(a[2 * b : 2 * b + size])
        pieces.append(a[2 * b + size : 2 * b + 2 * size] - odd[b : b + size])
    return jnp.concatenate(pieces, axis=0)


def rims_kernel(*refs):
    *inputs, packed_ref, arrived = refs
    copies = []
    for i, x_ref in enumerate(inputs):
        last = x_ref.at[pl.ds(x_ref.shape[0] - RIM, RIM)]
        here = packed_ref.at[pl.ds(i * RIM, RIM)]
        copies.append(pltpu.make_async_copy(last, here, arrived.at[i]))
    for copy in copies:
        copy.start()
    for copy in copies:
        copy.wait()


def filters_kernel(
    key_ref, value_ref, taps_in_ref, unit_ref, value_out_ref, first_ref,
    raw, padded, taps_ref, arrived, taps_arrived,
):
    length, heads, depth = key_ref.shape
    chunks = length // CHUNK
    taps_copy = pltpu.make_async_copy(taps_in_ref, taps_ref, taps_arrived)
    taps_copy.start()
    copies = {}
    for c in range(chunks):
        for i, x_ref in enumerate((key_ref, value_ref)):
            here = pl.ds(c * CHUNK, CHUNK)
            copies[c, i] = pltpu.make_async_copy(
                x_ref.at[here], raw.at[i, here], arrived.at[c, i]
            )
            copies[c, i].start()
    padded[:, :, 0:RIM] = jnp.zeros((2, heads, RIM, depth), F32)
    taps_copy.wait()
    for c in range(chunks):
        begin = RIM + c * CHUNK
        for i in range(2):
            copies[c, i].wait()
            padded[i, :, begin : begin + CHUNK] = jnp.swapaxes(raw[i, rows_of(c)], 0, 1).astype(F32)

        def one_head(h, carry):
            for i in range(2):
                rows = filtered(padded.at[i, h], taps_of(taps_ref, 1 + i, h), c * CHUNK, CHUNK)
                if i == 0:
                    unit_ref[h, rows_of(c)] = unit(rows).astype(BF16)
                else:
                    value_out_ref[h, rows_of(c)] = rows.astype(BF16)
            return carry

        lax.fori_loop(0, heads, one_head, 0)
    first_ref[...] = padded[:, :, RIM : RIM + AGAIN]


def maps_kernel(
    base, resets, unit_in_ref, value_in_ref, first_ref, rim_ref, taps_ref, decay_ref, strength_ref,
    unit_ref, solved_ref, starts_ref, map_ref,
    rims, padded, value_s, step_s,
):
    heads, length, depth = unit_ref.shape
    chunks = length // CHUNK
    total_heads = decay_ref.shape[0]
    row, col = indices()
    rims[...] = rim_ref[...].astype(F32)
    for g in range(heads):
        h = base + g
        unit_ref[g] = unit_in_ref[h]
        value_s[g] = value_in_ref[h]
        for i in range(2):
            padded[g, i, 0:RIM] = rims[(1 + i) * RIM : (2 + i) * RIM, h, :]
            padded[g, i, RIM : RIM + AGAIN] = first_ref[i, h]
            rows = filtered(padded.at[g, i], taps_of(taps_ref, 1 + i, h), 0, AGAIN)
            if i == 0:
                unit_ref[g, 0:AGAIN] = unit(rows).astype(BF16)
            else:
                value_s[g, 0:AGAIN] = rows.astype(BF16)

    parts = []
    lowers = []
    for c in range(chunks):
        cum, _, columns = token_scalars(decay_ref, strength_ref, c)
        first, second = resets[2 * c], resets[2 * c + 1]
        strictly = (row > col) & same_document(second, row, col)
        for g in range(heads):
            h = base + g
            cum_col = columns[:, h : h + 1]
            cum_row = cum[h : h + 1]
            key = unit_ref[g, rows_of(c)]
            fading = jnp.exp(jnp.where(strictly, cum_col - cum_row, FAR))
            strength_col = columns[:, total_heads + h : total_heads + h + 1]
            lowers.append(strength_col * fading * mul(key, key, NT))
            parts.append((g, c, first, second, cum_col, cum_row, strength_col))
    inverses = lower_inverse(lowers, row, col)
    eye = (row == col).astype(F32)
    first_rows = lax.broadcasted_iota(jnp.int32, (CHUNK, 1), 0) < BLOCK
    for (g, c, first, second, cum_col, cum_row, strength_col), inverse in zip(parts, inverses):
        keep_first = (1 - first).astype(F32)
        keep_second = (1 - second).astype(F32)
        keep_both = keep_first * keep_second
        key = unit_ref[g, rows_of(c)]
        growth = jnp.exp(cum_col) * jnp.where(first_rows, keep_first, keep_both)
        targets = jnp.concatenate(
            [
                (strength_col * growth) * key.astype(F32),
                strength_col * value_s[g, rows_of(c)].astype(F32),
            ],
            axis=1,
        )
        solved = targets + mul((inverse - eye).astype(BF16), targets.astype(BF16))
        solved_ref[g, rows_of(c)] = solved
        end = cum_row[:, CHUNK - 1 : CHUNK]
        tail = jnp.exp(end - cum_col) * jnp.where(first_rows, keep_second, 1.0)
        product = mul(key, (tail * solved).astype(BF16), TN)
        passed = jnp.exp(end) * keep_both
        step_s[g, c, :, :depth] = jnp.where(row == col, passed, 0.0) - product[:, :depth]
        step_s[g, c, :, depth:] = product[:, depth:]

    def compose(later, earlier):
        high, low = split(earlier)
        trans = later[:, :depth].astype(BF16)
        joined = mul(trans, high) + mul(trans, low)
        return jnp.concatenate([joined[:, :depth], joined[:, depth:] + later[:, depth:]], axis=1)

    every = range(heads)
    states = [step_s[g, 0] for g in every]
    half = chunks // 2
    for c in range(1, half):
        for g in every:
            starts_ref[g, c - 1] = states[g]
        states = [compose(step_s[g, c], states[g]) for g in every]
    rest = [step_s[g, half] for g in every]
    for c in range(half + 1, chunks):
        rest = [compose(step_s[g, c], rest[g]) for g in every]
    for g in every:
        map_ref[g] = compose(rest[g], states[g]).astype(BF16)
    for c in range(half, chunks):
        for g in every:
            starts_ref[g, c - 1] = states[g]
        if c + 1 < chunks:
            states = [compose(step_s[g, c], states[g]) for g in every]


def reads_kernel(
    base, resets, query_ref, gate_ref, gain_ref, rim_ref, taps_ref, decay_ref, strength_ref,
    unit_ref, solved_ref, starts_ref,
    reach_ref, part_ref, gating_ref,
    rims, padded, query_s,
):
    heads, length, depth = unit_ref.shape
    chunks = length // CHUNK
    row, col = indices()
    first_rows = lax.broadcasted_iota(jnp.int32, (CHUNK, 1), 0) < BLOCK
    rims[...] = rim_ref[...].astype(F32)
    for g in range(heads):
        h = base + g
        padded[g, 0:RIM] = rims[0:RIM, h, :]
        padded[g, RIM : RIM + length] = query_ref[h].astype(F32)
        taps = taps_of(taps_ref, 0, h)
        for c in range(chunks):
            rows = filtered(padded.at[g], taps, c * CHUNK, CHUNK)
            query_s[g, rows_of(c)] = (unit(rows) * depth**-0.5).astype(BF16)

    for c in range(chunks):
        here = rows_of(c)
        cum, _, columns = token_scalars(decay_ref, strength_ref, c)
        first, second = resets[2 * c], resets[2 * c + 1]
        keep_first = (1 - first).astype(F32)
        keep_both = keep_first * (1 - second).astype(F32)
        upto = (row >= col) & same_document(second, row, col)
        for g in range(heads):
            h = base + g
            cum_col = columns[:, h : h + 1]
            query = query_s[g, here]
            fading = jnp.exp(jnp.where(upto, cum_col - cum[h : h + 1], FAR))
            mixing = fading * mul(query, unit_ref[g, here], NT)
            own = mul_split(mixing, solved_ref[g, here])
            growth = jnp.exp(cum_col) * jnp.where(first_rows, keep_first, keep_both)
            reach = growth * query.astype(F32) - own[:, :depth]
            part = own[:, depth:]
            if c:
                both = mul_split(reach, starts_ref[g, c - 1])
                reach = both[:, :depth]
                part = part + both[:, depth:]
            reach_ref[g, here] = reach.astype(BF16)
            part_ref[g, here] = part
            gate = gate_ref[h, here].astype(F32)
            gating_ref[g, here] = gain_ref[...] * silu(gate)


def partner(place, k, count):
    if count & (count - 1) == 0:
        return place ^ k
    return lax.rem(place + count - k, count)


def pairs_at(k, count):
    if count & (count - 1) == 0:
        return [(i, i ^ k) for i in range(count)]
    return [(i, (i + k) % count) for i in range(count)]


def join_kernel(count, place, *refs):
    maps = refs[:count]
    before_ref, state_ref, *trans_ref, ordered = refs[count:]
    heads, depth, _ = before_ref.shape
    me = place[0]
    for k in range(count):
        ordered[partner(me, k, count)] = maps[k][...]
    row, col = indices()
    eye = (row == col).astype(F32)
    states = [jnp.concatenate([eye, jnp.zeros((depth, depth), F32)], axis=1)] * heads
    for lap in range(count):

        @pl.when(lap == me)
        def _():
            for h in range(heads):
                before_ref[h] = states[h]

        for h in range(heads):
            step = ordered[lap, h]
            if lap:
                high, low = split(states[h])
                trans = step[:, :depth]
                joined = mul(trans, high) + mul(trans, low)
                states[h] = jnp.concatenate(
                    [joined[:, :depth], joined[:, depth:] + step[:, depth:].astype(F32)], axis=1
                )
            else:
                states[h] = step.astype(F32)
    for h in range(heads):
        state_ref[h] = states[h][:, depth:].astype(state_ref.dtype)
        for ref in trans_ref:
            ref[h] = states[h][:, :depth]


def outputs_kernel(base, arrived_ref, before_ref, reach_ref, part_ref, gating_ref, normed_ref):
    _, length, depth = reach_ref.shape
    for g in range(normed_ref.shape[1] // depth):
        h = base + g
        before = before_ref[h]
        incoming = mul_split(before[:, :depth], arrived_ref[h].astype(F32)) + before[:, depth:]
        high, low = split(incoming)
        for c in range(length // CHUNK):
            here = rows_of(c)
            reach = reach_ref[h, here]
            core = part_ref[h, here] + (mul(reach, high) + mul(reach, low))
            scale = lax.rsqrt(jnp.sum(core * core, axis=-1, keepdims=True) / depth + EPSILON)
            normed_ref[here, g * depth : (g + 1) * depth] = (
                core * scale * gating_ref[h, here]
            ).astype(BF16)


def projected_kernel(section, total_ref, block_ref, weights_ref, out_ref):
    out_ref[...] = total_ref[...] + mul(block_ref[...], weights_ref[...])


def last_kernel(section, total_ref, block_ref, weights_ref, out_ref, tiles, written):
    width = block_ref.shape[1]
    rows = weights_ref[pl.ds(pl.multiple_of(section[0] * width, width), width), :]
    copies = []
    for i in range(total_ref.shape[0] // CHUNK):
        here = rows_of(i)
        tiles[here] = (total_ref[here] + mul(block_ref[here], rows)).astype(BF16)
        copies.append(pltpu.make_async_copy(tiles.at[here], out_ref.at[here], written.at[i]))
        copies[-1].start()
    for copy in copies:
        copy.wait()


def from_behind(value, axis, steps):
    count = lax.axis_size(axis)
    return lax.ppermute(value, axis, [(i, i + steps) for i in range(count - steps)])


VMEM = pl.BlockSpec(memory_space=pltpu.VMEM)
SMEM = pl.BlockSpec(memory_space=pltpu.SMEM)
HBM = pl.BlockSpec(memory_space=pltpu.HBM)
PARAMS = pltpu.CompilerParams(vmem_limit_bytes=12 * 1024 * 1024)


def pack_rims(inputs):
    _, heads, depth = inputs[0].shape
    return pl.pallas_call(
        rims_kernel,
        out_shape=jax.ShapeDtypeStruct((len(inputs) * RIM, heads, depth), BF16),
        in_specs=[HBM] * len(inputs),
        out_specs=HBM,
        scratch_shapes=[pltpu.SemaphoreType.DMA((len(inputs),))],
    )(*inputs)


def filters_of(key_in, value_in, taps):
    length, heads, depth = key_in.shape
    chunks = length // CHUNK
    per_token = jax.ShapeDtypeStruct((heads, length, depth), BF16)
    return pl.pallas_call(
        filters_kernel,
        out_shape=(per_token, per_token, jax.ShapeDtypeStruct((2, heads, AGAIN, depth), F32)),
        in_specs=[HBM] * 3,
        out_specs=[VMEM] * 3,
        scratch_shapes=[
            pltpu.VMEM((2, length, heads, depth), BF16),
            pltpu.VMEM((2, heads, length + RIM, depth), F32),
            pltpu.VMEM(taps.shape, F32),
            pltpu.SemaphoreType.DMA((chunks, 2)),
            pltpu.SemaphoreType.DMA(()),
        ],
        compiler_params=PARAMS,
        cost_estimate=pl.CostEstimate(
            flops=3 * 10**9, bytes_accessed=4 * 2**20, transcendentals=10**6
        ),
    )(key_in, value_in, taps)


def maps_of(base, heads, resets, unit_in, value_in, first, rims, taps, decay, strength):
    _, length, depth = unit_in.shape
    chunks = length // CHUNK
    return pl.pallas_call(
        functools.partial(maps_kernel, base),
        out_shape=(
            jax.ShapeDtypeStruct((heads, length, depth), BF16),
            jax.ShapeDtypeStruct((heads, length, 2 * depth), F32),
            jax.ShapeDtypeStruct((heads, chunks - 1, depth, 2 * depth), F32),
            jax.ShapeDtypeStruct((heads, depth, 2 * depth), BF16),
        ),
        in_specs=[SMEM] + [VMEM] * 7,
        out_specs=[VMEM] * 4,
        scratch_shapes=[
            pltpu.VMEM(rims.shape, F32),
            pltpu.VMEM((heads, 2, RIM + AGAIN, depth), F32),
            pltpu.VMEM((heads, length, depth), BF16),
            pltpu.VMEM((heads, chunks, depth, 2 * depth), F32),
        ],
        compiler_params=PARAMS,
        cost_estimate=pl.CostEstimate(
            flops=5 * 10**9, bytes_accessed=4 * 2**20, transcendentals=10**6
        ),
    )(resets, unit_in, value_in, first, rims, taps, decay, strength)


def reads_of(base, heads, resets, query, gate, gain, rims, taps, decay, strength, made):
    _, length, depth = query.shape
    per_token = jax.ShapeDtypeStruct((heads, length, depth), F32)
    return pl.pallas_call(
        functools.partial(reads_kernel, base),
        out_shape=(jax.ShapeDtypeStruct(per_token.shape, BF16), per_token, per_token),
        in_specs=[SMEM] + [VMEM] * 10,
        out_specs=[VMEM] * 3,
        scratch_shapes=[
            pltpu.VMEM(rims.shape, F32),
            pltpu.VMEM((heads, length + RIM, depth), F32),
            pltpu.VMEM((heads, length, depth), BF16),
        ],
        compiler_params=PARAMS,
        cost_estimate=pl.CostEstimate(
            flops=3 * 10**9, bytes_accessed=4 * 2**20, transcendentals=10**6
        ),
    )(resets, query, gate, gain, rims, taps, decay, strength, *made)


def join(place, maps, links):
    count = len(maps)
    heads, depth, _ = maps[0].shape
    pair = jax.ShapeDtypeStruct((heads, depth, 2 * depth), F32)
    square = (heads, depth, depth)
    if links == 1:
        totals = (jax.ShapeDtypeStruct(square, BF16),)
    else:
        totals = (jax.ShapeDtypeStruct(square, F32),) * 2
    return pl.pallas_call(
        functools.partial(join_kernel, count),
        out_shape=(pair, *totals),
        in_specs=[SMEM] + [VMEM] * count,
        out_specs=[VMEM] * (1 + len(totals)),
        scratch_shapes=[pltpu.VMEM((count, heads, depth, 2 * depth), BF16)],
        compiler_params=PARAMS,
    )(place, *maps)


def outputs_of(base, heads, arrived, before, reads):
    _, length, depth = reads[0].shape
    return pl.pallas_call(
        functools.partial(outputs_kernel, base),
        out_shape=jax.ShapeDtypeStruct((length, heads * depth), BF16),
        in_specs=[VMEM] * 5,
        out_specs=VMEM,
        compiler_params=PARAMS,
    )(arrived, before, *reads)


def projected(section, total, block, weights):
    length, columns = total.shape
    width = block.shape[1]
    return pl.pallas_call(
        projected_kernel,
        out_shape=jax.ShapeDtypeStruct(total.shape, F32),
        grid_spec=pltpu.PrefetchScalarGridSpec(
            num_scalar_prefetch=1,
            grid=(length // CHUNK,),
            in_specs=[
                pl.BlockSpec((CHUNK, columns), lambda i, s: (i, 0)),
                pl.BlockSpec((CHUNK, width), lambda i, s: (i, 0)),
                pl.BlockSpec((width, columns), lambda i, s: (s[0], 0)),
            ],
            out_specs=pl.BlockSpec((CHUNK, columns), lambda i, s: (i, 0)),
        ),
        compiler_params=PARAMS,
        cost_estimate=pl.CostEstimate(
            flops=2 * length * columns * width,
            bytes_accessed=4 * length * columns,
            transcendentals=0,
        ),
    )(section.astype(jnp.int32).reshape(1), total, block, weights)


def last_projected(section, total, block, weights):
    return pl.pallas_call(
        last_kernel,
        out_shape=jax.ShapeDtypeStruct(total.shape, BF16),
        in_specs=[SMEM] + [VMEM] * 3,
        out_specs=pl.BlockSpec(memory_space=pl.ANY),
        scratch_shapes=[
            pltpu.VMEM(total.shape, BF16),
            pltpu.SemaphoreType.DMA((total.shape[0] // CHUNK,)),
        ],
        compiler_params=PARAMS,
    )(section.astype(jnp.int32).reshape(1), total, block, weights)


def after(first, *values):
    return lax.optimization_barrier((first, *values))[1:]


def on_device(
    query_in,
    key_in,
    value_in,
    gate_in,
    write_strength,
    log_decay,
    doc_resets,
    conv_weight,
    output_norm_gain,
    output_projection_weight,
):
    length, heads, depth = query_in.shape
    size = heads // GROUPS
    rims = from_behind(pack_rims((query_in, key_in, value_in)), ("chain", "leaf"), 1)
    key, value, first = filters_of(key_in, value_in, conv_weight)
    gain = output_norm_gain.reshape(1, depth)
    leaves = lax.axis_size("leaf")
    place = lax.axis_index("leaf").astype(jnp.int32).reshape(1)

    links = lax.axis_size("chain") - 1
    *made, own_map = maps_of(
        0, heads, doc_resets, key, value, first, rims, conv_weight, log_decay, write_strength
    )
    maps = [own_map] + [
        lax.ppermute(own_map, "leaf", pairs_at(k, leaves)) for k in range(1, leaves)
    ]
    query_in, gate_in = after(own_map, query_in, gate_in)
    query, gate = (jnp.transpose(x, (1, 0, 2)) for x in (query_in, gate_in))
    reads = reads_of(
        0, heads, doc_resets, query, gate, gain, rims, conv_weight, log_decay, write_strength, made
    )
    maps, reads = lax.optimization_barrier((maps, reads))
    before, state, *trans = join(place, maps, links)
    arrived = from_behind(state.astype(BF16), "chain", 1)
    for _ in range(links - 1):
        passed = jnp.einsum(
            "hij,hjk->hik", trans[0], arrived.astype(F32), precision=lax.Precision.HIGHEST
        )
        arrived = from_behind((passed + state).astype(BF16), "chain", 1)
    blocks = []
    for g in range(GROUPS):
        blocks.append(outputs_of(g * size, size, arrived, before, reads))
        arrived = after(blocks[g], arrived)[0]

    ring = lax.axis_size("head")
    mine = lax.axis_index("head")
    width = size * depth
    around = [(i, (i + 1) % ring) for i in range(ring)]
    mixed = None
    for k in range(ring):
        owner = lax.rem(mine + ring - k, ring)
        if k + 1 < ring:
            following = [lax.ppermute(block, "head", around) for block in blocks]
        for g, block in enumerate(blocks):
            section = owner * GROUPS + g
            if k + 1 == ring:
                add = last_projected if g + 1 == GROUPS else projected
                mixed = add(section, mixed, block, output_projection_weight)
                continue
            rows = lax.dynamic_slice_in_dim(output_projection_weight, section * width, width, 0)
            term = jnp.dot(block, rows, preferred_element_type=F32)
            mixed = term if mixed is None else mixed + term
        if k + 1 < ring:
            blocks = following
    return mixed


def solution(mesh):
    return jax.shard_map(
        on_device,
        mesh=mesh,
        in_specs=(
            P(("chain", "leaf"), "head", None),
            P(("chain", "leaf"), "head", None),
            P(("chain", "leaf"), "head", None),
            P(("chain", "leaf"), "head", None),
            P("head", ("chain", "leaf")),
            P("head", ("chain", "leaf")),
            P(("chain", "leaf")),
            P(None, None, "head", None),
            P(),
            P(None, "head"),
        ),
        out_specs=P(("chain", "leaf"), "head"),
        check_vma=False,
    )
```

```python
import functools

import jax
import jax.numpy as jnp
from jax import lax
from jax.experimental import pallas as pl
from jax.experimental.pallas import tpu as pltpu
from jax.sharding import PartitionSpec as P

BLOCK = 64
CHUNK = 128
PARTS = 2
RIM = 8
EPSILON = 1e-06
FAR = -1e30
LARGE = 1e38
AGAIN = 16
F32 = jnp.float32
BF16 = jnp.bfloat16
NN = (((1,), (0,)), ((), ()))
NT = (((1,), (1,)), ((), ()))
TN = (((0,), (0,)), ((), ()))


def split(a):
    high = a.astype(BF16)
    return high, (a - high.astype(F32)).astype(BF16)


def mul(a, b, dims=NN):
    return lax.dot_general(a, b, dims, preferred_element_type=F32)


def mul_split(a, b):
    a_high, a_low = split(a)
    b_high, b_low = split(b)
    return mul(a_high, b_high) + (mul(a_low, b_high) + mul(a_high, b_low))


def rows_of(c):
    return slice(c * CHUNK, (c + 1) * CHUNK)


def indices():
    shape = (CHUNK, CHUNK)
    return (
        lax.broadcasted_iota(jnp.int32, shape, 0),
        lax.broadcasted_iota(jnp.int32, shape, 1),
    )


def token_scalars(decay_ref, strength_ref, c):
    row, col = indices()
    cum = lax.dot_general(
        decay_ref[:, rows_of(c)],
        (row <= col).astype(F32),
        NN,
        precision=lax.Precision.HIGHEST,
        preferred_element_type=F32,
    )
    strength = strength_ref[:, rows_of(c)]
    stacked = [cum, strength]
    missing = 8 - 2 * cum.shape[0]
    if missing > 0:
        stacked.append(jnp.zeros((missing, CHUNK), F32))
    return cum, strength, jnp.transpose(jnp.concatenate(stacked, axis=0))


def silu(x):
    below = jnp.minimum(1.0 + jnp.exp(-x), LARGE)
    inverse = pl.reciprocal(below, approx=True)
    return x * (inverse * (2.0 - below * inverse))


def filtered(padded, taps, begin, length):
    first = begin + RIM + 1 - len(taps)
    total = taps[0] * padded[first : first + length]
    for j in range(1, len(taps)):
        total = total + taps[j] * padded[first + j : first + j + length]
    return silu(total)


def taps_of(taps_ref, which, head):
    return [taps_ref[which, j, pl.ds(head, 1), :] for j in range(taps_ref.shape[1])]


def unit(rows):
    return rows * lax.rsqrt(jnp.sum(rows * rows, axis=-1, keepdims=True) + EPSILON)


def same_document(second_resets, row, col):
    return ((row // BLOCK) - (col // BLOCK)) * second_resets == 0


def lower_inverse(lowers, row, col):
    differ = row ^ col
    eye = (row == col).astype(F32)
    in_block = (differ < 8).astype(F32)
    diagonal = [low * in_block for low in lowers]
    powers = [d.astype(BF16) for d in diagonal]
    squares = [mul(p, p).astype(BF16) for p in powers]
    inverse = [eye - d for d in diagonal]
    fourths = [mul(s, s).astype(BF16) for s in squares]
    inverse = [x + mul(x.astype(BF16), s) for x, s in zip(inverse, squares)]
    inverse = [x + mul(x.astype(BF16), s) for x, s in zip(inverse, fourths)]
    size = 8
    while size < CHUNK:
        joint = odd_blocks(((differ >= size) & (differ < 2 * size)).astype(F32), size)
        rounded = [x.astype(BF16) for x in inverse]
        inner = [
            mul((odd_blocks(low, size) * joint).astype(BF16), x)
            for low, x in zip(lowers, rounded)
        ]
        outer = [
            mul(odd_blocks(x, size).astype(BF16), with_even_zeros(i, size).astype(BF16))
            for x, i in zip(inverse, inner)
        ]
        inverse = [less_in_odd(x, o, size) for x, o in zip(inverse, outer)]
        size *= 2
    return inverse


def odd_blocks(a, size):
    return jnp.concatenate([a[b : b + size] for b in range(size, a.shape[0], 2 * size)], axis=0)


def with_even_zeros(odd, size):
    zeros = jnp.zeros((size, odd.shape[1]), odd.dtype)
    pieces = []
    for b in range(0, odd.shape[0], size):
        pieces += [zeros, odd[b : b + size]]
    return jnp.concatenate(pieces, axis=0)


def less_in_odd(a, odd, size):
    pieces = []
    for b in range(0, odd.shape[0], size):
        pieces.append(a[2 * b : 2 * b + size])
        pieces.append(a[2 * b + size : 2 * b + 2 * size] - odd[b : b + size])
    return jnp.concatenate(pieces, axis=0)


def load_kernel(query_ref, key_ref, value_ref, taps_ref, rims_ref, *refs):
    copied, arrived = refs[:-1], refs[-1]
    copies = []
    for i, x_ref in enumerate((query_ref, key_ref, value_ref)):
        last = x_ref.at[pl.ds(x_ref.shape[0] - RIM, RIM)]
        copies.append((last, rims_ref.at[pl.ds(i * RIM, RIM)]))
    copies += zip((key_ref, value_ref, taps_ref), copied)
    copies = [
        pltpu.make_async_copy(source, target, arrived.at[i])
        for i, (source, target) in enumerate(copies)
    ]
    for copy in copies:
        copy.start()
    for copy in copies:
        copy.wait()


def filters_kernel(key_ref, value_ref, taps_ref, unit_ref, value_out_ref, first_ref, padded):
    length, heads, _ = key_ref.shape
    for i, x_ref in enumerate((key_ref, value_ref)):
        for c in range(length // CHUNK):
            begin = RIM + c * CHUNK
            padded[i, :, begin : begin + CHUNK] = jnp.swapaxes(x_ref[rows_of(c)], 0, 1).astype(F32)
        padded[i, :, 0:RIM] = jnp.zeros((heads, RIM, padded.shape[3]), F32)
    first_ref[...] = padded[:, :, RIM : RIM + AGAIN]

    def one_head(h, carry):
        for i in range(2):
            taps = taps_of(taps_ref, 1 + i, h)
            for c in range(length // CHUNK):
                rows = filtered(padded.at[i, h], taps, c * CHUNK, CHUNK)
                if i == 0:
                    unit_ref[h, rows_of(c)] = unit(rows).astype(BF16)
                else:
                    value_out_ref[h, rows_of(c)] = rows.astype(BF16)
        return carry

    lax.fori_loop(0, heads, one_head, 0)


def maps_kernel(
    base, resets, unit_in_ref, value_in_ref, first_ref, rim_ref, taps_ref, decay_ref, strength_ref,
    unit_ref, solved_ref, starts_ref, map_ref,
    rims, padded, value_s, step_s,
):
    heads, length, depth = unit_ref.shape
    chunks = length // CHUNK
    total_heads = decay_ref.shape[0]
    row, col = indices()
    rims[...] = rim_ref[...].astype(F32)
    for g in range(heads):
        h = base + g
        unit_ref[g] = unit_in_ref[h]
        value_s[g] = value_in_ref[h]
        for i in range(2):
            padded[g, i, 0:RIM] = rims[(1 + i) * RIM : (2 + i) * RIM, h, :]
            padded[g, i, RIM : RIM + AGAIN] = first_ref[i, h]
            rows = filtered(padded.at[g, i], taps_of(taps_ref, 1 + i, h), 0, AGAIN)
            if i == 0:
                unit_ref[g, 0:AGAIN] = unit(rows).astype(BF16)
            else:
                value_s[g, 0:AGAIN] = rows.astype(BF16)

    parts = []
    lowers = []
    for c in range(chunks):
        cum, _, columns = token_scalars(decay_ref, strength_ref, c)
        first, second = resets[2 * c], resets[2 * c + 1]
        strictly = (row > col) & same_document(second, row, col)
        for g in range(heads):
            h = base + g
            cum_col = columns[:, h : h + 1]
            cum_row = cum[h : h + 1]
            key = unit_ref[g, rows_of(c)]
            fading = jnp.exp(jnp.where(strictly, cum_col - cum_row, FAR))
            strength_col = columns[:, total_heads + h : total_heads + h + 1]
            lowers.append(strength_col * fading * mul(key, key, NT))
            parts.append((g, c, first, second, cum_col, cum_row, strength_col))
    inverses = lower_inverse(lowers, row, col)
    eye = (row == col).astype(F32)
    first_rows = lax.broadcasted_iota(jnp.int32, (CHUNK, 1), 0) < BLOCK
    for (g, c, first, second, cum_col, cum_row, strength_col), inverse in zip(parts, inverses):
        keep_first = (1 - first).astype(F32)
        keep_second = (1 - second).astype(F32)
        keep_both = keep_first * keep_second
        key = unit_ref[g, rows_of(c)]
        growth = jnp.exp(cum_col) * jnp.where(first_rows, keep_first, keep_both)
        targets = jnp.concatenate(
            [
                (strength_col * growth) * key.astype(F32),
                strength_col * value_s[g, rows_of(c)].astype(F32),
            ],
            axis=1,
        )
        solved = targets + mul((inverse - eye).astype(BF16), targets.astype(BF16))
        solved_ref[g, rows_of(c)] = solved
        end = cum_row[:, CHUNK - 1 : CHUNK]
        tail = jnp.exp(end - cum_col) * jnp.where(first_rows, keep_second, 1.0)
        product = mul(key, (tail * solved).astype(BF16), TN)
        passed = jnp.exp(end) * keep_both
        step_s[g, c, :, :depth] = jnp.where(row == col, passed, 0.0) - product[:, :depth]
        step_s[g, c, :, depth:] = product[:, depth:]

    def compose(later, earlier):
        high, low = split(earlier)
        trans = later[:, :depth].astype(BF16)
        joined = mul(trans, high) + mul(trans, low)
        return jnp.concatenate([joined[:, :depth], joined[:, depth:] + later[:, depth:]], axis=1)

    every = range(heads)
    states = [step_s[g, 0] for g in every]
    half = chunks // 2
    for c in range(1, half):
        for g in every:
            starts_ref[g, c - 1] = states[g]
        states = [compose(step_s[g, c], states[g]) for g in every]
    rest = [step_s[g, half] for g in every]
    for c in range(half + 1, chunks):
        rest = [compose(step_s[g, c], rest[g]) for g in every]
    for g in every:
        map_ref[g] = compose(rest[g], states[g]).astype(BF16)
    for c in range(half, chunks):
        for g in every:
            starts_ref[g, c - 1] = states[g]
        if c + 1 < chunks:
            states = [compose(step_s[g, c], states[g]) for g in every]


def reads_kernel(
    base, resets, query_ref, gate_ref, gain_ref, rim_ref, taps_ref, decay_ref, strength_ref,
    unit_ref, solved_ref, starts_ref,
    reach_ref, part_ref, gating_ref,
    rims, padded, query_s,
):
    heads, length, depth = unit_ref.shape
    chunks = length // CHUNK
    row, col = indices()
    first_rows = lax.broadcasted_iota(jnp.int32, (CHUNK, 1), 0) < BLOCK
    rims[...] = rim_ref[...].astype(F32)
    for g in range(heads):
        h = base + g
        padded[g, 0:RIM] = rims[0:RIM, h, :]
        padded[g, RIM : RIM + length] = query_ref[h].astype(F32)
        taps = taps_of(taps_ref, 0, h)
        for c in range(chunks):
            rows = filtered(padded.at[g], taps, c * CHUNK, CHUNK)
            query_s[g, rows_of(c)] = (unit(rows) * depth**-0.5).astype(BF16)

    for c in range(chunks):
        here = rows_of(c)
        cum, _, columns = token_scalars(decay_ref, strength_ref, c)
        first, second = resets[2 * c], resets[2 * c + 1]
        keep_first = (1 - first).astype(F32)
        keep_both = keep_first * (1 - second).astype(F32)
        upto = (row >= col) & same_document(second, row, col)
        for g in range(heads):
            h = base + g
            cum_col = columns[:, h : h + 1]
            query = query_s[g, here]
            fading = jnp.exp(jnp.where(upto, cum_col - cum[h : h + 1], FAR))
            mixing = fading * mul(query, unit_ref[g, here], NT)
            own = mul_split(mixing, solved_ref[g, here])
            growth = jnp.exp(cum_col) * jnp.where(first_rows, keep_first, keep_both)
            reach = growth * query.astype(F32) - own[:, :depth]
            part = own[:, depth:]
            if c:
                both = mul_split(reach, starts_ref[g, c - 1])
                reach = both[:, :depth]
                part = part + both[:, depth:]
            reach_ref[g, here] = reach.astype(BF16)
            part_ref[g, here] = part
            gate = gate_ref[h, here].astype(F32)
            gating_ref[g, here] = gain_ref[...] * silu(gate)


def partner(place, k, count):
    if count & (count - 1) == 0:
        return place ^ k
    return lax.rem(place + count - k, count)


def pairs_at(k, count):
    if count & (count - 1) == 0:
        return [(i, i ^ k) for i in range(count)]
    return [(i, (i + k) % count) for i in range(count)]


def join_kernel(count, place, *refs):
    maps = refs[:count]
    before_ref, state_ref, *trans_ref, ordered = refs[count:]
    heads, depth, _ = before_ref.shape
    me = place[0]
    for k in range(count):
        ordered[partner(me, k, count)] = maps[k][...]
    row, col = indices()
    eye = (row == col).astype(F32)
    states = [jnp.concatenate([eye, jnp.zeros((depth, depth), F32)], axis=1)] * heads
    for lap in range(count):

        @pl.when(lap == me)
        def _():
            for h in range(heads):
                before_ref[h] = states[h]

        for h in range(heads):
            step = ordered[lap, h]
            if lap:
                high, low = split(states[h])
                trans = step[:, :depth]
                joined = mul(trans, high) + mul(trans, low)
                states[h] = jnp.concatenate(
                    [joined[:, :depth], joined[:, depth:] + step[:, depth:].astype(F32)], axis=1
                )
            else:
                states[h] = step.astype(F32)
    for h in range(heads):
        state_ref[h] = states[h][:, depth:].astype(state_ref.dtype)
        for ref in trans_ref:
            ref[h] = states[h][:, :depth]


def outputs_kernel(begin, arrived_ref, before_ref, reach_ref, part_ref, gating_ref, normed_ref):
    heads, _, depth = reach_ref.shape
    for h in range(heads):
        before = before_ref[h]
        incoming = mul_split(before[:, :depth], arrived_ref[h].astype(F32)) + before[:, depth:]
        high, low = split(incoming)
        for c in range(normed_ref.shape[0] // CHUNK):
            here = slice(begin + c * CHUNK, begin + (c + 1) * CHUNK)
            reach = reach_ref[h, here]
            core = part_ref[h, here] + (mul(reach, high) + mul(reach, low))
            scale = lax.rsqrt(jnp.sum(core * core, axis=-1, keepdims=True) / depth + EPSILON)
            normed_ref[rows_of(c), h * depth : (h + 1) * depth] = (
                core * scale * gating_ref[h, here]
            ).astype(BF16)


def last_kernel(begin, section, total_ref, block_ref, weights_ref, *refs):
    out_ref, tiles, written = refs[-3:]
    width = block_ref.shape[1]
    rows = weights_ref[pl.ds(pl.multiple_of(section[0] * width, width), width), :]
    copies = []
    for i in range(total_ref.shape[0] // CHUNK):
        here = rows_of(i)
        tiles[here] = (total_ref[here] + mul(block_ref[here], rows)).astype(BF16)
        target = out_ref.at[pl.ds(begin + i * CHUNK, CHUNK)]
        copies.append(pltpu.make_async_copy(tiles.at[here], target, written.at[i]))
        copies[-1].start()
    for copy in copies:
        copy.wait()


def from_behind(value, axis, steps):
    count = lax.axis_size(axis)
    return lax.ppermute(value, axis, [(i, i + steps) for i in range(count - steps)])


VMEM = pl.BlockSpec(memory_space=pltpu.VMEM)
SMEM = pl.BlockSpec(memory_space=pltpu.SMEM)
HBM = pl.BlockSpec(memory_space=pltpu.HBM)
PARAMS = pltpu.CompilerParams(vmem_limit_bytes=12 * 1024 * 1024)


def load(query_in, key_in, value_in, taps):
    _, heads, depth = query_in.shape
    like = [jax.ShapeDtypeStruct(x.shape, x.dtype) for x in (key_in, value_in, taps)]
    return pl.pallas_call(
        load_kernel,
        out_shape=[jax.ShapeDtypeStruct((3 * RIM, heads, depth), BF16)] + like,
        in_specs=[HBM] * 4,
        out_specs=[VMEM] * 4,
        scratch_shapes=[pltpu.SemaphoreType.DMA((6,))],
        compiler_params=PARAMS,
    )(query_in, key_in, value_in, taps)


def filters_of(key, value, taps):
    length, heads, depth = key.shape
    per_token = jax.ShapeDtypeStruct((heads, length, depth), BF16)
    return pl.pallas_call(
        filters_kernel,
        out_shape=(per_token, per_token, jax.ShapeDtypeStruct((2, heads, AGAIN, depth), F32)),
        in_specs=[VMEM] * 3,
        out_specs=[VMEM] * 3,
        scratch_shapes=[pltpu.VMEM((2, heads, length + RIM, depth), F32)],
        compiler_params=PARAMS,
        cost_estimate=pl.CostEstimate(
            flops=3 * 10**9, bytes_accessed=4 * 2**20, transcendentals=10**6
        ),
    )(key, value, taps)


def maps_of(base, heads, resets, unit_in, value_in, first, rims, taps, decay, strength):
    _, length, depth = unit_in.shape
    chunks = length // CHUNK
    return pl.pallas_call(
        functools.partial(maps_kernel, base),
        out_shape=(
            jax.ShapeDtypeStruct((heads, length, depth), BF16),
            jax.ShapeDtypeStruct((heads, length, 2 * depth), F32),
            jax.ShapeDtypeStruct((heads, chunks - 1, depth, 2 * depth), F32),
            jax.ShapeDtypeStruct((heads, depth, 2 * depth), BF16),
        ),
        in_specs=[SMEM] + [VMEM] * 7,
        out_specs=[VMEM] * 4,
        scratch_shapes=[
            pltpu.VMEM(rims.shape, F32),
            pltpu.VMEM((heads, 2, RIM + AGAIN, depth), F32),
            pltpu.VMEM((heads, length, depth), BF16),
            pltpu.VMEM((heads, chunks, depth, 2 * depth), F32),
        ],
        compiler_params=PARAMS,
        cost_estimate=pl.CostEstimate(
            flops=5 * 10**9, bytes_accessed=4 * 2**20, transcendentals=10**6
        ),
    )(resets, unit_in, value_in, first, rims, taps, decay, strength)


def reads_of(base, heads, resets, query, gate, gain, rims, taps, decay, strength, made):
    _, length, depth = query.shape
    per_token = jax.ShapeDtypeStruct((heads, length, depth), F32)
    return pl.pallas_call(
        functools.partial(reads_kernel, base),
        out_shape=(jax.ShapeDtypeStruct(per_token.shape, BF16), per_token, per_token),
        in_specs=[SMEM] + [VMEM] * 10,
        out_specs=[VMEM] * 3,
        scratch_shapes=[
            pltpu.VMEM(rims.shape, F32),
            pltpu.VMEM((heads, length + RIM, depth), F32),
            pltpu.VMEM((heads, length, depth), BF16),
        ],
        compiler_params=PARAMS,
        cost_estimate=pl.CostEstimate(
            flops=3 * 10**9, bytes_accessed=4 * 2**20, transcendentals=10**6
        ),
    )(resets, query, gate, gain, rims, taps, decay, strength, *made)


def join(place, maps, links):
    count = len(maps)
    heads, depth, _ = maps[0].shape
    pair = jax.ShapeDtypeStruct((heads, depth, 2 * depth), F32)
    square = (heads, depth, depth)
    if links == 1:
        totals = (jax.ShapeDtypeStruct(square, BF16),)
    else:
        totals = (jax.ShapeDtypeStruct(square, F32),) * 2
    return pl.pallas_call(
        functools.partial(join_kernel, count),
        out_shape=(pair, *totals),
        in_specs=[SMEM] + [VMEM] * count,
        out_specs=[VMEM] * (1 + len(totals)),
        scratch_shapes=[pltpu.VMEM((count, heads, depth, 2 * depth), BF16)],
        compiler_params=PARAMS,
    )(place, *maps)


def outputs_of(begin, count, arrived, before, reads):
    heads, _, depth = reads[0].shape
    return pl.pallas_call(
        functools.partial(outputs_kernel, begin),
        out_shape=jax.ShapeDtypeStruct((count, heads * depth), BF16),
        in_specs=[VMEM] * 5,
        out_specs=VMEM,
        compiler_params=PARAMS,
    )(arrived, before, *reads)


def last_projected(begin, section, total, block, weights, length, result):
    count, columns = total.shape
    whole = pl.BlockSpec(memory_space=pl.ANY)
    earlier = [] if result is None else [result]
    return pl.pallas_call(
        functools.partial(last_kernel, begin),
        out_shape=jax.ShapeDtypeStruct((length, columns), BF16),
        in_specs=[SMEM] + [VMEM] * 3 + [whole] * len(earlier),
        out_specs=whole,
        scratch_shapes=[
            pltpu.VMEM((count, columns), BF16),
            pltpu.SemaphoreType.DMA((count // CHUNK,)),
        ],
        input_output_aliases={4: 0} if earlier else {},
        compiler_params=PARAMS,
    )(section.astype(jnp.int32).reshape(1), total, block, weights, *earlier)


def after(first, *values):
    return lax.optimization_barrier((first, *values))[1:]


def on_device(
    query_in,
    key_in,
    value_in,
    gate_in,
    write_strength,
    log_decay,
    doc_resets,
    conv_weight,
    output_norm_gain,
    output_projection_weight,
):
    length, heads, depth = query_in.shape
    last_rows, key, value, taps = load(query_in, key_in, value_in, conv_weight)
    rims = from_behind(last_rows, ("chain", "leaf"), 1)
    key, value, first = filters_of(key, value, taps)
    gain = output_norm_gain.reshape(1, depth)
    leaves = lax.axis_size("leaf")
    place = lax.axis_index("leaf").astype(jnp.int32).reshape(1)

    links = lax.axis_size("chain") - 1
    *made, own_map = maps_of(
        0, heads, doc_resets, key, value, first, rims, taps, log_decay, write_strength
    )
    maps = [own_map] + [
        lax.ppermute(own_map, "leaf", pairs_at(k, leaves)) for k in range(1, leaves)
    ]
    query_in, gate_in = after(own_map, query_in, gate_in)
    query, gate = (jnp.transpose(x, (1, 0, 2)) for x in (query_in, gate_in))
    reads = reads_of(
        0, heads, doc_resets, query, gate, gain, rims, taps, log_decay, write_strength, made
    )
    maps, reads = lax.optimization_barrier((maps, reads))
    before, state, *trans = join(place, maps, links)
    arrived = from_behind(state.astype(BF16), "chain", 1)
    for _ in range(links - 1):
        passed = jnp.einsum(
            "hij,hjk->hik", trans[0], arrived.astype(F32), precision=lax.Precision.HIGHEST
        )
        arrived = from_behind((passed + state).astype(BF16), "chain", 1)
    count = length // PARTS
    blocks = []
    for p in range(PARTS):
        blocks.append(outputs_of(p * count, count, arrived, before, reads))
        arrived = after(blocks[p], arrived)[0]

    ring = lax.axis_size("head")
    mine = lax.axis_index("head")
    width = heads * depth
    around = [(i, (i + 1) % ring) for i in range(ring)]
    mixed = [None] * PARTS
    for k in range(ring - 1):
        owner = lax.rem(mine + ring - k, ring)
        rows = lax.dynamic_slice_in_dim(output_projection_weight, owner * width, width, 0)
        following = [lax.ppermute(block, "head", around) for block in blocks]
        for p, block in enumerate(blocks):
            term = jnp.dot(block, rows, preferred_element_type=F32)
            mixed[p] = term if mixed[p] is None else mixed[p] + term
        blocks = following
    result = None
    for p, block in enumerate(blocks):
        result = last_projected(
            p * count, lax.rem(mine + 1, ring), mixed[p], block, output_projection_weight, length,
            result,
        )
    return result


def solution(mesh):
    return jax.shard_map(
        on_device,
        mesh=mesh,
        in_specs=(
            P(("chain", "leaf"), "head", None),
            P(("chain", "leaf"), "head", None),
            P(("chain", "leaf"), "head", None),
            P(("chain", "leaf"), "head", None),
            P("head", ("chain", "leaf")),
            P("head", ("chain", "leaf")),
            P(("chain", "leaf")),
            P(None, None, "head", None),
            P(),
            P(None, "head"),
        ),
        out_specs=P(("chain", "leaf"), "head"),
        check_vma=False,
    )
```

```python
import functools

import jax
import jax.numpy as jnp
from jax import lax
from jax.experimental import pallas as pl
from jax.experimental.pallas import tpu as pltpu
from jax.sharding import PartitionSpec as P

BLOCK = 64
CHUNK = 128
PARTS = 2
RIM = 8
EPSILON = 1e-06
FAR = -1e30
LARGE = 1e38
AGAIN = 16
F32 = jnp.float32
BF16 = jnp.bfloat16
NN = (((1,), (0,)), ((), ()))
NT = (((1,), (1,)), ((), ()))
TN = (((0,), (0,)), ((), ()))


def split(a):
    high = a.astype(BF16)
    return high, (a - high.astype(F32)).astype(BF16)


def mul(a, b, dims=NN):
    return lax.dot_general(a, b, dims, preferred_element_type=F32)


def mul_split(a, b):
    a_high, a_low = split(a)
    b_high, b_low = split(b)
    return mul(a_high, b_high) + (mul(a_low, b_high) + mul(a_high, b_low))


def rows_of(c):
    return slice(c * CHUNK, (c + 1) * CHUNK)


def indices():
    shape = (CHUNK, CHUNK)
    return (
        lax.broadcasted_iota(jnp.int32, shape, 0),
        lax.broadcasted_iota(jnp.int32, shape, 1),
    )


def token_scalars(decay_ref, strength_ref, c):
    row, col = indices()
    cum = lax.dot_general(
        decay_ref[:, rows_of(c)],
        (row <= col).astype(F32),
        NN,
        precision=lax.Precision.HIGHEST,
        preferred_element_type=F32,
    )
    strength = strength_ref[:, rows_of(c)]
    stacked = [cum, strength]
    missing = 8 - 2 * cum.shape[0]
    if missing > 0:
        stacked.append(jnp.zeros((missing, CHUNK), F32))
    return cum, strength, jnp.transpose(jnp.concatenate(stacked, axis=0))


def silu(x):
    below = jnp.minimum(1.0 + jnp.exp(-x), LARGE)
    inverse = pl.reciprocal(below, approx=True)
    return x * (inverse * (2.0 - below * inverse))


def filtered(padded, taps, begin, length):
    first = begin + RIM + 1 - len(taps)
    total = taps[0] * padded[first : first + length]
    for j in range(1, len(taps)):
        total = total + taps[j] * padded[first + j : first + j + length]
    return silu(total)


def taps_of(taps_ref, which, head):
    return [taps_ref[which, j, pl.ds(head, 1), :] for j in range(taps_ref.shape[1])]


def unit(rows):
    return rows * lax.rsqrt(jnp.sum(rows * rows, axis=-1, keepdims=True) + EPSILON)


def same_document(second_resets, row, col):
    return ((row // BLOCK) - (col // BLOCK)) * second_resets == 0


def lower_inverse(lowers, row, col):
    differ = row ^ col
    eye = (row == col).astype(F32)
    in_block = (differ < 8).astype(F32)
    diagonal = [low * in_block for low in lowers]
    powers = [d.astype(BF16) for d in diagonal]
    squares = [mul(p, p).astype(BF16) for p in powers]
    inverse = [eye - d for d in diagonal]
    fourths = [mul(s, s).astype(BF16) for s in squares]
    inverse = [x + mul(x.astype(BF16), s) for x, s in zip(inverse, squares)]
    inverse = [x + mul(x.astype(BF16), s) for x, s in zip(inverse, fourths)]
    size = 8
    while size < CHUNK:
        joint = odd_blocks(((differ >= size) & (differ < 2 * size)).astype(F32), size)
        rounded = [x.astype(BF16) for x in inverse]
        inner = [
            mul((odd_blocks(low, size) * joint).astype(BF16), x)
            for low, x in zip(lowers, rounded)
        ]
        outer = [
            mul(odd_blocks(x, size).astype(BF16), with_even_zeros(i, size).astype(BF16))
            for x, i in zip(inverse, inner)
        ]
        inverse = [less_in_odd(x, o, size) for x, o in zip(inverse, outer)]
        size *= 2
    return inverse


def odd_blocks(a, size):
    return jnp.concatenate([a[b : b + size] for b in range(size, a.shape[0], 2 * size)], axis=0)


def with_even_zeros(odd, size):
    zeros = jnp.zeros((size, odd.shape[1]), odd.dtype)
    pieces = []
    for b in range(0, odd.shape[0], size):
        pieces += [zeros, odd[b : b + size]]
    return jnp.concatenate(pieces, axis=0)


def less_in_odd(a, odd, size):
    pieces = []
    for b in range(0, odd.shape[0], size):
        pieces.append(a[2 * b : 2 * b + size])
        pieces.append(a[2 * b + size : 2 * b + 2 * size] - odd[b : b + size])
    return jnp.concatenate(pieces, axis=0)


def rims_kernel(*refs):
    *inputs, packed_ref, arrived = refs
    copies = []
    for i, x_ref in enumerate(inputs):
        last = x_ref.at[pl.ds(x_ref.shape[0] - RIM, RIM)]
        here = packed_ref.at[pl.ds(i * RIM, RIM)]
        copies.append(pltpu.make_async_copy(last, here, arrived.at[i]))
    for copy in copies:
        copy.start()
    for copy in copies:
        copy.wait()


def filters_kernel(key_ref, value_ref, taps_ref, unit_ref, value_out_ref, first_ref, padded):
    heads, length, _ = key_ref.shape
    for i, x_ref in enumerate((key_ref, value_ref)):
        padded[i, :, RIM:] = x_ref[...].astype(F32)
        padded[i, :, 0:RIM] = jnp.zeros((heads, RIM, padded.shape[3]), F32)
    first_ref[...] = padded[:, :, RIM : RIM + AGAIN]

    def one_head(h, carry):
        for i in range(2):
            taps = taps_of(taps_ref, 1 + i, h)
            for c in range(length // CHUNK):
                rows = filtered(padded.at[i, h], taps, c * CHUNK, CHUNK)
                if i == 0:
                    unit_ref[h, rows_of(c)] = unit(rows).astype(BF16)
                else:
                    value_out_ref[h, rows_of(c)] = rows.astype(BF16)
        return carry

    lax.fori_loop(0, heads, one_head, 0)


def maps_kernel(
    base, resets, unit_in_ref, value_in_ref, first_ref, rim_ref, taps_ref, decay_ref, strength_ref,
    unit_ref, solved_ref, starts_ref, map_ref,
    rims, padded, value_s, step_s,
):
    heads, length, depth = unit_ref.shape
    chunks = length // CHUNK
    total_heads = decay_ref.shape[0]
    row, col = indices()
    rims[...] = rim_ref[...].astype(F32)
    for g in range(heads):
        h = base + g
        unit_ref[g] = unit_in_ref[h]
        value_s[g] = value_in_ref[h]
        for i in range(2):
            padded[g, i, 0:RIM] = rims[(1 + i) * RIM : (2 + i) * RIM, h, :]
            padded[g, i, RIM : RIM + AGAIN] = first_ref[i, h]
            rows = filtered(padded.at[g, i], taps_of(taps_ref, 1 + i, h), 0, AGAIN)
            if i == 0:
                unit_ref[g, 0:AGAIN] = unit(rows).astype(BF16)
            else:
                value_s[g, 0:AGAIN] = rows.astype(BF16)

    parts = []
    lowers = []
    for c in range(chunks):
        cum, _, columns = token_scalars(decay_ref, strength_ref, c)
        first, second = resets[2 * c], resets[2 * c + 1]
        strictly = (row > col) & same_document(second, row, col)
        for g in range(heads):
            h = base + g
            cum_col = columns[:, h : h + 1]
            cum_row = cum[h : h + 1]
            key = unit_ref[g, rows_of(c)]
            fading = jnp.exp(jnp.where(strictly, cum_col - cum_row, FAR))
            strength_col = columns[:, total_heads + h : total_heads + h + 1]
            lowers.append(strength_col * fading * mul(key, key, NT))
            parts.append((g, c, first, second, cum_col, cum_row, strength_col))
    inverses = lower_inverse(lowers, row, col)
    eye = (row == col).astype(F32)
    first_rows = lax.broadcasted_iota(jnp.int32, (CHUNK, 1), 0) < BLOCK
    for (g, c, first, second, cum_col, cum_row, strength_col), inverse in zip(parts, inverses):
        keep_first = (1 - first).astype(F32)
        keep_second = (1 - second).astype(F32)
        keep_both = keep_first * keep_second
        key = unit_ref[g, rows_of(c)]
        growth = jnp.exp(cum_col) * jnp.where(first_rows, keep_first, keep_both)
        targets = jnp.concatenate(
            [
                (strength_col * growth) * key.astype(F32),
                strength_col * value_s[g, rows_of(c)].astype(F32),
            ],
            axis=1,
        )
        solved = targets + mul((inverse - eye).astype(BF16), targets.astype(BF16))
        solved_ref[g, rows_of(c)] = solved
        end = cum_row[:, CHUNK - 1 : CHUNK]
        tail = jnp.exp(end - cum_col) * jnp.where(first_rows, keep_second, 1.0)
        product = mul(key, (tail * solved).astype(BF16), TN)
        passed = jnp.exp(end) * keep_both
        step_s[g, c, :, :depth] = jnp.where(row == col, passed, 0.0) - product[:, :depth]
        step_s[g, c, :, depth:] = product[:, depth:]

    def compose(later, earlier):
        high, low = split(earlier)
        trans = later[:, :depth].astype(BF16)
        joined = mul(trans, high) + mul(trans, low)
        return jnp.concatenate([joined[:, :depth], joined[:, depth:] + later[:, depth:]], axis=1)

    every = range(heads)
    states = [step_s[g, 0] for g in every]
    half = chunks // 2
    for c in range(1, half):
        for g in every:
            starts_ref[g, c - 1] = states[g]
        states = [compose(step_s[g, c], states[g]) for g in every]
    rest = [step_s[g, half] for g in every]
    for c in range(half + 1, chunks):
        rest = [compose(step_s[g, c], rest[g]) for g in every]
    for g in every:
        map_ref[g] = compose(rest[g], states[g]).astype(BF16)
    for c in range(half, chunks):
        for g in every:
            starts_ref[g, c - 1] = states[g]
        if c + 1 < chunks:
            states = [compose(step_s[g, c], states[g]) for g in every]


def reads_kernel(
    base, resets, query_ref, gate_ref, gain_ref, rim_ref, taps_ref, decay_ref, strength_ref,
    unit_ref, solved_ref, starts_ref,
    reach_ref, part_ref, gating_ref,
    rims, padded, query_s,
):
    heads, length, depth = unit_ref.shape
    chunks = length // CHUNK
    row, col = indices()
    first_rows = lax.broadcasted_iota(jnp.int32, (CHUNK, 1), 0) < BLOCK
    rims[...] = rim_ref[...].astype(F32)
    for g in range(heads):
        h = base + g
        padded[g, 0:RIM] = rims[0:RIM, h, :]
        padded[g, RIM : RIM + length] = query_ref[h].astype(F32)
        taps = taps_of(taps_ref, 0, h)
        for c in range(chunks):
            rows = filtered(padded.at[g], taps, c * CHUNK, CHUNK)
            query_s[g, rows_of(c)] = (unit(rows) * depth**-0.5).astype(BF16)

    for c in range(chunks):
        here = rows_of(c)
        cum, _, columns = token_scalars(decay_ref, strength_ref, c)
        first, second = resets[2 * c], resets[2 * c + 1]
        keep_first = (1 - first).astype(F32)
        keep_both = keep_first * (1 - second).astype(F32)
        upto = (row >= col) & same_document(second, row, col)
        for g in range(heads):
            h = base + g
            cum_col = columns[:, h : h + 1]
            query = query_s[g, here]
            fading = jnp.exp(jnp.where(upto, cum_col - cum[h : h + 1], FAR))
            mixing = fading * mul(query, unit_ref[g, here], NT)
            own = mul_split(mixing, solved_ref[g, here])
            growth = jnp.exp(cum_col) * jnp.where(first_rows, keep_first, keep_both)
            reach = growth * query.astype(F32) - own[:, :depth]
            part = own[:, depth:]
            if c:
                both = mul_split(reach, starts_ref[g, c - 1])
                reach = both[:, :depth]
                part = part + both[:, depth:]
            reach_ref[g, here] = reach.astype(BF16)
            part_ref[g, here] = part
            gate = gate_ref[h, here].astype(F32)
            gating_ref[g, here] = gain_ref[...] * silu(gate)


def partner(place, k, count):
    if count & (count - 1) == 0:
        return place ^ k
    return lax.rem(place + count - k, count)


def pairs_at(k, count):
    if count & (count - 1) == 0:
        return [(i, i ^ k) for i in range(count)]
    return [(i, (i + k) % count) for i in range(count)]


def join_kernel(count, place, *refs):
    maps = refs[:count]
    before_ref, state_ref, *trans_ref, ordered = refs[count:]
    heads, depth, _ = before_ref.shape
    me = place[0]
    for k in range(count):
        ordered[partner(me, k, count)] = maps[k][...]
    row, col = indices()
    eye = (row == col).astype(F32)
    states = [jnp.concatenate([eye, jnp.zeros((depth, depth), F32)], axis=1)] * heads
    for lap in range(count):

        @pl.when(lap == me)
        def _():
            for h in range(heads):
                before_ref[h] = states[h]

        for h in range(heads):
            step = ordered[lap, h]
            if lap:
                high, low = split(states[h])
                trans = step[:, :depth]
                joined = mul(trans, high) + mul(trans, low)
                states[h] = jnp.concatenate(
                    [joined[:, :depth], joined[:, depth:] + step[:, depth:].astype(F32)], axis=1
                )
            else:
                states[h] = step.astype(F32)
    for h in range(heads):
        state_ref[h] = states[h][:, depth:].astype(state_ref.dtype)
        for ref in trans_ref:
            ref[h] = states[h][:, :depth]


def outputs_kernel(begin, arrived_ref, before_ref, reach_ref, part_ref, gating_ref, normed_ref):
    heads, _, depth = reach_ref.shape
    for h in range(heads):
        before = before_ref[h]
        incoming = mul_split(before[:, :depth], arrived_ref[h].astype(F32)) + before[:, depth:]
        high, low = split(incoming)
        for c in range(normed_ref.shape[0] // CHUNK):
            here = slice(begin + c * CHUNK, begin + (c + 1) * CHUNK)
            reach = reach_ref[h, here]
            core = part_ref[h, here] + (mul(reach, high) + mul(reach, low))
            scale = lax.rsqrt(jnp.sum(core * core, axis=-1, keepdims=True) / depth + EPSILON)
            normed_ref[rows_of(c), h * depth : (h + 1) * depth] = (
                core * scale * gating_ref[h, here]
            ).astype(BF16)


def last_kernel(begin, section, total_ref, block_ref, weights_ref, *refs):
    out_ref, tiles, written = refs[-3:]
    width = block_ref.shape[1]
    rows = weights_ref[pl.ds(pl.multiple_of(section[0] * width, width), width), :]
    copies = []
    for i in range(total_ref.shape[0] // CHUNK):
        here = rows_of(i)
        tiles[here] = (total_ref[here] + mul(block_ref[here], rows)).astype(BF16)
        target = out_ref.at[pl.ds(begin + i * CHUNK, CHUNK)]
        copies.append(pltpu.make_async_copy(tiles.at[here], target, written.at[i]))
        copies[-1].start()
    for copy in copies:
        copy.wait()


def from_behind(value, axis, steps):
    count = lax.axis_size(axis)
    return lax.ppermute(value, axis, [(i, i + steps) for i in range(count - steps)])


VMEM = pl.BlockSpec(memory_space=pltpu.VMEM)
SMEM = pl.BlockSpec(memory_space=pltpu.SMEM)
HBM = pl.BlockSpec(memory_space=pltpu.HBM)
PARAMS = pltpu.CompilerParams(vmem_limit_bytes=12 * 1024 * 1024)


def pack_rims(inputs):
    _, heads, depth = inputs[0].shape
    return pl.pallas_call(
        rims_kernel,
        out_shape=jax.ShapeDtypeStruct((len(inputs) * RIM, heads, depth), BF16),
        in_specs=[HBM] * len(inputs),
        out_specs=VMEM,
        scratch_shapes=[pltpu.SemaphoreType.DMA((len(inputs),))],
    )(*inputs)


def filters_of(key, value, taps):
    heads, length, depth = key.shape
    per_token = jax.ShapeDtypeStruct((heads, length, depth), BF16)
    return pl.pallas_call(
        filters_kernel,
        out_shape=(per_token, per_token, jax.ShapeDtypeStruct((2, heads, AGAIN, depth), F32)),
        in_specs=[VMEM] * 3,
        out_specs=[VMEM] * 3,
        scratch_shapes=[pltpu.VMEM((2, heads, length + RIM, depth), F32)],
        compiler_params=PARAMS,
        cost_estimate=pl.CostEstimate(
            flops=3 * 10**9, bytes_accessed=4 * 2**20, transcendentals=10**6
        ),
    )(key, value, taps)


def maps_of(base, heads, resets, unit_in, value_in, first, rims, taps, decay, strength):
    _, length, depth = unit_in.shape
    chunks = length // CHUNK
    return pl.pallas_call(
        functools.partial(maps_kernel, base),
        out_shape=(
            jax.ShapeDtypeStruct((heads, length, depth), BF16),
            jax.ShapeDtypeStruct((heads, length, 2 * depth), F32),
            jax.ShapeDtypeStruct((heads, chunks - 1, depth, 2 * depth), F32),
            jax.ShapeDtypeStruct((heads, depth, 2 * depth), BF16),
        ),
        in_specs=[SMEM] + [VMEM] * 7,
        out_specs=[VMEM] * 4,
        scratch_shapes=[
            pltpu.VMEM(rims.shape, F32),
            pltpu.VMEM((heads, 2, RIM + AGAIN, depth), F32),
            pltpu.VMEM((heads, length, depth), BF16),
            pltpu.VMEM((heads, chunks, depth, 2 * depth), F32),
        ],
        compiler_params=PARAMS,
        cost_estimate=pl.CostEstimate(
            flops=5 * 10**9, bytes_accessed=4 * 2**20, transcendentals=10**6
        ),
    )(resets, unit_in, value_in, first, rims, taps, decay, strength)


def reads_of(base, heads, resets, query, gate, gain, rims, taps, decay, strength, made):
    _, length, depth = query.shape
    per_token = jax.ShapeDtypeStruct((heads, length, depth), F32)
    return pl.pallas_call(
        functools.partial(reads_kernel, base),
        out_shape=(jax.ShapeDtypeStruct(per_token.shape, BF16), per_token, per_token),
        in_specs=[SMEM] + [VMEM] * 10,
        out_specs=[VMEM] * 3,
        scratch_shapes=[
            pltpu.VMEM(rims.shape, F32),
            pltpu.VMEM((heads, length + RIM, depth), F32),
            pltpu.VMEM((heads, length, depth), BF16),
        ],
        compiler_params=PARAMS,
        cost_estimate=pl.CostEstimate(
            flops=3 * 10**9, bytes_accessed=4 * 2**20, transcendentals=10**6
        ),
    )(resets, query, gate, gain, rims, taps, decay, strength, *made)


def join(place, maps, links):
    count = len(maps)
    heads, depth, _ = maps[0].shape
    pair = jax.ShapeDtypeStruct((heads, depth, 2 * depth), F32)
    square = (heads, depth, depth)
    if links == 1:
        totals = (jax.ShapeDtypeStruct(square, BF16),)
    else:
        totals = (jax.ShapeDtypeStruct(square, F32),) * 2
    return pl.pallas_call(
        functools.partial(join_kernel, count),
        out_shape=(pair, *totals),
        in_specs=[SMEM] + [VMEM] * count,
        out_specs=[VMEM] * (1 + len(totals)),
        scratch_shapes=[pltpu.VMEM((count, heads, depth, 2 * depth), BF16)],
        compiler_params=PARAMS,
    )(place, *maps)


def outputs_of(begin, count, arrived, before, reads):
    heads, _, depth = reads[0].shape
    return pl.pallas_call(
        functools.partial(outputs_kernel, begin),
        out_shape=jax.ShapeDtypeStruct((count, heads * depth), BF16),
        in_specs=[VMEM] * 5,
        out_specs=VMEM,
        compiler_params=PARAMS,
    )(arrived, before, *reads)


def last_projected(begin, section, total, block, weights, length, result):
    count, columns = total.shape
    whole = pl.BlockSpec(memory_space=pl.ANY)
    earlier = [] if result is None else [result]
    return pl.pallas_call(
        functools.partial(last_kernel, begin),
        out_shape=jax.ShapeDtypeStruct((length, columns), BF16),
        in_specs=[SMEM] + [VMEM] * 3 + [whole] * len(earlier),
        out_specs=whole,
        scratch_shapes=[
            pltpu.VMEM((count, columns), BF16),
            pltpu.SemaphoreType.DMA((count // CHUNK,)),
        ],
        input_output_aliases={4: 0} if earlier else {},
        compiler_params=PARAMS,
    )(section.astype(jnp.int32).reshape(1), total, block, weights, *earlier)


def after(first, *values):
    return lax.optimization_barrier((first, *values))[1:]


def on_device(
    query_in,
    key_in,
    value_in,
    gate_in,
    write_strength,
    log_decay,
    doc_resets,
    conv_weight,
    output_norm_gain,
    output_projection_weight,
):
    length, heads, depth = query_in.shape
    taps = conv_weight
    rims = from_behind(pack_rims((query_in, key_in, value_in)), ("chain", "leaf"), 1)
    key, value = (jnp.transpose(x, (1, 0, 2)) for x in (key_in, value_in))
    key, value, first = filters_of(key, value, taps)
    gain = output_norm_gain.reshape(1, depth)
    leaves = lax.axis_size("leaf")
    place = lax.axis_index("leaf").astype(jnp.int32).reshape(1)

    links = lax.axis_size("chain") - 1
    *made, own_map = maps_of(
        0, heads, doc_resets, key, value, first, rims, taps, log_decay, write_strength
    )
    maps = [own_map] + [
        lax.ppermute(own_map, "leaf", pairs_at(k, leaves)) for k in range(1, leaves)
    ]
    query_in, gate_in = after(own_map, query_in, gate_in)
    query, gate = (jnp.transpose(x, (1, 0, 2)) for x in (query_in, gate_in))
    reads = reads_of(
        0, heads, doc_resets, query, gate, gain, rims, taps, log_decay, write_strength, made
    )
    maps, reads = lax.optimization_barrier((maps, reads))
    before, state, *trans = join(place, maps, links)
    arrived = from_behind(state.astype(BF16), "chain", 1)
    for _ in range(links - 1):
        passed = jnp.einsum(
            "hij,hjk->hik", trans[0], arrived.astype(F32), precision=lax.Precision.HIGHEST
        )
        arrived = from_behind((passed + state).astype(BF16), "chain", 1)
    count = length // PARTS
    blocks = []
    for p in range(PARTS):
        blocks.append(outputs_of(p * count, count, arrived, before, reads))
        arrived = after(blocks[p], arrived)[0]

    ring = lax.axis_size("head")
    mine = lax.axis_index("head")
    width = heads * depth
    around = [(i, (i + 1) % ring) for i in range(ring)]
    mixed = [None] * PARTS
    for k in range(ring - 1):
        owner = lax.rem(mine + ring - k, ring)
        rows = lax.dynamic_slice_in_dim(output_projection_weight, owner * width, width, 0)
        following = [lax.ppermute(block, "head", around) for block in blocks]
        for p, block in enumerate(blocks):
            term = jnp.dot(block, rows, preferred_element_type=F32)
            mixed[p] = term if mixed[p] is None else mixed[p] + term
        blocks = following
    result = None
    for p, block in enumerate(blocks):
        result = last_projected(
            p * count, lax.rem(mine + 1, ring), mixed[p], block, output_projection_weight, length,
            result,
        )
    return result


def solution(mesh):
    return jax.shard_map(
        on_device,
        mesh=mesh,
        in_specs=(
            P(("chain", "leaf"), "head", None),
            P(("chain", "leaf"), "head", None),
            P(("chain", "leaf"), "head", None),
            P(("chain", "leaf"), "head", None),
            P("head", ("chain", "leaf")),
            P("head", ("chain", "leaf")),
            P(("chain", "leaf")),
            P(None, None, "head", None),
            P(),
            P(None, "head"),
        ),
        out_specs=P(("chain", "leaf"), "head"),
        check_vma=False,
    )
```

```python
import functools

import jax
import jax.numpy as jnp
from jax import lax
from jax.experimental import pallas as pl
from jax.experimental.pallas import tpu as pltpu
from jax.sharding import PartitionSpec as P

BLOCK = 64
CHUNK = 128
GROUPS = 2
RIM = 8
EPSILON = 1e-06
FAR = -1e30
LARGE = 1e38
AGAIN = 16
F32 = jnp.float32
BF16 = jnp.bfloat16
NN = (((1,), (0,)), ((), ()))
NT = (((1,), (1,)), ((), ()))
TN = (((0,), (0,)), ((), ()))


def split(a):
    high = a.astype(BF16)
    return high, (a - high.astype(F32)).astype(BF16)


def mul(a, b, dims=NN):
    return lax.dot_general(a, b, dims, preferred_element_type=F32)


def mul_split(a, b):
    a_high, a_low = split(a)
    b_high, b_low = split(b)
    return mul(a_high, b_high) + (mul(a_low, b_high) + mul(a_high, b_low))


def rows_of(c):
    return slice(c * CHUNK, (c + 1) * CHUNK)


def indices():
    shape = (CHUNK, CHUNK)
    return (
        lax.broadcasted_iota(jnp.int32, shape, 0),
        lax.broadcasted_iota(jnp.int32, shape, 1),
    )


def token_scalars(decay_ref, strength_ref, c):
    row, col = indices()
    cum = lax.dot_general(
        decay_ref[:, rows_of(c)],
        (row <= col).astype(F32),
        NN,
        precision=lax.Precision.HIGHEST,
        preferred_element_type=F32,
    )
    strength = strength_ref[:, rows_of(c)]
    stacked = [cum, strength]
    missing = 8 - 2 * cum.shape[0]
    if missing > 0:
        stacked.append(jnp.zeros((missing, CHUNK), F32))
    return cum, strength, jnp.transpose(jnp.concatenate(stacked, axis=0))


def silu(x):
    below = jnp.minimum(1.0 + jnp.exp(-x), LARGE)
    inverse = pl.reciprocal(below, approx=True)
    return x * (inverse * (2.0 - below * inverse))


def filtered(padded, taps, begin, length):
    first = begin + RIM + 1 - len(taps)
    total = taps[0] * padded[first : first + length]
    for j in range(1, len(taps)):
        total = total + taps[j] * padded[first + j : first + j + length]
    return silu(total)


def taps_of(taps_ref, which, head):
    return [taps_ref[which, j, pl.ds(head, 1), :] for j in range(taps_ref.shape[1])]


def unit(rows):
    return rows * lax.rsqrt(jnp.sum(rows * rows, axis=-1, keepdims=True) + EPSILON)


def same_document(second_resets, row, col):
    return ((row // BLOCK) - (col // BLOCK)) * second_resets == 0


def lower_inverse(lowers, row, col):
    differ = row ^ col
    eye = (row == col).astype(F32)
    in_block = (differ < 8).astype(F32)
    diagonal = [low * in_block for low in lowers]
    powers = [d.astype(BF16) for d in diagonal]
    squares = [mul(p, p).astype(BF16) for p in powers]
    inverse = [eye - d for d in diagonal]
    stacked = [
        mul(jnp.concatenate([s, x.astype(BF16)], axis=0), s) for x, s in zip(inverse, squares)
    ]
    fourths = [both[:CHUNK].astype(BF16) for both in stacked]
    inverse = [x + both[CHUNK:] for x, both in zip(inverse, stacked)]
    inverse = [x + mul(x.astype(BF16), s) for x, s in zip(inverse, fourths)]
    size = 8
    while size < CHUNK:
        joint = odd_blocks(((differ >= size) & (differ < 2 * size)).astype(F32), size)
        rounded = [x.astype(BF16) for x in inverse]
        inner = [
            mul((odd_blocks(low, size) * joint).astype(BF16), x)
            for low, x in zip(lowers, rounded)
        ]
        outer = [
            mul(odd_blocks(x, size).astype(BF16), with_even_zeros(i, size).astype(BF16))
            for x, i in zip(inverse, inner)
        ]
        inverse = [less_in_odd(x, o, size) for x, o in zip(inverse, outer)]
        size *= 2
    return inverse


def odd_blocks(a, size):
    return jnp.concatenate([a[b : b + size] for b in range(size, a.shape[0], 2 * size)], axis=0)


def with_even_zeros(odd, size):
    zeros = jnp.zeros((size, odd.shape[1]), odd.dtype)
    pieces = []
    for b in range(0, odd.shape[0], size):
        pieces += [zeros, odd[b : b + size]]
    return jnp.concatenate(pieces, axis=0)


def less_in_odd(a, odd, size):
    pieces = []
    for b in range(0, odd.shape[0], size):
        pieces.append(a[2 * b : 2 * b + size])
        pieces.append(a[2 * b + size : 2 * b + 2 * size] - odd[b : b + size])
    return jnp.concatenate(pieces, axis=0)


def rims_kernel(*refs):
    *inputs, packed_ref, arrived = refs
    copies = []
    for i, x_ref in enumerate(inputs):
        last = x_ref.at[pl.ds(x_ref.shape[0] - RIM, RIM)]
        here = packed_ref.at[pl.ds(i * RIM, RIM)]
        copies.append(pltpu.make_async_copy(last, here, arrived.at[i]))
    for copy in copies:
        copy.start()
    for copy in copies:
        copy.wait()


def filters_kernel(key_ref, value_ref, taps_ref, unit_ref, value_out_ref, first_ref, padded):
    heads, length, _ = key_ref.shape
    for i, x_ref in enumerate((key_ref, value_ref)):
        padded[i, :, RIM:] = x_ref[...].astype(F32)
        padded[i, :, 0:RIM] = jnp.zeros((heads, RIM, padded.shape[3]), F32)
    first_ref[...] = padded[:, :, RIM : RIM + AGAIN]

    def one_head(h, carry):
        for i in range(2):
            taps = taps_of(taps_ref, 1 + i, h)
            for c in range(length // CHUNK):
                rows = filtered(padded.at[i, h], taps, c * CHUNK, CHUNK)
                if i == 0:
                    unit_ref[h, rows_of(c)] = unit(rows).astype(BF16)
                else:
                    value_out_ref[h, rows_of(c)] = rows.astype(BF16)
        return carry

    lax.fori_loop(0, heads, one_head, 0)


def maps_kernel(
    base, resets, unit_in_ref, value_in_ref, first_ref, rim_ref, taps_ref, decay_ref, strength_ref,
    unit_ref, solved_ref, starts_ref, *refs,
):
    *map_refs, rims, padded, value_s, step_s = refs
    heads, length, depth = unit_ref.shape
    chunks = length // CHUNK
    size = heads // len(map_refs)
    total_heads = decay_ref.shape[0]
    row, col = indices()
    rims[...] = rim_ref[...].astype(F32)
    for g in range(heads):
        h = base + g
        unit_ref[g] = unit_in_ref[h]
        value_s[g] = value_in_ref[h]
        for i in range(2):
            padded[g, i, 0:RIM] = rims[(1 + i) * RIM : (2 + i) * RIM, h, :]
            padded[g, i, RIM : RIM + AGAIN] = first_ref[i, h]
            rows = filtered(padded.at[g, i], taps_of(taps_ref, 1 + i, h), 0, AGAIN)
            if i == 0:
                unit_ref[g, 0:AGAIN] = unit(rows).astype(BF16)
            else:
                value_s[g, 0:AGAIN] = rows.astype(BF16)

    parts = []
    lowers = []
    for c in range(chunks):
        cum, _, columns = token_scalars(decay_ref, strength_ref, c)
        first, second = resets[2 * c], resets[2 * c + 1]
        strictly = (row > col) & same_document(second, row, col)
        for g in range(heads):
            h = base + g
            cum_col = columns[:, h : h + 1]
            cum_row = cum[h : h + 1]
            key = unit_ref[g, rows_of(c)]
            fading = jnp.exp(jnp.where(strictly, cum_col - cum_row, FAR))
            strength_col = columns[:, total_heads + h : total_heads + h + 1]
            lowers.append(strength_col * fading * mul(key, key, NT))
            parts.append((g, c, first, second, cum_col, cum_row, strength_col))
    inverses = lower_inverse(lowers, row, col)
    eye = (row == col).astype(F32)
    first_rows = lax.broadcasted_iota(jnp.int32, (CHUNK, 1), 0) < BLOCK
    for (g, c, first, second, cum_col, cum_row, strength_col), inverse in zip(parts, inverses):
        keep_first = (1 - first).astype(F32)
        keep_second = (1 - second).astype(F32)
        keep_both = keep_first * keep_second
        key = unit_ref[g, rows_of(c)]
        growth = jnp.exp(cum_col) * jnp.where(first_rows, keep_first, keep_both)
        targets = jnp.concatenate(
            [
                (strength_col * growth) * key.astype(F32),
                strength_col * value_s[g, rows_of(c)].astype(F32),
            ],
            axis=1,
        )
        solved = targets + mul((inverse - eye).astype(BF16), targets.astype(BF16))
        solved_ref[g, rows_of(c)] = solved
        end = cum_row[:, CHUNK - 1 : CHUNK]
        tail = jnp.exp(end - cum_col) * jnp.where(first_rows, keep_second, 1.0)
        product = mul(key, (tail * solved).astype(BF16), TN)
        passed = jnp.exp(end) * keep_both
        step_s[g, c, :, :depth] = jnp.where(row == col, passed, 0.0) - product[:, :depth]
        step_s[g, c, :, depth:] = product[:, depth:]

    def compose(later, earlier):
        high, low = split(earlier)
        trans = later[:, :depth].astype(BF16)
        joined = mul(trans, high) + mul(trans, low)
        return jnp.concatenate([joined[:, :depth], joined[:, depth:] + later[:, depth:]], axis=1)

    every = range(heads)
    states = [step_s[g, 0] for g in every]
    half = chunks // 2
    for c in range(1, half):
        for g in every:
            starts_ref[g, c - 1] = states[g]
        states = [compose(step_s[g, c], states[g]) for g in every]
    rest = [step_s[g, half] for g in every]
    for c in range(half + 1, chunks):
        rest = [compose(step_s[g, c], rest[g]) for g in every]
    for g in every:
        map_refs[g // size][g % size] = compose(rest[g], states[g]).astype(BF16)
    for c in range(half, chunks):
        for g in every:
            starts_ref[g, c - 1] = states[g]
        if c + 1 < chunks:
            states = [compose(step_s[g, c], states[g]) for g in every]


def reads_kernel(
    base, resets, query_ref, gate_ref, gain_ref, rim_ref, taps_ref, decay_ref, strength_ref,
    unit_ref, solved_ref, starts_ref,
    reach_ref, part_ref, gating_ref,
    rims, padded, query_s,
):
    heads, length, depth = unit_ref.shape
    chunks = length // CHUNK
    row, col = indices()
    first_rows = lax.broadcasted_iota(jnp.int32, (CHUNK, 1), 0) < BLOCK
    rims[...] = rim_ref[...].astype(F32)
    for g in range(heads):
        h = base + g
        padded[g, 0:RIM] = rims[0:RIM, h, :]
        padded[g, RIM : RIM + length] = query_ref[h].astype(F32)
        taps = taps_of(taps_ref, 0, h)
        for c in range(chunks):
            rows = filtered(padded.at[g], taps, c * CHUNK, CHUNK)
            query_s[g, rows_of(c)] = (unit(rows) * depth**-0.5).astype(BF16)

    for c in range(chunks):
        here = rows_of(c)
        cum, _, columns = token_scalars(decay_ref, strength_ref, c)
        first, second = resets[2 * c], resets[2 * c + 1]
        keep_first = (1 - first).astype(F32)
        keep_both = keep_first * (1 - second).astype(F32)
        upto = (row >= col) & same_document(second, row, col)
        for g in range(heads):
            h = base + g
            cum_col = columns[:, h : h + 1]
            query = query_s[g, here]
            fading = jnp.exp(jnp.where(upto, cum_col - cum[h : h + 1], FAR))
            mixing = fading * mul(query, unit_ref[g, here], NT)
            own = mul_split(mixing, solved_ref[g, here])
            growth = jnp.exp(cum_col) * jnp.where(first_rows, keep_first, keep_both)
            reach = growth * query.astype(F32) - own[:, :depth]
            part = own[:, depth:]
            if c:
                both = mul_split(reach, starts_ref[g, c - 1])
                reach = both[:, :depth]
                part = part + both[:, depth:]
            reach_ref[g, here] = reach.astype(BF16)
            part_ref[g, here] = part
            gate = gate_ref[h, here].astype(F32)
            gating_ref[g, here] = gain_ref[...] * silu(gate)


def partner(place, k, count):
    if count & (count - 1) == 0:
        return place ^ k
    return lax.rem(place + count - k, count)


def pairs_at(k, count):
    if count & (count - 1) == 0:
        return [(i, i ^ k) for i in range(count)]
    return [(i, (i + k) % count) for i in range(count)]


def join_kernel(count, place, *refs):
    maps = refs[:count]
    before_ref, state_ref, *trans_ref, ordered = refs[count:]
    heads, depth, _ = before_ref.shape
    me = place[0]
    for k in range(count):
        ordered[partner(me, k, count)] = maps[k][...]
    row, col = indices()
    eye = (row == col).astype(F32)
    states = [jnp.concatenate([eye, jnp.zeros((depth, depth), F32)], axis=1)] * heads
    for lap in range(count):

        @pl.when(lap == me)
        def _():
            for h in range(heads):
                before_ref[h] = states[h]

        for h in range(heads):
            step = ordered[lap, h]
            if lap:
                high, low = split(states[h])
                trans = step[:, :depth]
                joined = mul(trans, high) + mul(trans, low)
                states[h] = jnp.concatenate(
                    [joined[:, :depth], joined[:, depth:] + step[:, depth:].astype(F32)], axis=1
                )
            else:
                states[h] = step.astype(F32)
    for h in range(heads):
        state_ref[h] = states[h][:, depth:].astype(state_ref.dtype)
        for ref in trans_ref:
            ref[h] = states[h][:, :depth]


def outputs_kernel(base, arrived_ref, before_ref, reach_ref, part_ref, gating_ref, normed_ref):
    heads, depth, _ = arrived_ref.shape
    for g in range(heads):
        h = base + g
        before = before_ref[g]
        incoming = mul_split(before[:, :depth], arrived_ref[g].astype(F32)) + before[:, depth:]
        high, low = split(incoming)
        for c in range(normed_ref.shape[0] // CHUNK):
            here = rows_of(c)
            reach = reach_ref[h, here]
            core = part_ref[h, here] + (mul(reach, high) + mul(reach, low))
            scale = lax.rsqrt(jnp.sum(core * core, axis=-1, keepdims=True) / depth + EPSILON)
            normed_ref[here, g * depth : (g + 1) * depth] = (
                core * scale * gating_ref[h, here]
            ).astype(BF16)


def last_kernel(section, first_ref, second_ref, block_ref, weights_ref, out_ref, tiles, written):
    width = block_ref.shape[1]
    rows = weights_ref[pl.ds(pl.multiple_of(section[0] * width, width), width), :]
    copies = []
    for i in range(first_ref.shape[0] // CHUNK):
        here = rows_of(i)
        total = (first_ref[here] + second_ref[here]) + mul(block_ref[here], rows)
        tiles[here] = total.astype(BF16)
        copies.append(pltpu.make_async_copy(tiles.at[here], out_ref.at[here], written.at[i]))
        copies[-1].start()
    for copy in copies:
        copy.wait()


def from_behind(value, axis, steps):
    count = lax.axis_size(axis)
    return lax.ppermute(value, axis, [(i, i + steps) for i in range(count - steps)])


VMEM = pl.BlockSpec(memory_space=pltpu.VMEM)
SMEM = pl.BlockSpec(memory_space=pltpu.SMEM)
HBM = pl.BlockSpec(memory_space=pltpu.HBM)
PARAMS = pltpu.CompilerParams(vmem_limit_bytes=12 * 1024 * 1024)


def pack_rims(inputs):
    _, heads, depth = inputs[0].shape
    return pl.pallas_call(
        rims_kernel,
        out_shape=jax.ShapeDtypeStruct((len(inputs) * RIM, heads, depth), BF16),
        in_specs=[HBM] * len(inputs),
        out_specs=VMEM,
        scratch_shapes=[pltpu.SemaphoreType.DMA((len(inputs),))],
        compiler_params=pltpu.CompilerParams(vmem_limit_bytes=63 * 2**20),
        cost_estimate=pl.CostEstimate(flops=10**9, bytes_accessed=2**16, transcendentals=0),
    )(*inputs)


def filters_of(key, value, taps):
    heads, length, depth = key.shape
    per_token = jax.ShapeDtypeStruct((heads, length, depth), BF16)
    return pl.pallas_call(
        filters_kernel,
        out_shape=(per_token, per_token, jax.ShapeDtypeStruct((2, heads, AGAIN, depth), F32)),
        in_specs=[VMEM] * 3,
        out_specs=[VMEM] * 3,
        scratch_shapes=[pltpu.VMEM((2, heads, length + RIM, depth), F32)],
        compiler_params=PARAMS,
        cost_estimate=pl.CostEstimate(
            flops=3 * 10**9, bytes_accessed=4 * 2**20, transcendentals=10**6
        ),
    )(key, value, taps)


def maps_of(base, heads, resets, unit_in, value_in, first, rims, taps, decay, strength):
    _, length, depth = unit_in.shape
    chunks = length // CHUNK
    return pl.pallas_call(
        functools.partial(maps_kernel, base),
        out_shape=(
            jax.ShapeDtypeStruct((heads, length, depth), BF16),
            jax.ShapeDtypeStruct((heads, length, 2 * depth), F32),
            jax.ShapeDtypeStruct((heads, chunks - 1, depth, 2 * depth), F32),
            *[jax.ShapeDtypeStruct((heads // GROUPS, depth, 2 * depth), BF16)] * GROUPS,
        ),
        in_specs=[SMEM] + [VMEM] * 7,
        out_specs=[VMEM] * (3 + GROUPS),
        scratch_shapes=[
            pltpu.VMEM(rims.shape, F32),
            pltpu.VMEM((heads, 2, RIM + AGAIN, depth), F32),
            pltpu.VMEM((heads, length, depth), BF16),
            pltpu.VMEM((heads, chunks, depth, 2 * depth), F32),
        ],
        compiler_params=PARAMS,
        cost_estimate=pl.CostEstimate(
            flops=5 * 10**9, bytes_accessed=4 * 2**20, transcendentals=10**6
        ),
    )(resets, unit_in, value_in, first, rims, taps, decay, strength)


def reads_of(base, heads, resets, query, gate, gain, rims, taps, decay, strength, made):
    _, length, depth = query.shape
    per_token = jax.ShapeDtypeStruct((heads, length, depth), F32)
    return pl.pallas_call(
        functools.partial(reads_kernel, base),
        out_shape=(jax.ShapeDtypeStruct(per_token.shape, BF16), per_token, per_token),
        in_specs=[SMEM] + [VMEM] * 10,
        out_specs=[VMEM] * 3,
        scratch_shapes=[
            pltpu.VMEM(rims.shape, F32),
            pltpu.VMEM((heads, length + RIM, depth), F32),
            pltpu.VMEM((heads, length, depth), BF16),
        ],
        compiler_params=PARAMS,
        cost_estimate=pl.CostEstimate(
            flops=3 * 10**9, bytes_accessed=4 * 2**20, transcendentals=10**6
        ),
    )(resets, query, gate, gain, rims, taps, decay, strength, *made)


def join(place, maps, links):
    count = len(maps)
    heads, depth, _ = maps[0].shape
    pair = jax.ShapeDtypeStruct((heads, depth, 2 * depth), F32)
    square = (heads, depth, depth)
    if links == 1:
        totals = (jax.ShapeDtypeStruct(square, BF16),)
    else:
        totals = (jax.ShapeDtypeStruct(square, F32),) * 2
    return pl.pallas_call(
        functools.partial(join_kernel, count),
        out_shape=(pair, *totals),
        in_specs=[SMEM] + [VMEM] * count,
        out_specs=[VMEM] * (1 + len(totals)),
        scratch_shapes=[pltpu.VMEM((count, heads, depth, 2 * depth), BF16)],
        compiler_params=PARAMS,
    )(place, *maps)


def outputs_of(base, arrived, before, reads):
    heads, depth, _ = arrived.shape
    length = reads[0].shape[1]
    return pl.pallas_call(
        functools.partial(outputs_kernel, base),
        out_shape=jax.ShapeDtypeStruct((length, heads * depth), BF16),
        in_specs=[VMEM] * 5,
        out_specs=VMEM,
        compiler_params=PARAMS,
    )(arrived, before, *reads)


def last_projected(section, first, second, block, weights):
    length, columns = first.shape
    return pl.pallas_call(
        last_kernel,
        out_shape=jax.ShapeDtypeStruct((length, columns), BF16),
        in_specs=[SMEM] + [VMEM] * 4,
        out_specs=pl.BlockSpec(memory_space=pl.ANY),
        scratch_shapes=[
            pltpu.VMEM((length, columns), BF16),
            pltpu.SemaphoreType.DMA((length // CHUNK,)),
        ],
        compiler_params=PARAMS,
    )(section.astype(jnp.int32).reshape(1), first, second, block, weights)


def after(first, *values):
    return lax.optimization_barrier((first, *values))[1:]


def on_device(
    query_in,
    key_in,
    value_in,
    gate_in,
    write_strength,
    log_decay,
    doc_resets,
    conv_weight,
    output_norm_gain,
    output_projection_weight,
):
    length, heads, depth = query_in.shape
    taps = conv_weight
    rims = from_behind(pack_rims((query_in, key_in, value_in)), ("chain", "leaf"), 1)
    key, value = (jnp.transpose(x, (1, 0, 2)) for x in (key_in, value_in))
    key, value, first = filters_of(key, value, taps)
    gain = output_norm_gain.reshape(1, depth)
    leaves = lax.axis_size("leaf")
    place = lax.axis_index("leaf").astype(jnp.int32).reshape(1)

    links = lax.axis_size("chain") - 1
    unit_key, solved, starts, *own_maps = maps_of(
        0, heads, doc_resets, key, value, first, rims, taps, log_decay, write_strength
    )
    exchanged = [
        [own_map] + [lax.ppermute(own_map, "leaf", pairs_at(k, leaves)) for k in range(1, leaves)]
        for own_map in own_maps
    ]
    query_in, gate_in = after(own_maps[-1], query_in, gate_in)
    query, gate = (jnp.transpose(x, (1, 0, 2)) for x in (query_in, gate_in))
    reads = reads_of(
        0, heads, doc_resets, query, gate, gain, rims, taps, log_decay, write_strength,
        (unit_key, solved, starts),
    )
    size = heads // GROUPS
    blocks = []
    for g, maps in enumerate(exchanged):
        earlier = blocks[-1] if blocks else reads[0]
        maps = after(earlier, *maps)
        before, state, *trans = join(place, maps, links)
        arrived = from_behind(state.astype(BF16), "chain", 1)
        for _ in range(links - 1):
            passed = jnp.einsum(
                "hij,hjk->hik", trans[0], arrived.astype(F32), precision=lax.Precision.HIGHEST
            )
            arrived = from_behind((passed + state).astype(BF16), "chain", 1)
        blocks.append(outputs_of(g * size, arrived, before, reads))

    ring = lax.axis_size("head")
    mine = lax.axis_index("head")
    width = size * depth
    weights = output_projection_weight
    around = [(i, (i + 1) % ring) for i in range(ring)]
    sums = [None] * GROUPS
    for k in range(ring):
        owner = lax.rem(mine + ring - k, ring)
        last = k + 1 == ring
        following = blocks if last else [lax.ppermute(x, "head", around) for x in blocks]
        for g, block in enumerate(blocks):
            section = owner * GROUPS + g
            if last and g + 1 == GROUPS:
                return last_projected(section, *sums, block, weights)
            rows = lax.dynamic_slice_in_dim(weights, section * width, width, 0)
            term = jnp.dot(block, rows, preferred_element_type=F32)
            sums[g] = term if sums[g] is None else sums[g] + term
        blocks = following


def solution(mesh):
    return jax.shard_map(
        on_device,
        mesh=mesh,
        in_specs=(
            P(("chain", "leaf"), "head", None),
            P(("chain", "leaf"), "head", None),
            P(("chain", "leaf"), "head", None),
            P(("chain", "leaf"), "head", None),
            P("head", ("chain", "leaf")),
            P("head", ("chain", "leaf")),
            P(("chain", "leaf")),
            P(None, None, "head", None),
            P(),
            P(None, "head"),
        ),
        out_specs=P(("chain", "leaf"), "head"),
        check_vma=False,
    )
```

```python
import functools

import jax
import jax.numpy as jnp
from jax import lax
from jax.experimental import pallas as pl
from jax.experimental.pallas import tpu as pltpu
from jax.sharding import PartitionSpec as P

BLOCK = 64
CHUNK = 128
GROUPS = 2
RIM = 8
EPSILON = 1e-06
FAR = -1e30
LARGE = 1e38
AGAIN = 16
F32 = jnp.float32
BF16 = jnp.bfloat16
NN = (((1,), (0,)), ((), ()))
NT = (((1,), (1,)), ((), ()))
TN = (((0,), (0,)), ((), ()))


def split(a):
    high = a.astype(BF16)
    return high, (a - high.astype(F32)).astype(BF16)


def mul(a, b, dims=NN):
    return lax.dot_general(a, b, dims, preferred_element_type=F32)


def mul_split(a, b):
    a_high, a_low = split(a)
    b_high, b_low = split(b)
    return mul(a_high, b_high) + (mul(a_low, b_high) + mul(a_high, b_low))


def rows_of(c):
    return slice(c * CHUNK, (c + 1) * CHUNK)


def indices():
    shape = (CHUNK, CHUNK)
    return (
        lax.broadcasted_iota(jnp.int32, shape, 0),
        lax.broadcasted_iota(jnp.int32, shape, 1),
    )


def token_scalars(decay_ref, strength_ref, c):
    row, col = indices()
    cum = lax.dot_general(
        decay_ref[:, rows_of(c)],
        (row <= col).astype(F32),
        NN,
        precision=lax.Precision.HIGHEST,
        preferred_element_type=F32,
    )
    strength = strength_ref[:, rows_of(c)]
    stacked = [cum, strength]
    missing = 8 - 2 * cum.shape[0]
    if missing > 0:
        stacked.append(jnp.zeros((missing, CHUNK), F32))
    return cum, strength, jnp.transpose(jnp.concatenate(stacked, axis=0))


def silu(x):
    below = jnp.minimum(1.0 + jnp.exp(-x), LARGE)
    inverse = pl.reciprocal(below, approx=True)
    return x * (inverse * (2.0 - below * inverse))


def filtered(padded, taps, begin, length):
    first = begin + RIM + 1 - len(taps)
    total = taps[0] * padded[first : first + length]
    for j in range(1, len(taps)):
        total = total + taps[j] * padded[first + j : first + j + length]
    return silu(total)


def taps_of(taps_ref, which, head):
    return [taps_ref[which, j, pl.ds(head, 1), :] for j in range(taps_ref.shape[1])]


def unit(rows):
    return rows * lax.rsqrt(jnp.sum(rows * rows, axis=-1, keepdims=True) + EPSILON)


def same_document(second_resets, row, col):
    return ((row // BLOCK) - (col // BLOCK)) * second_resets == 0


def lower_inverse(lowers, row, col):
    differ = row ^ col
    eye = (row == col).astype(F32)
    in_block = (differ < 8).astype(F32)
    diagonal = [low * in_block for low in lowers]
    powers = [d.astype(BF16) for d in diagonal]
    squares = [mul(p, p).astype(BF16) for p in powers]
    inverse = [eye - d for d in diagonal]
    stacked = [
        mul(jnp.concatenate([s, x.astype(BF16)], axis=0), s) for x, s in zip(inverse, squares)
    ]
    fourths = [both[:CHUNK].astype(BF16) for both in stacked]
    inverse = [x + both[CHUNK:] for x, both in zip(inverse, stacked)]
    inverse = [x + mul(x.astype(BF16), s) for x, s in zip(inverse, fourths)]
    size = 8
    while size < CHUNK:
        joint = odd_blocks(((differ >= size) & (differ < 2 * size)).astype(F32), size)
        rounded = [x.astype(BF16) for x in inverse]
        inner = [
            mul((odd_blocks(low, size) * joint).astype(BF16), x)
            for low, x in zip(lowers, rounded)
        ]
        outer = [
            mul(odd_blocks(x, size).astype(BF16), with_even_zeros(i, size).astype(BF16))
            for x, i in zip(inverse, inner)
        ]
        inverse = [less_in_odd(x, o, size) for x, o in zip(inverse, outer)]
        size *= 2
    return inverse


def odd_blocks(a, size):
    return jnp.concatenate([a[b : b + size] for b in range(size, a.shape[0], 2 * size)], axis=0)


def with_even_zeros(odd, size):
    zeros = jnp.zeros((size, odd.shape[1]), odd.dtype)
    pieces = []
    for b in range(0, odd.shape[0], size):
        pieces += [zeros, odd[b : b + size]]
    return jnp.concatenate(pieces, axis=0)


def less_in_odd(a, odd, size):
    pieces = []
    for b in range(0, odd.shape[0], size):
        pieces.append(a[2 * b : 2 * b + size])
        pieces.append(a[2 * b + size : 2 * b + 2 * size] - odd[b : b + size])
    return jnp.concatenate(pieces, axis=0)


def rims_kernel(*refs):
    *inputs, packed_ref, arrived = refs
    copies = []
    for i, x_ref in enumerate(inputs):
        last = x_ref.at[pl.ds(x_ref.shape[0] - RIM, RIM)]
        here = packed_ref.at[pl.ds(i * RIM, RIM)]
        copies.append(pltpu.make_async_copy(last, here, arrived.at[i]))
    for copy in copies:
        copy.start()
    for copy in copies:
        copy.wait()


def filters_kernel(key_ref, value_ref, taps_ref, unit_ref, value_out_ref, first_ref, padded):
    heads, length, _ = key_ref.shape
    for i, x_ref in enumerate((key_ref, value_ref)):
        padded[i, :, RIM:] = x_ref[...].astype(F32)
        padded[i, :, 0:RIM] = jnp.zeros((heads, RIM, padded.shape[3]), F32)
    first_ref[...] = padded[:, :, RIM : RIM + AGAIN]

    def one_head(h, carry):
        for i in range(2):
            taps = taps_of(taps_ref, 1 + i, h)
            for c in range(length // CHUNK):
                rows = filtered(padded.at[i, h], taps, c * CHUNK, CHUNK)
                if i == 0:
                    unit_ref[h, rows_of(c)] = unit(rows).astype(BF16)
                else:
                    value_out_ref[h, rows_of(c)] = rows.astype(BF16)
        return carry

    lax.fori_loop(0, heads, one_head, 0)


def maps_kernel(
    base, resets, unit_in_ref, value_in_ref, first_ref, rim_ref, taps_ref, decay_ref, strength_ref,
    unit_ref, solved_ref, starts_ref, *refs,
):
    *map_refs, rims, padded, value_s, step_s = refs
    heads, length, depth = unit_ref.shape
    chunks = length // CHUNK
    size = heads // len(map_refs)
    total_heads = decay_ref.shape[0]
    row, col = indices()
    rims[...] = rim_ref[...].astype(F32)
    for g in range(heads):
        h = base + g
        unit_ref[g] = unit_in_ref[h]
        value_s[g] = value_in_ref[h]
        for i in range(2):
            padded[g, i, 0:RIM] = rims[(1 + i) * RIM : (2 + i) * RIM, h, :]
            padded[g, i, RIM : RIM + AGAIN] = first_ref[i, h]
            rows = filtered(padded.at[g, i], taps_of(taps_ref, 1 + i, h), 0, AGAIN)
            if i == 0:
                unit_ref[g, 0:AGAIN] = unit(rows).astype(BF16)
            else:
                value_s[g, 0:AGAIN] = rows.astype(BF16)

    parts = []
    lowers = []
    for c in range(chunks):
        cum, _, columns = token_scalars(decay_ref, strength_ref, c)
        first, second = resets[2 * c], resets[2 * c + 1]
        strictly = (row > col) & same_document(second, row, col)
        for g in range(heads):
            h = base + g
            cum_col = columns[:, h : h + 1]
            cum_row = cum[h : h + 1]
            key = unit_ref[g, rows_of(c)]
            fading = jnp.exp(jnp.where(strictly, cum_col - cum_row, FAR))
            strength_col = columns[:, total_heads + h : total_heads + h + 1]
            lowers.append(strength_col * fading * mul(key, key, NT))
            parts.append((g, c, first, second, cum_col, cum_row, strength_col))
    inverses = lower_inverse(lowers, row, col)
    eye = (row == col).astype(F32)
    first_rows = lax.broadcasted_iota(jnp.int32, (CHUNK, 1), 0) < BLOCK
    for (g, c, first, second, cum_col, cum_row, strength_col), inverse in zip(parts, inverses):
        keep_first = (1 - first).astype(F32)
        keep_second = (1 - second).astype(F32)
        keep_both = keep_first * keep_second
        key = unit_ref[g, rows_of(c)]
        growth = jnp.exp(cum_col) * jnp.where(first_rows, keep_first, keep_both)
        targets = jnp.concatenate(
            [
                (strength_col * growth) * key.astype(F32),
                strength_col * value_s[g, rows_of(c)].astype(F32),
            ],
            axis=1,
        )
        solved = targets + mul((inverse - eye).astype(BF16), targets.astype(BF16))
        solved_ref[g, rows_of(c)] = solved
        end = cum_row[:, CHUNK - 1 : CHUNK]
        tail = jnp.exp(end - cum_col) * jnp.where(first_rows, keep_second, 1.0)
        product = mul(key, (tail * solved).astype(BF16), TN)
        passed = jnp.exp(end) * keep_both
        step_s[g, c, :, :depth] = jnp.where(row == col, passed, 0.0) - product[:, :depth]
        step_s[g, c, :, depth:] = product[:, depth:]

    def compose(later, earlier):
        high, low = split(earlier)
        trans = later[:, :depth].astype(BF16)
        joined = mul(trans, high) + mul(trans, low)
        return jnp.concatenate([joined[:, :depth], joined[:, depth:] + later[:, depth:]], axis=1)

    every = range(heads)
    states = [step_s[g, 0] for g in every]
    half = chunks // 2
    for c in range(1, half):
        for g in every:
            starts_ref[g, c - 1] = states[g]
        states = [compose(step_s[g, c], states[g]) for g in every]
    rest = [step_s[g, half] for g in every]
    for c in range(half + 1, chunks):
        rest = [compose(step_s[g, c], rest[g]) for g in every]
    for g in every:
        map_refs[g // size][g % size] = compose(rest[g], states[g]).astype(BF16)
    for c in range(half, chunks):
        for g in every:
            starts_ref[g, c - 1] = states[g]
        if c + 1 < chunks:
            states = [compose(step_s[g, c], states[g]) for g in every]


def reads_kernel(
    base, resets, query_ref, gate_ref, gain_ref, rim_ref, taps_ref, decay_ref, strength_ref,
    unit_ref, solved_ref, starts_ref,
    reach_ref, part_ref, gating_ref,
    rims, padded, query_s,
):
    heads, length, depth = unit_ref.shape
    chunks = length // CHUNK
    row, col = indices()
    first_rows = lax.broadcasted_iota(jnp.int32, (CHUNK, 1), 0) < BLOCK
    rims[...] = rim_ref[...].astype(F32)
    for g in range(heads):
        h = base + g
        padded[g, 0:RIM] = rims[0:RIM, h, :]
        padded[g, RIM : RIM + length] = query_ref[h].astype(F32)
        taps = taps_of(taps_ref, 0, h)
        for c in range(chunks):
            rows = filtered(padded.at[g], taps, c * CHUNK, CHUNK)
            query_s[g, rows_of(c)] = (unit(rows) * depth**-0.5).astype(BF16)

    for c in range(chunks):
        here = rows_of(c)
        cum, _, columns = token_scalars(decay_ref, strength_ref, c)
        first, second = resets[2 * c], resets[2 * c + 1]
        keep_first = (1 - first).astype(F32)
        keep_both = keep_first * (1 - second).astype(F32)
        upto = (row >= col) & same_document(second, row, col)
        for g in range(heads):
            h = base + g
            cum_col = columns[:, h : h + 1]
            query = query_s[g, here]
            fading = jnp.exp(jnp.where(upto, cum_col - cum[h : h + 1], FAR))
            mixing = fading * mul(query, unit_ref[g, here], NT)
            own = mul_split(mixing, solved_ref[g, here])
            growth = jnp.exp(cum_col) * jnp.where(first_rows, keep_first, keep_both)
            reach = growth * query.astype(F32) - own[:, :depth]
            part = own[:, depth:]
            if c:
                both = mul_split(reach, starts_ref[g, c - 1])
                reach = both[:, :depth]
                part = part + both[:, depth:]
            reach_ref[g, here] = reach.astype(BF16)
            part_ref[g, here] = part
            gate = gate_ref[h, here].astype(F32)
            gating_ref[g, here] = gain_ref[...] * silu(gate)


def partner(place, k, count):
    if count & (count - 1) == 0:
        return place ^ k
    return lax.rem(place + count - k, count)


def pairs_at(k, count):
    if count & (count - 1) == 0:
        return [(i, i ^ k) for i in range(count)]
    return [(i, (i + k) % count) for i in range(count)]


def join_kernel(count, place, *refs):
    maps = refs[:count]
    before_ref, state_ref, *trans_ref, ordered = refs[count:]
    heads, depth, _ = before_ref.shape
    me = place[0]
    for k in range(count):
        ordered[partner(me, k, count)] = maps[k][...]
    row, col = indices()
    eye = (row == col).astype(F32)
    states = [jnp.concatenate([eye, jnp.zeros((depth, depth), F32)], axis=1)] * heads
    for lap in range(count):

        @pl.when(lap == me)
        def _():
            for h in range(heads):
                before_ref[h] = states[h]

        for h in range(heads):
            step = ordered[lap, h]
            if lap:
                high, low = split(states[h])
                trans = step[:, :depth]
                joined = mul(trans, high) + mul(trans, low)
                states[h] = jnp.concatenate(
                    [joined[:, :depth], joined[:, depth:] + step[:, depth:].astype(F32)], axis=1
                )
            else:
                states[h] = step.astype(F32)
    for h in range(heads):
        state_ref[h] = states[h][:, depth:].astype(state_ref.dtype)
        for ref in trans_ref:
            ref[h] = states[h][:, :depth]


def outputs_kernel(base, arrived_ref, before_ref, reach_ref, part_ref, gating_ref, normed_ref):
    heads, depth, _ = arrived_ref.shape
    for g in range(heads):
        h = base + g
        before = before_ref[g]
        incoming = mul_split(before[:, :depth], arrived_ref[g].astype(F32)) + before[:, depth:]
        high, low = split(incoming)
        for c in range(normed_ref.shape[0] // CHUNK):
            here = rows_of(c)
            reach = reach_ref[h, here]
            core = part_ref[h, here] + (mul(reach, high) + mul(reach, low))
            scale = lax.rsqrt(jnp.sum(core * core, axis=-1, keepdims=True) / depth + EPSILON)
            normed_ref[here, g * depth : (g + 1) * depth] = (
                core * scale * gating_ref[h, here]
            ).astype(BF16)


def last_kernel(section, first_ref, second_ref, block_ref, weights_ref, out_ref, tiles, written):
    width = block_ref.shape[1]
    rows = weights_ref[pl.ds(pl.multiple_of(section[0] * width, width), width), :]
    copies = []
    for i in range(first_ref.shape[0] // CHUNK):
        here = rows_of(i)
        total = (first_ref[here] + second_ref[here]) + mul(block_ref[here], rows)
        tiles[here] = total.astype(BF16)
        copies.append(pltpu.make_async_copy(tiles.at[here], out_ref.at[here], written.at[i]))
        copies[-1].start()
    for copy in copies:
        copy.wait()


def from_behind(value, axis, steps):
    count = lax.axis_size(axis)
    return lax.ppermute(value, axis, [(i, i + steps) for i in range(count - steps)])


VMEM = pl.BlockSpec(memory_space=pltpu.VMEM)
SMEM = pl.BlockSpec(memory_space=pltpu.SMEM)
HBM = pl.BlockSpec(memory_space=pltpu.HBM)
PARAMS = pltpu.CompilerParams(vmem_limit_bytes=12 * 1024 * 1024)


def pack_rims(inputs):
    _, heads, depth = inputs[0].shape
    return pl.pallas_call(
        rims_kernel,
        out_shape=jax.ShapeDtypeStruct((len(inputs) * RIM, heads, depth), BF16),
        in_specs=[HBM] * len(inputs),
        out_specs=VMEM,
        scratch_shapes=[pltpu.SemaphoreType.DMA((len(inputs),))],
        compiler_params=pltpu.CompilerParams(vmem_limit_bytes=63 * 2**20),
        cost_estimate=pl.CostEstimate(flops=10**9, bytes_accessed=2**16, transcendentals=0),
    )(*inputs)


def filters_of(key, value, taps):
    heads, length, depth = key.shape
    per_token = jax.ShapeDtypeStruct((heads, length, depth), BF16)
    return pl.pallas_call(
        filters_kernel,
        out_shape=(per_token, per_token, jax.ShapeDtypeStruct((2, heads, AGAIN, depth), F32)),
        in_specs=[VMEM] * 3,
        out_specs=[VMEM] * 3,
        scratch_shapes=[pltpu.VMEM((2, heads, length + RIM, depth), F32)],
        compiler_params=PARAMS,
        cost_estimate=pl.CostEstimate(
            flops=3 * 10**9, bytes_accessed=4 * 2**20, transcendentals=10**6
        ),
    )(key, value, taps)


def maps_of(base, heads, resets, unit_in, value_in, first, rims, taps, decay, strength):
    _, length, depth = unit_in.shape
    chunks = length // CHUNK
    return pl.pallas_call(
        functools.partial(maps_kernel, base),
        out_shape=(
            jax.ShapeDtypeStruct((heads, length, depth), BF16),
            jax.ShapeDtypeStruct((heads, length, 2 * depth), F32),
            jax.ShapeDtypeStruct((heads, chunks - 1, depth, 2 * depth), F32),
            *[jax.ShapeDtypeStruct((heads // GROUPS, depth, 2 * depth), BF16)] * GROUPS,
        ),
        in_specs=[SMEM] + [VMEM] * 7,
        out_specs=[VMEM] * (3 + GROUPS),
        scratch_shapes=[
            pltpu.VMEM(rims.shape, F32),
            pltpu.VMEM((heads, 2, RIM + AGAIN, depth), F32),
            pltpu.VMEM((heads, length, depth), BF16),
            pltpu.VMEM((heads, chunks, depth, 2 * depth), F32),
        ],
        compiler_params=PARAMS,
        cost_estimate=pl.CostEstimate(
            flops=5 * 10**9, bytes_accessed=4 * 2**20, transcendentals=10**6
        ),
    )(resets, unit_in, value_in, first, rims, taps, decay, strength)


def reads_of(base, heads, resets, query, gate, gain, rims, taps, decay, strength, made):
    _, length, depth = query.shape
    per_token = jax.ShapeDtypeStruct((heads, length, depth), F32)
    return pl.pallas_call(
        functools.partial(reads_kernel, base),
        out_shape=(jax.ShapeDtypeStruct(per_token.shape, BF16), per_token, per_token),
        in_specs=[SMEM] + [VMEM] * 10,
        out_specs=[VMEM] * 3,
        scratch_shapes=[
            pltpu.VMEM(rims.shape, F32),
            pltpu.VMEM((heads, length + RIM, depth), F32),
            pltpu.VMEM((heads, length, depth), BF16),
        ],
        compiler_params=PARAMS,
        cost_estimate=pl.CostEstimate(
            flops=3 * 10**9, bytes_accessed=4 * 2**20, transcendentals=10**6
        ),
    )(resets, query, gate, gain, rims, taps, decay, strength, *made)


def join(place, maps, links):
    count = len(maps)
    heads, depth, _ = maps[0].shape
    pair = jax.ShapeDtypeStruct((heads, depth, 2 * depth), F32)
    square = (heads, depth, depth)
    if links == 1:
        totals = (jax.ShapeDtypeStruct(square, BF16),)
    else:
        totals = (jax.ShapeDtypeStruct(square, F32),) * 2
    return pl.pallas_call(
        functools.partial(join_kernel, count),
        out_shape=(pair, *totals),
        in_specs=[SMEM] + [VMEM] * count,
        out_specs=[VMEM] * (1 + len(totals)),
        scratch_shapes=[pltpu.VMEM((count, heads, depth, 2 * depth), BF16)],
        compiler_params=PARAMS,
    )(place, *maps)


def outputs_of(base, arrived, before, reads):
    heads, depth, _ = arrived.shape
    length = reads[0].shape[1]
    return pl.pallas_call(
        functools.partial(outputs_kernel, base),
        out_shape=jax.ShapeDtypeStruct((length, heads * depth), BF16),
        in_specs=[VMEM] * 5,
        out_specs=VMEM,
        compiler_params=PARAMS,
    )(arrived, before, *reads)


def last_projected(section, first, second, block, weights):
    length, columns = first.shape
    return pl.pallas_call(
        last_kernel,
        out_shape=jax.ShapeDtypeStruct((length, columns), BF16),
        in_specs=[SMEM] + [VMEM] * 4,
        out_specs=pl.BlockSpec(memory_space=pl.ANY),
        scratch_shapes=[
            pltpu.VMEM((length, columns), BF16),
            pltpu.SemaphoreType.DMA((length // CHUNK,)),
        ],
        compiler_params=PARAMS,
    )(section.astype(jnp.int32).reshape(1), first, second, block, weights)


def after(first, *values):
    return lax.optimization_barrier((first, *values))[1:]


def on_device(
    query_in,
    key_in,
    value_in,
    gate_in,
    write_strength,
    log_decay,
    doc_resets,
    conv_weight,
    output_norm_gain,
    output_projection_weight,
):
    length, heads, depth = query_in.shape
    taps = conv_weight
    rims = from_behind(pack_rims((query_in, key_in, value_in)), ("chain", "leaf"), 1)
    key, value = (jnp.transpose(x, (1, 0, 2)) for x in (key_in, value_in))
    key, value, first = filters_of(key, value, taps)
    gain = output_norm_gain.reshape(1, depth)
    leaves = lax.axis_size("leaf")
    place = lax.axis_index("leaf").astype(jnp.int32).reshape(1)

    links = lax.axis_size("chain") - 1
    unit_key, solved, starts, *own_maps = maps_of(
        0, heads, doc_resets, key, value, first, rims, taps, log_decay, write_strength
    )
    exchanged = [
        [own_map] + [lax.ppermute(own_map, "leaf", pairs_at(k, leaves)) for k in range(1, leaves)]
        for own_map in own_maps[:-1]
    ]
    query_in, gate_in = after(own_maps[-1], query_in, gate_in)
    query, gate = (jnp.transpose(x, (1, 0, 2)) for x in (query_in, gate_in))
    reads = reads_of(
        0, heads, doc_resets, query, gate, gain, rims, taps, log_decay, write_strength,
        (unit_key, solved, starts),
    )
    own_map = own_maps[-1]
    later = after(reads[0], own_map)[0]
    exchanged.append(
        [own_map]
        + [
            lax.ppermute(later if 2 * k == leaves else own_map, "leaf", pairs_at(k, leaves))
            for k in range(1, leaves)
        ]
    )
    size = heads // GROUPS
    blocks = []
    for g, maps in enumerate(exchanged):
        earlier = blocks[-1] if blocks else reads[0]
        maps = after(earlier, *maps)
        before, state, *trans = join(place, maps, links)
        arrived = from_behind(state.astype(BF16), "chain", 1)
        for _ in range(links - 1):
            passed = jnp.einsum(
                "hij,hjk->hik", trans[0], arrived.astype(F32), precision=lax.Precision.HIGHEST
            )
            arrived = from_behind((passed + state).astype(BF16), "chain", 1)
        blocks.append(outputs_of(g * size, arrived, before, reads))

    ring = lax.axis_size("head")
    mine = lax.axis_index("head")
    width = size * depth
    weights = output_projection_weight
    around = [(i, (i + 1) % ring) for i in range(ring)]
    sums = [None] * GROUPS
    for k in range(ring):
        owner = lax.rem(mine + ring - k, ring)
        last = k + 1 == ring
        following = blocks if last else [lax.ppermute(x, "head", around) for x in blocks]
        for g, block in enumerate(blocks):
            section = owner * GROUPS + g
            if last and g + 1 == GROUPS:
                return last_projected(section, *sums, block, weights)
            rows = lax.dynamic_slice_in_dim(weights, section * width, width, 0)
            term = jnp.dot(block, rows, preferred_element_type=F32)
            sums[g] = term if sums[g] is None else sums[g] + term
        blocks = following


def solution(mesh):
    return jax.shard_map(
        on_device,
        mesh=mesh,
        in_specs=(
            P(("chain", "leaf"), "head", None),
            P(("chain", "leaf"), "head", None),
            P(("chain", "leaf"), "head", None),
            P(("chain", "leaf"), "head", None),
            P("head", ("chain", "leaf")),
            P("head", ("chain", "leaf")),
            P(("chain", "leaf")),
            P(None, None, "head", None),
            P(),
            P(None, "head"),
        ),
        out_specs=P(("chain", "leaf"), "head"),
        check_vma=False,
    )
```

```python
import functools

import jax
import jax.numpy as jnp
from jax import lax
from jax.experimental import pallas as pl
from jax.experimental.pallas import tpu as pltpu
from jax.sharding import PartitionSpec as P

BLOCK = 64
CHUNK = 128
GROUPS = 2
RIM = 8
EPSILON = 1e-06
FAR = -1e30
LARGE = 1e38
AGAIN = 16
F32 = jnp.float32
BF16 = jnp.bfloat16
NN = (((1,), (0,)), ((), ()))
NT = (((1,), (1,)), ((), ()))
TN = (((0,), (0,)), ((), ()))


def split(a):
    high = a.astype(BF16)
    return high, (a - high.astype(F32)).astype(BF16)


def mul(a, b, dims=NN):
    return lax.dot_general(a, b, dims, preferred_element_type=F32)


def mul_split(a, b):
    a_high, a_low = split(a)
    b_high, b_low = split(b)
    return mul(a_high, b_high) + (mul(a_low, b_high) + mul(a_high, b_low))


def rows_of(c):
    return slice(c * CHUNK, (c + 1) * CHUNK)


def indices():
    shape = (CHUNK, CHUNK)
    return (
        lax.broadcasted_iota(jnp.int32, shape, 0),
        lax.broadcasted_iota(jnp.int32, shape, 1),
    )


def token_scalars(decay_ref, strength_ref, c):
    row, col = indices()
    cum = lax.dot_general(
        decay_ref[:, rows_of(c)],
        (row <= col).astype(F32),
        NN,
        precision=lax.Precision.HIGHEST,
        preferred_element_type=F32,
    )
    strength = strength_ref[:, rows_of(c)]
    stacked = [cum, strength]
    missing = 8 - 2 * cum.shape[0]
    if missing > 0:
        stacked.append(jnp.zeros((missing, CHUNK), F32))
    return cum, strength, jnp.transpose(jnp.concatenate(stacked, axis=0))


def silu(x):
    below = jnp.minimum(1.0 + jnp.exp(-x), LARGE)
    inverse = pl.reciprocal(below, approx=True)
    return x * (inverse * (2.0 - below * inverse))


def filtered(padded, taps, begin, length):
    first = begin + RIM + 1 - len(taps)
    total = taps[0] * padded[first : first + length]
    for j in range(1, len(taps)):
        total = total + taps[j] * padded[first + j : first + j + length]
    return silu(total)


def taps_of(taps_ref, which, head):
    return [taps_ref[which, j, pl.ds(head, 1), :] for j in range(taps_ref.shape[1])]


def unit(rows):
    return rows * lax.rsqrt(jnp.sum(rows * rows, axis=-1, keepdims=True) + EPSILON)


def same_document(second_resets, row, col):
    return ((row // BLOCK) - (col // BLOCK)) * second_resets == 0


def lower_inverse(lowers, row, col):
    differ = row ^ col
    eye = (row == col).astype(F32)
    in_block = (differ < 8).astype(F32)
    diagonal = [low * in_block for low in lowers]
    powers = [d.astype(BF16) for d in diagonal]
    squares = [mul(p, p).astype(BF16) for p in powers]
    inverse = [eye - d for d in diagonal]
    stacked = [
        mul(jnp.concatenate([s, x.astype(BF16)], axis=0), s) for x, s in zip(inverse, squares)
    ]
    fourths = [both[:CHUNK].astype(BF16) for both in stacked]
    inverse = [x + both[CHUNK:] for x, both in zip(inverse, stacked)]
    inverse = [x + mul(x.astype(BF16), s) for x, s in zip(inverse, fourths)]
    size = 8
    while size < CHUNK:
        joint = odd_blocks(((differ >= size) & (differ < 2 * size)).astype(F32), size)
        rounded = [x.astype(BF16) for x in inverse]
        inner = [
            mul((odd_blocks(low, size) * joint).astype(BF16), x)
            for low, x in zip(lowers, rounded)
        ]
        outer = [
            mul(odd_blocks(x, size).astype(BF16), with_even_zeros(i, size).astype(BF16))
            for x, i in zip(inverse, inner)
        ]
        inverse = [less_in_odd(x, o, size) for x, o in zip(inverse, outer)]
        size *= 2
    return inverse


def odd_blocks(a, size):
    return jnp.concatenate([a[b : b + size] for b in range(size, a.shape[0], 2 * size)], axis=0)


def with_even_zeros(odd, size):
    zeros = jnp.zeros((size, odd.shape[1]), odd.dtype)
    pieces = []
    for b in range(0, odd.shape[0], size):
        pieces += [zeros, odd[b : b + size]]
    return jnp.concatenate(pieces, axis=0)


def less_in_odd(a, odd, size):
    pieces = []
    for b in range(0, odd.shape[0], size):
        pieces.append(a[2 * b : 2 * b + size])
        pieces.append(a[2 * b + size : 2 * b + 2 * size] - odd[b : b + size])
    return jnp.concatenate(pieces, axis=0)


def rims_kernel(*refs):
    *inputs, packed_ref, arrived = refs
    copies = []
    for i, x_ref in enumerate(inputs):
        last = x_ref.at[pl.ds(x_ref.shape[0] - RIM, RIM)]
        here = packed_ref.at[pl.ds(i * RIM, RIM)]
        copies.append(pltpu.make_async_copy(last, here, arrived.at[i]))
    for copy in copies:
        copy.start()
    for copy in copies:
        copy.wait()


def filters_kernel(key_ref, value_ref, taps_ref, unit_ref, value_out_ref, first_ref, padded):
    heads, length, _ = key_ref.shape
    for i, x_ref in enumerate((key_ref, value_ref)):
        padded[i, :, RIM:] = x_ref[...].astype(F32)
        padded[i, :, 0:RIM] = jnp.zeros((heads, RIM, padded.shape[3]), F32)
    first_ref[...] = padded[:, :, RIM : RIM + AGAIN]

    def one_head(h, carry):
        for i in range(2):
            taps = taps_of(taps_ref, 1 + i, h)
            for c in range(length // CHUNK):
                rows = filtered(padded.at[i, h], taps, c * CHUNK, CHUNK)
                if i == 0:
                    unit_ref[h, rows_of(c)] = unit(rows).astype(BF16)
                else:
                    value_out_ref[h, rows_of(c)] = rows.astype(BF16)
        return carry

    lax.fori_loop(0, heads, one_head, 0)


def maps_kernel(
    base, resets, unit_in_ref, value_in_ref, first_ref, rim_ref, taps_ref, decay_ref, strength_ref,
    unit_ref, solved_ref, starts_ref, *refs,
):
    *map_refs, rims, padded, value_s, step_s = refs
    heads, length, depth = unit_ref.shape
    chunks = length // CHUNK
    size = heads // len(map_refs)
    total_heads = decay_ref.shape[0]
    row, col = indices()
    rims[...] = rim_ref[...].astype(F32)
    for g in range(heads):
        h = base + g
        unit_ref[g] = unit_in_ref[h]
        value_s[g] = value_in_ref[h]
        for i in range(2):
            padded[g, i, 0:RIM] = rims[(1 + i) * RIM : (2 + i) * RIM, h, :]
            padded[g, i, RIM : RIM + AGAIN] = first_ref[i, h]
            rows = filtered(padded.at[g, i], taps_of(taps_ref, 1 + i, h), 0, AGAIN)
            if i == 0:
                unit_ref[g, 0:AGAIN] = unit(rows).astype(BF16)
            else:
                value_s[g, 0:AGAIN] = rows.astype(BF16)

    parts = []
    lowers = []
    for c in range(chunks):
        cum, _, columns = token_scalars(decay_ref, strength_ref, c)
        first, second = resets[2 * c], resets[2 * c + 1]
        strictly = (row > col) & same_document(second, row, col)
        for g in range(heads):
            h = base + g
            cum_col = columns[:, h : h + 1]
            cum_row = cum[h : h + 1]
            key = unit_ref[g, rows_of(c)]
            fading = jnp.exp(jnp.where(strictly, cum_col - cum_row, FAR))
            strength_col = columns[:, total_heads + h : total_heads + h + 1]
            lowers.append(strength_col * fading * mul(key, key, NT))
            parts.append((g, c, first, second, cum_col, cum_row, strength_col))
    inverses = lower_inverse(lowers, row, col)
    eye = (row == col).astype(F32)
    first_rows = lax.broadcasted_iota(jnp.int32, (CHUNK, 1), 0) < BLOCK
    for (g, c, first, second, cum_col, cum_row, strength_col), inverse in zip(parts, inverses):
        keep_first = (1 - first).astype(F32)
        keep_second = (1 - second).astype(F32)
        keep_both = keep_first * keep_second
        key = unit_ref[g, rows_of(c)]
        growth = jnp.exp(cum_col) * jnp.where(first_rows, keep_first, keep_both)
        targets = jnp.concatenate(
            [
                (strength_col * growth) * key.astype(F32),
                strength_col * value_s[g, rows_of(c)].astype(F32),
            ],
            axis=1,
        )
        solved = targets + mul((inverse - eye).astype(BF16), targets.astype(BF16))
        solved_ref[g, rows_of(c)] = solved
        end = cum_row[:, CHUNK - 1 : CHUNK]
        tail = jnp.exp(end - cum_col) * jnp.where(first_rows, keep_second, 1.0)
        product = mul(key, (tail * solved).astype(BF16), TN)
        passed = jnp.exp(end) * keep_both
        step_s[g, c, :, :depth] = jnp.where(row == col, passed, 0.0) - product[:, :depth]
        step_s[g, c, :, depth:] = product[:, depth:]

    def compose(later, earlier):
        high, low = split(earlier)
        trans = later[:, :depth].astype(BF16)
        joined = mul(trans, high) + mul(trans, low)
        return jnp.concatenate([joined[:, :depth], joined[:, depth:] + later[:, depth:]], axis=1)

    every = range(heads)
    states = [step_s[g, 0] for g in every]
    half = chunks // 2
    for c in range(1, half):
        for g in every:
            starts_ref[g, c - 1] = states[g]
        states = [compose(step_s[g, c], states[g]) for g in every]
    rest = [step_s[g, half] for g in every]
    for c in range(half + 1, chunks):
        rest = [compose(step_s[g, c], rest[g]) for g in every]
    for g in every:
        map_refs[g // size][g % size] = compose(rest[g], states[g]).astype(BF16)
    for c in range(half, chunks):
        for g in every:
            starts_ref[g, c - 1] = states[g]
        if c + 1 < chunks:
            states = [compose(step_s[g, c], states[g]) for g in every]


def reads_kernel(
    base, resets, query_ref, gate_ref, gain_ref, rim_ref, taps_ref, decay_ref, strength_ref,
    unit_ref, solved_ref, starts_ref,
    reach_ref, part_ref, gating_ref,
    rims, padded, query_s,
):
    heads, length, depth = unit_ref.shape
    chunks = length // CHUNK
    row, col = indices()
    first_rows = lax.broadcasted_iota(jnp.int32, (CHUNK, 1), 0) < BLOCK
    rims[...] = rim_ref[...].astype(F32)
    for g in range(heads):
        h = base + g
        padded[g, 0:RIM] = rims[0:RIM, h, :]
        padded[g, RIM : RIM + length] = query_ref[h].astype(F32)
        taps = taps_of(taps_ref, 0, h)
        for c in range(chunks):
            rows = filtered(padded.at[g], taps, c * CHUNK, CHUNK)
            query_s[g, rows_of(c)] = (unit(rows) * depth**-0.5).astype(BF16)

    for c in range(chunks):
        here = rows_of(c)
        cum, _, columns = token_scalars(decay_ref, strength_ref, c)
        first, second = resets[2 * c], resets[2 * c + 1]
        keep_first = (1 - first).astype(F32)
        keep_both = keep_first * (1 - second).astype(F32)
        upto = (row >= col) & same_document(second, row, col)
        for g in range(heads):
            h = base + g
            cum_col = columns[:, h : h + 1]
            query = query_s[g, here]
            fading = jnp.exp(jnp.where(upto, cum_col - cum[h : h + 1], FAR))
            mixing = fading * mul(query, unit_ref[g, here], NT)
            own = mul_split(mixing, solved_ref[g, here])
            growth = jnp.exp(cum_col) * jnp.where(first_rows, keep_first, keep_both)
            reach = growth * query.astype(F32) - own[:, :depth]
            part = own[:, depth:]
            if c:
                both = mul_split(reach, starts_ref[g, c - 1])
                reach = both[:, :depth]
                part = part + both[:, depth:]
            reach_ref[g, here] = reach.astype(BF16)
            part_ref[g, here] = part
            gate = gate_ref[h, here].astype(F32)
            gating_ref[g, here] = gain_ref[...] * silu(gate)


def partner(place, k, count):
    if count & (count - 1) == 0:
        return place ^ k
    return lax.rem(place + count - k, count)


def pairs_at(k, count):
    if count & (count - 1) == 0:
        return [(i, i ^ k) for i in range(count)]
    return [(i, (i + k) % count) for i in range(count)]


def join_kernel(count, place, *refs):
    maps = refs[:count]
    before_ref, state_ref, *trans_ref, ordered = refs[count:]
    heads, depth, _ = before_ref.shape
    me = place[0]
    for k in range(count):
        ordered[partner(me, k, count)] = maps[k][...]
    row, col = indices()
    eye = (row == col).astype(F32)
    states = [jnp.concatenate([eye, jnp.zeros((depth, depth), F32)], axis=1)] * heads
    for lap in range(count):

        @pl.when(lap == me)
        def _():
            for h in range(heads):
                before_ref[h] = states[h]

        for h in range(heads):
            step = ordered[lap, h]
            if lap:
                high, low = split(states[h])
                trans = step[:, :depth]
                joined = mul(trans, high) + mul(trans, low)
                states[h] = jnp.concatenate(
                    [joined[:, :depth], joined[:, depth:] + step[:, depth:].astype(F32)], axis=1
                )
            else:
                states[h] = step.astype(F32)
    for h in range(heads):
        state_ref[h] = states[h][:, depth:].astype(state_ref.dtype)
        for ref in trans_ref:
            ref[h] = states[h][:, :depth]


def outputs_kernel(base, arrived_ref, before_ref, reach_ref, part_ref, gating_ref, normed_ref):
    heads, depth, _ = arrived_ref.shape
    for g in range(heads):
        h = base + g
        before = before_ref[g]
        incoming = mul_split(before[:, :depth], arrived_ref[g].astype(F32)) + before[:, depth:]
        high, low = split(incoming)
        for c in range(normed_ref.shape[0] // CHUNK):
            here = rows_of(c)
            reach = reach_ref[h, here]
            core = part_ref[h, here] + (mul(reach, high) + mul(reach, low))
            scale = lax.rsqrt(jnp.sum(core * core, axis=-1, keepdims=True) / depth + EPSILON)
            normed_ref[here, g * depth : (g + 1) * depth] = (
                core * scale * gating_ref[h, here]
            ).astype(BF16)


def last_kernel(section, first_ref, second_ref, block_ref, weights_ref, out_ref, tiles, written):
    width = block_ref.shape[1]
    rows = weights_ref[pl.ds(pl.multiple_of(section[0] * width, width), width), :]
    copies = []
    for i in range(first_ref.shape[0] // CHUNK):
        here = rows_of(i)
        total = (first_ref[here] + second_ref[here]) + mul(block_ref[here], rows)
        tiles[here] = total.astype(BF16)
        copies.append(pltpu.make_async_copy(tiles.at[here], out_ref.at[here], written.at[i]))
        copies[-1].start()
    for copy in copies:
        copy.wait()


def from_behind(value, axis, steps):
    count = lax.axis_size(axis)
    return lax.ppermute(value, axis, [(i, i + steps) for i in range(count - steps)])


def exchange(own_map, leaves):
    received = [lax.ppermute(own_map, "leaf", pairs_at(k, leaves)) for k in range(1, leaves)]
    return [own_map] + received


VMEM = pl.BlockSpec(memory_space=pltpu.VMEM)
SMEM = pl.BlockSpec(memory_space=pltpu.SMEM)
HBM = pl.BlockSpec(memory_space=pltpu.HBM)
PARAMS = pltpu.CompilerParams(vmem_limit_bytes=8 * 1024 * 1024)
LAST_PARAMS = pltpu.CompilerParams(vmem_limit_bytes=12 * 1024 * 1024)


def pack_rims(inputs):
    _, heads, depth = inputs[0].shape
    return pl.pallas_call(
        rims_kernel,
        out_shape=jax.ShapeDtypeStruct((len(inputs) * RIM, heads, depth), BF16),
        in_specs=[HBM] * len(inputs),
        out_specs=VMEM,
        scratch_shapes=[pltpu.SemaphoreType.DMA((len(inputs),))],
        compiler_params=pltpu.CompilerParams(vmem_limit_bytes=63 * 2**20),
        cost_estimate=pl.CostEstimate(flops=10**9, bytes_accessed=2**16, transcendentals=0),
    )(*inputs)


def filters_of(key, value, taps):
    heads, length, depth = key.shape
    per_token = jax.ShapeDtypeStruct((heads, length, depth), BF16)
    return pl.pallas_call(
        filters_kernel,
        out_shape=(per_token, per_token, jax.ShapeDtypeStruct((2, heads, AGAIN, depth), F32)),
        in_specs=[VMEM] * 3,
        out_specs=[VMEM] * 3,
        scratch_shapes=[pltpu.VMEM((2, heads, length + RIM, depth), F32)],
        compiler_params=PARAMS,
        cost_estimate=pl.CostEstimate(
            flops=3 * 10**9, bytes_accessed=4 * 2**20, transcendentals=10**6
        ),
    )(key, value, taps)


def maps_of(base, heads, resets, unit_in, value_in, first, rims, taps, decay, strength):
    _, length, depth = unit_in.shape
    chunks = length // CHUNK
    return pl.pallas_call(
        functools.partial(maps_kernel, base),
        out_shape=(
            jax.ShapeDtypeStruct((heads, length, depth), BF16),
            jax.ShapeDtypeStruct((heads, length, 2 * depth), F32),
            jax.ShapeDtypeStruct((heads, chunks - 1, depth, 2 * depth), F32),
            *[jax.ShapeDtypeStruct((heads // GROUPS, depth, 2 * depth), BF16)] * GROUPS,
        ),
        in_specs=[SMEM] + [VMEM] * 7,
        out_specs=[VMEM] * (3 + GROUPS),
        scratch_shapes=[
            pltpu.VMEM(rims.shape, F32),
            pltpu.VMEM((heads, 2, RIM + AGAIN, depth), F32),
            pltpu.VMEM((heads, length, depth), BF16),
            pltpu.VMEM((heads, chunks, depth, 2 * depth), F32),
        ],
        compiler_params=PARAMS,
        cost_estimate=pl.CostEstimate(
            flops=5 * 10**9, bytes_accessed=4 * 2**20, transcendentals=10**6
        ),
    )(resets, unit_in, value_in, first, rims, taps, decay, strength)


def reads_of(base, heads, resets, query, gate, gain, rims, taps, decay, strength, made):
    _, length, depth = query.shape
    per_token = jax.ShapeDtypeStruct((heads, length, depth), F32)
    return pl.pallas_call(
        functools.partial(reads_kernel, base),
        out_shape=(jax.ShapeDtypeStruct(per_token.shape, BF16), per_token, per_token),
        in_specs=[SMEM] + [VMEM] * 10,
        out_specs=[VMEM] * 3,
        scratch_shapes=[
            pltpu.VMEM(rims.shape, F32),
            pltpu.VMEM((heads, length + RIM, depth), F32),
            pltpu.VMEM((heads, length, depth), BF16),
        ],
        compiler_params=PARAMS,
        cost_estimate=pl.CostEstimate(
            flops=3 * 10**9, bytes_accessed=4 * 2**20, transcendentals=10**6
        ),
    )(resets, query, gate, gain, rims, taps, decay, strength, *made)


def join(place, maps, links):
    count = len(maps)
    heads, depth, _ = maps[0].shape
    pair = jax.ShapeDtypeStruct((heads, depth, 2 * depth), F32)
    square = (heads, depth, depth)
    if links == 1:
        totals = (jax.ShapeDtypeStruct(square, BF16),)
    else:
        totals = (jax.ShapeDtypeStruct(square, F32),) * 2
    return pl.pallas_call(
        functools.partial(join_kernel, count),
        out_shape=(pair, *totals),
        in_specs=[SMEM] + [VMEM] * count,
        out_specs=[VMEM] * (1 + len(totals)),
        scratch_shapes=[pltpu.VMEM((count, heads, depth, 2 * depth), BF16)],
        compiler_params=PARAMS,
    )(place, *maps)


def outputs_of(base, arrived, before, reads):
    heads, depth, _ = arrived.shape
    length = reads[0].shape[1]
    return pl.pallas_call(
        functools.partial(outputs_kernel, base),
        out_shape=jax.ShapeDtypeStruct((length, heads * depth), BF16),
        in_specs=[VMEM] * 5,
        out_specs=VMEM,
        compiler_params=PARAMS,
    )(arrived, before, *reads)


def last_projected(section, first, second, block, weights):
    length, columns = first.shape
    return pl.pallas_call(
        last_kernel,
        out_shape=jax.ShapeDtypeStruct((length, columns), BF16),
        in_specs=[SMEM] + [VMEM] * 4,
        out_specs=pl.BlockSpec(memory_space=pl.ANY),
        scratch_shapes=[
            pltpu.VMEM((length, columns), BF16),
            pltpu.SemaphoreType.DMA((length // CHUNK,)),
        ],
        compiler_params=LAST_PARAMS,
    )(section.astype(jnp.int32).reshape(1), first, second, block, weights)


def after(first, *values):
    return lax.optimization_barrier((first, *values))[1:]


def on_device(
    query_in,
    key_in,
    value_in,
    gate_in,
    write_strength,
    log_decay,
    doc_resets,
    conv_weight,
    output_norm_gain,
    output_projection_weight,
):
    length, heads, depth = query_in.shape
    taps = conv_weight
    rims = from_behind(pack_rims((query_in, key_in, value_in)), ("chain", "leaf"), 1)
    key, value = (jnp.transpose(x, (1, 0, 2)) for x in (key_in, value_in))
    key, value, first = filters_of(key, value, taps)
    gain = output_norm_gain.reshape(1, depth)
    leaves = lax.axis_size("leaf")
    place = lax.axis_index("leaf").astype(jnp.int32).reshape(1)

    links = lax.axis_size("chain") - 1
    unit_key, solved, starts, *own_maps = maps_of(
        0, heads, doc_resets, key, value, first, rims, taps, log_decay, write_strength
    )
    query_in, gate_in = after(own_maps[-1], query_in, gate_in)
    query, gate = (jnp.transpose(x, (1, 0, 2)) for x in (query_in, gate_in))
    reads = reads_of(
        0, heads, doc_resets, query, gate, gain, rims, taps, log_decay, write_strength,
        (unit_key, solved, starts),
    )
    size = heads // GROUPS
    blocks = []
    exchanged = [exchange(own_maps[0], leaves)]
    for g in range(GROUPS):
        earlier = blocks[-1] if blocks else reads[0]
        maps = after(earlier, *exchanged[g])
        before, state, *trans = join(place, maps, links)
        if g + 1 < GROUPS:
            exchanged.append(exchange(*after(state, own_maps[g + 1]), leaves))
        arrived = from_behind(state.astype(BF16), "chain", 1)
        for _ in range(links - 1):
            passed = jnp.einsum(
                "hij,hjk->hik", trans[0], arrived.astype(F32), precision=lax.Precision.HIGHEST
            )
            arrived = from_behind((passed + state).astype(BF16), "chain", 1)
        blocks.append(outputs_of(g * size, arrived, before, reads))

    ring = lax.axis_size("head")
    mine = lax.axis_index("head")
    width = size * depth
    weights = output_projection_weight
    around = [(i, (i + 1) % ring) for i in range(ring)]
    sums = [None] * GROUPS
    for k in range(ring):
        owner = lax.rem(mine + ring - k, ring)
        last = k + 1 == ring
        following = blocks if last else [lax.ppermute(x, "head", around) for x in blocks]
        for g, block in enumerate(blocks):
            section = owner * GROUPS + g
            if last and g + 1 == GROUPS:
                return last_projected(section, *sums, block, weights)
            rows = lax.dynamic_slice_in_dim(weights, section * width, width, 0)
            term = jnp.dot(block, rows, preferred_element_type=F32)
            sums[g] = term if sums[g] is None else sums[g] + term
        blocks = following


def solution(mesh):
    return jax.shard_map(
        on_device,
        mesh=mesh,
        in_specs=(
            P(("chain", "leaf"), "head", None),
            P(("chain", "leaf"), "head", None),
            P(("chain", "leaf"), "head", None),
            P(("chain", "leaf"), "head", None),
            P("head", ("chain", "leaf")),
            P("head", ("chain", "leaf")),
            P(("chain", "leaf")),
            P(None, None, "head", None),
            P(),
            P(None, "head"),
        ),
        out_specs=P(("chain", "leaf"), "head"),
        check_vma=False,
    )
```

```python
import functools

import jax
import jax.numpy as jnp
from jax import lax
from jax.experimental import pallas as pl
from jax.experimental.pallas import tpu as pltpu
from jax.sharding import PartitionSpec as P

BLOCK = 64
CHUNK = 128
GROUPS = 2
RIM = 8
EPSILON = 1e-06
FAR = -1e30
LARGE = 1e38
AGAIN = 16
F32 = jnp.float32
BF16 = jnp.bfloat16
NN = (((1,), (0,)), ((), ()))
NT = (((1,), (1,)), ((), ()))
TN = (((0,), (0,)), ((), ()))


def split(a):
    high = a.astype(BF16)
    return high, (a - high.astype(F32)).astype(BF16)


def mul(a, b, dims=NN):
    return lax.dot_general(a, b, dims, preferred_element_type=F32)


def mul_split(a, b):
    a_high, a_low = split(a)
    b_high, b_low = split(b)
    return mul(a_high, b_high) + (mul(a_low, b_high) + mul(a_high, b_low))


def rows_of(c):
    return slice(c * CHUNK, (c + 1) * CHUNK)


def indices():
    shape = (CHUNK, CHUNK)
    return (
        lax.broadcasted_iota(jnp.int32, shape, 0),
        lax.broadcasted_iota(jnp.int32, shape, 1),
    )


def token_scalars(decay_ref, strength_ref, c):
    row, col = indices()
    cum = lax.dot_general(
        decay_ref[:, rows_of(c)],
        (row <= col).astype(F32),
        NN,
        precision=lax.Precision.HIGHEST,
        preferred_element_type=F32,
    )
    stacked = [cum, strength_ref[:, rows_of(c)]]
    missing = 8 - 2 * cum.shape[0]
    if missing > 0:
        stacked.append(jnp.zeros((missing, CHUNK), F32))
    return jnp.concatenate(stacked, axis=0)


def lower_of(key, cum_col, cum_row, strength_col, strictly):
    fading = jnp.exp(jnp.where(strictly, cum_col - cum_row, FAR))
    return strength_col * fading * mul(key, key, NT)


def silu(x):
    below = jnp.minimum(1.0 + jnp.exp(-x), LARGE)
    inverse = pl.reciprocal(below, approx=True)
    return x * (inverse * (2.0 - below * inverse))


def filtered(padded, taps, begin, length):
    first = begin + RIM + 1 - len(taps)
    total = taps[0] * padded[first : first + length]
    for j in range(1, len(taps)):
        total = total + taps[j] * padded[first + j : first + j + length]
    return silu(total)


def taps_of(taps_ref, which, head):
    return [taps_ref[which, j, pl.ds(head, 1), :] for j in range(taps_ref.shape[1])]


def unit(rows):
    return rows * lax.rsqrt(jnp.sum(rows * rows, axis=-1, keepdims=True) + EPSILON)


def same_document(second_resets, row, col):
    return ((row // BLOCK) - (col // BLOCK)) * second_resets == 0


def lower_inverse(lowers, row, col):
    differ = row ^ col
    eye = (row == col).astype(F32)
    in_block = (differ < 8).astype(F32)
    diagonal = [low * in_block for low in lowers]
    powers = [d.astype(BF16) for d in diagonal]
    squares = [mul(p, p).astype(BF16) for p in powers]
    inverse = [eye - d for d in diagonal]
    stacked = [
        mul(jnp.concatenate([s, x.astype(BF16)], axis=0), s) for x, s in zip(inverse, squares)
    ]
    fourths = [both[:CHUNK].astype(BF16) for both in stacked]
    inverse = [x + both[CHUNK:] for x, both in zip(inverse, stacked)]
    inverse = [x + mul(x.astype(BF16), s) for x, s in zip(inverse, fourths)]
    size = 8
    while size < CHUNK:
        joint = odd_blocks(((differ >= size) & (differ < 2 * size)).astype(F32), size)
        rounded = [x.astype(BF16) for x in inverse]
        inner = [
            mul((odd_blocks(low, size) * joint).astype(BF16), x)
            for low, x in zip(lowers, rounded)
        ]
        outer = [
            mul(odd_blocks(x, size).astype(BF16), with_even_zeros(i, size).astype(BF16))
            for x, i in zip(inverse, inner)
        ]
        inverse = [less_in_odd(x, o, size) for x, o in zip(inverse, outer)]
        size *= 2
    return inverse


def odd_blocks(a, size):
    return jnp.concatenate([a[b : b + size] for b in range(size, a.shape[0], 2 * size)], axis=0)


def with_even_zeros(odd, size):
    zeros = jnp.zeros((size, odd.shape[1]), odd.dtype)
    pieces = []
    for b in range(0, odd.shape[0], size):
        pieces += [zeros, odd[b : b + size]]
    return jnp.concatenate(pieces, axis=0)


def less_in_odd(a, odd, size):
    pieces = []
    for b in range(0, odd.shape[0], size):
        pieces.append(a[2 * b : 2 * b + size])
        pieces.append(a[2 * b + size : 2 * b + 2 * size] - odd[b : b + size])
    return jnp.concatenate(pieces, axis=0)


def rims_kernel(*refs):
    *inputs, packed_ref, arrived = refs
    copies = []
    for i, x_ref in enumerate(inputs):
        last = x_ref.at[pl.ds(x_ref.shape[0] - RIM, RIM)]
        here = packed_ref.at[pl.ds(i * RIM, RIM)]
        copies.append(pltpu.make_async_copy(last, here, arrived.at[i]))
    for copy in copies:
        copy.start()
    for copy in copies:
        copy.wait()


def filters_kernel(
    resets, key_ref, value_ref, taps_ref, decay_ref, strength_ref,
    unit_ref, value_out_ref, first_ref, across_ref, down_ref, lowers_ref,
    padded,
):
    heads, length, _ = key_ref.shape
    row, col = indices()
    for i, x_ref in enumerate((key_ref, value_ref)):
        padded[i, :, RIM:] = x_ref[...].astype(F32)
        padded[i, :, 0:RIM] = jnp.zeros((heads, RIM, padded.shape[3]), F32)
    first_ref[...] = padded[:, :, RIM : RIM + AGAIN]

    def one_head(h, carry):
        for i in range(2):
            taps = taps_of(taps_ref, 1 + i, h)
            for c in range(length // CHUNK):
                rows = filtered(padded.at[i, h], taps, c * CHUNK, CHUNK)
                if i == 0:
                    unit_ref[h, rows_of(c)] = unit(rows).astype(BF16)
                else:
                    value_out_ref[h, rows_of(c)] = rows.astype(BF16)
        return carry

    lax.fori_loop(0, heads, one_head, 0)
    for c in range(length // CHUNK):
        across = token_scalars(decay_ref, strength_ref, c)
        down = jnp.transpose(across)
        across_ref[c] = across
        down_ref[c] = down
        if c:
            strictly = (row > col) & same_document(resets[2 * c + 1], row, col)
            for h in range(heads):
                lowers_ref[c - 1, h] = lower_of(
                    unit_ref[h, rows_of(c)], down[:, h : h + 1], across[h : h + 1],
                    down[:, heads + h : heads + h + 1], strictly,
                )


def maps_kernel(
    resets, unit_in_ref, value_in_ref, first_ref, across_ref, down_ref, lowers_ref, rim_ref, taps_ref,
    unit_ref, solved_ref, starts_ref, *refs,
):
    *map_refs, rims, padded, value_s, step_s = refs
    heads, length, depth = unit_ref.shape
    chunks = length // CHUNK
    size = heads // len(map_refs)
    row, col = indices()
    rims[...] = rim_ref[...].astype(F32)
    for g in range(heads):
        h = g
        unit_ref[g] = unit_in_ref[h]
        value_s[g] = value_in_ref[h]
        for i in range(2):
            padded[g, i, 0:RIM] = rims[(1 + i) * RIM : (2 + i) * RIM, h, :]
            padded[g, i, RIM : RIM + AGAIN] = first_ref[i, h]
            rows = filtered(padded.at[g, i], taps_of(taps_ref, 1 + i, h), 0, AGAIN)
            if i == 0:
                unit_ref[g, 0:AGAIN] = unit(rows).astype(BF16)
            else:
                value_s[g, 0:AGAIN] = rows.astype(BF16)

    parts = []
    lowers = []
    for c in range(chunks):
        first, second = resets[2 * c], resets[2 * c + 1]
        across, down = across_ref[c], down_ref[c]
        strictly = (row > col) & same_document(second, row, col)
        for g in range(heads):
            cum_col, cum_row = down[:, g : g + 1], across[g : g + 1]
            strength_col = down[:, heads + g : heads + g + 1]
            if c:
                lowers.append(lowers_ref[c - 1, g])
            else:
                key = unit_ref[g, rows_of(c)]
                lowers.append(lower_of(key, cum_col, cum_row, strength_col, strictly))
            parts.append((g, c, first, second, cum_col, cum_row, strength_col))
    inverses = lower_inverse(lowers, row, col)
    eye = (row == col).astype(F32)
    first_rows = lax.broadcasted_iota(jnp.int32, (CHUNK, 1), 0) < BLOCK
    for (g, c, first, second, cum_col, cum_row, strength_col), inverse in zip(parts, inverses):
        keep_first = (1 - first).astype(F32)
        keep_second = (1 - second).astype(F32)
        keep_both = keep_first * keep_second
        key = unit_ref[g, rows_of(c)]
        growth = jnp.exp(cum_col) * jnp.where(first_rows, keep_first, keep_both)
        targets = jnp.concatenate(
            [
                (strength_col * growth) * key.astype(F32),
                strength_col * value_s[g, rows_of(c)].astype(F32),
            ],
            axis=1,
        )
        solved = targets + mul((inverse - eye).astype(BF16), targets.astype(BF16))
        solved_ref[g, rows_of(c)] = solved
        end = cum_row[:, CHUNK - 1 : CHUNK]
        tail = jnp.exp(end - cum_col) * jnp.where(first_rows, keep_second, 1.0)
        product = mul(key, (tail * solved).astype(BF16), TN)
        passed = jnp.exp(end) * keep_both
        step_s[g, c, :, :depth] = jnp.where(row == col, passed, 0.0) - product[:, :depth]
        step_s[g, c, :, depth:] = product[:, depth:]

    def compose(later, earlier):
        high, low = split(earlier)
        trans = later[:, :depth].astype(BF16)
        joined = mul(trans, high) + mul(trans, low)
        return jnp.concatenate([joined[:, :depth], joined[:, depth:] + later[:, depth:]], axis=1)

    every = range(heads)
    states = [step_s[g, 0] for g in every]
    half = chunks // 2
    for c in range(1, half):
        for g in every:
            starts_ref[g, c - 1] = states[g]
        states = [compose(step_s[g, c], states[g]) for g in every]
    rest = [step_s[g, half] for g in every]
    for c in range(half + 1, chunks):
        rest = [compose(step_s[g, c], rest[g]) for g in every]
    for g in every:
        map_refs[g // size][g % size] = compose(rest[g], states[g]).astype(BF16)
    for c in range(half, chunks):
        for g in every:
            starts_ref[g, c - 1] = states[g]
        if c + 1 < chunks:
            states = [compose(step_s[g, c], states[g]) for g in every]


def reads_kernel(
    resets, query_ref, gate_ref, gain_ref, across_ref, down_ref, rim_ref, taps_ref,
    unit_ref, solved_ref, starts_ref,
    reach_ref, part_ref, gating_ref,
    rims, padded, query_s,
):
    heads, length, depth = unit_ref.shape
    chunks = length // CHUNK
    row, col = indices()
    first_rows = lax.broadcasted_iota(jnp.int32, (CHUNK, 1), 0) < BLOCK
    rims[...] = rim_ref[...].astype(F32)
    for g in range(heads):
        h = g
        padded[g, 0:RIM] = rims[0:RIM, h, :]
        padded[g, RIM : RIM + length] = query_ref[h].astype(F32)
        taps = taps_of(taps_ref, 0, h)
        for c in range(chunks):
            rows = filtered(padded.at[g], taps, c * CHUNK, CHUNK)
            query_s[g, rows_of(c)] = (unit(rows) * depth**-0.5).astype(BF16)

    for c in range(chunks):
        here = rows_of(c)
        cum, columns = across_ref[c], down_ref[c]
        first, second = resets[2 * c], resets[2 * c + 1]
        keep_first = (1 - first).astype(F32)
        keep_both = keep_first * (1 - second).astype(F32)
        upto = (row >= col) & same_document(second, row, col)
        for g in range(heads):
            h = g
            cum_col = columns[:, h : h + 1]
            query = query_s[g, here]
            fading = jnp.exp(jnp.where(upto, cum_col - cum[h : h + 1], FAR))
            mixing = fading * mul(query, unit_ref[g, here], NT)
            own = mul_split(mixing, solved_ref[g, here])
            growth = jnp.exp(cum_col) * jnp.where(first_rows, keep_first, keep_both)
            reach = growth * query.astype(F32) - own[:, :depth]
            part = own[:, depth:]
            if c:
                high, low = split(starts_ref[g, c - 1])
                rounded = reach.astype(BF16)
                both = mul(rounded, high) + mul(rounded, low)
                reach = both[:, :depth]
                part = part + both[:, depth:]
            reach_ref[g, here] = reach.astype(BF16)
            part_ref[g, here] = part
            gate = gate_ref[h, here].astype(F32)
            gating_ref[g, here] = gain_ref[...] * silu(gate)


def partner(place, k, count):
    if count & (count - 1) == 0:
        return place ^ k
    return lax.rem(place + count - k, count)


def pairs_at(k, count):
    if count & (count - 1) == 0:
        return [(i, i ^ k) for i in range(count)]
    return [(i, (i + k) % count) for i in range(count)]


def join_kernel(count, place, *refs):
    maps = refs[:count]
    before_ref, state_ref, *trans_ref, ordered = refs[count:]
    heads, depth, _ = before_ref.shape
    me = place[0]
    for k in range(count):
        ordered[partner(me, k, count)] = maps[k][...]
    row, col = indices()
    eye = (row == col).astype(F32)
    states = [jnp.concatenate([eye, jnp.zeros((depth, depth), F32)], axis=1)] * heads
    for lap in range(count):

        @pl.when(lap == me)
        def _():
            for h in range(heads):
                before_ref[h] = states[h]

        for h in range(heads):
            step = ordered[lap, h]
            if lap:
                high, low = split(states[h])
                trans = step[:, :depth]
                joined = mul(trans, high) + mul(trans, low)
                states[h] = jnp.concatenate(
                    [joined[:, :depth], joined[:, depth:] + step[:, depth:].astype(F32)], axis=1
                )
            else:
                states[h] = step.astype(F32)
    for h in range(heads):
        state_ref[h] = states[h][:, depth:].astype(state_ref.dtype)
        for ref in trans_ref:
            ref[h] = states[h][:, :depth]


def outputs_kernel(base, arrived_ref, before_ref, reach_ref, part_ref, gating_ref, normed_ref):
    heads, depth, _ = arrived_ref.shape
    for g in range(heads):
        h = base + g
        before = before_ref[g]
        incoming = mul_split(before[:, :depth], arrived_ref[g].astype(F32)) + before[:, depth:]
        high, low = split(incoming)
        for c in range(normed_ref.shape[0] // CHUNK):
            here = rows_of(c)
            reach = reach_ref[h, here]
            core = part_ref[h, here] + (mul(reach, high) + mul(reach, low))
            scale = lax.rsqrt(jnp.sum(core * core, axis=-1, keepdims=True) / depth + EPSILON)
            normed_ref[here, g * depth : (g + 1) * depth] = (
                core * scale * gating_ref[h, here]
            ).astype(BF16)


def last_kernel(section, first_ref, second_ref, block_ref, weights_ref, out_ref, tiles, written):
    width = block_ref.shape[1]
    rows = weights_ref[pl.ds(pl.multiple_of(section[0] * width, width), width), :]
    copies = []
    for i in range(first_ref.shape[0] // BLOCK):
        here = slice(i * BLOCK, (i + 1) * BLOCK)
        total = (first_ref[here] + second_ref[here]) + mul(block_ref[here], rows)
        tiles[here] = total.astype(BF16)
        copies.append(pltpu.make_async_copy(tiles.at[here], out_ref.at[here], written.at[i]))
        copies[-1].start()
    for copy in copies:
        copy.wait()


def from_behind(value, axis, steps):
    count = lax.axis_size(axis)
    return lax.ppermute(value, axis, [(i, i + steps) for i in range(count - steps)])


def exchange(own_map, leaves):
    received = [lax.ppermute(own_map, "leaf", pairs_at(k, leaves)) for k in range(1, leaves)]
    return [own_map] + received


VMEM = pl.BlockSpec(memory_space=pltpu.VMEM)
SMEM = pl.BlockSpec(memory_space=pltpu.SMEM)
HBM = pl.BlockSpec(memory_space=pltpu.HBM)
PARAMS = pltpu.CompilerParams(vmem_limit_bytes=8 * 1024 * 1024)
LAST_PARAMS = pltpu.CompilerParams(vmem_limit_bytes=12 * 1024 * 1024)


def pack_rims(inputs):
    _, heads, depth = inputs[0].shape
    return pl.pallas_call(
        rims_kernel,
        out_shape=jax.ShapeDtypeStruct((len(inputs) * RIM, heads, depth), BF16),
        in_specs=[HBM] * len(inputs),
        out_specs=VMEM,
        scratch_shapes=[pltpu.SemaphoreType.DMA((len(inputs),))],
        compiler_params=pltpu.CompilerParams(vmem_limit_bytes=63 * 2**20),
        cost_estimate=pl.CostEstimate(flops=10**9, bytes_accessed=2**16, transcendentals=0),
    )(*inputs)


def filters_of(resets, key, value, taps, decay, strength):
    heads, length, depth = key.shape
    chunks = length // CHUNK
    lines = max(8, 2 * heads)
    per_token = jax.ShapeDtypeStruct((heads, length, depth), BF16)
    return pl.pallas_call(
        filters_kernel,
        out_shape=(
            per_token,
            per_token,
            jax.ShapeDtypeStruct((2, heads, AGAIN, depth), F32),
            jax.ShapeDtypeStruct((chunks, lines, CHUNK), F32),
            jax.ShapeDtypeStruct((chunks, CHUNK, lines), F32),
            jax.ShapeDtypeStruct((chunks - 1, heads, CHUNK, CHUNK), F32),
        ),
        in_specs=[SMEM] + [VMEM] * 5,
        out_specs=[VMEM] * 6,
        scratch_shapes=[pltpu.VMEM((2, heads, length + RIM, depth), F32)],
        compiler_params=PARAMS,
        cost_estimate=pl.CostEstimate(
            flops=3 * 10**9, bytes_accessed=4 * 2**20, transcendentals=10**6
        ),
    )(resets, key, value, taps, decay, strength)


def maps_of(resets, made, rims, taps):
    heads, length, depth = made[0].shape
    chunks = length // CHUNK
    return pl.pallas_call(
        maps_kernel,
        out_shape=(
            jax.ShapeDtypeStruct((heads, length, depth), BF16),
            jax.ShapeDtypeStruct((heads, length, 2 * depth), F32),
            jax.ShapeDtypeStruct((heads, chunks - 1, depth, 2 * depth), F32),
            *[jax.ShapeDtypeStruct((heads // GROUPS, depth, 2 * depth), BF16)] * GROUPS,
        ),
        in_specs=[SMEM] + [VMEM] * 8,
        out_specs=[VMEM] * (3 + GROUPS),
        scratch_shapes=[
            pltpu.VMEM(rims.shape, F32),
            pltpu.VMEM((heads, 2, RIM + AGAIN, depth), F32),
            pltpu.VMEM((heads, length, depth), BF16),
            pltpu.VMEM((heads, chunks, depth, 2 * depth), F32),
        ],
        compiler_params=PARAMS,
        cost_estimate=pl.CostEstimate(
            flops=5 * 10**9, bytes_accessed=4 * 2**20, transcendentals=10**6
        ),
    )(resets, *made, rims, taps)


def reads_of(resets, query, gate, gain, across, down, rims, taps, made):
    heads, length, depth = query.shape
    per_token = jax.ShapeDtypeStruct((heads, length, depth), F32)
    return pl.pallas_call(
        reads_kernel,
        out_shape=(jax.ShapeDtypeStruct(per_token.shape, BF16), per_token, per_token),
        in_specs=[SMEM] + [VMEM] * 10,
        out_specs=[VMEM] * 3,
        scratch_shapes=[
            pltpu.VMEM(rims.shape, F32),
            pltpu.VMEM((heads, length + RIM, depth), F32),
            pltpu.VMEM((heads, length, depth), BF16),
        ],
        compiler_params=PARAMS,
        cost_estimate=pl.CostEstimate(
            flops=3 * 10**9, bytes_accessed=4 * 2**20, transcendentals=10**6
        ),
    )(resets, query, gate, gain, across, down, rims, taps, *made)


def join(place, maps, links):
    count = len(maps)
    heads, depth, _ = maps[0].shape
    pair = jax.ShapeDtypeStruct((heads, depth, 2 * depth), F32)
    square = (heads, depth, depth)
    if links == 1:
        totals = (jax.ShapeDtypeStruct(square, BF16),)
    else:
        totals = (jax.ShapeDtypeStruct(square, F32),) * 2
    return pl.pallas_call(
        functools.partial(join_kernel, count),
        out_shape=(pair, *totals),
        in_specs=[SMEM] + [VMEM] * count,
        out_specs=[VMEM] * (1 + len(totals)),
        scratch_shapes=[pltpu.VMEM((count, heads, depth, 2 * depth), BF16)],
        compiler_params=PARAMS,
    )(place, *maps)


def outputs_of(base, arrived, before, reads):
    heads, depth, _ = arrived.shape
    length = reads[0].shape[1]
    return pl.pallas_call(
        functools.partial(outputs_kernel, base),
        out_shape=jax.ShapeDtypeStruct((length, heads * depth), BF16),
        in_specs=[VMEM] * 5,
        out_specs=VMEM,
        compiler_params=PARAMS,
    )(arrived, before, *reads)


def last_projected(section, first, second, block, weights):
    length, columns = first.shape
    return pl.pallas_call(
        last_kernel,
        out_shape=jax.ShapeDtypeStruct((length, columns), BF16),
        in_specs=[SMEM] + [VMEM] * 4,
        out_specs=pl.BlockSpec(memory_space=pl.ANY),
        scratch_shapes=[
            pltpu.VMEM((length, columns), BF16),
            pltpu.SemaphoreType.DMA((length // BLOCK,)),
        ],
        compiler_params=LAST_PARAMS,
    )(section.astype(jnp.int32).reshape(1), first, second, block, weights)


def after(first, *values):
    return lax.optimization_barrier((first, *values))[1:]


def on_device(
    query_in,
    key_in,
    value_in,
    gate_in,
    write_strength,
    log_decay,
    doc_resets,
    conv_weight,
    output_norm_gain,
    output_projection_weight,
):
    length, heads, depth = query_in.shape
    taps = conv_weight
    rims = from_behind(pack_rims((query_in, key_in, value_in)), ("chain", "leaf"), 1)
    key, value = (jnp.transpose(x, (1, 0, 2)) for x in (key_in, value_in))
    filtered_keys = filters_of(doc_resets, key, value, taps, log_decay, write_strength)
    across, down = filtered_keys[3:5]
    gain = output_norm_gain.reshape(1, depth)
    leaves = lax.axis_size("leaf")
    place = lax.axis_index("leaf").astype(jnp.int32).reshape(1)
    links = lax.axis_size("chain") - 1

    unit_key, solved, starts, *own_maps = maps_of(doc_resets, filtered_keys, rims, taps)
    query_in, gate_in = after(own_maps[-1], query_in, gate_in)
    query, gate = (jnp.transpose(x, (1, 0, 2)) for x in (query_in, gate_in))
    reads = reads_of(
        doc_resets, query, gate, gain, across, down, rims, taps, (unit_key, solved, starts)
    )
    size = heads // GROUPS
    blocks = []
    exchanged = [exchange(own_maps[0], leaves)]
    for g in range(GROUPS):
        earlier = blocks[-1] if blocks else reads[0]
        maps = after(earlier, *exchanged[g])
        before, state, *trans = join(place, maps, links)
        if g + 1 < GROUPS:
            exchanged.append(exchange(*after(state, own_maps[g + 1]), leaves))
        arrived = from_behind(state.astype(BF16), "chain", 1)
        for _ in range(links - 1):
            passed = jnp.einsum(
                "hij,hjk->hik", trans[0], arrived.astype(F32), precision=lax.Precision.HIGHEST
            )
            arrived = from_behind((passed + state).astype(BF16), "chain", 1)
        blocks.append(outputs_of(g * size, arrived, before, reads))

    ring = lax.axis_size("head")
    mine = lax.axis_index("head")
    width = size * depth
    weights = output_projection_weight
    around = [(i, (i + 1) % ring) for i in range(ring)]
    sums = [None] * GROUPS
    for k in range(ring):
        owner = lax.rem(mine + ring - k, ring)
        last = k + 1 == ring
        following = blocks if last else [lax.ppermute(x, "head", around) for x in blocks]
        if k == 0:
            blocks[:-1] = after(following[0], *blocks[:-1])
        for g, block in enumerate(blocks):
            section = owner * GROUPS + g
            if last and g + 1 == GROUPS:
                return last_projected(section, *sums, block, weights)
            rows = lax.dynamic_slice_in_dim(weights, section * width, width, 0)
            term = jnp.dot(block, rows, preferred_element_type=F32)
            sums[g] = term if sums[g] is None else sums[g] + term
        blocks = following


def solution(mesh):
    return jax.shard_map(
        on_device,
        mesh=mesh,
        in_specs=(
            P(("chain", "leaf"), "head", None),
            P(("chain", "leaf"), "head", None),
            P(("chain", "leaf"), "head", None),
            P(("chain", "leaf"), "head", None),
            P("head", ("chain", "leaf")),
            P("head", ("chain", "leaf")),
            P(("chain", "leaf")),
            P(None, None, "head", None),
            P(),
            P(None, "head"),
        ),
        out_specs=P(("chain", "leaf"), "head"),
        check_vma=False,
    )
```

```python
import functools

import jax
import jax.numpy as jnp
from jax import lax
from jax.experimental import pallas as pl
from jax.experimental.pallas import tpu as pltpu
from jax.sharding import PartitionSpec as P

BLOCK = 64
CHUNK = 128
GROUPS = 2
RIM = 8
EPSILON = 1e-06
FAR = -1e30
LARGE = 1e38
AGAIN = 16
F32 = jnp.float32
BF16 = jnp.bfloat16
NN = (((1,), (0,)), ((), ()))
NT = (((1,), (1,)), ((), ()))
TN = (((0,), (0,)), ((), ()))


def split(a):
    high = a.astype(BF16)
    return high, (a - high.astype(F32)).astype(BF16)


def mul(a, b, dims=NN):
    return lax.dot_general(a, b, dims, preferred_element_type=F32)


def mul_split(a, b):
    a_high, a_low = split(a)
    b_high, b_low = split(b)
    return mul(a_high, b_high) + (mul(a_low, b_high) + mul(a_high, b_low))


def rows_of(c):
    return slice(c * CHUNK, (c + 1) * CHUNK)


def indices():
    shape = (CHUNK, CHUNK)
    return (
        lax.broadcasted_iota(jnp.int32, shape, 0),
        lax.broadcasted_iota(jnp.int32, shape, 1),
    )


def token_scalars(decay_ref, strength_ref, c):
    row, col = indices()
    cum = lax.dot_general(
        decay_ref[:, rows_of(c)],
        (row <= col).astype(F32),
        NN,
        precision=lax.Precision.HIGHEST,
        preferred_element_type=F32,
    )
    strength = strength_ref[:, rows_of(c)]
    stacked = [cum, strength]
    missing = 8 - 2 * cum.shape[0]
    if missing > 0:
        stacked.append(jnp.zeros((missing, CHUNK), F32))
    return cum, strength, jnp.transpose(jnp.concatenate(stacked, axis=0))


def silu(x):
    below = jnp.minimum(1.0 + jnp.exp(-x), LARGE)
    inverse = pl.reciprocal(below, approx=True)
    return x * (inverse * (2.0 - below * inverse))


def filtered(padded, taps, begin, length):
    first = begin + RIM + 1 - len(taps)
    total = taps[0] * padded[first : first + length]
    for j in range(1, len(taps)):
        total = total + taps[j] * padded[first + j : first + j + length]
    return silu(total)


def taps_of(taps_ref, which, head):
    return [taps_ref[which, j, pl.ds(head, 1), :] for j in range(taps_ref.shape[1])]


def unit(rows):
    return rows * lax.rsqrt(jnp.sum(rows * rows, axis=-1, keepdims=True) + EPSILON)


def same_document(second_resets, row, col):
    return ((row // BLOCK) - (col // BLOCK)) * second_resets == 0


def lower_inverse(lowers, row, col):
    differ = row ^ col
    eye = (row == col).astype(F32)
    in_block = (differ < 8).astype(F32)
    diagonal = [low * in_block for low in lowers]
    powers = [d.astype(BF16) for d in diagonal]
    squares = [mul(p, p).astype(BF16) for p in powers]
    inverse = [eye - d for d in diagonal]
    stacked = [
        mul(jnp.concatenate([s, x.astype(BF16)], axis=0), s) for x, s in zip(inverse, squares)
    ]
    fourths = [both[:CHUNK].astype(BF16) for both in stacked]
    inverse = [x + both[CHUNK:] for x, both in zip(inverse, stacked)]
    inverse = [x + mul(x.astype(BF16), s) for x, s in zip(inverse, fourths)]
    size = 8
    while size < CHUNK:
        joint = odd_blocks(((differ >= size) & (differ < 2 * size)).astype(F32), size)
        rounded = [x.astype(BF16) for x in inverse]
        inner = [
            mul((odd_blocks(low, size) * joint).astype(BF16), x)
            for low, x in zip(lowers, rounded)
        ]
        outer = [
            mul(odd_blocks(x, size).astype(BF16), with_even_zeros(i, size).astype(BF16))
            for x, i in zip(inverse, inner)
        ]
        inverse = [less_in_odd(x, o, size) for x, o in zip(inverse, outer)]
        size *= 2
    return inverse


def odd_blocks(a, size):
    return jnp.concatenate([a[b : b + size] for b in range(size, a.shape[0], 2 * size)], axis=0)


def with_even_zeros(odd, size):
    zeros = jnp.zeros((size, odd.shape[1]), odd.dtype)
    pieces = []
    for b in range(0, odd.shape[0], size):
        pieces += [zeros, odd[b : b + size]]
    return jnp.concatenate(pieces, axis=0)


def less_in_odd(a, odd, size):
    pieces = []
    for b in range(0, odd.shape[0], size):
        pieces.append(a[2 * b : 2 * b + size])
        pieces.append(a[2 * b + size : 2 * b + 2 * size] - odd[b : b + size])
    return jnp.concatenate(pieces, axis=0)


def rims_kernel(*refs):
    *inputs, packed_ref, arrived = refs
    copies = []
    for i, x_ref in enumerate(inputs):
        last = x_ref.at[pl.ds(x_ref.shape[0] - RIM, RIM)]
        here = packed_ref.at[pl.ds(i * RIM, RIM)]
        copies.append(pltpu.make_async_copy(last, here, arrived.at[i]))
    for copy in copies:
        copy.start()
    for copy in copies:
        copy.wait()


def filters_kernel(key_ref, value_ref, taps_ref, unit_ref, value_out_ref, first_ref, padded):
    heads, length, _ = key_ref.shape
    for i, x_ref in enumerate((key_ref, value_ref)):
        padded[i, :, RIM:] = x_ref[...].astype(F32)
        padded[i, :, 0:RIM] = jnp.zeros((heads, RIM, padded.shape[3]), F32)
    first_ref[...] = padded[:, :, RIM : RIM + AGAIN]

    def one_head(h, carry):
        for i in range(2):
            taps = taps_of(taps_ref, 1 + i, h)
            for c in range(length // CHUNK):
                rows = filtered(padded.at[i, h], taps, c * CHUNK, CHUNK)
                if i == 0:
                    unit_ref[h, rows_of(c)] = unit(rows).astype(BF16)
                else:
                    value_out_ref[h, rows_of(c)] = rows.astype(BF16)
        return carry

    lax.fori_loop(0, heads, one_head, 0)


def maps_kernel(
    base, resets, unit_in_ref, value_in_ref, first_ref, rim_ref, taps_ref, decay_ref, strength_ref,
    unit_ref, solved_ref, starts_ref, *refs,
):
    *map_refs, rims, padded, value_s, step_s = refs
    heads, length, depth = unit_ref.shape
    chunks = length // CHUNK
    size = heads // len(map_refs)
    total_heads = decay_ref.shape[0]
    row, col = indices()
    rims[...] = rim_ref[...].astype(F32)
    for g in range(heads):
        h = base + g
        unit_ref[g] = unit_in_ref[h]
        value_s[g] = value_in_ref[h]
        for i in range(2):
            padded[g, i, 0:RIM] = rims[(1 + i) * RIM : (2 + i) * RIM, h, :]
            padded[g, i, RIM : RIM + AGAIN] = first_ref[i, h]
            rows = filtered(padded.at[g, i], taps_of(taps_ref, 1 + i, h), 0, AGAIN)
            if i == 0:
                unit_ref[g, 0:AGAIN] = unit(rows).astype(BF16)
            else:
                value_s[g, 0:AGAIN] = rows.astype(BF16)

    parts = []
    lowers = []
    for c in range(chunks):
        cum, _, columns = token_scalars(decay_ref, strength_ref, c)
        first, second = resets[2 * c], resets[2 * c + 1]
        strictly = (row > col) & same_document(second, row, col)
        for g in range(heads):
            h = base + g
            cum_col = columns[:, h : h + 1]
            cum_row = cum[h : h + 1]
            key = unit_ref[g, rows_of(c)]
            fading = jnp.exp(jnp.where(strictly, cum_col - cum_row, FAR))
            strength_col = columns[:, total_heads + h : total_heads + h + 1]
            lowers.append(strength_col * fading * mul(key, key, NT))
            parts.append((g, c, first, second, cum_col, cum_row, strength_col))
    inverses = lower_inverse(lowers, row, col)
    eye = (row == col).astype(F32)
    first_rows = lax.broadcasted_iota(jnp.int32, (CHUNK, 1), 0) < BLOCK
    for (g, c, first, second, cum_col, cum_row, strength_col), inverse in zip(parts, inverses):
        keep_first = (1 - first).astype(F32)
        keep_second = (1 - second).astype(F32)
        keep_both = keep_first * keep_second
        key = unit_ref[g, rows_of(c)]
        growth = jnp.exp(cum_col) * jnp.where(first_rows, keep_first, keep_both)
        targets = jnp.concatenate(
            [
                (strength_col * growth) * key.astype(F32),
                strength_col * value_s[g, rows_of(c)].astype(F32),
            ],
            axis=1,
        )
        solved = targets + mul((inverse - eye).astype(BF16), targets.astype(BF16))
        solved_ref[g, rows_of(c)] = solved
        end = cum_row[:, CHUNK - 1 : CHUNK]
        tail = jnp.exp(end - cum_col) * jnp.where(first_rows, keep_second, 1.0)
        product = mul(key, (tail * solved).astype(BF16), TN)
        passed = jnp.exp(end) * keep_both
        step_s[g, c, :, :depth] = jnp.where(row == col, passed, 0.0) - product[:, :depth]
        step_s[g, c, :, depth:] = product[:, depth:]

    def compose(later, earlier):
        high, low = split(earlier)
        trans = later[:, :depth].astype(BF16)
        joined = mul(trans, high) + mul(trans, low)
        return jnp.concatenate([joined[:, :depth], joined[:, depth:] + later[:, depth:]], axis=1)

    every = range(heads)
    states = [step_s[g, 0] for g in every]
    half = chunks // 2
    for c in range(1, half):
        for g in every:
            starts_ref[g, c - 1] = states[g]
        states = [compose(step_s[g, c], states[g]) for g in every]
    rest = [step_s[g, half] for g in every]
    for c in range(half + 1, chunks):
        rest = [compose(step_s[g, c], rest[g]) for g in every]
    for g in every:
        map_refs[g // size][g % size] = compose(rest[g], states[g]).astype(BF16)
    for c in range(half, chunks):
        for g in every:
            starts_ref[g, c - 1] = states[g]
        if c + 1 < chunks:
            states = [compose(step_s[g, c], states[g]) for g in every]


def reads_kernel(
    base, resets, query_ref, gate_ref, gain_ref, rim_ref, taps_ref, decay_ref, strength_ref,
    unit_ref, solved_ref, starts_ref,
    reach_ref, part_ref, gating_ref,
    rims, padded, query_s,
):
    heads, length, depth = unit_ref.shape
    chunks = length // CHUNK
    row, col = indices()
    first_rows = lax.broadcasted_iota(jnp.int32, (CHUNK, 1), 0) < BLOCK
    rims[...] = rim_ref[...].astype(F32)
    for g in range(heads):
        h = base + g
        padded[g, 0:RIM] = rims[0:RIM, h, :]
        padded[g, RIM : RIM + length] = query_ref[h].astype(F32)
        taps = taps_of(taps_ref, 0, h)
        for c in range(chunks):
            rows = filtered(padded.at[g], taps, c * CHUNK, CHUNK)
            query_s[g, rows_of(c)] = (unit(rows) * depth**-0.5).astype(BF16)

    for c in range(chunks):
        here = rows_of(c)
        cum, _, columns = token_scalars(decay_ref, strength_ref, c)
        first, second = resets[2 * c], resets[2 * c + 1]
        keep_first = (1 - first).astype(F32)
        keep_both = keep_first * (1 - second).astype(F32)
        upto = (row >= col) & same_document(second, row, col)
        for g in range(heads):
            h = base + g
            cum_col = columns[:, h : h + 1]
            query = query_s[g, here]
            fading = jnp.exp(jnp.where(upto, cum_col - cum[h : h + 1], FAR))
            mixing = fading * mul(query, unit_ref[g, here], NT)
            own = mul_split(mixing, solved_ref[g, here])
            growth = jnp.exp(cum_col) * jnp.where(first_rows, keep_first, keep_both)
            reach = growth * query.astype(F32) - own[:, :depth]
            part = own[:, depth:]
            if c:
                both = mul_split(reach, starts_ref[g, c - 1])
                reach = both[:, :depth]
                part = part + both[:, depth:]
            reach_ref[g, here] = reach.astype(BF16)
            part_ref[g, here] = part
            gate = gate_ref[h, here].astype(F32)
            gating_ref[g, here] = gain_ref[...] * silu(gate)


def partner(place, k, count):
    if count & (count - 1) == 0:
        return place ^ k
    return lax.rem(place + count - k, count)


def pairs_at(k, count):
    if count & (count - 1) == 0:
        return [(i, i ^ k) for i in range(count)]
    return [(i, (i + k) % count) for i in range(count)]


def join_kernel(count, place, *refs):
    maps = refs[:count]
    before_ref, state_ref, *trans_ref, ordered = refs[count:]
    heads, depth, _ = before_ref.shape
    me = place[0]
    for k in range(count):
        ordered[partner(me, k, count)] = maps[k][...]
    row, col = indices()
    eye = (row == col).astype(F32)
    states = [jnp.concatenate([eye, jnp.zeros((depth, depth), F32)], axis=1)] * heads
    for lap in range(count):

        @pl.when(lap == me)
        def _():
            for h in range(heads):
                before_ref[h] = states[h]

        for h in range(heads):
            step = ordered[lap, h]
            if lap:
                high, low = split(states[h])
                trans = step[:, :depth]
                joined = mul(trans, high) + mul(trans, low)
                states[h] = jnp.concatenate(
                    [joined[:, :depth], joined[:, depth:] + step[:, depth:].astype(F32)], axis=1
                )
            else:
                states[h] = step.astype(F32)
    for h in range(heads):
        state_ref[h] = states[h][:, depth:].astype(state_ref.dtype)
        for ref in trans_ref:
            ref[h] = states[h][:, :depth]


def placed_kernel(base, before_ref, reach_ref, part_ref, through_ref, fixed_ref):
    heads, depth, _ = before_ref.shape
    for g in range(heads):
        high, low = split(before_ref[g])
        for c in range(through_ref.shape[1] // CHUNK):
            here = rows_of(c)
            reach = reach_ref[base + g, here]
            both = mul(reach, high) + mul(reach, low)
            through_ref[g, here] = both[:, :depth].astype(BF16)
            fixed_ref[g, here] = part_ref[base + g, here] + both[:, depth:]


def outputs_kernel(base, arrived_ref, through_ref, fixed_ref, gating_ref, normed_ref):
    heads, depth, _ = arrived_ref.shape
    for g in range(heads):
        arrived = arrived_ref[g]
        for c in range(normed_ref.shape[0] // CHUNK):
            here = rows_of(c)
            core = fixed_ref[g, here] + mul(through_ref[g, here], arrived)
            scale = lax.rsqrt(jnp.sum(core * core, axis=-1, keepdims=True) / depth + EPSILON)
            normed_ref[here, g * depth : (g + 1) * depth] = (
                core * scale * gating_ref[base + g, here]
            ).astype(BF16)


def last_kernel(section, first_ref, second_ref, block_ref, weights_ref, out_ref, tiles, written):
    width = block_ref.shape[1]
    rows = weights_ref[pl.ds(pl.multiple_of(section[0] * width, width), width), :]
    copies = []
    for i in range(first_ref.shape[0] // CHUNK):
        here = rows_of(i)
        total = (first_ref[here] + second_ref[here]) + mul(block_ref[here], rows)
        tiles[here] = total.astype(BF16)
        copies.append(pltpu.make_async_copy(tiles.at[here], out_ref.at[here], written.at[i]))
        copies[-1].start()
    for copy in copies:
        copy.wait()


def from_behind(value, axis, steps):
    count = lax.axis_size(axis)
    return lax.ppermute(value, axis, [(i, i + steps) for i in range(count - steps)])


def exchange(own_map, leaves):
    received = [lax.ppermute(own_map, "leaf", pairs_at(k, leaves)) for k in range(1, leaves)]
    return [own_map] + received


VMEM = pl.BlockSpec(memory_space=pltpu.VMEM)
SMEM = pl.BlockSpec(memory_space=pltpu.SMEM)
HBM = pl.BlockSpec(memory_space=pltpu.HBM)
PARAMS = pltpu.CompilerParams(vmem_limit_bytes=8 * 1024 * 1024)
LAST_PARAMS = pltpu.CompilerParams(vmem_limit_bytes=12 * 1024 * 1024)


def pack_rims(inputs):
    _, heads, depth = inputs[0].shape
    return pl.pallas_call(
        rims_kernel,
        out_shape=jax.ShapeDtypeStruct((len(inputs) * RIM, heads, depth), BF16),
        in_specs=[HBM] * len(inputs),
        out_specs=VMEM,
        scratch_shapes=[pltpu.SemaphoreType.DMA((len(inputs),))],
        compiler_params=pltpu.CompilerParams(vmem_limit_bytes=63 * 2**20),
        cost_estimate=pl.CostEstimate(flops=10**9, bytes_accessed=2**16, transcendentals=0),
    )(*inputs)


def filters_of(key, value, taps):
    heads, length, depth = key.shape
    per_token = jax.ShapeDtypeStruct((heads, length, depth), BF16)
    return pl.pallas_call(
        filters_kernel,
        out_shape=(per_token, per_token, jax.ShapeDtypeStruct((2, heads, AGAIN, depth), F32)),
        in_specs=[VMEM] * 3,
        out_specs=[VMEM] * 3,
        scratch_shapes=[pltpu.VMEM((2, heads, length + RIM, depth), F32)],
        compiler_params=PARAMS,
        cost_estimate=pl.CostEstimate(
            flops=3 * 10**9, bytes_accessed=4 * 2**20, transcendentals=10**6
        ),
    )(key, value, taps)


def maps_of(base, heads, resets, unit_in, value_in, first, rims, taps, decay, strength):
    _, length, depth = unit_in.shape
    chunks = length // CHUNK
    return pl.pallas_call(
        functools.partial(maps_kernel, base),
        out_shape=(
            jax.ShapeDtypeStruct((heads, length, depth), BF16),
            jax.ShapeDtypeStruct((heads, length, 2 * depth), F32),
            jax.ShapeDtypeStruct((heads, chunks - 1, depth, 2 * depth), F32),
            *[jax.ShapeDtypeStruct((heads // GROUPS, depth, 2 * depth), BF16)] * GROUPS,
        ),
        in_specs=[SMEM] + [VMEM] * 7,
        out_specs=[VMEM] * (3 + GROUPS),
        scratch_shapes=[
            pltpu.VMEM(rims.shape, F32),
            pltpu.VMEM((heads, 2, RIM + AGAIN, depth), F32),
            pltpu.VMEM((heads, length, depth), BF16),
            pltpu.VMEM((heads, chunks, depth, 2 * depth), F32),
        ],
        compiler_params=PARAMS,
        cost_estimate=pl.CostEstimate(
            flops=5 * 10**9, bytes_accessed=4 * 2**20, transcendentals=10**6
        ),
    )(resets, unit_in, value_in, first, rims, taps, decay, strength)


def reads_of(base, heads, resets, query, gate, gain, rims, taps, decay, strength, made):
    _, length, depth = query.shape
    per_token = jax.ShapeDtypeStruct((heads, length, depth), F32)
    return pl.pallas_call(
        functools.partial(reads_kernel, base),
        out_shape=(jax.ShapeDtypeStruct(per_token.shape, BF16), per_token, per_token),
        in_specs=[SMEM] + [VMEM] * 10,
        out_specs=[VMEM] * 3,
        scratch_shapes=[
            pltpu.VMEM(rims.shape, F32),
            pltpu.VMEM((heads, length + RIM, depth), F32),
            pltpu.VMEM((heads, length, depth), BF16),
        ],
        compiler_params=PARAMS,
        cost_estimate=pl.CostEstimate(
            flops=3 * 10**9, bytes_accessed=4 * 2**20, transcendentals=10**6
        ),
    )(resets, query, gate, gain, rims, taps, decay, strength, *made)


def join(place, maps, links):
    count = len(maps)
    heads, depth, _ = maps[0].shape
    pair = jax.ShapeDtypeStruct((heads, depth, 2 * depth), F32)
    square = (heads, depth, depth)
    if links == 1:
        totals = (jax.ShapeDtypeStruct(square, BF16),)
    else:
        totals = (jax.ShapeDtypeStruct(square, F32),) * 2
    return pl.pallas_call(
        functools.partial(join_kernel, count),
        out_shape=(pair, *totals),
        in_specs=[SMEM] + [VMEM] * count,
        out_specs=[VMEM] * (1 + len(totals)),
        scratch_shapes=[pltpu.VMEM((count, heads, depth, 2 * depth), BF16)],
        compiler_params=PARAMS,
    )(place, *maps)


def placed_of(base, before, reach, part):
    heads, depth, _ = before.shape
    length = reach.shape[1]
    per_token = (heads, length, depth)
    return pl.pallas_call(
        functools.partial(placed_kernel, base),
        out_shape=(
            jax.ShapeDtypeStruct(per_token, BF16),
            jax.ShapeDtypeStruct(per_token, F32),
        ),
        in_specs=[VMEM] * 3,
        out_specs=[VMEM] * 2,
        compiler_params=PARAMS,
        cost_estimate=pl.CostEstimate(flops=2 * 10**9, bytes_accessed=2**20, transcendentals=0),
    )(before, reach, part)


def outputs_of(base, arrived, placed, gating):
    heads, depth, _ = arrived.shape
    length = gating.shape[1]
    return pl.pallas_call(
        functools.partial(outputs_kernel, base),
        out_shape=jax.ShapeDtypeStruct((length, heads * depth), BF16),
        in_specs=[VMEM] * 4,
        out_specs=VMEM,
        compiler_params=PARAMS,
    )(arrived, *placed, gating)


def last_projected(section, first, second, block, weights):
    length, columns = first.shape
    return pl.pallas_call(
        last_kernel,
        out_shape=jax.ShapeDtypeStruct((length, columns), BF16),
        in_specs=[SMEM] + [VMEM] * 4,
        out_specs=pl.BlockSpec(memory_space=pl.ANY),
        scratch_shapes=[
            pltpu.VMEM((length, columns), BF16),
            pltpu.SemaphoreType.DMA((length // CHUNK,)),
        ],
        compiler_params=LAST_PARAMS,
    )(section.astype(jnp.int32).reshape(1), first, second, block, weights)


def after(first, *values):
    return lax.optimization_barrier((first, *values))[1:]


def on_device(
    query_in,
    key_in,
    value_in,
    gate_in,
    write_strength,
    log_decay,
    doc_resets,
    conv_weight,
    output_norm_gain,
    output_projection_weight,
):
    length, heads, depth = query_in.shape
    taps = conv_weight
    rims = from_behind(pack_rims((query_in, key_in, value_in)), ("chain", "leaf"), 1)
    key, value = (jnp.transpose(x, (1, 0, 2)) for x in (key_in, value_in))
    key, value, first = filters_of(key, value, taps)
    gain = output_norm_gain.reshape(1, depth)
    leaves = lax.axis_size("leaf")
    place = lax.axis_index("leaf").astype(jnp.int32).reshape(1)

    links = lax.axis_size("chain") - 1
    unit_key, solved, starts, *own_maps = maps_of(
        0, heads, doc_resets, key, value, first, rims, taps, log_decay, write_strength
    )
    query_in, gate_in = after(own_maps[-1], query_in, gate_in)
    query, gate = (jnp.transpose(x, (1, 0, 2)) for x in (query_in, gate_in))
    reads = reads_of(
        0, heads, doc_resets, query, gate, gain, rims, taps, log_decay, write_strength,
        (unit_key, solved, starts),
    )
    size = heads // GROUPS
    blocks = []
    exchanged = [exchange(own_maps[0], leaves)]
    for g in range(GROUPS):
        earlier = blocks[-1] if blocks else reads[0]
        maps = after(earlier, *exchanged[g])
        before, state, *trans = join(place, maps, links)
        if g + 1 < GROUPS:
            exchanged.append(exchange(*after(state, own_maps[g + 1]), leaves))
        arrived = from_behind(state.astype(BF16), "chain", 1)
        for _ in range(links - 1):
            passed = jnp.einsum(
                "hij,hjk->hik", trans[0], arrived.astype(F32), precision=lax.Precision.HIGHEST
            )
            arrived = from_behind((passed + state).astype(BF16), "chain", 1)
        reach, part, gating = reads
        placed = placed_of(g * size, before, reach, part)
        blocks.append(outputs_of(g * size, arrived, placed, gating))

    ring = lax.axis_size("head")
    mine = lax.axis_index("head")
    width = size * depth
    weights = output_projection_weight
    around = [(i, (i + 1) % ring) for i in range(ring)]
    sums = [None] * GROUPS
    for k in range(ring):
        owner = lax.rem(mine + ring - k, ring)
        last = k + 1 == ring
        following = blocks if last else [lax.ppermute(x, "head", around) for x in blocks]
        if k == 0:
            blocks[:-1] = after(following[0], *blocks[:-1])
        for g, block in enumerate(blocks):
            section = owner * GROUPS + g
            if last and g + 1 == GROUPS:
                return last_projected(section, *sums, block, weights)
            rows = lax.dynamic_slice_in_dim(weights, section * width, width, 0)
            term = jnp.dot(block, rows, preferred_element_type=F32)
            sums[g] = term if sums[g] is None else sums[g] + term
        blocks = following


def solution(mesh):
    return jax.shard_map(
        on_device,
        mesh=mesh,
        in_specs=(
            P(("chain", "leaf"), "head", None),
            P(("chain", "leaf"), "head", None),
            P(("chain", "leaf"), "head", None),
            P(("chain", "leaf"), "head", None),
            P("head", ("chain", "leaf")),
            P("head", ("chain", "leaf")),
            P(("chain", "leaf")),
            P(None, None, "head", None),
            P(),
            P(None, "head"),
        ),
        out_specs=P(("chain", "leaf"), "head"),
        check_vma=False,
    )
```

```python
import functools

import jax
import jax.numpy as jnp
from jax import lax
from jax.experimental import pallas as pl
from jax.experimental.pallas import tpu as pltpu
from jax.sharding import PartitionSpec as P

BLOCK = 64
CHUNK = 128
GROUPS = 2
RIM = 8
EPSILON = 1e-06
FAR = -1e30
LARGE = 1e38
AGAIN = 16
F32 = jnp.float32
BF16 = jnp.bfloat16
NN = (((1,), (0,)), ((), ()))
NT = (((1,), (1,)), ((), ()))
TN = (((0,), (0,)), ((), ()))


def split(a):
    high = a.astype(BF16)
    return high, (a - high.astype(F32)).astype(BF16)


def mul(a, b, dims=NN):
    return lax.dot_general(a, b, dims, preferred_element_type=F32)


def mul_split(a, b):
    a_high, a_low = split(a)
    b_high, b_low = split(b)
    return mul(a_high, b_high) + (mul(a_low, b_high) + mul(a_high, b_low))


def rows_of(c):
    return slice(c * CHUNK, (c + 1) * CHUNK)


def indices():
    shape = (CHUNK, CHUNK)
    return (
        lax.broadcasted_iota(jnp.int32, shape, 0),
        lax.broadcasted_iota(jnp.int32, shape, 1),
    )


def token_scalars(decay_ref, strength_ref, c):
    row, col = indices()
    cum = lax.dot_general(
        decay_ref[:, rows_of(c)],
        (row <= col).astype(F32),
        NN,
        precision=lax.Precision.HIGHEST,
        preferred_element_type=F32,
    )
    strength = strength_ref[:, rows_of(c)]
    stacked = [cum, strength]
    missing = 8 - 2 * cum.shape[0]
    if missing > 0:
        stacked.append(jnp.zeros((missing, CHUNK), F32))
    return cum, strength, jnp.transpose(jnp.concatenate(stacked, axis=0))


def silu(x):
    below = jnp.minimum(1.0 + jnp.exp(-x), LARGE)
    inverse = pl.reciprocal(below, approx=True)
    return x * (inverse * (2.0 - below * inverse))


def filtered(padded, taps, begin, length):
    first = begin + RIM + 1 - len(taps)
    total = taps[0] * padded[first : first + length]
    for j in range(1, len(taps)):
        total = total + taps[j] * padded[first + j : first + j + length]
    return silu(total)


def taps_of(taps_ref, which, head):
    return [taps_ref[which, j, pl.ds(head, 1), :] for j in range(taps_ref.shape[1])]


def unit(rows):
    return rows * lax.rsqrt(jnp.sum(rows * rows, axis=-1, keepdims=True) + EPSILON)


def same_document(second_resets, row, col):
    return ((row // BLOCK) - (col // BLOCK)) * second_resets == 0


def lower_inverse(lowers, row, col):
    differ = row ^ col
    eye = (row == col).astype(F32)
    in_block = (differ < 8).astype(F32)
    diagonal = [low * in_block for low in lowers]
    powers = [d.astype(BF16) for d in diagonal]
    squares = [mul(p, p).astype(BF16) for p in powers]
    inverse = [eye - d for d in diagonal]
    stacked = [
        mul(jnp.concatenate([s, x.astype(BF16)], axis=0), s) for x, s in zip(inverse, squares)
    ]
    fourths = [both[:CHUNK].astype(BF16) for both in stacked]
    inverse = [x + both[CHUNK:] for x, both in zip(inverse, stacked)]
    inverse = [x + mul(x.astype(BF16), s) for x, s in zip(inverse, fourths)]
    size = 8
    while size < CHUNK:
        joint = odd_blocks(((differ >= size) & (differ < 2 * size)).astype(F32), size)
        rounded = [x.astype(BF16) for x in inverse]
        inner = [
            mul((odd_blocks(low, size) * joint).astype(BF16), x)
            for low, x in zip(lowers, rounded)
        ]
        outer = [
            mul(odd_blocks(x, size).astype(BF16), with_even_zeros(i, size).astype(BF16))
            for x, i in zip(inverse, inner)
        ]
        inverse = [less_in_odd(x, o, size) for x, o in zip(inverse, outer)]
        size *= 2
    return inverse


def odd_blocks(a, size):
    return jnp.concatenate([a[b : b + size] for b in range(size, a.shape[0], 2 * size)], axis=0)


def with_even_zeros(odd, size):
    zeros = jnp.zeros((size, odd.shape[1]), odd.dtype)
    pieces = []
    for b in range(0, odd.shape[0], size):
        pieces += [zeros, odd[b : b + size]]
    return jnp.concatenate(pieces, axis=0)


def less_in_odd(a, odd, size):
    pieces = []
    for b in range(0, odd.shape[0], size):
        pieces.append(a[2 * b : 2 * b + size])
        pieces.append(a[2 * b + size : 2 * b + 2 * size] - odd[b : b + size])
    return jnp.concatenate(pieces, axis=0)


def rims_kernel(*refs):
    *inputs, packed_ref, arrived = refs
    copies = []
    for i, x_ref in enumerate(inputs):
        last = x_ref.at[pl.ds(x_ref.shape[0] - RIM, RIM)]
        here = packed_ref.at[pl.ds(i * RIM, RIM)]
        copies.append(pltpu.make_async_copy(last, here, arrived.at[i]))
    for copy in copies:
        copy.start()
    for copy in copies:
        copy.wait()


def filters_kernel(key_ref, value_ref, taps_ref, unit_ref, value_out_ref, first_ref, padded):
    heads, length, _ = key_ref.shape
    for i, x_ref in enumerate((key_ref, value_ref)):
        padded[i, :, RIM:] = x_ref[...].astype(F32)
        padded[i, :, 0:RIM] = jnp.zeros((heads, RIM, padded.shape[3]), F32)
    first_ref[...] = padded[:, :, RIM : RIM + AGAIN]

    def one_head(h, carry):
        for i in range(2):
            taps = taps_of(taps_ref, 1 + i, h)
            for c in range(length // CHUNK):
                rows = filtered(padded.at[i, h], taps, c * CHUNK, CHUNK)
                if i == 0:
                    unit_ref[h, rows_of(c)] = unit(rows).astype(BF16)
                else:
                    value_out_ref[h, rows_of(c)] = rows.astype(BF16)
        return carry

    lax.fori_loop(0, heads, one_head, 0)


def maps_kernel(
    base, resets, unit_in_ref, value_in_ref, first_ref, rim_ref, taps_ref, decay_ref, strength_ref,
    unit_ref, solved_ref, starts_ref, *refs,
):
    *map_refs, rims, padded, value_s, step_s = refs
    heads, length, depth = unit_ref.shape
    chunks = length // CHUNK
    size = heads // len(map_refs)
    total_heads = decay_ref.shape[0]
    row, col = indices()
    rims[...] = rim_ref[...].astype(F32)
    for g in range(heads):
        h = base + g
        unit_ref[g] = unit_in_ref[h]
        value_s[g] = value_in_ref[h]
        for i in range(2):
            padded[g, i, 0:RIM] = rims[(1 + i) * RIM : (2 + i) * RIM, h, :]
            padded[g, i, RIM : RIM + AGAIN] = first_ref[i, h]
            rows = filtered(padded.at[g, i], taps_of(taps_ref, 1 + i, h), 0, AGAIN)
            if i == 0:
                unit_ref[g, 0:AGAIN] = unit(rows).astype(BF16)
            else:
                value_s[g, 0:AGAIN] = rows.astype(BF16)

    parts = []
    lowers = []
    for c in range(chunks):
        cum, _, columns = token_scalars(decay_ref, strength_ref, c)
        first, second = resets[2 * c], resets[2 * c + 1]
        strictly = (row > col) & same_document(second, row, col)
        for g in range(heads):
            h = base + g
            cum_col = columns[:, h : h + 1]
            cum_row = cum[h : h + 1]
            key = unit_ref[g, rows_of(c)]
            fading = jnp.exp(jnp.where(strictly, cum_col - cum_row, FAR))
            strength_col = columns[:, total_heads + h : total_heads + h + 1]
            lowers.append(strength_col * fading * mul(key, key, NT))
            parts.append((g, c, first, second, cum_col, cum_row, strength_col))
    inverses = lower_inverse(lowers, row, col)
    eye = (row == col).astype(F32)
    first_rows = lax.broadcasted_iota(jnp.int32, (CHUNK, 1), 0) < BLOCK
    for (g, c, first, second, cum_col, cum_row, strength_col), inverse in zip(parts, inverses):
        keep_first = (1 - first).astype(F32)
        keep_second = (1 - second).astype(F32)
        keep_both = keep_first * keep_second
        key = unit_ref[g, rows_of(c)]
        growth = jnp.exp(cum_col) * jnp.where(first_rows, keep_first, keep_both)
        targets = jnp.concatenate(
            [
                (strength_col * growth) * key.astype(F32),
                strength_col * value_s[g, rows_of(c)].astype(F32),
            ],
            axis=1,
        )
        solved = targets + mul((inverse - eye).astype(BF16), targets.astype(BF16))
        solved_ref[g, rows_of(c)] = solved
        end = cum_row[:, CHUNK - 1 : CHUNK]
        tail = jnp.exp(end - cum_col) * jnp.where(first_rows, keep_second, 1.0)
        product = mul(key, (tail * solved).astype(BF16), TN)
        passed = jnp.exp(end) * keep_both
        step_s[g, c, :, :depth] = jnp.where(row == col, passed, 0.0) - product[:, :depth]
        step_s[g, c, :, depth:] = product[:, depth:]

    def compose(later, earlier):
        high, low = split(earlier)
        trans = later[:, :depth].astype(BF16)
        joined = mul(trans, high) + mul(trans, low)
        return jnp.concatenate([joined[:, :depth], joined[:, depth:] + later[:, depth:]], axis=1)

    every = range(heads)
    states = [step_s[g, 0] for g in every]
    half = chunks // 2
    for c in range(1, half):
        for g in every:
            starts_ref[g, c - 1] = states[g]
        states = [compose(step_s[g, c], states[g]) for g in every]
    rest = [step_s[g, half] for g in every]
    for c in range(half + 1, chunks):
        rest = [compose(step_s[g, c], rest[g]) for g in every]
    for g in every:
        map_refs[g // size][g % size] = compose(rest[g], states[g]).astype(BF16)
    for c in range(half, chunks):
        for g in every:
            starts_ref[g, c - 1] = states[g]
        if c + 1 < chunks:
            states = [compose(step_s[g, c], states[g]) for g in every]


def reads_kernel(
    base, resets, query_ref, gate_ref, gain_ref, rim_ref, taps_ref, decay_ref, strength_ref,
    unit_ref, solved_ref, starts_ref,
    reach_ref, part_ref, gating_ref,
    rims, padded, query_s,
):
    heads, length, depth = unit_ref.shape
    chunks = length // CHUNK
    row, col = indices()
    first_rows = lax.broadcasted_iota(jnp.int32, (CHUNK, 1), 0) < BLOCK
    rims[...] = rim_ref[...].astype(F32)
    for g in range(heads):
        h = base + g
        padded[g, 0:RIM] = rims[0:RIM, h, :]
        padded[g, RIM : RIM + length] = query_ref[h].astype(F32)
        taps = taps_of(taps_ref, 0, h)
        for c in range(chunks):
            rows = filtered(padded.at[g], taps, c * CHUNK, CHUNK)
            query_s[g, rows_of(c)] = (unit(rows) * depth**-0.5).astype(BF16)

    for c in range(chunks):
        here = rows_of(c)
        cum, _, columns = token_scalars(decay_ref, strength_ref, c)
        first, second = resets[2 * c], resets[2 * c + 1]
        keep_first = (1 - first).astype(F32)
        keep_both = keep_first * (1 - second).astype(F32)
        upto = (row >= col) & same_document(second, row, col)
        for g in range(heads):
            h = base + g
            cum_col = columns[:, h : h + 1]
            query = query_s[g, here]
            fading = jnp.exp(jnp.where(upto, cum_col - cum[h : h + 1], FAR))
            mixing = fading * mul(query, unit_ref[g, here], NT)
            own = mul_split(mixing, solved_ref[g, here])
            growth = jnp.exp(cum_col) * jnp.where(first_rows, keep_first, keep_both)
            reach = growth * query.astype(F32) - own[:, :depth]
            part = own[:, depth:]
            if c:
                both = mul_split(reach, starts_ref[g, c - 1])
                reach = both[:, :depth]
                part = part + both[:, depth:]
            reach_ref[g, here] = reach.astype(BF16)
            part_ref[g, here] = part
            gate = gate_ref[h, here].astype(F32)
            gating_ref[g, here] = gain_ref[...] * silu(gate)


def partner(place, k, count):
    if count & (count - 1) == 0:
        return place ^ k
    return lax.rem(place + count - k, count)


def pairs_at(k, count):
    if count & (count - 1) == 0:
        return [(i, i ^ k) for i in range(count)]
    return [(i, (i + k) % count) for i in range(count)]


def join_kernel(count, place, *refs):
    maps = refs[:count]
    before_ref, state_ref, *trans_ref, ordered = refs[count:]
    heads, depth, _ = before_ref.shape
    me = place[0]
    for k in range(count):
        ordered[partner(me, k, count)] = maps[k][...]
    row, col = indices()
    eye = (row == col).astype(F32)
    states = [jnp.concatenate([eye, jnp.zeros((depth, depth), F32)], axis=1)] * heads
    for lap in range(count):

        @pl.when(lap == me)
        def _():
            for h in range(heads):
                before_ref[h] = states[h]

        for h in range(heads):
            step = ordered[lap, h]
            if lap:
                high, low = split(states[h])
                trans = step[:, :depth]
                joined = mul(trans, high) + mul(trans, low)
                states[h] = jnp.concatenate(
                    [joined[:, :depth], joined[:, depth:] + step[:, depth:].astype(F32)], axis=1
                )
            else:
                states[h] = step.astype(F32)
    for h in range(heads):
        state_ref[h] = states[h][:, depth:].astype(state_ref.dtype)
        for ref in trans_ref:
            ref[h] = states[h][:, :depth]


def placed_kernel(base, before_ref, reach_ref, part_ref, through_ref, fixed_ref):
    heads, depth, _ = before_ref.shape
    for g in range(heads):
        high, low = split(before_ref[g])
        for c in range(through_ref.shape[1] // CHUNK):
            here = rows_of(c)
            reach = reach_ref[base + g, here]
            both = mul(reach, high) + mul(reach, low)
            through_ref[g, here] = both[:, :depth].astype(BF16)
            fixed_ref[g, here] = part_ref[base + g, here] + both[:, depth:]


def outputs_kernel(base, arrived_ref, through_ref, fixed_ref, gating_ref, normed_ref):
    heads, depth, _ = arrived_ref.shape
    for g in range(heads):
        arrived = arrived_ref[g]
        for c in range(normed_ref.shape[0] // CHUNK):
            here = rows_of(c)
            core = fixed_ref[g, here] + mul(through_ref[g, here], arrived)
            scale = lax.rsqrt(jnp.sum(core * core, axis=-1, keepdims=True) / depth + EPSILON)
            normed_ref[here, g * depth : (g + 1) * depth] = (
                core * scale * gating_ref[base + g, here]
            ).astype(BF16)


def last_kernel(section, first_ref, second_ref, block_ref, weights_ref, out_ref, tiles, written):
    width = block_ref.shape[1]
    rows = weights_ref[pl.ds(pl.multiple_of(section[0] * width, width), width), :]
    copies = []
    for i in range(first_ref.shape[0] // CHUNK):
        here = rows_of(i)
        total = (first_ref[here] + second_ref[here]) + mul(block_ref[here], rows)
        tiles[here] = total.astype(BF16)
        copies.append(pltpu.make_async_copy(tiles.at[here], out_ref.at[here], written.at[i]))
        copies[-1].start()
    for copy in copies:
        copy.wait()


def from_behind(value, axis, steps):
    count = lax.axis_size(axis)
    return lax.ppermute(value, axis, [(i, i + steps) for i in range(count - steps)])


def exchange(own_map, later, leaves):
    received = [
        lax.ppermute(later if k == 1 else own_map, "leaf", pairs_at(k, leaves))
        for k in range(1, leaves)
    ]
    return [own_map] + received


VMEM = pl.BlockSpec(memory_space=pltpu.VMEM)
SMEM = pl.BlockSpec(memory_space=pltpu.SMEM)
HBM = pl.BlockSpec(memory_space=pltpu.HBM)
PARAMS = pltpu.CompilerParams(vmem_limit_bytes=8 * 1024 * 1024)
LAST_PARAMS = pltpu.CompilerParams(vmem_limit_bytes=12 * 1024 * 1024)


def pack_rims(inputs):
    _, heads, depth = inputs[0].shape
    return pl.pallas_call(
        rims_kernel,
        out_shape=jax.ShapeDtypeStruct((len(inputs) * RIM, heads, depth), BF16),
        in_specs=[HBM] * len(inputs),
        out_specs=VMEM,
        scratch_shapes=[pltpu.SemaphoreType.DMA((len(inputs),))],
        compiler_params=pltpu.CompilerParams(vmem_limit_bytes=63 * 2**20),
        cost_estimate=pl.CostEstimate(flops=10**9, bytes_accessed=2**16, transcendentals=0),
    )(*inputs)


def filters_of(key, value, taps):
    heads, length, depth = key.shape
    per_token = jax.ShapeDtypeStruct((heads, length, depth), BF16)
    return pl.pallas_call(
        filters_kernel,
        out_shape=(per_token, per_token, jax.ShapeDtypeStruct((2, heads, AGAIN, depth), F32)),
        in_specs=[VMEM] * 3,
        out_specs=[VMEM] * 3,
        scratch_shapes=[pltpu.VMEM((2, heads, length + RIM, depth), F32)],
        compiler_params=PARAMS,
        cost_estimate=pl.CostEstimate(
            flops=3 * 10**9, bytes_accessed=4 * 2**20, transcendentals=10**6
        ),
    )(key, value, taps)


def maps_of(base, heads, resets, unit_in, value_in, first, rims, taps, decay, strength):
    _, length, depth = unit_in.shape
    chunks = length // CHUNK
    return pl.pallas_call(
        functools.partial(maps_kernel, base),
        out_shape=(
            jax.ShapeDtypeStruct((heads, length, depth), BF16),
            jax.ShapeDtypeStruct((heads, length, 2 * depth), F32),
            jax.ShapeDtypeStruct((heads, chunks - 1, depth, 2 * depth), F32),
            *[jax.ShapeDtypeStruct((heads // GROUPS, depth, 2 * depth), BF16)] * GROUPS,
        ),
        in_specs=[SMEM] + [VMEM] * 7,
        out_specs=[VMEM] * (3 + GROUPS),
        scratch_shapes=[
            pltpu.VMEM(rims.shape, F32),
            pltpu.VMEM((heads, 2, RIM + AGAIN, depth), F32),
            pltpu.VMEM((heads, length, depth), BF16),
            pltpu.VMEM((heads, chunks, depth, 2 * depth), F32),
        ],
        compiler_params=PARAMS,
        cost_estimate=pl.CostEstimate(
            flops=5 * 10**9, bytes_accessed=4 * 2**20, transcendentals=10**6
        ),
    )(resets, unit_in, value_in, first, rims, taps, decay, strength)


def reads_of(base, heads, resets, query, gate, gain, rims, taps, decay, strength, made):
    _, length, depth = query.shape
    per_token = jax.ShapeDtypeStruct((heads, length, depth), F32)
    return pl.pallas_call(
        functools.partial(reads_kernel, base),
        out_shape=(jax.ShapeDtypeStruct(per_token.shape, BF16), per_token, per_token),
        in_specs=[SMEM] + [VMEM] * 10,
        out_specs=[VMEM] * 3,
        scratch_shapes=[
            pltpu.VMEM(rims.shape, F32),
            pltpu.VMEM((heads, length + RIM, depth), F32),
            pltpu.VMEM((heads, length, depth), BF16),
        ],
        compiler_params=PARAMS,
        cost_estimate=pl.CostEstimate(
            flops=3 * 10**9, bytes_accessed=4 * 2**20, transcendentals=10**6
        ),
    )(resets, query, gate, gain, rims, taps, decay, strength, *made)


def join(place, maps, links):
    count = len(maps)
    heads, depth, _ = maps[0].shape
    pair = jax.ShapeDtypeStruct((heads, depth, 2 * depth), F32)
    square = (heads, depth, depth)
    if links == 1:
        totals = (jax.ShapeDtypeStruct(square, BF16),)
    else:
        totals = (jax.ShapeDtypeStruct(square, F32),) * 2
    return pl.pallas_call(
        functools.partial(join_kernel, count),
        out_shape=(pair, *totals),
        in_specs=[SMEM] + [VMEM] * count,
        out_specs=[VMEM] * (1 + len(totals)),
        scratch_shapes=[pltpu.VMEM((count, heads, depth, 2 * depth), BF16)],
        compiler_params=PARAMS,
    )(place, *maps)


def placed_of(base, before, reach, part):
    heads, depth, _ = before.shape
    length = reach.shape[1]
    per_token = (heads, length, depth)
    return pl.pallas_call(
        functools.partial(placed_kernel, base),
        out_shape=(
            jax.ShapeDtypeStruct(per_token, BF16),
            jax.ShapeDtypeStruct(per_token, F32),
        ),
        in_specs=[VMEM] * 3,
        out_specs=[VMEM] * 2,
        compiler_params=PARAMS,
        cost_estimate=pl.CostEstimate(flops=2 * 10**9, bytes_accessed=2**20, transcendentals=0),
    )(before, reach, part)


def outputs_of(base, arrived, placed, gating):
    heads, depth, _ = arrived.shape
    length = gating.shape[1]
    return pl.pallas_call(
        functools.partial(outputs_kernel, base),
        out_shape=jax.ShapeDtypeStruct((length, heads * depth), BF16),
        in_specs=[VMEM] * 4,
        out_specs=VMEM,
        compiler_params=PARAMS,
    )(arrived, *placed, gating)


def last_projected(section, first, second, block, weights):
    length, columns = first.shape
    return pl.pallas_call(
        last_kernel,
        out_shape=jax.ShapeDtypeStruct((length, columns), BF16),
        in_specs=[SMEM] + [VMEM] * 4,
        out_specs=pl.BlockSpec(memory_space=pl.ANY),
        scratch_shapes=[
            pltpu.VMEM((length, columns), BF16),
            pltpu.SemaphoreType.DMA((length // CHUNK,)),
        ],
        compiler_params=LAST_PARAMS,
    )(section.astype(jnp.int32).reshape(1), first, second, block, weights)


def after(first, *values):
    return lax.optimization_barrier((first, *values))[1:]


def on_device(
    query_in,
    key_in,
    value_in,
    gate_in,
    write_strength,
    log_decay,
    doc_resets,
    conv_weight,
    output_norm_gain,
    output_projection_weight,
):
    length, heads, depth = query_in.shape
    taps = conv_weight
    rims = from_behind(pack_rims((query_in, key_in, value_in)), ("chain", "leaf"), 1)
    key, value = (jnp.transpose(x, (1, 0, 2)) for x in (key_in, value_in))
    key, value, first = filters_of(key, value, taps)
    gain = output_norm_gain.reshape(1, depth)
    leaves = lax.axis_size("leaf")
    place = lax.axis_index("leaf").astype(jnp.int32).reshape(1)

    links = lax.axis_size("chain") - 1
    unit_key, solved, starts, *own_maps = maps_of(
        0, heads, doc_resets, key, value, first, rims, taps, log_decay, write_strength
    )
    query_in, gate_in = after(own_maps[-1], query_in, gate_in)
    query, gate = (jnp.transpose(x, (1, 0, 2)) for x in (query_in, gate_in))
    reads = reads_of(
        0, heads, doc_resets, query, gate, gain, rims, taps, log_decay, write_strength,
        (unit_key, solved, starts),
    )
    size = heads // GROUPS
    blocks = []
    exchanged = [exchange(own_maps[0], own_maps[0], leaves)]
    for g in range(GROUPS):
        earlier = blocks[-1] if blocks else reads[0]
        maps = after(earlier, *exchanged[g])
        before, state, *trans = join(place, maps, links)
        if g + 1 < GROUPS:
            own_map = own_maps[g + 1]
            exchanged.append(exchange(*after(earlier, own_map), *after(state, own_map), leaves))
        arrived = from_behind(state.astype(BF16), "chain", 1)
        for _ in range(links - 1):
            passed = jnp.einsum(
                "hij,hjk->hik", trans[0], arrived.astype(F32), precision=lax.Precision.HIGHEST
            )
            arrived = from_behind((passed + state).astype(BF16), "chain", 1)
        reach, part, gating = reads
        placed = placed_of(g * size, before, reach, part)
        blocks.append(outputs_of(g * size, arrived, placed, gating))

    ring = lax.axis_size("head")
    mine = lax.axis_index("head")
    width = size * depth
    weights = output_projection_weight
    around = [(i, (i + 1) % ring) for i in range(ring)]
    sums = [None] * GROUPS
    for k in range(ring):
        owner = lax.rem(mine + ring - k, ring)
        last = k + 1 == ring
        following = blocks if last else [lax.ppermute(x, "head", around) for x in blocks]
        if k == 0:
            blocks[:-1] = after(following[0], *blocks[:-1])
        for g, block in enumerate(blocks):
            section = owner * GROUPS + g
            if last and g + 1 == GROUPS:
                return last_projected(section, *sums, block, weights)
            rows = lax.dynamic_slice_in_dim(weights, section * width, width, 0)
            term = jnp.dot(block, rows, preferred_element_type=F32)
            sums[g] = term if sums[g] is None else sums[g] + term
        blocks = following


def solution(mesh):
    return jax.shard_map(
        on_device,
        mesh=mesh,
        in_specs=(
            P(("chain", "leaf"), "head", None),
            P(("chain", "leaf"), "head", None),
            P(("chain", "leaf"), "head", None),
            P(("chain", "leaf"), "head", None),
            P("head", ("chain", "leaf")),
            P("head", ("chain", "leaf")),
            P(("chain", "leaf")),
            P(None, None, "head", None),
            P(),
            P(None, "head"),
        ),
        out_specs=P(("chain", "leaf"), "head"),
        check_vma=False,
    )
```

```python
import functools

import jax
import jax.numpy as jnp
from jax import lax
from jax.experimental import pallas as pl
from jax.experimental.pallas import tpu as pltpu
from jax.sharding import PartitionSpec as P

BLOCK = 64
CHUNK = 128
GROUPS = 2
RIM = 8
EPSILON = 1e-06
FAR = -1e30
LARGE = 1e38
AGAIN = 16
F32 = jnp.float32
BF16 = jnp.bfloat16
NN = (((1,), (0,)), ((), ()))
NT = (((1,), (1,)), ((), ()))
TN = (((0,), (0,)), ((), ()))


def split(a):
    high = a.astype(BF16)
    return high, (a - high.astype(F32)).astype(BF16)


def mul(a, b, dims=NN):
    return lax.dot_general(a, b, dims, preferred_element_type=F32)


def mul_split(a, b):
    a_high, a_low = split(a)
    b_high, b_low = split(b)
    return mul(a_high, b_high) + (mul(a_low, b_high) + mul(a_high, b_low))


def rows_of(c):
    return slice(c * CHUNK, (c + 1) * CHUNK)


def indices():
    shape = (CHUNK, CHUNK)
    return (
        lax.broadcasted_iota(jnp.int32, shape, 0),
        lax.broadcasted_iota(jnp.int32, shape, 1),
    )


def token_scalars(decay_ref, strength_ref, c):
    row, col = indices()
    cum = lax.dot_general(
        decay_ref[:, rows_of(c)],
        (row <= col).astype(F32),
        NN,
        precision=lax.Precision.HIGHEST,
        preferred_element_type=F32,
    )
    strength = strength_ref[:, rows_of(c)]
    stacked = [cum, strength]
    missing = 8 - 2 * cum.shape[0]
    if missing > 0:
        stacked.append(jnp.zeros((missing, CHUNK), F32))
    return cum, strength, jnp.transpose(jnp.concatenate(stacked, axis=0))


def silu(x):
    below = jnp.minimum(1.0 + jnp.exp(-x), LARGE)
    inverse = pl.reciprocal(below, approx=True)
    return x * (inverse * (2.0 - below * inverse))


def filtered(padded, taps, begin, length):
    first = begin + RIM + 1 - len(taps)
    total = taps[0] * padded[first : first + length]
    for j in range(1, len(taps)):
        total = total + taps[j] * padded[first + j : first + j + length]
    return silu(total)


def taps_of(taps_ref, which, head):
    return [taps_ref[which, j, pl.ds(head, 1), :] for j in range(taps_ref.shape[1])]


def unit(rows):
    return rows * lax.rsqrt(jnp.sum(rows * rows, axis=-1, keepdims=True) + EPSILON)


def same_document(second_resets, row, col):
    return ((row // BLOCK) - (col // BLOCK)) * second_resets == 0


def lower_inverse(lowers, row, col):
    differ = row ^ col
    eye = (row == col).astype(F32)
    in_block = (differ < 8).astype(F32)
    diagonal = [low * in_block for low in lowers]
    powers = [d.astype(BF16) for d in diagonal]
    squares = [mul(p, p).astype(BF16) for p in powers]
    inverse = [eye - d for d in diagonal]
    stacked = [
        mul(jnp.concatenate([s, x.astype(BF16)], axis=0), s) for x, s in zip(inverse, squares)
    ]
    fourths = [both[:CHUNK].astype(BF16) for both in stacked]
    inverse = [x + both[CHUNK:] for x, both in zip(inverse, stacked)]
    inverse = [x + mul(x.astype(BF16), s) for x, s in zip(inverse, fourths)]
    size = 8
    while size < CHUNK:
        joint = odd_blocks(((differ >= size) & (differ < 2 * size)).astype(F32), size)
        rounded = [x.astype(BF16) for x in inverse]
        inner = [
            mul((odd_blocks(low, size) * joint).astype(BF16), x)
            for low, x in zip(lowers, rounded)
        ]
        outer = [
            mul(odd_blocks(x, size).astype(BF16), with_even_zeros(i, size).astype(BF16))
            for x, i in zip(inverse, inner)
        ]
        inverse = [less_in_odd(x, o, size) for x, o in zip(inverse, outer)]
        size *= 2
    return inverse


def odd_blocks(a, size):
    return jnp.concatenate([a[b : b + size] for b in range(size, a.shape[0], 2 * size)], axis=0)


def with_even_zeros(odd, size):
    zeros = jnp.zeros((size, odd.shape[1]), odd.dtype)
    pieces = []
    for b in range(0, odd.shape[0], size):
        pieces += [zeros, odd[b : b + size]]
    return jnp.concatenate(pieces, axis=0)


def less_in_odd(a, odd, size):
    pieces = []
    for b in range(0, odd.shape[0], size):
        pieces.append(a[2 * b : 2 * b + size])
        pieces.append(a[2 * b + size : 2 * b + 2 * size] - odd[b : b + size])
    return jnp.concatenate(pieces, axis=0)


def rims_kernel(*refs):
    *inputs, packed_ref, arrived = refs
    copies = []
    for i, x_ref in enumerate(inputs):
        last = x_ref.at[pl.ds(x_ref.shape[0] - RIM, RIM)]
        here = packed_ref.at[pl.ds(i * RIM, RIM)]
        copies.append(pltpu.make_async_copy(last, here, arrived.at[i]))
    for copy in copies:
        copy.start()
    for copy in copies:
        copy.wait()


def filters_kernel(key_ref, value_ref, taps_ref, filtered_ref, first_ref, padded):
    heads, length, _ = key_ref.shape
    for i, x_ref in enumerate((key_ref, value_ref)):
        padded[i, :, RIM:] = x_ref[...].astype(F32)
        padded[i, :, 0:RIM] = jnp.zeros((heads, RIM, padded.shape[3]), F32)
    first_ref[...] = padded[:, :, RIM : RIM + AGAIN]

    def one_head(h, carry):
        for i in range(2):
            taps = taps_of(taps_ref, 1 + i, h)
            for c in range(length // CHUNK):
                rows = filtered(padded.at[i, h], taps, c * CHUNK, CHUNK)
                rows = unit(rows) if i == 0 else rows
                filtered_ref[i, h, rows_of(c)] = rows.astype(BF16)
        return carry

    lax.fori_loop(0, heads, one_head, 0)


def maps_kernel(
    base, resets, filtered_ref, first_ref, rim_ref, taps_ref, decay_ref, strength_ref,
    unit_ref, solved_ref, starts_ref, *refs,
):
    *map_refs, rims, padded, value_s, step_s = refs
    heads, length, depth = unit_ref.shape
    chunks = length // CHUNK
    size = heads // len(map_refs)
    total_heads = decay_ref.shape[0]
    row, col = indices()
    rims[...] = rim_ref[...].astype(F32)
    for g in range(heads):
        h = base + g
        unit_ref[g] = filtered_ref[0, h]
        value_s[g] = filtered_ref[1, h]
        for i in range(2):
            padded[g, i, 0:RIM] = rims[(1 + i) * RIM : (2 + i) * RIM, h, :]
            padded[g, i, RIM : RIM + AGAIN] = first_ref[i, h]
            rows = filtered(padded.at[g, i], taps_of(taps_ref, 1 + i, h), 0, AGAIN)
            if i == 0:
                unit_ref[g, 0:AGAIN] = unit(rows).astype(BF16)
            else:
                value_s[g, 0:AGAIN] = rows.astype(BF16)

    parts = []
    lowers = []
    for c in range(chunks):
        cum, _, columns = token_scalars(decay_ref, strength_ref, c)
        first, second = resets[2 * c], resets[2 * c + 1]
        strictly = (row > col) & same_document(second, row, col)
        for g in range(heads):
            h = base + g
            cum_col = columns[:, h : h + 1]
            cum_row = cum[h : h + 1]
            key = unit_ref[g, rows_of(c)]
            fading = jnp.exp(jnp.where(strictly, cum_col - cum_row, FAR))
            strength_col = columns[:, total_heads + h : total_heads + h + 1]
            lowers.append(strength_col * fading * mul(key, key, NT))
            parts.append((g, c, first, second, cum_col, cum_row, strength_col))
    inverses = lower_inverse(lowers, row, col)
    eye = (row == col).astype(F32)
    first_rows = lax.broadcasted_iota(jnp.int32, (CHUNK, 1), 0) < BLOCK
    for (g, c, first, second, cum_col, cum_row, strength_col), inverse in zip(parts, inverses):
        keep_first = (1 - first).astype(F32)
        keep_second = (1 - second).astype(F32)
        keep_both = keep_first * keep_second
        key = unit_ref[g, rows_of(c)]
        growth = jnp.exp(cum_col) * jnp.where(first_rows, keep_first, keep_both)
        targets = jnp.concatenate(
            [
                (strength_col * growth) * key.astype(F32),
                strength_col * value_s[g, rows_of(c)].astype(F32),
            ],
            axis=1,
        )
        solved = targets + mul((inverse - eye).astype(BF16), targets.astype(BF16))
        solved_ref[g, rows_of(c)] = solved
        end = cum_row[:, CHUNK - 1 : CHUNK]
        tail = jnp.exp(end - cum_col) * jnp.where(first_rows, keep_second, 1.0)
        product = mul(key, (tail * solved).astype(BF16), TN)
        passed = jnp.exp(end) * keep_both
        step_s[g, c, :, :depth] = jnp.where(row == col, passed, 0.0) - product[:, :depth]
        step_s[g, c, :, depth:] = product[:, depth:]

    def compose(later, earlier):
        high, low = split(earlier)
        trans = later[:, :depth].astype(BF16)
        joined = mul(trans, high) + mul(trans, low)
        return jnp.concatenate([joined[:, :depth], joined[:, depth:] + later[:, depth:]], axis=1)

    every = range(heads)
    states = [step_s[g, 0] for g in every]
    half = chunks // 2
    for c in range(1, half):
        for g in every:
            starts_ref[g, c - 1] = states[g]
        states = [compose(step_s[g, c], states[g]) for g in every]
    rest = [step_s[g, half] for g in every]
    for c in range(half + 1, chunks):
        rest = [compose(step_s[g, c], rest[g]) for g in every]
    for g in every:
        map_refs[g // size][g % size] = compose(rest[g], states[g]).astype(BF16)
    for c in range(half, chunks):
        for g in every:
            starts_ref[g, c - 1] = states[g]
        if c + 1 < chunks:
            states = [compose(step_s[g, c], states[g]) for g in every]


def reads_kernel(
    base, resets, query_ref, gate_ref, gain_ref, rim_ref, taps_ref, decay_ref, strength_ref,
    unit_ref, solved_ref, starts_ref,
    reach_ref, part_ref, gating_ref,
    rims, padded, query_s,
):
    heads, length, depth = unit_ref.shape
    chunks = length // CHUNK
    row, col = indices()
    first_rows = lax.broadcasted_iota(jnp.int32, (CHUNK, 1), 0) < BLOCK
    rims[...] = rim_ref[...].astype(F32)
    for g in range(heads):
        h = base + g
        padded[g, 0:RIM] = rims[0:RIM, h, :]
        padded[g, RIM : RIM + length] = query_ref[h].astype(F32)
        taps = taps_of(taps_ref, 0, h)
        for c in range(chunks):
            rows = filtered(padded.at[g], taps, c * CHUNK, CHUNK)
            query_s[g, rows_of(c)] = (unit(rows) * depth**-0.5).astype(BF16)

    for c in range(chunks):
        here = rows_of(c)
        cum, _, columns = token_scalars(decay_ref, strength_ref, c)
        first, second = resets[2 * c], resets[2 * c + 1]
        keep_first = (1 - first).astype(F32)
        keep_both = keep_first * (1 - second).astype(F32)
        upto = (row >= col) & same_document(second, row, col)
        for g in range(heads):
            h = base + g
            cum_col = columns[:, h : h + 1]
            query = query_s[g, here]
            fading = jnp.exp(jnp.where(upto, cum_col - cum[h : h + 1], FAR))
            mixing = fading * mul(query, unit_ref[g, here], NT)
            own = mul_split(mixing, solved_ref[g, here])
            growth = jnp.exp(cum_col) * jnp.where(first_rows, keep_first, keep_both)
            reach = growth * query.astype(F32) - own[:, :depth]
            part = own[:, depth:]
            if c:
                both = mul_split(reach, starts_ref[g, c - 1])
                reach = both[:, :depth]
                part = part + both[:, depth:]
            reach_ref[g, here] = reach.astype(BF16)
            part_ref[g, here] = part
            gate = gate_ref[h, here].astype(F32)
            gating_ref[g, here] = gain_ref[...] * silu(gate)


def partner(place, k, count):
    if count & (count - 1) == 0:
        return place ^ k
    return lax.rem(place + count - k, count)


def pairs_at(k, count):
    if count & (count - 1) == 0:
        return [(i, i ^ k) for i in range(count)]
    return [(i, (i + k) % count) for i in range(count)]


def join_kernel(count, place, *refs):
    maps = refs[:count]
    before_ref, state_ref, *trans_ref, ordered = refs[count:]
    heads, depth, _ = before_ref.shape
    me = place[0]
    for k in range(count):
        ordered[partner(me, k, count)] = maps[k][...]
    row, col = indices()
    eye = (row == col).astype(F32)
    states = [jnp.concatenate([eye, jnp.zeros((depth, depth), F32)], axis=1)] * heads
    for lap in range(count):

        @pl.when(lap == me)
        def _():
            for h in range(heads):
                before_ref[h] = states[h]

        for h in range(heads):
            step = ordered[lap, h]
            if lap:
                high, low = split(states[h])
                trans = step[:, :depth]
                joined = mul(trans, high) + mul(trans, low)
                states[h] = jnp.concatenate(
                    [joined[:, :depth], joined[:, depth:] + step[:, depth:].astype(F32)], axis=1
                )
            else:
                states[h] = step.astype(F32)
    for h in range(heads):
        state_ref[h] = states[h][:, depth:].astype(state_ref.dtype)
        for ref in trans_ref:
            ref[h] = states[h][:, :depth]


def placed_kernel(base, before_ref, reach_ref, part_ref, through_ref, fixed_ref):
    heads, depth, _ = before_ref.shape
    for g in range(heads):
        high, low = split(before_ref[g])
        for c in range(through_ref.shape[1] // CHUNK):
            here = rows_of(c)
            reach = reach_ref[base + g, here]
            both = mul(reach, high) + mul(reach, low)
            through_ref[g, here] = both[:, :depth].astype(BF16)
            fixed_ref[g, here] = part_ref[base + g, here] + both[:, depth:]


def outputs_kernel(base, arrived_ref, through_ref, fixed_ref, gating_ref, normed_ref):
    heads, depth, _ = arrived_ref.shape
    for g in range(heads):
        arrived = arrived_ref[g]
        for c in range(normed_ref.shape[0] // CHUNK):
            here = rows_of(c)
            core = fixed_ref[g, here] + mul(through_ref[g, here], arrived)
            scale = lax.rsqrt(jnp.sum(core * core, axis=-1, keepdims=True) / depth + EPSILON)
            normed_ref[here, g * depth : (g + 1) * depth] = (
                core * scale * gating_ref[base + g, here]
            ).astype(BF16)


def last_kernel(section, first_ref, second_ref, block_ref, weights_ref, out_ref, tiles, written):
    width = block_ref.shape[1]
    rows = weights_ref[pl.ds(pl.multiple_of(section[0] * width, width), width), :]
    copies = []
    for i in range(first_ref.shape[0] // CHUNK):
        here = rows_of(i)
        total = (first_ref[here] + second_ref[here]) + mul(block_ref[here], rows)
        tiles[here] = total.astype(BF16)
        copies.append(pltpu.make_async_copy(tiles.at[here], out_ref.at[here], written.at[i]))
        copies[-1].start()
    for copy in copies:
        copy.wait()


def from_behind(value, axis, steps):
    count = lax.axis_size(axis)
    return lax.ppermute(value, axis, [(i, i + steps) for i in range(count - steps)])


def exchange(own_map, later, leaves):
    received = [
        lax.ppermute(later if k == 1 else own_map, "leaf", pairs_at(k, leaves))
        for k in range(1, leaves)
    ]
    return [own_map] + received


VMEM = pl.BlockSpec(memory_space=pltpu.VMEM)
SMEM = pl.BlockSpec(memory_space=pltpu.SMEM)
HBM = pl.BlockSpec(memory_space=pltpu.HBM)
PARAMS = pltpu.CompilerParams(vmem_limit_bytes=6 * 1024 * 1024)
LAST_PARAMS = pltpu.CompilerParams(vmem_limit_bytes=12 * 1024 * 1024)


def pack_rims(inputs):
    _, heads, depth = inputs[0].shape
    return pl.pallas_call(
        rims_kernel,
        out_shape=jax.ShapeDtypeStruct((len(inputs) * RIM, heads, depth), BF16),
        in_specs=[HBM] * len(inputs),
        out_specs=VMEM,
        scratch_shapes=[pltpu.SemaphoreType.DMA((len(inputs),))],
        compiler_params=pltpu.CompilerParams(vmem_limit_bytes=63 * 2**20),
        cost_estimate=pl.CostEstimate(flops=10**9, bytes_accessed=2**16, transcendentals=0),
    )(*inputs)


def filters_of(key, value, taps):
    heads, length, depth = key.shape
    return pl.pallas_call(
        filters_kernel,
        out_shape=(
            jax.ShapeDtypeStruct((2, heads, length, depth), BF16),
            jax.ShapeDtypeStruct((2, heads, AGAIN, depth), F32),
        ),
        in_specs=[VMEM] * 3,
        out_specs=[VMEM] * 2,
        scratch_shapes=[pltpu.VMEM((2, heads, length + RIM, depth), F32)],
        compiler_params=PARAMS,
        cost_estimate=pl.CostEstimate(
            flops=3 * 10**9, bytes_accessed=4 * 2**20, transcendentals=10**6
        ),
    )(key, value, taps)


def maps_of(base, heads, resets, filtered, first, rims, taps, decay, strength):
    _, _, length, depth = filtered.shape
    chunks = length // CHUNK
    return pl.pallas_call(
        functools.partial(maps_kernel, base),
        out_shape=(
            jax.ShapeDtypeStruct((heads, length, depth), BF16),
            jax.ShapeDtypeStruct((heads, length, 2 * depth), F32),
            jax.ShapeDtypeStruct((heads, chunks - 1, depth, 2 * depth), F32),
            *[jax.ShapeDtypeStruct((heads // GROUPS, depth, 2 * depth), BF16)] * GROUPS,
        ),
        in_specs=[SMEM] + [VMEM] * 6,
        out_specs=[VMEM] * (3 + GROUPS),
        scratch_shapes=[
            pltpu.VMEM(rims.shape, F32),
            pltpu.VMEM((heads, 2, RIM + AGAIN, depth), F32),
            pltpu.VMEM((heads, length, depth), BF16),
            pltpu.VMEM((heads, chunks, depth, 2 * depth), F32),
        ],
        compiler_params=PARAMS,
        cost_estimate=pl.CostEstimate(
            flops=5 * 10**9, bytes_accessed=4 * 2**20, transcendentals=10**6
        ),
    )(resets, filtered, first, rims, taps, decay, strength)


def reads_of(base, heads, resets, query, gate, gain, rims, taps, decay, strength, made):
    _, length, depth = query.shape
    per_token = jax.ShapeDtypeStruct((heads, length, depth), F32)
    return pl.pallas_call(
        functools.partial(reads_kernel, base),
        out_shape=(jax.ShapeDtypeStruct(per_token.shape, BF16), per_token, per_token),
        in_specs=[SMEM] + [VMEM] * 10,
        out_specs=[VMEM] * 3,
        scratch_shapes=[
            pltpu.VMEM(rims.shape, F32),
            pltpu.VMEM((heads, length + RIM, depth), F32),
            pltpu.VMEM((heads, length, depth), BF16),
        ],
        compiler_params=PARAMS,
        cost_estimate=pl.CostEstimate(
            flops=3 * 10**9, bytes_accessed=4 * 2**20, transcendentals=10**6
        ),
    )(resets, query, gate, gain, rims, taps, decay, strength, *made)


def join(place, maps, links):
    count = len(maps)
    heads, depth, _ = maps[0].shape
    pair = jax.ShapeDtypeStruct((heads, depth, 2 * depth), F32)
    square = (heads, depth, depth)
    if links == 1:
        totals = (jax.ShapeDtypeStruct(square, BF16),)
    else:
        totals = (jax.ShapeDtypeStruct(square, F32),) * 2
    return pl.pallas_call(
        functools.partial(join_kernel, count),
        out_shape=(pair, *totals),
        in_specs=[SMEM] + [VMEM] * count,
        out_specs=[VMEM] * (1 + len(totals)),
        scratch_shapes=[pltpu.VMEM((count, heads, depth, 2 * depth), BF16)],
        compiler_params=PARAMS,
    )(place, *maps)


def placed_of(base, before, reach, part):
    heads, depth, _ = before.shape
    length = reach.shape[1]
    per_token = (heads, length, depth)
    return pl.pallas_call(
        functools.partial(placed_kernel, base),
        out_shape=(
            jax.ShapeDtypeStruct(per_token, BF16),
            jax.ShapeDtypeStruct(per_token, F32),
        ),
        in_specs=[VMEM] * 3,
        out_specs=[VMEM] * 2,
        compiler_params=PARAMS,
        cost_estimate=pl.CostEstimate(flops=2 * 10**9, bytes_accessed=2**20, transcendentals=0),
    )(before, reach, part)


def outputs_of(base, arrived, placed, gating):
    heads, depth, _ = arrived.shape
    length = gating.shape[1]
    return pl.pallas_call(
        functools.partial(outputs_kernel, base),
        out_shape=jax.ShapeDtypeStruct((length, heads * depth), BF16),
        in_specs=[VMEM] * 4,
        out_specs=VMEM,
        compiler_params=PARAMS,
    )(arrived, *placed, gating)


def last_projected(section, first, second, block, weights):
    length, columns = first.shape
    return pl.pallas_call(
        last_kernel,
        out_shape=jax.ShapeDtypeStruct((length, columns), BF16),
        in_specs=[SMEM] + [VMEM] * 4,
        out_specs=pl.BlockSpec(memory_space=pl.ANY),
        scratch_shapes=[
            pltpu.VMEM((length, columns), BF16),
            pltpu.SemaphoreType.DMA((length // CHUNK,)),
        ],
        compiler_params=LAST_PARAMS,
    )(section.astype(jnp.int32).reshape(1), first, second, block, weights)


def after(first, *values):
    return lax.optimization_barrier((first, *values))[1:]


def on_device(
    query_in,
    key_in,
    value_in,
    gate_in,
    write_strength,
    log_decay,
    doc_resets,
    conv_weight,
    output_norm_gain,
    output_projection_weight,
):
    length, heads, depth = query_in.shape
    taps = conv_weight
    rims = from_behind(pack_rims((query_in, key_in, value_in)), ("chain", "leaf"), 1)
    key, value = (jnp.transpose(x, (1, 0, 2)) for x in (key_in, value_in))
    filtered, first = filters_of(key, value, taps)
    gain = output_norm_gain.reshape(1, depth)
    leaves = lax.axis_size("leaf")
    place = lax.axis_index("leaf").astype(jnp.int32).reshape(1)

    links = lax.axis_size("chain") - 1
    unit_key, solved, starts, *own_maps = maps_of(
        0, heads, doc_resets, filtered, first, rims, taps, log_decay, write_strength
    )
    query_in, gate_in = after(own_maps[-1], query_in, gate_in)
    query, gate = (jnp.transpose(x, (1, 0, 2)) for x in (query_in, gate_in))
    reads = reads_of(
        0, heads, doc_resets, query, gate, gain, rims, taps, log_decay, write_strength,
        (unit_key, solved, starts),
    )
    size = heads // GROUPS
    blocks = []
    exchanged = [exchange(own_maps[0], own_maps[0], leaves)]
    for g in range(GROUPS):
        earlier = blocks[-1] if blocks else reads[0]
        maps = after(earlier, *exchanged[g])
        before, state, *trans = join(place, maps, links)
        if g + 1 < GROUPS:
            own_map = own_maps[g + 1]
            exchanged.append(exchange(*after(earlier, own_map), *after(state, own_map), leaves))
        arrived = from_behind(state.astype(BF16), "chain", 1)
        for _ in range(links - 1):
            passed = jnp.einsum(
                "hij,hjk->hik", trans[0], arrived.astype(F32), precision=lax.Precision.HIGHEST
            )
            arrived = from_behind((passed + state).astype(BF16), "chain", 1)
        reach, part, gating = reads
        placed = placed_of(g * size, before, reach, part)
        blocks.append(outputs_of(g * size, arrived, placed, gating))

    ring = lax.axis_size("head")
    mine = lax.axis_index("head")
    width = size * depth
    weights = output_projection_weight
    around = [(i, (i + 1) % ring) for i in range(ring)]
    sums = [None] * GROUPS
    for k in range(ring):
        owner = lax.rem(mine + ring - k, ring)
        last = k + 1 == ring
        following = blocks if last else [lax.ppermute(x, "head", around) for x in blocks]
        if k == 0:
            blocks[:-1] = after(following[-1], *blocks[:-1])
        for g, block in enumerate(blocks):
            section = owner * GROUPS + g
            if last and g + 1 == GROUPS:
                return last_projected(section, *sums, block, weights)
            rows = lax.dynamic_slice_in_dim(weights, section * width, width, 0)
            term = jnp.dot(block, rows, preferred_element_type=F32)
            sums[g] = term if sums[g] is None else sums[g] + term
        blocks = following


def solution(mesh):
    return jax.shard_map(
        on_device,
        mesh=mesh,
        in_specs=(
            P(("chain", "leaf"), "head", None),
            P(("chain", "leaf"), "head", None),
            P(("chain", "leaf"), "head", None),
            P(("chain", "leaf"), "head", None),
            P("head", ("chain", "leaf")),
            P("head", ("chain", "leaf")),
            P(("chain", "leaf")),
            P(None, None, "head", None),
            P(),
            P(None, "head"),
        ),
        out_specs=P(("chain", "leaf"), "head"),
        check_vma=False,
    )
```

```python
import functools

import jax
import jax.numpy as jnp
from jax import lax
from jax.experimental import pallas as pl
from jax.experimental.pallas import tpu as pltpu
from jax.sharding import PartitionSpec as P

BLOCK = 64
CHUNK = 128
GROUPS = 2
RIM = 8
EPSILON = 1e-06
FAR = -1e30
LARGE = 1e38
AGAIN = 16
F32 = jnp.float32
BF16 = jnp.bfloat16
NN = (((1,), (0,)), ((), ()))
NT = (((1,), (1,)), ((), ()))
TN = (((0,), (0,)), ((), ()))


def split(a):
    high = a.astype(BF16)
    return high, (a - high.astype(F32)).astype(BF16)


def mul(a, b, dims=NN):
    return lax.dot_general(a, b, dims, preferred_element_type=F32)


def mul_split(a, b):
    a_high, a_low = split(a)
    b_high, b_low = split(b)
    return mul(a_high, b_high) + (mul(a_low, b_high) + mul(a_high, b_low))


def rows_of(c):
    return slice(c * CHUNK, (c + 1) * CHUNK)


def indices():
    shape = (CHUNK, CHUNK)
    return (
        lax.broadcasted_iota(jnp.int32, shape, 0),
        lax.broadcasted_iota(jnp.int32, shape, 1),
    )


def token_scalars(decay_ref, strength_ref, c):
    row, col = indices()
    cum = lax.dot_general(
        decay_ref[:, rows_of(c)],
        (row <= col).astype(F32),
        NN,
        precision=lax.Precision.HIGHEST,
        preferred_element_type=F32,
    )
    strength = strength_ref[:, rows_of(c)]
    stacked = [cum, strength]
    missing = 8 - 2 * cum.shape[0]
    if missing > 0:
        stacked.append(jnp.zeros((missing, CHUNK), F32))
    return cum, strength, jnp.transpose(jnp.concatenate(stacked, axis=0))


def silu(x):
    below = jnp.minimum(1.0 + jnp.exp(-x), LARGE)
    inverse = pl.reciprocal(below, approx=True)
    return x * (inverse * (2.0 - below * inverse))


def filtered(padded, taps, begin, length):
    first = begin + RIM + 1 - len(taps)
    total = taps[0] * padded[first : first + length]
    for j in range(1, len(taps)):
        total = total + taps[j] * padded[first + j : first + j + length]
    return silu(total)


def taps_of(taps_ref, which, head):
    return [taps_ref[which, j, pl.ds(head, 1), :] for j in range(taps_ref.shape[1])]


def unit(rows):
    return rows * lax.rsqrt(jnp.sum(rows * rows, axis=-1, keepdims=True) + EPSILON)


def same_document(second_resets, row, col):
    return ((row // BLOCK) - (col // BLOCK)) * second_resets == 0


def lower_inverse(lowers, row, col):
    differ = row ^ col
    eye = (row == col).astype(F32)
    in_block = (differ < 8).astype(F32)
    diagonal = [low * in_block for low in lowers]
    powers = [d.astype(BF16) for d in diagonal]
    squares = [mul(p, p).astype(BF16) for p in powers]
    inverse = [eye - d for d in diagonal]
    stacked = [
        mul(jnp.concatenate([s, x.astype(BF16)], axis=0), s) for x, s in zip(inverse, squares)
    ]
    fourths = [both[:CHUNK].astype(BF16) for both in stacked]
    inverse = [x + both[CHUNK:] for x, both in zip(inverse, stacked)]
    inverse = [x + mul(x.astype(BF16), s) for x, s in zip(inverse, fourths)]
    size = 8
    while size < CHUNK:
        joint = odd_blocks(((differ >= size) & (differ < 2 * size)).astype(F32), size)
        rounded = [x.astype(BF16) for x in inverse]
        inner = [
            mul((odd_blocks(low, size) * joint).astype(BF16), x)
            for low, x in zip(lowers, rounded)
        ]
        outer = [
            mul(odd_blocks(x, size).astype(BF16), with_even_zeros(i, size).astype(BF16))
            for x, i in zip(inverse, inner)
        ]
        inverse = [less_in_odd(x, o, size) for x, o in zip(inverse, outer)]
        size *= 2
    return inverse


def odd_blocks(a, size):
    return jnp.concatenate([a[b : b + size] for b in range(size, a.shape[0], 2 * size)], axis=0)


def with_even_zeros(odd, size):
    zeros = jnp.zeros((size, odd.shape[1]), odd.dtype)
    pieces = []
    for b in range(0, odd.shape[0], size):
        pieces += [zeros, odd[b : b + size]]
    return jnp.concatenate(pieces, axis=0)


def less_in_odd(a, odd, size):
    pieces = []
    for b in range(0, odd.shape[0], size):
        pieces.append(a[2 * b : 2 * b + size])
        pieces.append(a[2 * b + size : 2 * b + 2 * size] - odd[b : b + size])
    return jnp.concatenate(pieces, axis=0)


def rims_kernel(*refs):
    *inputs, packed_ref, arrived = refs
    copies = []
    for i, x_ref in enumerate(inputs):
        last = x_ref.at[pl.ds(x_ref.shape[0] - RIM, RIM)]
        here = packed_ref.at[pl.ds(i * RIM, RIM)]
        copies.append(pltpu.make_async_copy(last, here, arrived.at[i]))
    for copy in copies:
        copy.start()
    for copy in copies:
        copy.wait()


def filters_kernel(key_ref, value_ref, taps_ref, unit_ref, value_out_ref, first_ref, padded):
    heads, length, _ = key_ref.shape
    for i, x_ref in enumerate((key_ref, value_ref)):
        padded[i, :, RIM:] = x_ref[...].astype(F32)
        padded[i, :, 0:RIM] = jnp.zeros((heads, RIM, padded.shape[3]), F32)
    first_ref[...] = padded[:, :, RIM : RIM + AGAIN]

    def one_head(h, carry):
        for i in range(2):
            taps = taps_of(taps_ref, 1 + i, h)
            for c in range(length // CHUNK):
                rows = filtered(padded.at[i, h], taps, c * CHUNK, CHUNK)
                if i == 0:
                    unit_ref[h, rows_of(c)] = unit(rows).astype(BF16)
                else:
                    value_out_ref[h, rows_of(c)] = rows.astype(BF16)
        return carry

    lax.fori_loop(0, heads, one_head, 0)


def maps_kernel(
    base, resets, unit_in_ref, value_in_ref, first_ref, rim_ref, taps_ref, decay_ref, strength_ref,
    unit_ref, solved_ref, starts_ref, *refs,
):
    *map_refs, rims, padded, value_s, step_s = refs
    heads, length, depth = unit_ref.shape
    chunks = length // CHUNK
    size = heads // len(map_refs)
    total_heads = decay_ref.shape[0]
    row, col = indices()
    rims[...] = rim_ref[...].astype(F32)
    for g in range(heads):
        h = base + g
        for c in range(1, chunks):
            unit_ref[g, rows_of(c)] = unit_in_ref[h, rows_of(c)]
        unit_ref[g, AGAIN:CHUNK] = unit_in_ref[h, AGAIN:CHUNK]
        value_s[g, AGAIN:CHUNK] = value_in_ref[h, AGAIN:CHUNK]
        for i in range(2):
            padded[g, i, 0:RIM] = rims[(1 + i) * RIM : (2 + i) * RIM, h, :]
            padded[g, i, RIM : RIM + AGAIN] = first_ref[i, h]
            rows = filtered(padded.at[g, i], taps_of(taps_ref, 1 + i, h), 0, AGAIN)
            if i == 0:
                unit_ref[g, 0:AGAIN] = unit(rows).astype(BF16)
            else:
                value_s[g, 0:AGAIN] = rows.astype(BF16)

    parts = []
    lowers = []
    for c in range(chunks):
        cum, _, columns = token_scalars(decay_ref, strength_ref, c)
        first, second = resets[2 * c], resets[2 * c + 1]
        strictly = (row > col) & same_document(second, row, col)
        for g in range(heads):
            h = base + g
            cum_col = columns[:, h : h + 1]
            cum_row = cum[h : h + 1]
            key = unit_in_ref[h, rows_of(c)] if c else unit_ref[g, rows_of(c)]
            fading = jnp.exp(jnp.where(strictly, cum_col - cum_row, FAR))
            strength_col = columns[:, total_heads + h : total_heads + h + 1]
            lowers.append(strength_col * fading * mul(key, key, NT))
            parts.append((g, c, first, second, cum_col, cum_row, strength_col))
    inverses = lower_inverse(lowers, row, col)
    eye = (row == col).astype(F32)
    first_rows = lax.broadcasted_iota(jnp.int32, (CHUNK, 1), 0) < BLOCK
    for (g, c, first, second, cum_col, cum_row, strength_col), inverse in zip(parts, inverses):
        keep_first = (1 - first).astype(F32)
        keep_second = (1 - second).astype(F32)
        keep_both = keep_first * keep_second
        h = base + g
        key = unit_in_ref[h, rows_of(c)] if c else unit_ref[g, rows_of(c)]
        value = value_in_ref[h, rows_of(c)] if c else value_s[g]
        growth = jnp.exp(cum_col) * jnp.where(first_rows, keep_first, keep_both)
        targets = jnp.concatenate(
            [
                (strength_col * growth) * key.astype(F32),
                strength_col * value.astype(F32),
            ],
            axis=1,
        )
        solved = targets + mul((inverse - eye).astype(BF16), targets.astype(BF16))
        solved_ref[g, rows_of(c)] = solved
        end = cum_row[:, CHUNK - 1 : CHUNK]
        tail = jnp.exp(end - cum_col) * jnp.where(first_rows, keep_second, 1.0)
        product = mul(key, (tail * solved).astype(BF16), TN)
        passed = jnp.exp(end) * keep_both
        step_s[g, c, :, :depth] = jnp.where(row == col, passed, 0.0) - product[:, :depth]
        step_s[g, c, :, depth:] = product[:, depth:]

    def compose(later, earlier):
        high, low = split(earlier)
        trans = later[:, :depth].astype(BF16)
        joined = mul(trans, high) + mul(trans, low)
        return jnp.concatenate([joined[:, :depth], joined[:, depth:] + later[:, depth:]], axis=1)

    every = range(heads)
    states = [step_s[g, 0] for g in every]
    half = chunks // 2
    for c in range(1, half):
        for g in every:
            starts_ref[g, c - 1] = states[g]
        states = [compose(step_s[g, c], states[g]) for g in every]
    rest = [step_s[g, half] for g in every]
    for c in range(half + 1, chunks):
        rest = [compose(step_s[g, c], rest[g]) for g in every]
    for g in every:
        map_refs[g // size][g % size] = compose(rest[g], states[g]).astype(BF16)
    for c in range(half, chunks):
        for g in every:
            starts_ref[g, c - 1] = states[g]
        if c + 1 < chunks:
            states = [compose(step_s[g, c], states[g]) for g in every]


def reads_kernel(
    base, resets, query_ref, gate_ref, gain_ref, rim_ref, taps_ref, decay_ref, strength_ref,
    unit_ref, solved_ref, starts_ref,
    reach_ref, part_ref, gating_ref,
    rims, padded,
):
    heads, length, depth = unit_ref.shape
    chunks = length // CHUNK
    row, col = indices()
    first_rows = lax.broadcasted_iota(jnp.int32, (CHUNK, 1), 0) < BLOCK
    rims[...] = rim_ref[...].astype(F32)
    for g in range(heads):
        h = base + g
        padded[g, 0:RIM] = rims[0:RIM, h, :]
        padded[g, RIM : RIM + length] = query_ref[h].astype(F32)

    for c in range(chunks):
        here = rows_of(c)
        cum, _, columns = token_scalars(decay_ref, strength_ref, c)
        first, second = resets[2 * c], resets[2 * c + 1]
        keep_first = (1 - first).astype(F32)
        keep_both = keep_first * (1 - second).astype(F32)
        upto = (row >= col) & same_document(second, row, col)
        for g in range(heads):
            h = base + g
            cum_col = columns[:, h : h + 1]
            filtered_rows = filtered(padded.at[g], taps_of(taps_ref, 0, h), c * CHUNK, CHUNK)
            query = (unit(filtered_rows) * depth**-0.5).astype(BF16)
            fading = jnp.exp(jnp.where(upto, cum_col - cum[h : h + 1], FAR))
            mixing = fading * mul(query, unit_ref[g, here], NT)
            own = mul_split(mixing, solved_ref[g, here])
            growth = jnp.exp(cum_col) * jnp.where(first_rows, keep_first, keep_both)
            reach = growth * query.astype(F32) - own[:, :depth]
            part = own[:, depth:]
            if c:
                both = mul_split(reach, starts_ref[g, c - 1])
                reach = both[:, :depth]
                part = part + both[:, depth:]
            reach_ref[g, here] = reach.astype(BF16)
            part_ref[g, here] = part
            gate = gate_ref[h, here].astype(F32)
            gating_ref[g, here] = gain_ref[...] * silu(gate)


def partner(place, k, count):
    if count & (count - 1) == 0:
        return place ^ k
    return lax.rem(place + count - k, count)


def pairs_at(k, count):
    if count & (count - 1) == 0:
        return [(i, i ^ k) for i in range(count)]
    return [(i, (i + k) % count) for i in range(count)]


def join_kernel(count, place, *refs):
    maps = refs[:count]
    before_ref, state_ref, *trans_ref, ordered = refs[count:]
    heads, depth, _ = before_ref.shape
    me = place[0]
    for k in range(count):
        ordered[partner(me, k, count)] = maps[k][...]
    row, col = indices()
    eye = (row == col).astype(F32)
    states = [jnp.concatenate([eye, jnp.zeros((depth, depth), F32)], axis=1)] * heads
    for lap in range(count):

        @pl.when(lap == me)
        def _():
            for h in range(heads):
                before_ref[h] = states[h]

        for h in range(heads):
            step = ordered[lap, h]
            if lap:
                high, low = split(states[h])
                trans = step[:, :depth]
                joined = mul(trans, high) + mul(trans, low)
                states[h] = jnp.concatenate(
                    [joined[:, :depth], joined[:, depth:] + step[:, depth:].astype(F32)], axis=1
                )
            else:
                states[h] = step.astype(F32)
    for h in range(heads):
        state_ref[h] = states[h][:, depth:].astype(state_ref.dtype)
        for ref in trans_ref:
            ref[h] = states[h][:, :depth]


def outputs_kernel(base, arrived_ref, before_ref, reach_ref, part_ref, gating_ref, normed_ref):
    heads, depth, _ = arrived_ref.shape
    for g in range(heads):
        h = base + g
        before = before_ref[g]
        incoming = mul_split(before[:, :depth], arrived_ref[g].astype(F32)) + before[:, depth:]
        high, low = split(incoming)
        for c in range(normed_ref.shape[0] // CHUNK):
            here = rows_of(c)
            reach = reach_ref[h, here]
            core = part_ref[h, here] + (mul(reach, high) + mul(reach, low))
            scale = lax.rsqrt(jnp.sum(core * core, axis=-1, keepdims=True) / depth + EPSILON)
            normed_ref[here, g * depth : (g + 1) * depth] = (
                core * scale * gating_ref[h, here]
            ).astype(BF16)


def last_kernel(section, first_ref, second_ref, block_ref, weights_ref, out_ref, tiles, written):
    width = block_ref.shape[1]
    rows = weights_ref[pl.ds(pl.multiple_of(section[0] * width, width), width), :]
    copies = []
    for i in range(first_ref.shape[0] // CHUNK):
        here = rows_of(i)
        total = (first_ref[here] + second_ref[here]) + mul(block_ref[here], rows)
        tiles[here] = total.astype(BF16)
        copies.append(pltpu.make_async_copy(tiles.at[here], out_ref.at[here], written.at[i]))
        copies[-1].start()
    for copy in copies:
        copy.wait()


def from_behind(value, axis, steps):
    count = lax.axis_size(axis)
    return lax.ppermute(value, axis, [(i, i + steps) for i in range(count - steps)])


def exchange(own_map, leaves):
    received = [lax.ppermute(own_map, "leaf", pairs_at(k, leaves)) for k in range(1, leaves)]
    return [own_map] + received


VMEM = pl.BlockSpec(memory_space=pltpu.VMEM)
SMEM = pl.BlockSpec(memory_space=pltpu.SMEM)
HBM = pl.BlockSpec(memory_space=pltpu.HBM)
PARAMS = pltpu.CompilerParams(vmem_limit_bytes=8 * 1024 * 1024)
LAST_PARAMS = pltpu.CompilerParams(vmem_limit_bytes=12 * 1024 * 1024)


def pack_rims(inputs):
    _, heads, depth = inputs[0].shape
    return pl.pallas_call(
        rims_kernel,
        out_shape=jax.ShapeDtypeStruct((len(inputs) * RIM, heads, depth), BF16),
        in_specs=[HBM] * len(inputs),
        out_specs=VMEM,
        scratch_shapes=[pltpu.SemaphoreType.DMA((len(inputs),))],
        compiler_params=pltpu.CompilerParams(vmem_limit_bytes=65_700_000),
        cost_estimate=pl.CostEstimate(flops=10**9, bytes_accessed=2**16, transcendentals=0),
    )(*inputs)


def filters_of(key, value, taps):
    heads, length, depth = key.shape
    per_token = jax.ShapeDtypeStruct((heads, length, depth), BF16)
    return pl.pallas_call(
        filters_kernel,
        out_shape=(per_token, per_token, jax.ShapeDtypeStruct((2, heads, AGAIN, depth), F32)),
        in_specs=[VMEM] * 3,
        out_specs=[VMEM] * 3,
        scratch_shapes=[pltpu.VMEM((2, heads, length + RIM, depth), F32)],
        compiler_params=PARAMS,
        cost_estimate=pl.CostEstimate(
            flops=3 * 10**9, bytes_accessed=4 * 2**20, transcendentals=10**6
        ),
    )(key, value, taps)


def maps_of(base, heads, resets, unit_in, value_in, first, rims, taps, decay, strength):
    _, length, depth = unit_in.shape
    chunks = length // CHUNK
    return pl.pallas_call(
        functools.partial(maps_kernel, base),
        out_shape=(
            jax.ShapeDtypeStruct((heads, length, depth), BF16),
            jax.ShapeDtypeStruct((heads, length, 2 * depth), F32),
            jax.ShapeDtypeStruct((heads, chunks - 1, depth, 2 * depth), F32),
            *[jax.ShapeDtypeStruct((heads // GROUPS, depth, 2 * depth), BF16)] * GROUPS,
        ),
        in_specs=[SMEM] + [VMEM] * 7,
        out_specs=[VMEM] * (3 + GROUPS),
        scratch_shapes=[
            pltpu.VMEM(rims.shape, F32),
            pltpu.VMEM((heads, 2, RIM + AGAIN, depth), F32),
            pltpu.VMEM((heads, CHUNK, depth), BF16),
            pltpu.VMEM((heads, chunks, depth, 2 * depth), F32),
        ],
        compiler_params=PARAMS,
        cost_estimate=pl.CostEstimate(
            flops=5 * 10**9, bytes_accessed=4 * 2**20, transcendentals=10**6
        ),
    )(resets, unit_in, value_in, first, rims, taps, decay, strength)


def reads_of(base, heads, resets, query, gate, gain, rims, taps, decay, strength, made):
    _, length, depth = query.shape
    per_token = jax.ShapeDtypeStruct((heads, length, depth), F32)
    return pl.pallas_call(
        functools.partial(reads_kernel, base),
        out_shape=(jax.ShapeDtypeStruct(per_token.shape, BF16), per_token, per_token),
        in_specs=[SMEM] + [VMEM] * 10,
        out_specs=[VMEM] * 3,
        scratch_shapes=[
            pltpu.VMEM(rims.shape, F32),
            pltpu.VMEM((heads, length + RIM, depth), F32),
        ],
        compiler_params=PARAMS,
        cost_estimate=pl.CostEstimate(
            flops=3 * 10**9, bytes_accessed=4 * 2**20, transcendentals=10**6
        ),
    )(resets, query, gate, gain, rims, taps, decay, strength, *made)


def join(place, maps, links):
    count = len(maps)
    heads, depth, _ = maps[0].shape
    pair = jax.ShapeDtypeStruct((heads, depth, 2 * depth), F32)
    square = (heads, depth, depth)
    if links == 1:
        totals = (jax.ShapeDtypeStruct(square, BF16),)
    else:
        totals = (jax.ShapeDtypeStruct(square, F32),) * 2
    return pl.pallas_call(
        functools.partial(join_kernel, count),
        out_shape=(pair, *totals),
        in_specs=[SMEM] + [VMEM] * count,
        out_specs=[VMEM] * (1 + len(totals)),
        scratch_shapes=[pltpu.VMEM((count, heads, depth, 2 * depth), BF16)],
        compiler_params=PARAMS,
    )(place, *maps)


def outputs_of(base, arrived, before, reads):
    heads, depth, _ = arrived.shape
    length = reads[0].shape[1]
    return pl.pallas_call(
        functools.partial(outputs_kernel, base),
        out_shape=jax.ShapeDtypeStruct((length, heads * depth), BF16),
        in_specs=[VMEM] * 5,
        out_specs=VMEM,
        compiler_params=PARAMS,
    )(arrived, before, *reads)


def last_projected(section, first, second, block, weights):
    length, columns = first.shape
    return pl.pallas_call(
        last_kernel,
        out_shape=jax.ShapeDtypeStruct((length, columns), BF16),
        in_specs=[SMEM] + [VMEM] * 4,
        out_specs=pl.BlockSpec(memory_space=pl.ANY),
        scratch_shapes=[
            pltpu.VMEM((length, columns), BF16),
            pltpu.SemaphoreType.DMA((length // CHUNK,)),
        ],
        compiler_params=LAST_PARAMS,
    )(section.astype(jnp.int32).reshape(1), first, second, block, weights)


def after(first, *values):
    return lax.optimization_barrier((first, *values))[1:]


def on_device(
    query_in,
    key_in,
    value_in,
    gate_in,
    write_strength,
    log_decay,
    doc_resets,
    conv_weight,
    output_norm_gain,
    output_projection_weight,
):
    length, heads, depth = query_in.shape
    taps = conv_weight
    rims = from_behind(pack_rims((query_in, key_in, value_in)), ("chain", "leaf"), 1)
    key, value = (jnp.transpose(x, (1, 0, 2)) for x in (key_in, value_in))
    key, value, first = filters_of(key, value, taps)
    gain = output_norm_gain.reshape(1, depth)
    leaves = lax.axis_size("leaf")
    place = lax.axis_index("leaf").astype(jnp.int32).reshape(1)

    links = lax.axis_size("chain") - 1
    unit_key, solved, starts, *own_maps = maps_of(
        0, heads, doc_resets, key, value, first, rims, taps, log_decay, write_strength
    )
    query_in, gate_in = after(own_maps[-1], query_in, gate_in)
    query, gate = (jnp.transpose(x, (1, 0, 2)) for x in (query_in, gate_in))
    reads = reads_of(
        0, heads, doc_resets, query, gate, gain, rims, taps, log_decay, write_strength,
        (unit_key, solved, starts),
    )
    size = heads // GROUPS
    blocks = []
    exchanged = [exchange(own_maps[0], leaves)]
    for g in range(GROUPS):
        earlier = blocks[-1] if blocks else reads[0]
        maps = after(earlier, *exchanged[g])
        before, state, *trans = join(place, maps, links)
        if g + 1 < GROUPS:
            exchanged.append(exchange(*after(state, own_maps[g + 1]), leaves))
        arrived = from_behind(state.astype(BF16), "chain", 1)
        for _ in range(links - 1):
            passed = jnp.einsum(
                "hij,hjk->hik", trans[0], arrived.astype(F32), precision=lax.Precision.HIGHEST
            )
            arrived = from_behind((passed + state).astype(BF16), "chain", 1)
        blocks.append(outputs_of(g * size, arrived, before, reads))

    ring = lax.axis_size("head")
    mine = lax.axis_index("head")
    width = size * depth
    weights = output_projection_weight
    around = [(i, (i + 1) % ring) for i in range(ring)]
    sums = [None] * GROUPS
    for k in range(ring):
        owner = lax.rem(mine + ring - k, ring)
        last = k + 1 == ring
        following = blocks if last else [lax.ppermute(x, "head", around) for x in blocks]
        for g, block in enumerate(blocks):
            section = owner * GROUPS + g
            if last and g + 1 == GROUPS:
                return last_projected(section, *sums, block, weights)
            rows = lax.dynamic_slice_in_dim(weights, section * width, width, 0)
            term = jnp.dot(block, rows, preferred_element_type=F32)
            sums[g] = term if sums[g] is None else sums[g] + term
        blocks = following


def solution(mesh):
    return jax.shard_map(
        on_device,
        mesh=mesh,
        in_specs=(
            P(("chain", "leaf"), "head", None),
            P(("chain", "leaf"), "head", None),
            P(("chain", "leaf"), "head", None),
            P(("chain", "leaf"), "head", None),
            P("head", ("chain", "leaf")),
            P("head", ("chain", "leaf")),
            P(("chain", "leaf")),
            P(None, None, "head", None),
            P(),
            P(None, "head"),
        ),
        out_specs=P(("chain", "leaf"), "head"),
        check_vma=False,
    )
```

```python
import functools

import jax
import jax.numpy as jnp
from jax import lax
from jax.experimental import pallas as pl
from jax.experimental.pallas import tpu as pltpu
from jax.sharding import PartitionSpec as P

BLOCK = 64
CHUNK = 128
GROUPS = 2
RIM = 8
EPSILON = 1e-06
FAR = -1e30
LARGE = 1e38
AGAIN = 16
F32 = jnp.float32
BF16 = jnp.bfloat16
NN = (((1,), (0,)), ((), ()))
NT = (((1,), (1,)), ((), ()))
TN = (((0,), (0,)), ((), ()))


def split(a):
    high = a.astype(BF16)
    return high, (a - high.astype(F32)).astype(BF16)


def mul(a, b, dims=NN):
    return lax.dot_general(a, b, dims, preferred_element_type=F32)


def mul_split(a, b):
    a_high, a_low = split(a)
    b_high, b_low = split(b)
    return mul(a_high, b_high) + (mul(a_low, b_high) + mul(a_high, b_low))


def mul_stacked(a, b_high, b_low=None):
    rows = a.shape[0]
    a_high, a_low = split(a)
    both = mul(jnp.concatenate([a_high, a_low], axis=0), b_high)
    product = both[:rows] + both[rows:]
    return product if b_low is None else product + mul(a_high, b_low)


def rows_of(c):
    return slice(c * CHUNK, (c + 1) * CHUNK)


def indices():
    shape = (CHUNK, CHUNK)
    return (
        lax.broadcasted_iota(jnp.int32, shape, 0),
        lax.broadcasted_iota(jnp.int32, shape, 1),
    )


def token_scalars(decay_ref, strength_ref, c):
    row, col = indices()
    cum = lax.dot_general(
        decay_ref[:, rows_of(c)],
        (row <= col).astype(F32),
        NN,
        precision=lax.Precision.HIGHEST,
        preferred_element_type=F32,
    )
    strength = strength_ref[:, rows_of(c)]
    stacked = [cum, strength]
    missing = 8 - 2 * cum.shape[0]
    if missing > 0:
        stacked.append(jnp.zeros((missing, CHUNK), F32))
    return cum, strength, jnp.transpose(jnp.concatenate(stacked, axis=0))


def silu(x):
    below = jnp.minimum(1.0 + jnp.exp(-x), LARGE)
    inverse = pl.reciprocal(below, approx=True)
    return x * (inverse * (2.0 - below * inverse))


def filtered(padded, taps, begin, length):
    first = begin + RIM + 1 - len(taps)
    total = taps[0] * padded[first : first + length]
    for j in range(1, len(taps)):
        total = total + taps[j] * padded[first + j : first + j + length]
    return silu(total)


def taps_of(taps_ref, which, head):
    return [taps_ref[which, j, pl.ds(head, 1), :] for j in range(taps_ref.shape[1])]


def unit(rows):
    return rows * lax.rsqrt(jnp.sum(rows * rows, axis=-1, keepdims=True) + EPSILON)


def same_document(second_resets, row, col):
    return ((row // BLOCK) - (col // BLOCK)) * second_resets == 0


def lower_inverse(lowers, row, col):
    differ = row ^ col
    eye = (row == col).astype(F32)
    in_block = (differ < 8).astype(F32)
    diagonal = [low * in_block for low in lowers]
    powers = [d.astype(BF16) for d in diagonal]
    squares = [mul(p, p).astype(BF16) for p in powers]
    inverse = [eye - d for d in diagonal]
    stacked = [
        mul(jnp.concatenate([s, x.astype(BF16)], axis=0), s) for x, s in zip(inverse, squares)
    ]
    fourths = [both[:CHUNK].astype(BF16) for both in stacked]
    inverse = [x + both[CHUNK:] for x, both in zip(inverse, stacked)]
    inverse = [x + mul(x.astype(BF16), s) for x, s in zip(inverse, fourths)]
    size = 8
    while size < CHUNK:
        joint = odd_blocks(((differ >= size) & (differ < 2 * size)).astype(F32), size)
        rounded = [x.astype(BF16) for x in inverse]
        inner = [
            mul((odd_blocks(low, size) * joint).astype(BF16), x)
            for low, x in zip(lowers, rounded)
        ]
        outer = [
            mul(odd_blocks(x, size).astype(BF16), with_even_zeros(i, size).astype(BF16))
            for x, i in zip(inverse, inner)
        ]
        inverse = [less_in_odd(x, o, size) for x, o in zip(inverse, outer)]
        size *= 2
    return inverse


def odd_blocks(a, size):
    return jnp.concatenate([a[b : b + size] for b in range(size, a.shape[0], 2 * size)], axis=0)


def with_even_zeros(odd, size):
    zeros = jnp.zeros((size, odd.shape[1]), odd.dtype)
    pieces = []
    for b in range(0, odd.shape[0], size):
        pieces += [zeros, odd[b : b + size]]
    return jnp.concatenate(pieces, axis=0)


def less_in_odd(a, odd, size):
    pieces = []
    for b in range(0, odd.shape[0], size):
        pieces.append(a[2 * b : 2 * b + size])
        pieces.append(a[2 * b + size : 2 * b + 2 * size] - odd[b : b + size])
    return jnp.concatenate(pieces, axis=0)


def rims_kernel(*refs):
    *inputs, packed_ref, arrived = refs
    copies = []
    for i, x_ref in enumerate(inputs):
        last = x_ref.at[pl.ds(x_ref.shape[0] - RIM, RIM)]
        here = packed_ref.at[pl.ds(i * RIM, RIM)]
        copies.append(pltpu.make_async_copy(last, here, arrived.at[i]))
    for copy in copies:
        copy.start()
    for copy in copies:
        copy.wait()


def filters_kernel(key_ref, value_ref, taps_ref, unit_ref, value_out_ref, first_ref, padded):
    heads, length, _ = key_ref.shape
    for i, x_ref in enumerate((key_ref, value_ref)):
        padded[i, :, RIM:] = x_ref[...].astype(F32)
        padded[i, :, 0:RIM] = jnp.zeros((heads, RIM, padded.shape[3]), F32)
    first_ref[...] = padded[:, :, RIM : RIM + AGAIN]

    def one_head(h, carry):
        for i in range(2):
            taps = taps_of(taps_ref, 1 + i, h)
            for c in range(length // CHUNK):
                rows = filtered(padded.at[i, h], taps, c * CHUNK, CHUNK)
                if i == 0:
                    unit_ref[h, rows_of(c)] = unit(rows).astype(BF16)
                else:
                    value_out_ref[h, rows_of(c)] = rows.astype(BF16)
        return carry

    lax.fori_loop(0, heads, one_head, 0)


def maps_kernel(
    base, resets, unit_in_ref, value_in_ref, first_ref, rim_ref, taps_ref, decay_ref, strength_ref,
    unit_ref, solved_ref, starts_ref, *refs,
):
    *map_refs, rims, padded, value_s, step_s = refs
    heads, length, depth = unit_ref.shape
    chunks = length // CHUNK
    size = heads // len(map_refs)
    total_heads = decay_ref.shape[0]
    row, col = indices()
    rims[...] = rim_ref[...].astype(F32)
    for g in range(heads):
        h = base + g
        for c in range(1, chunks):
            unit_ref[g, rows_of(c)] = unit_in_ref[h, rows_of(c)]
        unit_ref[g, AGAIN:CHUNK] = unit_in_ref[h, AGAIN:CHUNK]
        value_s[g, AGAIN:CHUNK] = value_in_ref[h, AGAIN:CHUNK]
        for i in range(2):
            padded[g, i, 0:RIM] = rims[(1 + i) * RIM : (2 + i) * RIM, h, :]
            padded[g, i, RIM : RIM + AGAIN] = first_ref[i, h]
            rows = filtered(padded.at[g, i], taps_of(taps_ref, 1 + i, h), 0, AGAIN)
            if i == 0:
                unit_ref[g, 0:AGAIN] = unit(rows).astype(BF16)
            else:
                value_s[g, 0:AGAIN] = rows.astype(BF16)

    parts = []
    lowers = []
    for c in range(chunks):
        cum, _, columns = token_scalars(decay_ref, strength_ref, c)
        first, second = resets[2 * c], resets[2 * c + 1]
        strictly = (row > col) & same_document(second, row, col)
        for g in range(heads):
            h = base + g
            cum_col = columns[:, h : h + 1]
            cum_row = cum[h : h + 1]
            key = unit_in_ref[h, rows_of(c)] if c else unit_ref[g, rows_of(c)]
            fading = jnp.exp(jnp.where(strictly, cum_col - cum_row, FAR))
            strength_col = columns[:, total_heads + h : total_heads + h + 1]
            lowers.append(strength_col * fading * mul(key, key, NT))
            parts.append((g, c, first, second, cum_col, cum_row, strength_col))
    inverses = lower_inverse(lowers, row, col)
    eye = (row == col).astype(F32)
    first_rows = lax.broadcasted_iota(jnp.int32, (CHUNK, 1), 0) < BLOCK
    for (g, c, first, second, cum_col, cum_row, strength_col), inverse in zip(parts, inverses):
        keep_first = (1 - first).astype(F32)
        keep_second = (1 - second).astype(F32)
        keep_both = keep_first * keep_second
        h = base + g
        key = unit_in_ref[h, rows_of(c)] if c else unit_ref[g, rows_of(c)]
        value = value_in_ref[h, rows_of(c)] if c else value_s[g]
        growth = jnp.exp(cum_col) * jnp.where(first_rows, keep_first, keep_both)
        targets = jnp.concatenate(
            [
                (strength_col * growth) * key.astype(F32),
                strength_col * value.astype(F32),
            ],
            axis=1,
        )
        solved = targets + mul((inverse - eye).astype(BF16), targets.astype(BF16))
        solved_ref[g, rows_of(c)] = solved
        end = cum_row[:, CHUNK - 1 : CHUNK]
        tail = jnp.exp(end - cum_col) * jnp.where(first_rows, keep_second, 1.0)
        product = mul(key, (tail * solved).astype(BF16), TN)
        passed = jnp.exp(end) * keep_both
        step_s[g, c, :, :depth] = jnp.where(row == col, passed, 0.0) - product[:, :depth]
        step_s[g, c, :, depth:] = product[:, depth:]

    def compose(later, earlier):
        high, low = split(earlier)
        trans = later[:, :depth].astype(BF16)
        joined = mul(trans, high) + mul(trans, low)
        return jnp.concatenate([joined[:, :depth], joined[:, depth:] + later[:, depth:]], axis=1)

    every = range(heads)
    states = [step_s[g, 0] for g in every]
    half = chunks // 2
    for c in range(1, half):
        for g in every:
            starts_ref[g, c - 1] = states[g].astype(BF16)
        states = [compose(step_s[g, c], states[g]) for g in every]
    rest = [step_s[g, half] for g in every]
    for c in range(half + 1, chunks):
        rest = [compose(step_s[g, c], rest[g]) for g in every]
    for g in every:
        map_refs[g // size][g % size] = compose(rest[g], states[g]).astype(BF16)
    for c in range(half, chunks):
        for g in every:
            starts_ref[g, c - 1] = states[g].astype(BF16)
        if c + 1 < chunks:
            states = [compose(step_s[g, c], states[g]) for g in every]


def reads_kernel(
    base, resets, query_ref, gate_ref, gain_ref, rim_ref, taps_ref, decay_ref, strength_ref,
    unit_ref, solved_ref, starts_ref,
    reach_ref, part_ref, gating_ref,
    rims, padded,
):
    heads, length, depth = unit_ref.shape
    chunks = length // CHUNK
    row, col = indices()
    first_rows = lax.broadcasted_iota(jnp.int32, (CHUNK, 1), 0) < BLOCK
    rims[...] = rim_ref[...].astype(F32)
    for g in range(heads):
        h = base + g
        padded[g, 0:RIM] = rims[0:RIM, h, :]
        padded[g, RIM : RIM + length] = query_ref[h].astype(F32)

    for c in range(chunks):
        here = rows_of(c)
        cum, _, columns = token_scalars(decay_ref, strength_ref, c)
        first, second = resets[2 * c], resets[2 * c + 1]
        keep_first = (1 - first).astype(F32)
        keep_both = keep_first * (1 - second).astype(F32)
        upto = (row >= col) & same_document(second, row, col)
        for g in range(heads):
            h = base + g
            cum_col = columns[:, h : h + 1]
            filtered_rows = filtered(padded.at[g], taps_of(taps_ref, 0, h), c * CHUNK, CHUNK)
            query = (unit(filtered_rows) * depth**-0.5).astype(BF16)
            fading = jnp.exp(jnp.where(upto, cum_col - cum[h : h + 1], FAR))
            mixing = fading * mul(query, unit_ref[g, here], NT)
            own = mul_stacked(mixing, *split(solved_ref[g, here]))
            growth = jnp.exp(cum_col) * jnp.where(first_rows, keep_first, keep_both)
            reach = growth * query.astype(F32) - own[:, :depth]
            part = own[:, depth:]
            if c:
                both = mul_stacked(reach, starts_ref[g, c - 1])
                reach = both[:, :depth]
                part = part + both[:, depth:]
            reach_ref[g, here] = reach.astype(BF16)
            part_ref[g, here] = part
            gate = gate_ref[h, here].astype(F32)
            gating_ref[g, here] = gain_ref[...] * silu(gate)


def partner(place, k, count):
    if count & (count - 1) == 0:
        return place ^ k
    return lax.rem(place + count - k, count)


def pairs_at(k, count):
    if count & (count - 1) == 0:
        return [(i, i ^ k) for i in range(count)]
    return [(i, (i + k) % count) for i in range(count)]


def join_kernel(count, place, *refs):
    maps = refs[:count]
    before_ref, state_ref, *trans_ref, ordered = refs[count:]
    heads, depth, _ = before_ref.shape
    me = place[0]
    for k in range(count):
        ordered[partner(me, k, count)] = maps[k][...]
    row, col = indices()
    eye = (row == col).astype(F32)
    states = [jnp.concatenate([eye, jnp.zeros((depth, depth), F32)], axis=1)] * heads
    for lap in range(count):

        @pl.when(lap == me)
        def _():
            for h in range(heads):
                before_ref[h] = states[h]

        for h in range(heads):
            step = ordered[lap, h]
            if lap:
                high, low = split(states[h])
                trans = step[:, :depth]
                joined = mul(trans, high) + mul(trans, low)
                states[h] = jnp.concatenate(
                    [joined[:, :depth], joined[:, depth:] + step[:, depth:].astype(F32)], axis=1
                )
            else:
                states[h] = step.astype(F32)
    for h in range(heads):
        state_ref[h] = states[h][:, depth:].astype(state_ref.dtype)
        for ref in trans_ref:
            ref[h] = states[h][:, :depth]


def outputs_kernel(base, arrived_ref, before_ref, reach_ref, part_ref, gating_ref, normed_ref):
    heads, depth, _ = arrived_ref.shape
    for g in range(heads):
        h = base + g
        before = before_ref[g]
        incoming = mul_split(before[:, :depth], arrived_ref[g].astype(F32)) + before[:, depth:]
        high, low = split(incoming)
        for c in range(normed_ref.shape[0] // CHUNK):
            here = rows_of(c)
            reach = reach_ref[h, here]
            core = part_ref[h, here] + (mul(reach, high) + mul(reach, low))
            scale = lax.rsqrt(jnp.sum(core * core, axis=-1, keepdims=True) / depth + EPSILON)
            normed_ref[here, g * depth : (g + 1) * depth] = (
                core * scale * gating_ref[h, here]
            ).astype(BF16)


def placed_kernel(base, before_ref, reach_ref, part_ref, through_ref, fixed_ref):
    heads, depth, _ = before_ref.shape
    for g in range(heads):
        high, low = split(before_ref[g])
        for c in range(through_ref.shape[1] // CHUNK):
            here = rows_of(c)
            reach = reach_ref[base + g, here]
            both = mul(reach, high) + mul(reach, low)
            through_ref[g, here] = both[:, :depth].astype(BF16)
            fixed_ref[g, here] = part_ref[base + g, here] + both[:, depth:]


def placed_outputs_kernel(base, arrived_ref, through_ref, fixed_ref, gating_ref, normed_ref):
    heads, depth, _ = arrived_ref.shape
    for g in range(heads):
        arrived = arrived_ref[g]
        for c in range(normed_ref.shape[0] // CHUNK):
            here = rows_of(c)
            core = fixed_ref[g, here] + mul(through_ref[g, here], arrived)
            scale = lax.rsqrt(jnp.sum(core * core, axis=-1, keepdims=True) / depth + EPSILON)
            normed_ref[here, g * depth : (g + 1) * depth] = (
                core * scale * gating_ref[base + g, here]
            ).astype(BF16)


def last_kernel(section, first_ref, second_ref, block_ref, weights_ref, out_ref, tiles, written):
    width = block_ref.shape[1]
    rows = weights_ref[pl.ds(pl.multiple_of(section[0] * width, width), width), :]
    copies = []
    for i in range(first_ref.shape[0] // CHUNK):
        here = rows_of(i)
        total = (first_ref[here] + second_ref[here]) + mul(block_ref[here], rows)
        tiles[here] = total.astype(BF16)
        copies.append(pltpu.make_async_copy(tiles.at[here], out_ref.at[here], written.at[i]))
        copies[-1].start()
    for copy in copies:
        copy.wait()


def from_behind(value, axis, steps):
    count = lax.axis_size(axis)
    return lax.ppermute(value, axis, [(i, i + steps) for i in range(count - steps)])


def exchange(own_map, leaves):
    received = [lax.ppermute(own_map, "leaf", pairs_at(k, leaves)) for k in range(1, leaves)]
    return [own_map] + received


VMEM = pl.BlockSpec(memory_space=pltpu.VMEM)
SMEM = pl.BlockSpec(memory_space=pltpu.SMEM)
HBM = pl.BlockSpec(memory_space=pltpu.HBM)
PARAMS = pltpu.CompilerParams(vmem_limit_bytes=8 * 1024 * 1024)
LAST_PARAMS = pltpu.CompilerParams(vmem_limit_bytes=12 * 1024 * 1024)


def pack_rims(inputs):
    _, heads, depth = inputs[0].shape
    return pl.pallas_call(
        rims_kernel,
        out_shape=jax.ShapeDtypeStruct((len(inputs) * RIM, heads, depth), BF16),
        in_specs=[HBM] * len(inputs),
        out_specs=VMEM,
        scratch_shapes=[pltpu.SemaphoreType.DMA((len(inputs),))],
        compiler_params=pltpu.CompilerParams(vmem_limit_bytes=65_700_000),
        cost_estimate=pl.CostEstimate(flops=10**9, bytes_accessed=2**16, transcendentals=0),
    )(*inputs)


def filters_of(key, value, taps):
    heads, length, depth = key.shape
    per_token = jax.ShapeDtypeStruct((heads, length, depth), BF16)
    return pl.pallas_call(
        filters_kernel,
        out_shape=(per_token, per_token, jax.ShapeDtypeStruct((2, heads, AGAIN, depth), F32)),
        in_specs=[VMEM] * 3,
        out_specs=[VMEM] * 3,
        scratch_shapes=[pltpu.VMEM((2, heads, length + RIM, depth), F32)],
        compiler_params=PARAMS,
        cost_estimate=pl.CostEstimate(
            flops=3 * 10**9, bytes_accessed=4 * 2**20, transcendentals=10**6
        ),
    )(key, value, taps)


def maps_of(base, heads, resets, unit_in, value_in, first, rims, taps, decay, strength):
    _, length, depth = unit_in.shape
    chunks = length // CHUNK
    return pl.pallas_call(
        functools.partial(maps_kernel, base),
        out_shape=(
            jax.ShapeDtypeStruct((heads, length, depth), BF16),
            jax.ShapeDtypeStruct((heads, length, 2 * depth), F32),
            jax.ShapeDtypeStruct((heads, chunks - 1, depth, 2 * depth), BF16),
            *[jax.ShapeDtypeStruct((heads // GROUPS, depth, 2 * depth), BF16)] * GROUPS,
        ),
        in_specs=[SMEM] + [VMEM] * 7,
        out_specs=[VMEM] * (3 + GROUPS),
        scratch_shapes=[
            pltpu.VMEM(rims.shape, F32),
            pltpu.VMEM((heads, 2, RIM + AGAIN, depth), F32),
            pltpu.VMEM((heads, CHUNK, depth), BF16),
            pltpu.VMEM((heads, chunks, depth, 2 * depth), F32),
        ],
        compiler_params=PARAMS,
        cost_estimate=pl.CostEstimate(
            flops=5 * 10**9, bytes_accessed=4 * 2**20, transcendentals=10**6
        ),
    )(resets, unit_in, value_in, first, rims, taps, decay, strength)


def reads_of(base, heads, resets, query, gate, gain, rims, taps, decay, strength, made):
    _, length, depth = query.shape
    per_token = jax.ShapeDtypeStruct((heads, length, depth), F32)
    return pl.pallas_call(
        functools.partial(reads_kernel, base),
        out_shape=(jax.ShapeDtypeStruct(per_token.shape, BF16), per_token, per_token),
        in_specs=[SMEM] + [VMEM] * 10,
        out_specs=[VMEM] * 3,
        scratch_shapes=[
            pltpu.VMEM(rims.shape, F32),
            pltpu.VMEM((heads, length + RIM, depth), F32),
        ],
        compiler_params=PARAMS,
        cost_estimate=pl.CostEstimate(
            flops=3 * 10**9, bytes_accessed=4 * 2**20, transcendentals=10**6
        ),
    )(resets, query, gate, gain, rims, taps, decay, strength, *made)


def join(place, maps, links):
    count = len(maps)
    heads, depth, _ = maps[0].shape
    pair = jax.ShapeDtypeStruct((heads, depth, 2 * depth), F32)
    square = (heads, depth, depth)
    if links == 1:
        totals = (jax.ShapeDtypeStruct(square, BF16),)
    else:
        totals = (jax.ShapeDtypeStruct(square, F32),) * 2
    return pl.pallas_call(
        functools.partial(join_kernel, count),
        out_shape=(pair, *totals),
        in_specs=[SMEM] + [VMEM] * count,
        out_specs=[VMEM] * (1 + len(totals)),
        scratch_shapes=[pltpu.VMEM((count, heads, depth, 2 * depth), BF16)],
        compiler_params=PARAMS,
    )(place, *maps)


def outputs_of(base, arrived, before, reads):
    heads, depth, _ = arrived.shape
    length = reads[0].shape[1]
    return pl.pallas_call(
        functools.partial(outputs_kernel, base),
        out_shape=jax.ShapeDtypeStruct((length, heads * depth), BF16),
        in_specs=[VMEM] * 5,
        out_specs=VMEM,
        compiler_params=PARAMS,
    )(arrived, before, *reads)


def placed_of(base, before, reach, part):
    heads, depth, _ = before.shape
    length = reach.shape[1]
    per_token = (heads, length, depth)
    return pl.pallas_call(
        functools.partial(placed_kernel, base),
        out_shape=(
            jax.ShapeDtypeStruct(per_token, BF16),
            jax.ShapeDtypeStruct(per_token, F32),
        ),
        in_specs=[VMEM] * 3,
        out_specs=[VMEM] * 2,
        compiler_params=PARAMS,
        cost_estimate=pl.CostEstimate(flops=2 * 10**9, bytes_accessed=2**20, transcendentals=0),
    )(before, reach, part)


def placed_outputs_of(base, arrived, placed, gating):
    heads, depth, _ = arrived.shape
    length = gating.shape[1]
    return pl.pallas_call(
        functools.partial(placed_outputs_kernel, base),
        out_shape=jax.ShapeDtypeStruct((length, heads * depth), BF16),
        in_specs=[VMEM] * 4,
        out_specs=VMEM,
        compiler_params=PARAMS,
    )(arrived, *placed, gating)


def last_projected(section, first, second, block, weights):
    length, columns = first.shape
    return pl.pallas_call(
        last_kernel,
        out_shape=jax.ShapeDtypeStruct((length, columns), BF16),
        in_specs=[SMEM] + [VMEM] * 4,
        out_specs=pl.BlockSpec(memory_space=pl.ANY),
        scratch_shapes=[
            pltpu.VMEM((length, columns), BF16),
            pltpu.SemaphoreType.DMA((length // CHUNK,)),
        ],
        compiler_params=LAST_PARAMS,
    )(section.astype(jnp.int32).reshape(1), first, second, block, weights)


def after(first, *values):
    return lax.optimization_barrier((first, *values))[1:]


def on_device(
    query_in,
    key_in,
    value_in,
    gate_in,
    write_strength,
    log_decay,
    doc_resets,
    conv_weight,
    output_norm_gain,
    output_projection_weight,
):
    length, heads, depth = query_in.shape
    taps = conv_weight
    rims = from_behind(pack_rims((query_in, key_in, value_in)), ("chain", "leaf"), 1)
    key, value = (jnp.transpose(x, (1, 0, 2)) for x in (key_in, value_in))
    key, value, first = filters_of(key, value, taps)
    gain = output_norm_gain.reshape(1, depth)
    leaves = lax.axis_size("leaf")
    place = lax.axis_index("leaf").astype(jnp.int32).reshape(1)

    links = lax.axis_size("chain") - 1
    unit_key, solved, starts, *own_maps = maps_of(
        0, heads, doc_resets, key, value, first, rims, taps, log_decay, write_strength
    )
    query_in, gate_in = after(own_maps[-1], query_in, gate_in)
    query, gate = (jnp.transpose(x, (1, 0, 2)) for x in (query_in, gate_in))
    reads = reads_of(
        0, heads, doc_resets, query, gate, gain, rims, taps, log_decay, write_strength,
        (unit_key, solved, starts),
    )
    size = heads // GROUPS
    blocks = []
    exchanged = [exchange(own_maps[0], leaves)]
    for g in range(GROUPS):
        earlier = blocks[-1] if blocks else reads[0]
        maps = after(earlier, *exchanged[g])
        before, state, *trans = join(place, maps, links)
        if g + 1 < GROUPS:
            exchanged.append(exchange(*after(state, own_maps[g + 1]), leaves))
        arrived = from_behind(state.astype(BF16), "chain", 1)
        for _ in range(links - 1):
            passed = jnp.einsum(
                "hij,hjk->hik", trans[0], arrived.astype(F32), precision=lax.Precision.HIGHEST
            )
            arrived = from_behind((passed + state).astype(BF16), "chain", 1)
        if g + 1 < GROUPS:
            blocks.append(outputs_of(g * size, arrived, before, reads))
        else:
            reach, part, gating = reads
            placed = placed_of(g * size, before, reach, part)
            blocks.append(placed_outputs_of(g * size, arrived, placed, gating))

    ring = lax.axis_size("head")
    mine = lax.axis_index("head")
    width = size * depth
    weights = output_projection_weight
    around = [(i, (i + 1) % ring) for i in range(ring)]
    sums = [None] * GROUPS
    for k in range(ring):
        owner = lax.rem(mine + ring - k, ring)
        last = k + 1 == ring
        following = blocks if last else [lax.ppermute(x, "head", around) for x in blocks]
        if k == 0:
            blocks[:-1] = after(following[-1], *blocks[:-1])
        for g, block in enumerate(blocks):
            section = owner * GROUPS + g
            if last and g + 1 == GROUPS:
                return last_projected(section, *sums, block, weights)
            rows = lax.dynamic_slice_in_dim(weights, section * width, width, 0)
            term = jnp.dot(block, rows, preferred_element_type=F32)
            sums[g] = term if sums[g] is None else sums[g] + term
        blocks = following


def solution(mesh):
    return jax.shard_map(
        on_device,
        mesh=mesh,
        in_specs=(
            P(("chain", "leaf"), "head", None),
            P(("chain", "leaf"), "head", None),
            P(("chain", "leaf"), "head", None),
            P(("chain", "leaf"), "head", None),
            P("head", ("chain", "leaf")),
            P("head", ("chain", "leaf")),
            P(("chain", "leaf")),
            P(None, None, "head", None),
            P(),
            P(None, "head"),
        ),
        out_specs=P(("chain", "leaf"), "head"),
        check_vma=False,
    )
```

```python
import functools

import jax
import jax.numpy as jnp
from jax import lax
from jax.experimental import pallas as pl
from jax.experimental.pallas import tpu as pltpu
from jax.sharding import PartitionSpec as P

BLOCK = 64
CHUNK = 128
GROUPS = 2
RIM = 8
EPSILON = 1e-06
FAR = -1e30
LARGE = 1e38
AGAIN = 16
F32 = jnp.float32
BF16 = jnp.bfloat16
NN = (((1,), (0,)), ((), ()))
NT = (((1,), (1,)), ((), ()))
TN = (((0,), (0,)), ((), ()))


def split(a):
    high = a.astype(BF16)
    return high, (a - high.astype(F32)).astype(BF16)


def mul(a, b, dims=NN):
    return lax.dot_general(a, b, dims, preferred_element_type=F32)


def mul_split(a, b):
    a_high, a_low = split(a)
    b_high, b_low = split(b)
    return mul(a_high, b_high) + (mul(a_low, b_high) + mul(a_high, b_low))


def rows_of(c):
    return slice(c * CHUNK, (c + 1) * CHUNK)


def indices():
    shape = (CHUNK, CHUNK)
    return (
        lax.broadcasted_iota(jnp.int32, shape, 0),
        lax.broadcasted_iota(jnp.int32, shape, 1),
    )


def token_scalars(decay_ref, strength_ref, c):
    row, col = indices()
    cum = lax.dot_general(
        decay_ref[:, rows_of(c)],
        (row <= col).astype(F32),
        NN,
        precision=lax.Precision.HIGHEST,
        preferred_element_type=F32,
    )
    strength = strength_ref[:, rows_of(c)]
    stacked = [cum, strength]
    missing = 8 - 2 * cum.shape[0]
    if missing > 0:
        stacked.append(jnp.zeros((missing, CHUNK), F32))
    return cum, strength, jnp.transpose(jnp.concatenate(stacked, axis=0))


def silu(x):
    below = jnp.minimum(1.0 + jnp.exp(-x), LARGE)
    inverse = pl.reciprocal(below, approx=True)
    return x * (inverse * (2.0 - below * inverse))


def filtered(padded, taps, begin, length):
    first = begin + RIM + 1 - len(taps)
    total = taps[0] * padded[first : first + length]
    for j in range(1, len(taps)):
        total = total + taps[j] * padded[first + j : first + j + length]
    return silu(total)


def taps_of(taps_ref, which, head):
    return [taps_ref[which, j, pl.ds(head, 1), :] for j in range(taps_ref.shape[1])]


def unit(rows):
    return rows * lax.rsqrt(jnp.sum(rows * rows, axis=-1, keepdims=True) + EPSILON)


def same_document(second_resets, row, col):
    return ((row // BLOCK) - (col // BLOCK)) * second_resets == 0


def lower_inverse(lowers, row, col):
    differ = row ^ col
    eye = (row == col).astype(F32)
    in_block = (differ < 8).astype(F32)
    diagonal = [low * in_block for low in lowers]
    powers = [d.astype(BF16) for d in diagonal]
    squares = [mul(p, p).astype(BF16) for p in powers]
    inverse = [eye - d for d in diagonal]
    stacked = [
        mul(jnp.concatenate([s, x.astype(BF16)], axis=0), s) for x, s in zip(inverse, squares)
    ]
    fourths = [both[:CHUNK].astype(BF16) for both in stacked]
    inverse = [x + both[CHUNK:] for x, both in zip(inverse, stacked)]
    inverse = [x + mul(x.astype(BF16), s) for x, s in zip(inverse, fourths)]
    size = 8
    while size < CHUNK:
        joint = odd_blocks(((differ >= size) & (differ < 2 * size)).astype(F32), size)
        rounded = [x.astype(BF16) for x in inverse]
        inner = [
            mul((odd_blocks(low, size) * joint).astype(BF16), x)
            for low, x in zip(lowers, rounded)
        ]
        outer = [
            mul(odd_blocks(x, size).astype(BF16), with_even_zeros(i, size).astype(BF16))
            for x, i in zip(inverse, inner)
        ]
        inverse = [less_in_odd(x, o, size) for x, o in zip(inverse, outer)]
        size *= 2
    return inverse


def odd_blocks(a, size):
    return jnp.concatenate([a[b : b + size] for b in range(size, a.shape[0], 2 * size)], axis=0)


def with_even_zeros(odd, size):
    zeros = jnp.zeros((size, odd.shape[1]), odd.dtype)
    pieces = []
    for b in range(0, odd.shape[0], size):
        pieces += [zeros, odd[b : b + size]]
    return jnp.concatenate(pieces, axis=0)


def less_in_odd(a, odd, size):
    pieces = []
    for b in range(0, odd.shape[0], size):
        pieces.append(a[2 * b : 2 * b + size])
        pieces.append(a[2 * b + size : 2 * b + 2 * size] - odd[b : b + size])
    return jnp.concatenate(pieces, axis=0)


def rims_kernel(*refs):
    *inputs, packed_ref, arrived = refs
    copies = []
    for i, x_ref in enumerate(inputs):
        last = x_ref.at[pl.ds(x_ref.shape[0] - RIM, RIM)]
        here = packed_ref.at[pl.ds(i * RIM, RIM)]
        copies.append(pltpu.make_async_copy(last, here, arrived.at[i]))
    for copy in copies:
        copy.start()
    for copy in copies:
        copy.wait()


def filters_kernel(key_ref, value_ref, taps_ref, unit_ref, value_out_ref, first_ref, padded):
    heads, length, _ = key_ref.shape
    for i, x_ref in enumerate((key_ref, value_ref)):
        padded[i, :, RIM:] = x_ref[...].astype(F32)
        padded[i, :, 0:RIM] = jnp.zeros((heads, RIM, padded.shape[3]), F32)
    first_ref[...] = padded[:, :, RIM : RIM + AGAIN]

    def one_head(h, carry):
        for i in range(2):
            taps = taps_of(taps_ref, 1 + i, h)
            for c in range(length // CHUNK):
                rows = filtered(padded.at[i, h], taps, c * CHUNK, CHUNK)
                if i == 0:
                    unit_ref[h, rows_of(c)] = unit(rows).astype(BF16)
                else:
                    value_out_ref[h, rows_of(c)] = rows.astype(BF16)
        return carry

    lax.fori_loop(0, heads, one_head, 0)


def maps_kernel(
    base, resets, unit_in_ref, value_in_ref, first_ref, rim_ref, taps_ref, decay_ref, strength_ref,
    unit_ref, solved_ref, starts_ref, *refs,
):
    *map_refs, rims, padded, value_s, step_s = refs
    heads, length, depth = unit_ref.shape
    chunks = length // CHUNK
    size = heads // len(map_refs)
    total_heads = decay_ref.shape[0]
    row, col = indices()
    rims[...] = rim_ref[...].astype(F32)
    for g in range(heads):
        h = base + g
        for c in range(1, chunks):
            unit_ref[g, rows_of(c)] = unit_in_ref[h, rows_of(c)]
        unit_ref[g, AGAIN:CHUNK] = unit_in_ref[h, AGAIN:CHUNK]
        value_s[g, AGAIN:CHUNK] = value_in_ref[h, AGAIN:CHUNK]
        for i in range(2):
            padded[g, i, 0:RIM] = rims[(1 + i) * RIM : (2 + i) * RIM, h, :]
            padded[g, i, RIM : RIM + AGAIN] = first_ref[i, h]
            rows = filtered(padded.at[g, i], taps_of(taps_ref, 1 + i, h), 0, AGAIN)
            if i == 0:
                unit_ref[g, 0:AGAIN] = unit(rows).astype(BF16)
            else:
                value_s[g, 0:AGAIN] = rows.astype(BF16)

    parts = []
    lowers = []
    for c in range(chunks):
        cum, _, columns = token_scalars(decay_ref, strength_ref, c)
        first, second = resets[2 * c], resets[2 * c + 1]
        strictly = (row > col) & same_document(second, row, col)
        for g in range(heads):
            h = base + g
            cum_col = columns[:, h : h + 1]
            cum_row = cum[h : h + 1]
            key = unit_in_ref[h, rows_of(c)] if c else unit_ref[g, rows_of(c)]
            fading = jnp.exp(jnp.where(strictly, cum_col - cum_row, FAR))
            strength_col = columns[:, total_heads + h : total_heads + h + 1]
            lowers.append(strength_col * fading * mul(key, key, NT))
            parts.append((g, c, first, second, cum_col, cum_row, strength_col))
    inverses = lower_inverse(lowers, row, col)
    eye = (row == col).astype(F32)
    first_rows = lax.broadcasted_iota(jnp.int32, (CHUNK, 1), 0) < BLOCK
    for (g, c, first, second, cum_col, cum_row, strength_col), inverse in zip(parts, inverses):
        keep_first = (1 - first).astype(F32)
        keep_second = (1 - second).astype(F32)
        keep_both = keep_first * keep_second
        h = base + g
        key = unit_in_ref[h, rows_of(c)] if c else unit_ref[g, rows_of(c)]
        value = value_in_ref[h, rows_of(c)] if c else value_s[g]
        growth = jnp.exp(cum_col) * jnp.where(first_rows, keep_first, keep_both)
        targets = jnp.concatenate(
            [
                (strength_col * growth) * key.astype(F32),
                strength_col * value.astype(F32),
            ],
            axis=1,
        )
        solved = targets + mul((inverse - eye).astype(BF16), targets.astype(BF16))
        solved_ref[g, rows_of(c)] = solved
        end = cum_row[:, CHUNK - 1 : CHUNK]
        tail = jnp.exp(end - cum_col) * jnp.where(first_rows, keep_second, 1.0)
        product = mul(key, (tail * solved).astype(BF16), TN)
        passed = jnp.exp(end) * keep_both
        step_s[g, c, :, :depth] = jnp.where(row == col, passed, 0.0) - product[:, :depth]
        step_s[g, c, :, depth:] = product[:, depth:]

    def compose(later, earlier):
        high, low = split(earlier)
        trans = later[:, :depth].astype(BF16)
        joined = mul(trans, high) + mul(trans, low)
        return jnp.concatenate([joined[:, :depth], joined[:, depth:] + later[:, depth:]], axis=1)

    every = range(heads)
    states = [step_s[g, 0] for g in every]
    half = chunks // 2
    for c in range(1, half):
        for g in every:
            starts_ref[g, c - 1] = states[g].astype(BF16)
        states = [compose(step_s[g, c], states[g]) for g in every]
    rest = [step_s[g, half] for g in every]
    for c in range(half + 1, chunks):
        rest = [compose(step_s[g, c], rest[g]) for g in every]
    for g in every:
        map_refs[g // size][g % size] = compose(rest[g], states[g]).astype(BF16)
    for c in range(half, chunks):
        for g in every:
            starts_ref[g, c - 1] = states[g].astype(BF16)
        if c + 1 < chunks:
            states = [compose(step_s[g, c], states[g]) for g in every]


def reads_kernel(
    base, resets, query_ref, gate_ref, gain_ref, rim_ref, taps_ref, decay_ref, strength_ref,
    unit_ref, solved_ref, starts_ref,
    reach_ref, part_ref, gating_ref,
    rims, padded,
):
    heads, length, depth = unit_ref.shape
    chunks = length // CHUNK
    row, col = indices()
    first_rows = lax.broadcasted_iota(jnp.int32, (CHUNK, 1), 0) < BLOCK
    rims[...] = rim_ref[...].astype(F32)
    for g in range(heads):
        h = base + g
        padded[g, 0:RIM] = rims[0:RIM, h, :]
        padded[g, RIM : RIM + length] = query_ref[h].astype(F32)

    for c in range(chunks):
        here = rows_of(c)
        cum, _, columns = token_scalars(decay_ref, strength_ref, c)
        first, second = resets[2 * c], resets[2 * c + 1]
        keep_first = (1 - first).astype(F32)
        keep_both = keep_first * (1 - second).astype(F32)
        upto = (row >= col) & same_document(second, row, col)
        for g in range(heads):
            h = base + g
            cum_col = columns[:, h : h + 1]
            filtered_rows = filtered(padded.at[g], taps_of(taps_ref, 0, h), c * CHUNK, CHUNK)
            query = (unit(filtered_rows) * depth**-0.5).astype(BF16)
            fading = jnp.exp(jnp.where(upto, cum_col - cum[h : h + 1], FAR))
            mixing = fading * mul(query, unit_ref[g, here], NT)
            own = mul_split(mixing, solved_ref[g, here])
            growth = jnp.exp(cum_col) * jnp.where(first_rows, keep_first, keep_both)
            reach = growth * query.astype(F32) - own[:, :depth]
            part = own[:, depth:]
            if c:
                high, low = split(reach)
                both = mul(high, starts_ref[g, c - 1]) + mul(low, starts_ref[g, c - 1])
                reach = both[:, :depth]
                part = part + both[:, depth:]
            reach_ref[g, here] = reach.astype(BF16)
            part_ref[g, here] = part
            gate = gate_ref[h, here].astype(F32)
            gating_ref[g, here] = gain_ref[...] * silu(gate)


def partner(place, k, count):
    if count & (count - 1) == 0:
        return place ^ k
    return lax.rem(place + count - k, count)


def pairs_at(k, count):
    if count & (count - 1) == 0:
        return [(i, i ^ k) for i in range(count)]
    return [(i, (i + k) % count) for i in range(count)]


def join_kernel(count, place, *refs):
    maps = refs[:count]
    before_ref, state_ref, *trans_ref, ordered = refs[count:]
    heads, depth, _ = before_ref.shape
    me = place[0]
    for k in range(count):
        ordered[partner(me, k, count)] = maps[k][...]
    row, col = indices()
    eye = (row == col).astype(F32)
    states = [jnp.concatenate([eye, jnp.zeros((depth, depth), F32)], axis=1)] * heads
    for lap in range(count):

        @pl.when(lap == me)
        def _():
            for h in range(heads):
                before_ref[h] = states[h]

        for h in range(heads):
            step = ordered[lap, h]
            if lap:
                high, low = split(states[h])
                trans = step[:, :depth]
                joined = mul(trans, high) + mul(trans, low)
                states[h] = jnp.concatenate(
                    [joined[:, :depth], joined[:, depth:] + step[:, depth:].astype(F32)], axis=1
                )
            else:
                states[h] = step.astype(F32)
    for h in range(heads):
        state_ref[h] = states[h][:, depth:].astype(state_ref.dtype)
        for ref in trans_ref:
            ref[h] = states[h][:, :depth]


def outputs_kernel(base, arrived_ref, before_ref, reach_ref, part_ref, gating_ref, normed_ref):
    heads, depth, _ = arrived_ref.shape
    for g in range(heads):
        h = base + g
        before = before_ref[g]
        incoming = mul_split(before[:, :depth], arrived_ref[g].astype(F32)) + before[:, depth:]
        high, low = split(incoming)
        for c in range(normed_ref.shape[0] // CHUNK):
            here = rows_of(c)
            reach = reach_ref[h, here]
            core = part_ref[h, here] + (mul(reach, high) + mul(reach, low))
            scale = lax.rsqrt(jnp.sum(core * core, axis=-1, keepdims=True) / depth + EPSILON)
            normed_ref[here, g * depth : (g + 1) * depth] = (
                core * scale * gating_ref[h, here]
            ).astype(BF16)


def last_kernel(section, first_ref, second_ref, block_ref, weights_ref, out_ref, tiles, written):
    width = block_ref.shape[1]
    rows = weights_ref[pl.ds(pl.multiple_of(section[0] * width, width), width), :]
    copies = []
    for i in range(first_ref.shape[0] // CHUNK):
        here = rows_of(i)
        total = (first_ref[here] + second_ref[here]) + mul(block_ref[here], rows)
        tiles[here] = total.astype(BF16)
        copies.append(pltpu.make_async_copy(tiles.at[here], out_ref.at[here], written.at[i]))
        copies[-1].start()
    for copy in copies:
        copy.wait()


def from_behind(value, axis, steps):
    count = lax.axis_size(axis)
    return lax.ppermute(value, axis, [(i, i + steps) for i in range(count - steps)])


def exchange(own_map, leaves):
    received = [lax.ppermute(own_map, "leaf", pairs_at(k, leaves)) for k in range(1, leaves)]
    return [own_map] + received


VMEM = pl.BlockSpec(memory_space=pltpu.VMEM)
SMEM = pl.BlockSpec(memory_space=pltpu.SMEM)
HBM = pl.BlockSpec(memory_space=pltpu.HBM)
PARAMS = pltpu.CompilerParams(vmem_limit_bytes=8 * 1024 * 1024)
LAST_PARAMS = pltpu.CompilerParams(vmem_limit_bytes=12 * 1024 * 1024)


def pack_rims(inputs):
    _, heads, depth = inputs[0].shape
    return pl.pallas_call(
        rims_kernel,
        out_shape=jax.ShapeDtypeStruct((len(inputs) * RIM, heads, depth), BF16),
        in_specs=[HBM] * len(inputs),
        out_specs=VMEM,
        scratch_shapes=[pltpu.SemaphoreType.DMA((len(inputs),))],
        compiler_params=pltpu.CompilerParams(vmem_limit_bytes=65_700_000),
        cost_estimate=pl.CostEstimate(flops=10**9, bytes_accessed=2**16, transcendentals=0),
    )(*inputs)


def filters_of(key, value, taps):
    heads, length, depth = key.shape
    per_token = jax.ShapeDtypeStruct((heads, length, depth), BF16)
    return pl.pallas_call(
        filters_kernel,
        out_shape=(per_token, per_token, jax.ShapeDtypeStruct((2, heads, AGAIN, depth), F32)),
        in_specs=[VMEM] * 3,
        out_specs=[VMEM] * 3,
        scratch_shapes=[pltpu.VMEM((2, heads, length + RIM, depth), F32)],
        compiler_params=PARAMS,
        cost_estimate=pl.CostEstimate(
            flops=3 * 10**9, bytes_accessed=4 * 2**20, transcendentals=10**6
        ),
    )(key, value, taps)


def maps_of(base, heads, resets, unit_in, value_in, first, rims, taps, decay, strength):
    _, length, depth = unit_in.shape
    chunks = length // CHUNK
    return pl.pallas_call(
        functools.partial(maps_kernel, base),
        out_shape=(
            jax.ShapeDtypeStruct((heads, length, depth), BF16),
            jax.ShapeDtypeStruct((heads, length, 2 * depth), F32),
            jax.ShapeDtypeStruct((heads, chunks - 1, depth, 2 * depth), BF16),
            *[jax.ShapeDtypeStruct((heads // GROUPS, depth, 2 * depth), BF16)] * GROUPS,
        ),
        in_specs=[SMEM] + [VMEM] * 7,
        out_specs=[VMEM] * (3 + GROUPS),
        scratch_shapes=[
            pltpu.VMEM(rims.shape, F32),
            pltpu.VMEM((heads, 2, RIM + AGAIN, depth), F32),
            pltpu.VMEM((heads, CHUNK, depth), BF16),
            pltpu.VMEM((heads, chunks, depth, 2 * depth), F32),
        ],
        compiler_params=PARAMS,
        cost_estimate=pl.CostEstimate(
            flops=5 * 10**9, bytes_accessed=4 * 2**20, transcendentals=10**6
        ),
    )(resets, unit_in, value_in, first, rims, taps, decay, strength)


def reads_of(base, heads, resets, query, gate, gain, rims, taps, decay, strength, made):
    _, length, depth = query.shape
    per_token = jax.ShapeDtypeStruct((heads, length, depth), F32)
    return pl.pallas_call(
        functools.partial(reads_kernel, base),
        out_shape=(jax.ShapeDtypeStruct(per_token.shape, BF16), per_token, per_token),
        in_specs=[SMEM] + [VMEM] * 10,
        out_specs=[VMEM] * 3,
        scratch_shapes=[
            pltpu.VMEM(rims.shape, F32),
            pltpu.VMEM((heads, length + RIM, depth), F32),
        ],
        compiler_params=PARAMS,
        cost_estimate=pl.CostEstimate(
            flops=3 * 10**9, bytes_accessed=4 * 2**20, transcendentals=10**6
        ),
    )(resets, query, gate, gain, rims, taps, decay, strength, *made)


def join(place, maps, links):
    count = len(maps)
    heads, depth, _ = maps[0].shape
    pair = jax.ShapeDtypeStruct((heads, depth, 2 * depth), F32)
    square = (heads, depth, depth)
    if links == 1:
        totals = (jax.ShapeDtypeStruct(square, BF16),)
    else:
        totals = (jax.ShapeDtypeStruct(square, F32),) * 2
    return pl.pallas_call(
        functools.partial(join_kernel, count),
        out_shape=(pair, *totals),
        in_specs=[SMEM] + [VMEM] * count,
        out_specs=[VMEM] * (1 + len(totals)),
        scratch_shapes=[pltpu.VMEM((count, heads, depth, 2 * depth), BF16)],
        compiler_params=PARAMS,
    )(place, *maps)


def outputs_of(base, arrived, before, reads):
    heads, depth, _ = arrived.shape
    length = reads[0].shape[1]
    return pl.pallas_call(
        functools.partial(outputs_kernel, base),
        out_shape=jax.ShapeDtypeStruct((length, heads * depth), BF16),
        in_specs=[VMEM] * 5,
        out_specs=VMEM,
        compiler_params=PARAMS,
    )(arrived, before, *reads)


def last_projected(section, first, second, block, weights):
    length, columns = first.shape
    return pl.pallas_call(
        last_kernel,
        out_shape=jax.ShapeDtypeStruct((length, columns), BF16),
        in_specs=[SMEM] + [VMEM] * 4,
        out_specs=pl.BlockSpec(memory_space=pl.ANY),
        scratch_shapes=[
            pltpu.VMEM((length, columns), BF16),
            pltpu.SemaphoreType.DMA((length // CHUNK,)),
        ],
        compiler_params=LAST_PARAMS,
    )(section.astype(jnp.int32).reshape(1), first, second, block, weights)


def after(first, *values):
    return lax.optimization_barrier((first, *values))[1:]


def on_device(
    query_in,
    key_in,
    value_in,
    gate_in,
    write_strength,
    log_decay,
    doc_resets,
    conv_weight,
    output_norm_gain,
    output_projection_weight,
):
    length, heads, depth = query_in.shape
    taps = conv_weight
    rims = from_behind(pack_rims((query_in, key_in, value_in)), ("chain", "leaf"), 1)
    key, value = (jnp.transpose(x, (1, 0, 2)) for x in (key_in, value_in))
    key, value, first = filters_of(key, value, taps)
    gain = output_norm_gain.reshape(1, depth)
    leaves = lax.axis_size("leaf")
    place = lax.axis_index("leaf").astype(jnp.int32).reshape(1)

    links = lax.axis_size("chain") - 1
    unit_key, solved, starts, *own_maps = maps_of(
        0, heads, doc_resets, key, value, first, rims, taps, log_decay, write_strength
    )
    query_in, gate_in = after(own_maps[-1], query_in, gate_in)
    query, gate = (jnp.transpose(x, (1, 0, 2)) for x in (query_in, gate_in))
    reads = reads_of(
        0, heads, doc_resets, query, gate, gain, rims, taps, log_decay, write_strength,
        (unit_key, solved, starts),
    )
    size = heads // GROUPS
    blocks = []
    exchanged = [exchange(own_maps[0], leaves)]
    for g in range(GROUPS):
        earlier = blocks[-1] if blocks else reads[0]
        maps = after(earlier, *exchanged[g])
        before, state, *trans = join(place, maps, links)
        if g + 1 < GROUPS:
            exchanged.append(exchange(*after(state, own_maps[g + 1]), leaves))
        arrived = from_behind(state.astype(BF16), "chain", 1)
        for _ in range(links - 1):
            passed = jnp.einsum(
                "hij,hjk->hik", trans[0], arrived.astype(F32), precision=lax.Precision.HIGHEST
            )
            arrived = from_behind((passed + state).astype(BF16), "chain", 1)
        blocks.append(outputs_of(g * size, arrived, before, reads))

    ring = lax.axis_size("head")
    mine = lax.axis_index("head")
    width = size * depth
    weights = output_projection_weight
    around = [(i, (i + 1) % ring) for i in range(ring)]
    sums = [None] * GROUPS
    for k in range(ring):
        owner = lax.rem(mine + ring - k, ring)
        last = k + 1 == ring
        following = blocks if last else [lax.ppermute(x, "head", around) for x in blocks]
        for g, block in enumerate(blocks):
            section = owner * GROUPS + g
            if last and g + 1 == GROUPS:
                return last_projected(section, *sums, block, weights)
            rows = lax.dynamic_slice_in_dim(weights, section * width, width, 0)
            term = jnp.dot(block, rows, preferred_element_type=F32)
            sums[g] = term if sums[g] is None else sums[g] + term
        blocks = following


def solution(mesh):
    return jax.shard_map(
        on_device,
        mesh=mesh,
        in_specs=(
            P(("chain", "leaf"), "head", None),
            P(("chain", "leaf"), "head", None),
            P(("chain", "leaf"), "head", None),
            P(("chain", "leaf"), "head", None),
            P("head", ("chain", "leaf")),
            P("head", ("chain", "leaf")),
            P(("chain", "leaf")),
            P(None, None, "head", None),
            P(),
            P(None, "head"),
        ),
        out_specs=P(("chain", "leaf"), "head"),
        check_vma=False,
    )
```

```python
import functools

import jax
import jax.numpy as jnp
from jax import lax
from jax.experimental import pallas as pl
from jax.experimental.pallas import tpu as pltpu
from jax.sharding import PartitionSpec as P

BLOCK = 64
CHUNK = 128
GROUPS = 2
RIM = 8
EPSILON = 1e-06
FAR = -1e30
LARGE = 1e38
AGAIN = 16
F32 = jnp.float32
BF16 = jnp.bfloat16
NN = (((1,), (0,)), ((), ()))
NT = (((1,), (1,)), ((), ()))
TN = (((0,), (0,)), ((), ()))


def split(a):
    high = a.astype(BF16)
    return high, (a - high.astype(F32)).astype(BF16)


def mul(a, b, dims=NN):
    return lax.dot_general(a, b, dims, preferred_element_type=F32)


def mul_split(a, b):
    a_high, a_low = split(a)
    b_high, b_low = split(b)
    return mul(a_high, b_high) + (mul(a_low, b_high) + mul(a_high, b_low))


def rows_of(c):
    return slice(c * CHUNK, (c + 1) * CHUNK)


def indices():
    shape = (CHUNK, CHUNK)
    return (
        lax.broadcasted_iota(jnp.int32, shape, 0),
        lax.broadcasted_iota(jnp.int32, shape, 1),
    )


def token_scalars(decay_ref, strength_ref, c):
    row, col = indices()
    cum = lax.dot_general(
        decay_ref[:, rows_of(c)],
        (row <= col).astype(F32),
        NN,
        precision=lax.Precision.HIGHEST,
        preferred_element_type=F32,
    )
    strength = strength_ref[:, rows_of(c)]
    stacked = [cum, strength]
    missing = 8 - 2 * cum.shape[0]
    if missing > 0:
        stacked.append(jnp.zeros((missing, CHUNK), F32))
    return cum, strength, jnp.transpose(jnp.concatenate(stacked, axis=0))


def silu(x):
    below = jnp.minimum(1.0 + jnp.exp(-x), LARGE)
    inverse = pl.reciprocal(below, approx=True)
    return x * (inverse * (2.0 - below * inverse))


def filtered(padded, taps, begin, length):
    first = begin + RIM + 1 - len(taps)
    total = taps[0] * padded[first : first + length]
    for j in range(1, len(taps)):
        total = total + taps[j] * padded[first + j : first + j + length]
    return silu(total)


def taps_of(taps_ref, which, head):
    return [taps_ref[which, j, pl.ds(head, 1), :] for j in range(taps_ref.shape[1])]


def unit(rows):
    return rows * lax.rsqrt(jnp.sum(rows * rows, axis=-1, keepdims=True) + EPSILON)


def same_document(second_resets, row, col):
    return ((row // BLOCK) - (col // BLOCK)) * second_resets == 0


def lower_inverse(lowers, row, col):
    differ = row ^ col
    eye = (row == col).astype(F32)
    in_block = (differ < 8).astype(F32)
    diagonal = [low * in_block for low in lowers]
    powers = [d.astype(BF16) for d in diagonal]
    squares = [mul(p, p).astype(BF16) for p in powers]
    inverse = [eye - d for d in diagonal]
    stacked = [
        mul(jnp.concatenate([s, x.astype(BF16)], axis=0), s) for x, s in zip(inverse, squares)
    ]
    fourths = [both[:CHUNK].astype(BF16) for both in stacked]
    inverse = [x + both[CHUNK:] for x, both in zip(inverse, stacked)]
    inverse = [x + mul(x.astype(BF16), s) for x, s in zip(inverse, fourths)]
    size = 8
    while size < CHUNK:
        joint = odd_blocks(((differ >= size) & (differ < 2 * size)).astype(F32), size)
        rounded = [x.astype(BF16) for x in inverse]
        inner = [
            mul((odd_blocks(low, size) * joint).astype(BF16), x)
            for low, x in zip(lowers, rounded)
        ]
        outer = [
            mul(odd_blocks(x, size).astype(BF16), with_even_zeros(i, size).astype(BF16))
            for x, i in zip(inverse, inner)
        ]
        inverse = [less_in_odd(x, o, size) for x, o in zip(inverse, outer)]
        size *= 2
    return inverse


def odd_blocks(a, size):
    return jnp.concatenate([a[b : b + size] for b in range(size, a.shape[0], 2 * size)], axis=0)


def with_even_zeros(odd, size):
    zeros = jnp.zeros((size, odd.shape[1]), odd.dtype)
    pieces = []
    for b in range(0, odd.shape[0], size):
        pieces += [zeros, odd[b : b + size]]
    return jnp.concatenate(pieces, axis=0)


def less_in_odd(a, odd, size):
    pieces = []
    for b in range(0, odd.shape[0], size):
        pieces.append(a[2 * b : 2 * b + size])
        pieces.append(a[2 * b + size : 2 * b + 2 * size] - odd[b : b + size])
    return jnp.concatenate(pieces, axis=0)


def rims_kernel(*refs):
    *inputs, packed_ref, arrived = refs
    copies = []
    for i, x_ref in enumerate(inputs):
        last = x_ref.at[pl.ds(x_ref.shape[0] - RIM, RIM)]
        here = packed_ref.at[pl.ds(i * RIM, RIM)]
        copies.append(pltpu.make_async_copy(last, here, arrived.at[i]))
    for copy in copies:
        copy.start()
    for copy in copies:
        copy.wait()


def filters_kernel(key_ref, value_ref, taps_ref, unit_ref, value_out_ref, first_ref, padded):
    heads, length, _ = key_ref.shape
    for i, x_ref in enumerate((key_ref, value_ref)):
        padded[i, :, RIM:] = x_ref[...].astype(F32)
        padded[i, :, 0:RIM] = jnp.zeros((heads, RIM, padded.shape[3]), F32)
    first_ref[...] = padded[:, :, RIM : RIM + AGAIN]

    def one_head(h, carry):
        for i in range(2):
            taps = taps_of(taps_ref, 1 + i, h)
            for c in range(length // CHUNK):
                rows = filtered(padded.at[i, h], taps, c * CHUNK, CHUNK)
                if i == 0:
                    unit_ref[h, rows_of(c)] = unit(rows).astype(BF16)
                else:
                    value_out_ref[h, rows_of(c)] = rows.astype(BF16)
        return carry

    lax.fori_loop(0, heads, one_head, 0)


def maps_kernel(
    base, resets, unit_in_ref, value_in_ref, first_ref, rim_ref, taps_ref, decay_ref, strength_ref,
    unit_ref, solved_ref, starts_ref, *refs,
):
    *map_refs, rims, padded, value_s, step_s = refs
    heads, length, depth = unit_ref.shape
    chunks = length // CHUNK
    size = heads // len(map_refs)
    total_heads = decay_ref.shape[0]
    row, col = indices()
    rims[...] = rim_ref[...].astype(F32)
    for g in range(heads):
        h = base + g
        for c in range(1, chunks):
            unit_ref[g, rows_of(c)] = unit_in_ref[h, rows_of(c)]
        unit_ref[g, AGAIN:CHUNK] = unit_in_ref[h, AGAIN:CHUNK]
        value_s[g, AGAIN:CHUNK] = value_in_ref[h, AGAIN:CHUNK]
        for i in range(2):
            padded[g, i, 0:RIM] = rims[(1 + i) * RIM : (2 + i) * RIM, h, :]
            padded[g, i, RIM : RIM + AGAIN] = first_ref[i, h]
            rows = filtered(padded.at[g, i], taps_of(taps_ref, 1 + i, h), 0, AGAIN)
            if i == 0:
                unit_ref[g, 0:AGAIN] = unit(rows).astype(BF16)
            else:
                value_s[g, 0:AGAIN] = rows.astype(BF16)

    parts = []
    lowers = []
    for c in range(chunks):
        cum, _, columns = token_scalars(decay_ref, strength_ref, c)
        first, second = resets[2 * c], resets[2 * c + 1]
        strictly = (row > col) & same_document(second, row, col)
        for g in range(heads):
            h = base + g
            cum_col = columns[:, h : h + 1]
            cum_row = cum[h : h + 1]
            key = unit_in_ref[h, rows_of(c)] if c else unit_ref[g, rows_of(c)]
            fading = jnp.exp(jnp.where(strictly, cum_col - cum_row, FAR))
            strength_col = columns[:, total_heads + h : total_heads + h + 1]
            lowers.append(strength_col * fading * mul(key, key, NT))
            parts.append((g, c, first, second, cum_col, cum_row, strength_col))
    inverses = lower_inverse(lowers, row, col)
    eye = (row == col).astype(F32)
    first_rows = lax.broadcasted_iota(jnp.int32, (CHUNK, 1), 0) < BLOCK
    for (g, c, first, second, cum_col, cum_row, strength_col), inverse in zip(parts, inverses):
        keep_first = (1 - first).astype(F32)
        keep_second = (1 - second).astype(F32)
        keep_both = keep_first * keep_second
        h = base + g
        key = unit_in_ref[h, rows_of(c)] if c else unit_ref[g, rows_of(c)]
        value = value_in_ref[h, rows_of(c)] if c else value_s[g]
        growth = jnp.exp(cum_col) * jnp.where(first_rows, keep_first, keep_both)
        targets = jnp.concatenate(
            [
                (strength_col * growth) * key.astype(F32),
                strength_col * value.astype(F32),
            ],
            axis=1,
        )
        solved = targets + mul((inverse - eye).astype(BF16), targets.astype(BF16))
        solved_ref[g, rows_of(c)] = solved
        end = cum_row[:, CHUNK - 1 : CHUNK]
        tail = jnp.exp(end - cum_col) * jnp.where(first_rows, keep_second, 1.0)
        product = mul(key, (tail * solved).astype(BF16), TN)
        passed = jnp.exp(end) * keep_both
        step_s[g, c, :, :depth] = jnp.where(row == col, passed, 0.0) - product[:, :depth]
        step_s[g, c, :, depth:] = product[:, depth:]

    def compose(later, earlier):
        high, low = split(earlier)
        trans = later[:, :depth].astype(BF16)
        joined = mul(trans, high) + mul(trans, low)
        return jnp.concatenate([joined[:, :depth], joined[:, depth:] + later[:, depth:]], axis=1)

    every = range(heads)
    states = [step_s[g, 0] for g in every]
    half = chunks // 2
    for c in range(1, half):
        for g in every:
            starts_ref[g, c - 1] = states[g]
        states = [compose(step_s[g, c], states[g]) for g in every]
    rest = [step_s[g, half] for g in every]
    for c in range(half + 1, chunks):
        rest = [compose(step_s[g, c], rest[g]) for g in every]
    for g in every:
        map_refs[g // size][g % size] = compose(rest[g], states[g]).astype(BF16)
    for c in range(half, chunks):
        for g in every:
            starts_ref[g, c - 1] = states[g]
        if c + 1 < chunks:
            states = [compose(step_s[g, c], states[g]) for g in every]


def reads_kernel(
    base, resets, query_ref, gate_ref, gain_ref, rim_ref, taps_ref, decay_ref, strength_ref,
    unit_ref, solved_ref, starts_ref,
    reach_ref, part_ref, gating_ref,
    rims, padded,
):
    heads, length, depth = unit_ref.shape
    chunks = length // CHUNK
    row, col = indices()
    first_rows = lax.broadcasted_iota(jnp.int32, (CHUNK, 1), 0) < BLOCK
    rims[...] = rim_ref[...].astype(F32)
    for g in range(heads):
        h = base + g
        padded[g, 0:RIM] = rims[0:RIM, h, :]
        padded[g, RIM : RIM + length] = query_ref[h].astype(F32)

    for c in range(chunks):
        here = rows_of(c)
        cum, _, columns = token_scalars(decay_ref, strength_ref, c)
        first, second = resets[2 * c], resets[2 * c + 1]
        keep_first = (1 - first).astype(F32)
        keep_both = keep_first * (1 - second).astype(F32)
        upto = (row >= col) & same_document(second, row, col)
        for g in range(heads):
            h = base + g
            cum_col = columns[:, h : h + 1]
            filtered_rows = filtered(padded.at[g], taps_of(taps_ref, 0, h), c * CHUNK, CHUNK)
            query = (unit(filtered_rows) * depth**-0.5).astype(BF16)
            fading = jnp.exp(jnp.where(upto, cum_col - cum[h : h + 1], FAR))
            mixing = fading * mul(query, unit_ref[g, here], NT)
            own = mul_split(mixing, solved_ref[g, here])
            growth = jnp.exp(cum_col) * jnp.where(first_rows, keep_first, keep_both)
            reach = growth * query.astype(F32) - own[:, :depth]
            part = own[:, depth:]
            if c:
                both = mul_split(reach, starts_ref[g, c - 1])
                reach = both[:, :depth]
                part = part + both[:, depth:]
            reach_ref[g, here] = reach.astype(BF16)
            part_ref[g, here] = part
            gate = gate_ref[h, here].astype(F32)
            gating_ref[g, here] = gain_ref[...] * silu(gate)


def partner(place, k, count):
    if count & (count - 1) == 0:
        return place ^ k
    return lax.rem(place + count - k, count)


def pairs_at(k, count):
    if count & (count - 1) == 0:
        return [(i, i ^ k) for i in range(count)]
    return [(i, (i + k) % count) for i in range(count)]


def join_kernel(count, place, *refs):
    maps = refs[:count]
    before_ref, state_ref, *trans_ref, ordered = refs[count:]
    heads, depth, _ = before_ref.shape
    me = place[0]
    for k in range(count):
        ordered[partner(me, k, count)] = maps[k][...]
    row, col = indices()
    eye = (row == col).astype(F32)
    states = [jnp.concatenate([eye, jnp.zeros((depth, depth), F32)], axis=1)] * heads
    for lap in range(count):

        @pl.when(lap == me)
        def _():
            for h in range(heads):
                before_ref[h] = states[h]

        for h in range(heads):
            step = ordered[lap, h]
            if lap:
                high, low = split(states[h])
                trans = step[:, :depth]
                joined = mul(trans, high) + mul(trans, low)
                states[h] = jnp.concatenate(
                    [joined[:, :depth], joined[:, depth:] + step[:, depth:].astype(F32)], axis=1
                )
            else:
                states[h] = step.astype(F32)
    for h in range(heads):
        state_ref[h] = states[h][:, depth:].astype(state_ref.dtype)
        for ref in trans_ref:
            ref[h] = states[h][:, :depth]


def outputs_kernel(base, arrived_ref, before_ref, reach_ref, part_ref, gating_ref, normed_ref):
    heads, depth, _ = arrived_ref.shape
    for g in range(heads):
        h = base + g
        before = before_ref[g]
        incoming = mul_split(before[:, :depth], arrived_ref[g].astype(F32)) + before[:, depth:]
        high, low = split(incoming)
        for c in range(normed_ref.shape[0] // CHUNK):
            here = rows_of(c)
            reach = reach_ref[h, here]
            core = part_ref[h, here] + (mul(reach, high) + mul(reach, low))
            scale = lax.rsqrt(jnp.sum(core * core, axis=-1, keepdims=True) / depth + EPSILON)
            normed_ref[here, g * depth : (g + 1) * depth] = (
                core * scale * gating_ref[h, here]
            ).astype(BF16)


def last_kernel(section, total_ref, block_ref, weights_ref, out_ref, tiles, written):
    width = block_ref.shape[1]
    rows = weights_ref[pl.ds(pl.multiple_of(section[0] * width, width), width), :]
    copies = []
    for i in range(total_ref.shape[0] // CHUNK):
        here = rows_of(i)
        tiles[here] = (total_ref[here] + mul(block_ref[here], rows)).astype(BF16)
        copies.append(pltpu.make_async_copy(tiles.at[here], out_ref.at[here], written.at[i]))
        copies[-1].start()
    for copy in copies:
        copy.wait()


def from_behind(value, axis, steps):
    count = lax.axis_size(axis)
    return lax.ppermute(value, axis, [(i, i + steps) for i in range(count - steps)])


def exchange(own_map, later, leaves):
    received = [
        lax.ppermute(later if k == 1 else own_map, "leaf", pairs_at(k, leaves))
        for k in range(1, leaves)
    ]
    return [own_map] + received


VMEM = pl.BlockSpec(memory_space=pltpu.VMEM)
SMEM = pl.BlockSpec(memory_space=pltpu.SMEM)
HBM = pl.BlockSpec(memory_space=pltpu.HBM)
PARAMS = pltpu.CompilerParams(vmem_limit_bytes=8 * 1024 * 1024)
LAST_PARAMS = pltpu.CompilerParams(vmem_limit_bytes=12 * 1024 * 1024)


def pack_rims(inputs):
    _, heads, depth = inputs[0].shape
    return pl.pallas_call(
        rims_kernel,
        out_shape=jax.ShapeDtypeStruct((len(inputs) * RIM, heads, depth), BF16),
        in_specs=[HBM] * len(inputs),
        out_specs=VMEM,
        scratch_shapes=[pltpu.SemaphoreType.DMA((len(inputs),))],
        compiler_params=pltpu.CompilerParams(vmem_limit_bytes=65_700_000),
        cost_estimate=pl.CostEstimate(flops=4 * 10**9, bytes_accessed=2**16, transcendentals=0),
    )(*inputs)


def filters_of(key, value, taps):
    heads, length, depth = key.shape
    per_token = jax.ShapeDtypeStruct((heads, length, depth), BF16)
    return pl.pallas_call(
        filters_kernel,
        out_shape=(per_token, per_token, jax.ShapeDtypeStruct((2, heads, AGAIN, depth), F32)),
        in_specs=[VMEM] * 3,
        out_specs=[VMEM] * 3,
        scratch_shapes=[pltpu.VMEM((2, heads, length + RIM, depth), F32)],
        compiler_params=PARAMS,
        cost_estimate=pl.CostEstimate(
            flops=3 * 10**9, bytes_accessed=4 * 2**20, transcendentals=10**6
        ),
    )(key, value, taps)


def maps_of(base, heads, resets, unit_in, value_in, first, rims, taps, decay, strength):
    _, length, depth = unit_in.shape
    chunks = length // CHUNK
    return pl.pallas_call(
        functools.partial(maps_kernel, base),
        out_shape=(
            jax.ShapeDtypeStruct((heads, length, depth), BF16),
            jax.ShapeDtypeStruct((heads, length, 2 * depth), F32),
            jax.ShapeDtypeStruct((heads, chunks - 1, depth, 2 * depth), F32),
            *[jax.ShapeDtypeStruct((heads // GROUPS, depth, 2 * depth), BF16)] * GROUPS,
        ),
        in_specs=[SMEM] + [VMEM] * 7,
        out_specs=[VMEM] * (3 + GROUPS),
        scratch_shapes=[
            pltpu.VMEM(rims.shape, F32),
            pltpu.VMEM((heads, 2, RIM + AGAIN, depth), F32),
            pltpu.VMEM((heads, CHUNK, depth), BF16),
            pltpu.VMEM((heads, chunks, depth, 2 * depth), F32),
        ],
        compiler_params=PARAMS,
        cost_estimate=pl.CostEstimate(
            flops=5 * 10**9, bytes_accessed=4 * 2**20, transcendentals=10**6
        ),
    )(resets, unit_in, value_in, first, rims, taps, decay, strength)


def reads_of(base, heads, resets, query, gate, gain, rims, taps, decay, strength, made):
    _, length, depth = query.shape
    per_token = jax.ShapeDtypeStruct((heads, length, depth), F32)
    return pl.pallas_call(
        functools.partial(reads_kernel, base),
        out_shape=(jax.ShapeDtypeStruct(per_token.shape, BF16), per_token, per_token),
        in_specs=[SMEM] + [VMEM] * 10,
        out_specs=[VMEM] * 3,
        scratch_shapes=[
            pltpu.VMEM(rims.shape, F32),
            pltpu.VMEM((heads, length + RIM, depth), F32),
        ],
        compiler_params=PARAMS,
        cost_estimate=pl.CostEstimate(
            flops=3 * 10**9, bytes_accessed=4 * 2**20, transcendentals=10**6
        ),
    )(resets, query, gate, gain, rims, taps, decay, strength, *made)


def join(place, maps, links):
    count = len(maps)
    heads, depth, _ = maps[0].shape
    pair = jax.ShapeDtypeStruct((heads, depth, 2 * depth), F32)
    square = (heads, depth, depth)
    if links == 1:
        totals = (jax.ShapeDtypeStruct(square, BF16),)
    else:
        totals = (jax.ShapeDtypeStruct(square, F32),) * 2
    return pl.pallas_call(
        functools.partial(join_kernel, count),
        out_shape=(pair, *totals),
        in_specs=[SMEM] + [VMEM] * count,
        out_specs=[VMEM] * (1 + len(totals)),
        scratch_shapes=[pltpu.VMEM((count, heads, depth, 2 * depth), BF16)],
        compiler_params=PARAMS,
    )(place, *maps)


def outputs_of(base, arrived, before, reads):
    heads, depth, _ = arrived.shape
    length = reads[0].shape[1]
    return pl.pallas_call(
        functools.partial(outputs_kernel, base),
        out_shape=jax.ShapeDtypeStruct((length, heads * depth), BF16),
        in_specs=[VMEM] * 5,
        out_specs=VMEM,
        compiler_params=PARAMS,
    )(arrived, before, *reads)


def last_projected(section, total, block, weights):
    length, columns = total.shape
    return pl.pallas_call(
        last_kernel,
        out_shape=jax.ShapeDtypeStruct((length, columns), BF16),
        in_specs=[SMEM] + [VMEM] * 3,
        out_specs=pl.BlockSpec(memory_space=pl.ANY),
        scratch_shapes=[
            pltpu.VMEM((length, columns), BF16),
            pltpu.SemaphoreType.DMA((length // CHUNK,)),
        ],
        compiler_params=LAST_PARAMS,
    )(section.astype(jnp.int32).reshape(1), total, block, weights)


def after(first, *values):
    return lax.optimization_barrier((first, *values))[1:]


def on_device(
    query_in,
    key_in,
    value_in,
    gate_in,
    write_strength,
    log_decay,
    doc_resets,
    conv_weight,
    output_norm_gain,
    output_projection_weight,
):
    length, heads, depth = query_in.shape
    taps = conv_weight
    rims = from_behind(pack_rims((query_in, key_in, value_in)), ("chain", "leaf"), 1)
    key, value = (jnp.transpose(x, (1, 0, 2)) for x in (key_in, value_in))
    key, value, first = filters_of(key, value, taps)
    gain = output_norm_gain.reshape(1, depth)
    leaves = lax.axis_size("leaf")
    place = lax.axis_index("leaf").astype(jnp.int32).reshape(1)

    links = lax.axis_size("chain") - 1
    unit_key, solved, starts, *own_maps = maps_of(
        0, heads, doc_resets, key, value, first, rims, taps, log_decay, write_strength
    )
    query_in, gate_in = after(own_maps[-1], query_in, gate_in)
    query, gate = (jnp.transpose(x, (1, 0, 2)) for x in (query_in, gate_in))
    reads = reads_of(
        0, heads, doc_resets, query, gate, gain, rims, taps, log_decay, write_strength,
        (unit_key, solved, starts),
    )
    size = heads // GROUPS
    blocks = []
    exchanged = [exchange(own_maps[0], own_maps[0], leaves)]
    for g in range(GROUPS):
        earlier = blocks[-1] if blocks else reads[0]
        maps = after(earlier, *exchanged[g])
        before, state, *trans = join(place, maps, links)
        if g + 1 < GROUPS:
            own_map = own_maps[g + 1]
            exchanged.append(exchange(own_map, *after(state, own_map), leaves))
        arrived = from_behind(state.astype(BF16), "chain", 1)
        for _ in range(links - 1):
            passed = jnp.einsum(
                "hij,hjk->hik", trans[0], arrived.astype(F32), precision=lax.Precision.HIGHEST
            )
            arrived = from_behind((passed + state).astype(BF16), "chain", 1)
        blocks.append(outputs_of(g * size, arrived, before, reads))

    ring = lax.axis_size("head")
    mine = lax.axis_index("head")
    width = size * depth
    weights = output_projection_weight
    around = [(i, (i + 1) % ring) for i in range(ring)]
    sums = [None] * GROUPS
    for k in range(ring):
        owner = lax.rem(mine + ring - k, ring)
        last = k + 1 == ring
        following = blocks if last else [lax.ppermute(x, "head", around) for x in blocks]
        for g, block in enumerate(blocks):
            section = owner * GROUPS + g
            if last and g + 1 == GROUPS:
                return last_projected(section, sum(sums[1:], sums[0]), block, weights)
            rows = lax.dynamic_slice_in_dim(weights, section * width, width, 0)
            term = jnp.dot(block, rows, preferred_element_type=F32)
            sums[g] = term if sums[g] is None else sums[g] + term
        blocks = following


def solution(mesh):
    return jax.shard_map(
        on_device,
        mesh=mesh,
        in_specs=(
            P(("chain", "leaf"), "head", None),
            P(("chain", "leaf"), "head", None),
            P(("chain", "leaf"), "head", None),
            P(("chain", "leaf"), "head", None),
            P("head", ("chain", "leaf")),
            P("head", ("chain", "leaf")),
            P(("chain", "leaf")),
            P(None, None, "head", None),
            P(),
            P(None, "head"),
        ),
        out_specs=P(("chain", "leaf"), "head"),
        check_vma=False,
    )
```

```python
import functools

import jax
import jax.numpy as jnp
from jax import lax
from jax.experimental import pallas as pl
from jax.experimental.pallas import tpu as pltpu
from jax.sharding import PartitionSpec as P

BLOCK = 64
CHUNK = 128
GROUPS = 2
RIM = 8
EPSILON = 1e-06
FAR = -1e30
LARGE = 1e38
AGAIN = 16
F32 = jnp.float32
BF16 = jnp.bfloat16
NN = (((1,), (0,)), ((), ()))
NT = (((1,), (1,)), ((), ()))
TN = (((0,), (0,)), ((), ()))


def split(a):
    high = a.astype(BF16)
    return high, (a - high.astype(F32)).astype(BF16)


def mul(a, b, dims=NN):
    return lax.dot_general(a, b, dims, preferred_element_type=F32)


def mul_split(a, b):
    a_high, a_low = split(a)
    b_high, b_low = split(b)
    return mul(a_high, b_high) + (mul(a_low, b_high) + mul(a_high, b_low))


def rows_of(c):
    return slice(c * CHUNK, (c + 1) * CHUNK)


def indices():
    shape = (CHUNK, CHUNK)
    return (
        lax.broadcasted_iota(jnp.int32, shape, 0),
        lax.broadcasted_iota(jnp.int32, shape, 1),
    )


def token_scalars(decay_ref, strength_ref, c):
    row, col = indices()
    cum = lax.dot_general(
        decay_ref[:, rows_of(c)],
        (row <= col).astype(F32),
        NN,
        precision=lax.Precision.HIGHEST,
        preferred_element_type=F32,
    )
    strength = strength_ref[:, rows_of(c)]
    stacked = [cum, strength]
    missing = 8 - 2 * cum.shape[0]
    if missing > 0:
        stacked.append(jnp.zeros((missing, CHUNK), F32))
    return cum, strength, jnp.transpose(jnp.concatenate(stacked, axis=0))


def silu(x):
    below = jnp.minimum(1.0 + jnp.exp(-x), LARGE)
    inverse = pl.reciprocal(below, approx=True)
    return x * (inverse * (2.0 - below * inverse))


def filtered(padded, taps, begin, length):
    first = begin + RIM + 1 - len(taps)
    total = taps[0] * padded[first : first + length]
    for j in range(1, len(taps)):
        total = total + taps[j] * padded[first + j : first + j + length]
    return silu(total)


def taps_of(taps_ref, which, head):
    return [taps_ref[which, j, pl.ds(head, 1), :] for j in range(taps_ref.shape[1])]


def unit(rows):
    return rows * lax.rsqrt(jnp.sum(rows * rows, axis=-1, keepdims=True) + EPSILON)


def same_document(second_resets, row, col):
    return ((row // BLOCK) - (col // BLOCK)) * second_resets == 0


def lower_inverse(lowers, row, col):
    differ = row ^ col
    eye = (row == col).astype(F32)
    in_block = (differ < 8).astype(F32)
    diagonal = [low * in_block for low in lowers]
    powers = [d.astype(BF16) for d in diagonal]
    squares = [mul(p, p).astype(BF16) for p in powers]
    inverse = [eye - d for d in diagonal]
    stacked = [
        mul(jnp.concatenate([s, x.astype(BF16)], axis=0), s) for x, s in zip(inverse, squares)
    ]
    fourths = [both[:CHUNK].astype(BF16) for both in stacked]
    inverse = [x + both[CHUNK:] for x, both in zip(inverse, stacked)]
    inverse = [x + mul(x.astype(BF16), s) for x, s in zip(inverse, fourths)]
    size = 8
    while size < CHUNK:
        joint = odd_blocks(((differ >= size) & (differ < 2 * size)).astype(F32), size)
        rounded = [x.astype(BF16) for x in inverse]
        inner = [
            mul((odd_blocks(low, size) * joint).astype(BF16), x)
            for low, x in zip(lowers, rounded)
        ]
        outer = [
            mul(odd_blocks(x, size).astype(BF16), with_even_zeros(i, size).astype(BF16))
            for x, i in zip(inverse, inner)
        ]
        inverse = [less_in_odd(x, o, size) for x, o in zip(inverse, outer)]
        size *= 2
    return inverse


def odd_blocks(a, size):
    return jnp.concatenate([a[b : b + size] for b in range(size, a.shape[0], 2 * size)], axis=0)


def with_even_zeros(odd, size):
    zeros = jnp.zeros((size, odd.shape[1]), odd.dtype)
    pieces = []
    for b in range(0, odd.shape[0], size):
        pieces += [zeros, odd[b : b + size]]
    return jnp.concatenate(pieces, axis=0)


def less_in_odd(a, odd, size):
    pieces = []
    for b in range(0, odd.shape[0], size):
        pieces.append(a[2 * b : 2 * b + size])
        pieces.append(a[2 * b + size : 2 * b + 2 * size] - odd[b : b + size])
    return jnp.concatenate(pieces, axis=0)


def rims_kernel(*refs):
    *inputs, packed_ref, arrived = refs
    copies = []
    for i, x_ref in enumerate(inputs):
        last = x_ref.at[pl.ds(x_ref.shape[0] - RIM, RIM)]
        here = packed_ref.at[pl.ds(i * RIM, RIM)]
        copies.append(pltpu.make_async_copy(last, here, arrived.at[i]))
    for copy in copies:
        copy.start()
    for copy in copies:
        copy.wait()


def filters_kernel(key_ref, value_ref, taps_ref, unit_ref, value_out_ref, first_ref, padded):
    heads, length, _ = key_ref.shape
    for i, x_ref in enumerate((key_ref, value_ref)):
        padded[i, :, RIM:] = x_ref[...].astype(F32)
        padded[i, :, 0:RIM] = jnp.zeros((heads, RIM, padded.shape[3]), F32)
    first_ref[...] = padded[:, :, RIM : RIM + AGAIN]

    def one_head(h, carry):
        for i in range(2):
            taps = taps_of(taps_ref, 1 + i, h)
            for c in range(length // CHUNK):
                rows = filtered(padded.at[i, h], taps, c * CHUNK, CHUNK)
                if i == 0:
                    unit_ref[h, rows_of(c)] = unit(rows).astype(BF16)
                else:
                    value_out_ref[h, rows_of(c)] = rows.astype(BF16)
        return carry

    lax.fori_loop(0, heads, one_head, 0)


def maps_kernel(
    base, resets, unit_in_ref, value_in_ref, first_ref, rim_ref, taps_ref, decay_ref, strength_ref,
    *refs,
):
    *results, rims, padded, value_s, step_s = refs
    heads, length, depth = unit_in_ref.shape
    unit_refs, solved_refs, starts_refs, map_refs = (
        results[i * GROUPS : (i + 1) * GROUPS] for i in range(4)
    )
    chunks = length // CHUNK
    size = heads // GROUPS
    total_heads = decay_ref.shape[0]
    row, col = indices()
    rims[...] = rim_ref[...].astype(F32)
    for g in range(heads):
        h = base + g
        for c in range(1, chunks):
            unit_refs[g // size][g % size, rows_of(c)] = unit_in_ref[h, rows_of(c)]
        unit_refs[g // size][g % size, AGAIN:CHUNK] = unit_in_ref[h, AGAIN:CHUNK]
        value_s[g, AGAIN:CHUNK] = value_in_ref[h, AGAIN:CHUNK]
        for i in range(2):
            padded[g, i, 0:RIM] = rims[(1 + i) * RIM : (2 + i) * RIM, h, :]
            padded[g, i, RIM : RIM + AGAIN] = first_ref[i, h]
            rows = filtered(padded.at[g, i], taps_of(taps_ref, 1 + i, h), 0, AGAIN)
            if i == 0:
                unit_refs[g // size][g % size, 0:AGAIN] = unit(rows).astype(BF16)
            else:
                value_s[g, 0:AGAIN] = rows.astype(BF16)

    parts = []
    lowers = []
    for c in range(chunks):
        cum, _, columns = token_scalars(decay_ref, strength_ref, c)
        first, second = resets[2 * c], resets[2 * c + 1]
        strictly = (row > col) & same_document(second, row, col)
        for g in range(heads):
            h = base + g
            cum_col = columns[:, h : h + 1]
            cum_row = cum[h : h + 1]
            key = unit_in_ref[h, rows_of(c)] if c else unit_refs[g // size][g % size, rows_of(c)]
            fading = jnp.exp(jnp.where(strictly, cum_col - cum_row, FAR))
            strength_col = columns[:, total_heads + h : total_heads + h + 1]
            lowers.append(strength_col * fading * mul(key, key, NT))
            parts.append((g, c, first, second, cum_col, cum_row, strength_col))
    inverses = lower_inverse(lowers, row, col)
    eye = (row == col).astype(F32)
    first_rows = lax.broadcasted_iota(jnp.int32, (CHUNK, 1), 0) < BLOCK
    for (g, c, first, second, cum_col, cum_row, strength_col), inverse in zip(parts, inverses):
        keep_first = (1 - first).astype(F32)
        keep_second = (1 - second).astype(F32)
        keep_both = keep_first * keep_second
        h = base + g
        key = unit_in_ref[h, rows_of(c)] if c else unit_refs[g // size][g % size, rows_of(c)]
        value = value_in_ref[h, rows_of(c)] if c else value_s[g]
        growth = jnp.exp(cum_col) * jnp.where(first_rows, keep_first, keep_both)
        targets = jnp.concatenate(
            [
                (strength_col * growth) * key.astype(F32),
                strength_col * value.astype(F32),
            ],
            axis=1,
        )
        solved = targets + mul((inverse - eye).astype(BF16), targets.astype(BF16))
        solved_refs[g // size][g % size, rows_of(c)] = solved
        end = cum_row[:, CHUNK - 1 : CHUNK]
        tail = jnp.exp(end - cum_col) * jnp.where(first_rows, keep_second, 1.0)
        product = mul(key, (tail * solved).astype(BF16), TN)
        passed = jnp.exp(end) * keep_both
        step_s[g, c, :, :depth] = jnp.where(row == col, passed, 0.0) - product[:, :depth]
        step_s[g, c, :, depth:] = product[:, depth:]

    def compose(later, earlier):
        high, low = split(earlier)
        trans = later[:, :depth].astype(BF16)
        joined = mul(trans, high) + mul(trans, low)
        return jnp.concatenate([joined[:, :depth], joined[:, depth:] + later[:, depth:]], axis=1)

    every = range(heads)
    states = [step_s[g, 0] for g in every]
    half = chunks // 2
    for c in range(1, half):
        for g in every:
            starts_refs[g // size][g % size, c - 1] = states[g]
        states = [compose(step_s[g, c], states[g]) for g in every]
    rest = [step_s[g, half] for g in every]
    for c in range(half + 1, chunks):
        rest = [compose(step_s[g, c], rest[g]) for g in every]
    for g in every:
        map_refs[g // size][g % size] = compose(rest[g], states[g]).astype(BF16)
    for c in range(half, chunks):
        for g in every:
            starts_refs[g // size][g % size, c - 1] = states[g]
        if c + 1 < chunks:
            states = [compose(step_s[g, c], states[g]) for g in every]


def reads_kernel(
    base, resets, query_ref, gate_ref, gain_ref, rim_ref, taps_ref, decay_ref, strength_ref,
    unit_ref, solved_ref, starts_ref,
    reach_ref, part_ref, gating_ref,
    rims, padded,
):
    heads, length, depth = unit_ref.shape
    chunks = length // CHUNK
    row, col = indices()
    first_rows = lax.broadcasted_iota(jnp.int32, (CHUNK, 1), 0) < BLOCK
    rims[...] = rim_ref[...].astype(F32)
    for g in range(heads):
        h = base + g
        padded[g, 0:RIM] = rims[0:RIM, h, :]
        padded[g, RIM : RIM + length] = query_ref[h].astype(F32)

    for c in range(chunks):
        here = rows_of(c)
        cum, _, columns = token_scalars(decay_ref, strength_ref, c)
        first, second = resets[2 * c], resets[2 * c + 1]
        keep_first = (1 - first).astype(F32)
        keep_both = keep_first * (1 - second).astype(F32)
        upto = (row >= col) & same_document(second, row, col)
        for g in range(heads):
            h = base + g
            cum_col = columns[:, h : h + 1]
            filtered_rows = filtered(padded.at[g], taps_of(taps_ref, 0, h), c * CHUNK, CHUNK)
            query = (unit(filtered_rows) * depth**-0.5).astype(BF16)
            fading = jnp.exp(jnp.where(upto, cum_col - cum[h : h + 1], FAR))
            mixing = fading * mul(query, unit_ref[g, here], NT)
            own = mul_split(mixing, solved_ref[g, here])
            growth = jnp.exp(cum_col) * jnp.where(first_rows, keep_first, keep_both)
            reach = growth * query.astype(F32) - own[:, :depth]
            part = own[:, depth:]
            if c:
                both = mul_split(reach, starts_ref[g, c - 1])
                reach = both[:, :depth]
                part = part + both[:, depth:]
            reach_ref[g, here] = reach.astype(BF16)
            part_ref[g, here] = part
            gate = gate_ref[h, here].astype(F32)
            gating_ref[g, here] = gain_ref[...] * silu(gate)


def partner(place, k, count):
    if count & (count - 1) == 0:
        return place ^ k
    return lax.rem(place + count - k, count)


def pairs_at(k, count):
    if count & (count - 1) == 0:
        return [(i, i ^ k) for i in range(count)]
    return [(i, (i + k) % count) for i in range(count)]


def join_kernel(count, place, *refs):
    maps = refs[:count]
    before_ref, state_ref, *trans_ref, ordered = refs[count:]
    heads, depth, _ = before_ref.shape
    me = place[0]
    for k in range(count):
        ordered[partner(me, k, count)] = maps[k][...]
    row, col = indices()
    eye = (row == col).astype(F32)
    states = [jnp.concatenate([eye, jnp.zeros((depth, depth), F32)], axis=1)] * heads
    for lap in range(count):

        @pl.when(lap == me)
        def _():
            for h in range(heads):
                before_ref[h] = states[h]

        for h in range(heads):
            step = ordered[lap, h]
            if lap:
                high, low = split(states[h])
                trans = step[:, :depth]
                joined = mul(trans, high) + mul(trans, low)
                states[h] = jnp.concatenate(
                    [joined[:, :depth], joined[:, depth:] + step[:, depth:].astype(F32)], axis=1
                )
            else:
                states[h] = step.astype(F32)
    for h in range(heads):
        state_ref[h] = states[h][:, depth:].astype(state_ref.dtype)
        for ref in trans_ref:
            ref[h] = states[h][:, :depth]


def outputs_kernel(base, arrived_ref, before_ref, reach_ref, part_ref, gating_ref, normed_ref):
    heads, depth, _ = arrived_ref.shape
    for g in range(heads):
        h = base + g
        before = before_ref[g]
        incoming = mul_split(before[:, :depth], arrived_ref[g].astype(F32)) + before[:, depth:]
        high, low = split(incoming)
        for c in range(normed_ref.shape[0] // CHUNK):
            here = rows_of(c)
            reach = reach_ref[h, here]
            core = part_ref[h, here] + (mul(reach, high) + mul(reach, low))
            scale = lax.rsqrt(jnp.sum(core * core, axis=-1, keepdims=True) / depth + EPSILON)
            normed_ref[here, g * depth : (g + 1) * depth] = (
                core * scale * gating_ref[h, here]
            ).astype(BF16)


def last_kernel(section, first_ref, second_ref, block_ref, weights_ref, out_ref, tiles, written):
    width = block_ref.shape[1]
    rows = weights_ref[pl.ds(pl.multiple_of(section[0] * width, width), width), :]
    copies = []
    for i in range(first_ref.shape[0] // CHUNK):
        here = rows_of(i)
        total = (first_ref[here] + second_ref[here]) + mul(block_ref[here], rows)
        tiles[here] = total.astype(BF16)
        copies.append(pltpu.make_async_copy(tiles.at[here], out_ref.at[here], written.at[i]))
        copies[-1].start()
    for copy in copies:
        copy.wait()


def from_behind(value, axis, steps):
    count = lax.axis_size(axis)
    return lax.ppermute(value, axis, [(i, i + steps) for i in range(count - steps)])


def exchange(own_map, later, leaves):
    received = [
        lax.ppermute(later if k == 1 else own_map, "leaf", pairs_at(k, leaves))
        for k in range(1, leaves)
    ]
    return [own_map] + received


VMEM = pl.BlockSpec(memory_space=pltpu.VMEM)
SMEM = pl.BlockSpec(memory_space=pltpu.SMEM)
HBM = pl.BlockSpec(memory_space=pltpu.HBM)
PARAMS = pltpu.CompilerParams(vmem_limit_bytes=8 * 1024 * 1024)
LAST_PARAMS = pltpu.CompilerParams(vmem_limit_bytes=12 * 1024 * 1024)


def pack_rims(inputs):
    _, heads, depth = inputs[0].shape
    return pl.pallas_call(
        rims_kernel,
        out_shape=jax.ShapeDtypeStruct((len(inputs) * RIM, heads, depth), BF16),
        in_specs=[HBM] * len(inputs),
        out_specs=VMEM,
        scratch_shapes=[pltpu.SemaphoreType.DMA((len(inputs),))],
        compiler_params=pltpu.CompilerParams(vmem_limit_bytes=65_700_000),
        cost_estimate=pl.CostEstimate(flops=10**9, bytes_accessed=2**16, transcendentals=0),
    )(*inputs)


def filters_of(key, value, taps):
    heads, length, depth = key.shape
    per_token = jax.ShapeDtypeStruct((heads, length, depth), BF16)
    return pl.pallas_call(
        filters_kernel,
        out_shape=(per_token, per_token, jax.ShapeDtypeStruct((2, heads, AGAIN, depth), F32)),
        in_specs=[VMEM] * 3,
        out_specs=[VMEM] * 3,
        scratch_shapes=[pltpu.VMEM((2, heads, length + RIM, depth), F32)],
        compiler_params=PARAMS,
        cost_estimate=pl.CostEstimate(
            flops=3 * 10**9, bytes_accessed=4 * 2**20, transcendentals=10**6
        ),
    )(key, value, taps)


def maps_of(base, heads, resets, unit_in, value_in, first, rims, taps, decay, strength):
    _, length, depth = unit_in.shape
    chunks = length // CHUNK
    size = heads // GROUPS
    return pl.pallas_call(
        functools.partial(maps_kernel, base),
        out_shape=(
            *[jax.ShapeDtypeStruct((size, length, depth), BF16)] * GROUPS,
            *[jax.ShapeDtypeStruct((size, length, 2 * depth), F32)] * GROUPS,
            *[jax.ShapeDtypeStruct((size, chunks - 1, depth, 2 * depth), F32)] * GROUPS,
            *[jax.ShapeDtypeStruct((size, depth, 2 * depth), BF16)] * GROUPS,
        ),
        in_specs=[SMEM] + [VMEM] * 7,
        out_specs=[VMEM] * (4 * GROUPS),
        scratch_shapes=[
            pltpu.VMEM(rims.shape, F32),
            pltpu.VMEM((heads, 2, RIM + AGAIN, depth), F32),
            pltpu.VMEM((heads, CHUNK, depth), BF16),
            pltpu.VMEM((heads, chunks, depth, 2 * depth), F32),
        ],
        compiler_params=PARAMS,
        cost_estimate=pl.CostEstimate(
            flops=5 * 10**9, bytes_accessed=4 * 2**20, transcendentals=10**6
        ),
    )(resets, unit_in, value_in, first, rims, taps, decay, strength)


def reads_of(base, heads, resets, query, gate, gain, rims, taps, decay, strength, made):
    _, length, depth = query.shape
    per_token = jax.ShapeDtypeStruct((heads, length, depth), F32)
    return pl.pallas_call(
        functools.partial(reads_kernel, base),
        out_shape=(jax.ShapeDtypeStruct(per_token.shape, BF16), per_token, per_token),
        in_specs=[SMEM] + [VMEM] * 10,
        out_specs=[VMEM] * 3,
        scratch_shapes=[
            pltpu.VMEM(rims.shape, F32),
            pltpu.VMEM((heads, length + RIM, depth), F32),
        ],
        compiler_params=PARAMS,
        cost_estimate=pl.CostEstimate(
            flops=3 * 10**9, bytes_accessed=4 * 2**20, transcendentals=10**6
        ),
    )(resets, query, gate, gain, rims, taps, decay, strength, *made)


def join(place, maps, links):
    count = len(maps)
    heads, depth, _ = maps[0].shape
    pair = jax.ShapeDtypeStruct((heads, depth, 2 * depth), F32)
    square = (heads, depth, depth)
    if links == 1:
        totals = (jax.ShapeDtypeStruct(square, BF16),)
    else:
        totals = (jax.ShapeDtypeStruct(square, F32),) * 2
    return pl.pallas_call(
        functools.partial(join_kernel, count),
        out_shape=(pair, *totals),
        in_specs=[SMEM] + [VMEM] * count,
        out_specs=[VMEM] * (1 + len(totals)),
        scratch_shapes=[pltpu.VMEM((count, heads, depth, 2 * depth), BF16)],
        compiler_params=PARAMS,
    )(place, *maps)


def outputs_of(base, arrived, before, reads):
    heads, depth, _ = arrived.shape
    length = reads[0].shape[1]
    return pl.pallas_call(
        functools.partial(outputs_kernel, base),
        out_shape=jax.ShapeDtypeStruct((length, heads * depth), BF16),
        in_specs=[VMEM] * 5,
        out_specs=VMEM,
        compiler_params=PARAMS,
    )(arrived, before, *reads)


def last_projected(section, first, second, block, weights):
    length, columns = first.shape
    return pl.pallas_call(
        last_kernel,
        out_shape=jax.ShapeDtypeStruct((length, columns), BF16),
        in_specs=[SMEM] + [VMEM] * 4,
        out_specs=pl.BlockSpec(memory_space=pl.ANY),
        scratch_shapes=[
            pltpu.VMEM((length, columns), BF16),
            pltpu.SemaphoreType.DMA((length // CHUNK,)),
        ],
        compiler_params=LAST_PARAMS,
    )(section.astype(jnp.int32).reshape(1), first, second, block, weights)


def after(first, *values):
    return lax.optimization_barrier((first, *values))[1:]


def on_device(
    query_in,
    key_in,
    value_in,
    gate_in,
    write_strength,
    log_decay,
    doc_resets,
    conv_weight,
    output_norm_gain,
    output_projection_weight,
):
    length, heads, depth = query_in.shape
    taps = conv_weight
    rims = from_behind(pack_rims((query_in, key_in, value_in)), ("chain", "leaf"), 1)
    key, value = (jnp.transpose(x, (1, 0, 2)) for x in (key_in, value_in))
    key, value, first = filters_of(key, value, taps)
    gain = output_norm_gain.reshape(1, depth)
    leaves = lax.axis_size("leaf")
    place = lax.axis_index("leaf").astype(jnp.int32).reshape(1)

    links = lax.axis_size("chain") - 1
    made = maps_of(0, heads, doc_resets, key, value, first, rims, taps, log_decay, write_strength)
    own_maps = made[3 * GROUPS :]
    size = heads // GROUPS
    query_in, gate_in = after(own_maps[-1], query_in, gate_in)
    query, gate = (jnp.transpose(x, (1, 0, 2)) for x in (query_in, gate_in))
    exchanged = exchange(own_maps[0], own_maps[0], leaves)
    blocks = []
    for g in range(GROUPS):
        reads = reads_of(
            g * size, size, doc_resets, query, gate, gain, rims, taps, log_decay, write_strength,
            made[g : 3 * GROUPS : GROUPS],
        )
        maps = after(blocks[-1] if blocks else reads[0], *exchanged)
        before, state, *trans = join(place, maps, links)
        if g + 1 < GROUPS:
            own_map = own_maps[g + 1]
            exchanged = exchange(*after(reads[0], own_map), *after(state, own_map), leaves)
        arrived = from_behind(state.astype(BF16), "chain", 1)
        for _ in range(links - 1):
            passed = jnp.einsum(
                "hij,hjk->hik", trans[0], arrived.astype(F32), precision=lax.Precision.HIGHEST
            )
            arrived = from_behind((passed + state).astype(BF16), "chain", 1)
        blocks.append(outputs_of(0, arrived, before, reads))
        query, gate = after(blocks[-1], query, gate)

    ring = lax.axis_size("head")
    mine = lax.axis_index("head")
    width = size * depth
    weights = output_projection_weight
    around = [(i, (i + 1) % ring) for i in range(ring)]
    sums = [None] * GROUPS
    for k in range(ring):
        owner = lax.rem(mine + ring - k, ring)
        last = k + 1 == ring
        following = blocks if last else [lax.ppermute(x, "head", around) for x in blocks]
        if k == 0:
            blocks[:-1] = after(following[-1], *blocks[:-1])
        for g, block in enumerate(blocks):
            section = owner * GROUPS + g
            if last and g + 1 == GROUPS:
                return last_projected(section, *sums, block, weights)
            rows = lax.dynamic_slice_in_dim(weights, section * width, width, 0)
            term = jnp.dot(block, rows, preferred_element_type=F32)
            sums[g] = term if sums[g] is None else sums[g] + term
        blocks = following


def solution(mesh):
    return jax.shard_map(
        on_device,
        mesh=mesh,
        in_specs=(
            P(("chain", "leaf"), "head", None),
            P(("chain", "leaf"), "head", None),
            P(("chain", "leaf"), "head", None),
            P(("chain", "leaf"), "head", None),
            P("head", ("chain", "leaf")),
            P("head", ("chain", "leaf")),
            P(("chain", "leaf")),
            P(None, None, "head", None),
            P(),
            P(None, "head"),
        ),
        out_specs=P(("chain", "leaf"), "head"),
        check_vma=False,
    )
```

```python
import functools

import jax
import jax.numpy as jnp
from jax import lax
from jax.experimental import pallas as pl
from jax.experimental.pallas import tpu as pltpu
from jax.sharding import PartitionSpec as P

BLOCK = 64
CHUNK = 128
GROUPS = 2
RIM = 8
EPSILON = 1e-06
FAR = -1e30
LARGE = 1e38
AGAIN = 16
TILE = 256
F32 = jnp.float32
BF16 = jnp.bfloat16
NN = (((1,), (0,)), ((), ()))
NT = (((1,), (1,)), ((), ()))
TN = (((0,), (0,)), ((), ()))


def split(a):
    high = a.astype(BF16)
    return high, (a - high.astype(F32)).astype(BF16)


def mul(a, b, dims=NN):
    return lax.dot_general(a, b, dims, preferred_element_type=F32)


def mul_split(a, b):
    a_high, a_low = split(a)
    b_high, b_low = split(b)
    return mul(a_high, b_high) + (mul(a_low, b_high) + mul(a_high, b_low))


def rows_of(c):
    return slice(c * CHUNK, (c + 1) * CHUNK)


def indices():
    shape = (CHUNK, CHUNK)
    return (
        lax.broadcasted_iota(jnp.int32, shape, 0),
        lax.broadcasted_iota(jnp.int32, shape, 1),
    )


def token_scalars(decay_ref, strength_ref, c):
    row, col = indices()
    cum = lax.dot_general(
        decay_ref[:, rows_of(c)],
        (row <= col).astype(F32),
        NN,
        precision=lax.Precision.HIGHEST,
        preferred_element_type=F32,
    )
    strength = strength_ref[:, rows_of(c)]
    stacked = [cum, strength]
    missing = 8 - 2 * cum.shape[0]
    if missing > 0:
        stacked.append(jnp.zeros((missing, CHUNK), F32))
    return cum, strength, jnp.transpose(jnp.concatenate(stacked, axis=0))


def silu(x):
    below = jnp.minimum(1.0 + jnp.exp(-x), LARGE)
    inverse = pl.reciprocal(below, approx=True)
    return x * (inverse * (2.0 - below * inverse))


def filtered(padded, taps, begin, length):
    first = begin + RIM + 1 - len(taps)
    total = taps[0] * padded[first : first + length]
    for j in range(1, len(taps)):
        total = total + taps[j] * padded[first + j : first + j + length]
    return silu(total)


def taps_of(taps_ref, which, head):
    return [taps_ref[which, j, pl.ds(head, 1), :] for j in range(taps_ref.shape[1])]


def unit(rows):
    return rows * lax.rsqrt(jnp.sum(rows * rows, axis=-1, keepdims=True) + EPSILON)


def same_document(second_resets, row, col):
    return ((row // BLOCK) - (col // BLOCK)) * second_resets == 0


def lower_inverse(lowers, row, col):
    differ = row ^ col
    eye = (row == col).astype(F32)
    in_block = (differ < 8).astype(F32)
    diagonal = [low * in_block for low in lowers]
    powers = [d.astype(BF16) for d in diagonal]
    squares = [mul(p, p).astype(BF16) for p in powers]
    inverse = [eye - d for d in diagonal]
    stacked = [
        mul(jnp.concatenate([s, x.astype(BF16)], axis=0), s) for x, s in zip(inverse, squares)
    ]
    fourths = [both[:CHUNK].astype(BF16) for both in stacked]
    inverse = [x + both[CHUNK:] for x, both in zip(inverse, stacked)]
    inverse = [x + mul(x.astype(BF16), s) for x, s in zip(inverse, fourths)]
    size = 8
    while size < CHUNK:
        joint = odd_blocks(((differ >= size) & (differ < 2 * size)).astype(F32), size)
        rounded = [x.astype(BF16) for x in inverse]
        inner = [
            mul((odd_blocks(low, size) * joint).astype(BF16), x)
            for low, x in zip(lowers, rounded)
        ]
        outer = [
            mul(odd_blocks(x, size).astype(BF16), with_even_zeros(i, size).astype(BF16))
            for x, i in zip(inverse, inner)
        ]
        inverse = [less_in_odd(x, o, size) for x, o in zip(inverse, outer)]
        size *= 2
    return inverse


def odd_blocks(a, size):
    return jnp.concatenate([a[b : b + size] for b in range(size, a.shape[0], 2 * size)], axis=0)


def with_even_zeros(odd, size):
    zeros = jnp.zeros((size, odd.shape[1]), odd.dtype)
    pieces = []
    for b in range(0, odd.shape[0], size):
        pieces += [zeros, odd[b : b + size]]
    return jnp.concatenate(pieces, axis=0)


def less_in_odd(a, odd, size):
    pieces = []
    for b in range(0, odd.shape[0], size):
        pieces.append(a[2 * b : 2 * b + size])
        pieces.append(a[2 * b + size : 2 * b + 2 * size] - odd[b : b + size])
    return jnp.concatenate(pieces, axis=0)


def rims_kernel(*refs):
    *inputs, packed_ref, arrived = refs
    copies = []
    for i, x_ref in enumerate(inputs):
        last = x_ref.at[pl.ds(x_ref.shape[0] - RIM, RIM)]
        here = packed_ref.at[pl.ds(i * RIM, RIM)]
        copies.append(pltpu.make_async_copy(last, here, arrived.at[i]))
    for copy in copies:
        copy.start()
    for copy in copies:
        copy.wait()


def filters_kernel(key_ref, value_ref, taps_ref, unit_ref, value_out_ref, first_ref, padded):
    heads, length, _ = key_ref.shape
    for i, x_ref in enumerate((key_ref, value_ref)):
        padded[i, :, RIM:] = x_ref[...].astype(F32)
        padded[i, :, 0:RIM] = jnp.zeros((heads, RIM, padded.shape[3]), F32)
    first_ref[...] = padded[:, :, RIM : RIM + AGAIN]

    def one_head(h, carry):
        for i in range(2):
            taps = taps_of(taps_ref, 1 + i, h)
            for c in range(length // CHUNK):
                rows = filtered(padded.at[i, h], taps, c * CHUNK, CHUNK)
                if i == 0:
                    unit_ref[h, rows_of(c)] = unit(rows).astype(BF16)
                else:
                    value_out_ref[h, rows_of(c)] = rows.astype(BF16)
        return carry

    lax.fori_loop(0, heads, one_head, 0)


def maps_kernel(
    base, resets, unit_in_ref, value_in_ref, first_ref, rim_ref, taps_ref, decay_ref, strength_ref,
    unit_ref, solved_ref, starts_ref, *refs,
):
    *map_refs, rims, padded, value_s, step_s = refs
    heads, length, depth = unit_ref.shape
    chunks = length // CHUNK
    size = heads // len(map_refs)
    total_heads = decay_ref.shape[0]
    row, col = indices()
    rims[...] = rim_ref[...].astype(F32)
    for g in range(heads):
        h = base + g
        for c in range(1, chunks):
            unit_ref[g, rows_of(c)] = unit_in_ref[h, rows_of(c)]
        unit_ref[g, AGAIN:CHUNK] = unit_in_ref[h, AGAIN:CHUNK]
        value_s[g, AGAIN:CHUNK] = value_in_ref[h, AGAIN:CHUNK]
        for i in range(2):
            padded[g, i, 0:RIM] = rims[(1 + i) * RIM : (2 + i) * RIM, h, :]
            padded[g, i, RIM : RIM + AGAIN] = first_ref[i, h]
            rows = filtered(padded.at[g, i], taps_of(taps_ref, 1 + i, h), 0, AGAIN)
            if i == 0:
                unit_ref[g, 0:AGAIN] = unit(rows).astype(BF16)
            else:
                value_s[g, 0:AGAIN] = rows.astype(BF16)

    parts = []
    lowers = []
    for c in range(chunks):
        cum, _, columns = token_scalars(decay_ref, strength_ref, c)
        first, second = resets[2 * c], resets[2 * c + 1]
        strictly = (row > col) & same_document(second, row, col)
        for g in range(heads):
            h = base + g
            cum_col = columns[:, h : h + 1]
            cum_row = cum[h : h + 1]
            key = unit_in_ref[h, rows_of(c)] if c else unit_ref[g, rows_of(c)]
            fading = jnp.exp(jnp.where(strictly, cum_col - cum_row, FAR))
            strength_col = columns[:, total_heads + h : total_heads + h + 1]
            lowers.append(strength_col * fading * mul(key, key, NT))
            parts.append((g, c, first, second, cum_col, cum_row, strength_col))
    inverses = lower_inverse(lowers, row, col)
    eye = (row == col).astype(F32)
    first_rows = lax.broadcasted_iota(jnp.int32, (CHUNK, 1), 0) < BLOCK
    for (g, c, first, second, cum_col, cum_row, strength_col), inverse in zip(parts, inverses):
        keep_first = (1 - first).astype(F32)
        keep_second = (1 - second).astype(F32)
        keep_both = keep_first * keep_second
        h = base + g
        key = unit_in_ref[h, rows_of(c)] if c else unit_ref[g, rows_of(c)]
        value = value_in_ref[h, rows_of(c)] if c else value_s[g]
        growth = jnp.exp(cum_col) * jnp.where(first_rows, keep_first, keep_both)
        targets = jnp.concatenate(
            [
                (strength_col * growth) * key.astype(F32),
                strength_col * value.astype(F32),
            ],
            axis=1,
        )
        solved = targets + mul((inverse - eye).astype(BF16), targets.astype(BF16))
        solved_ref[g, rows_of(c)] = solved
        end = cum_row[:, CHUNK - 1 : CHUNK]
        tail = jnp.exp(end - cum_col) * jnp.where(first_rows, keep_second, 1.0)
        product = mul(key, (tail * solved).astype(BF16), TN)
        passed = jnp.exp(end) * keep_both
        step_s[g, c, :, :depth] = jnp.where(row == col, passed, 0.0) - product[:, :depth]
        step_s[g, c, :, depth:] = product[:, depth:]

    def compose(later, earlier):
        high, low = split(earlier)
        trans = later[:, :depth].astype(BF16)
        joined = mul(trans, high) + mul(trans, low)
        return jnp.concatenate([joined[:, :depth], joined[:, depth:] + later[:, depth:]], axis=1)

    every = range(heads)
    states = [step_s[g, 0] for g in every]
    half = chunks // 2
    for c in range(1, half):
        for g in every:
            starts_ref[g, c - 1] = states[g]
        states = [compose(step_s[g, c], states[g]) for g in every]
    rest = [step_s[g, half] for g in every]
    for c in range(half + 1, chunks):
        rest = [compose(step_s[g, c], rest[g]) for g in every]
    for g in every:
        map_refs[g // size][g % size] = compose(rest[g], states[g]).astype(BF16)
    for c in range(half, chunks):
        for g in every:
            starts_ref[g, c - 1] = states[g]
        if c + 1 < chunks:
            states = [compose(step_s[g, c], states[g]) for g in every]


def reads_kernel(
    base, resets, query_ref, gate_ref, gain_ref, rim_ref, taps_ref, decay_ref, strength_ref,
    unit_ref, solved_ref, starts_ref,
    reach_ref, part_ref, gating_ref,
    rims, padded,
):
    heads, length, depth = unit_ref.shape
    chunks = length // CHUNK
    row, col = indices()
    first_rows = lax.broadcasted_iota(jnp.int32, (CHUNK, 1), 0) < BLOCK
    rims[...] = rim_ref[...].astype(F32)
    for g in range(heads):
        h = base + g
        padded[g, 0:RIM] = rims[0:RIM, h, :]
        padded[g, RIM : RIM + length] = query_ref[h].astype(F32)

    for c in range(chunks):
        here = rows_of(c)
        cum, _, columns = token_scalars(decay_ref, strength_ref, c)
        first, second = resets[2 * c], resets[2 * c + 1]
        keep_first = (1 - first).astype(F32)
        keep_both = keep_first * (1 - second).astype(F32)
        upto = (row >= col) & same_document(second, row, col)
        for g in range(heads):
            h = base + g
            cum_col = columns[:, h : h + 1]
            filtered_rows = filtered(padded.at[g], taps_of(taps_ref, 0, h), c * CHUNK, CHUNK)
            query = (unit(filtered_rows) * depth**-0.5).astype(BF16)
            fading = jnp.exp(jnp.where(upto, cum_col - cum[h : h + 1], FAR))
            mixing = fading * mul(query, unit_ref[g, here], NT)
            own = mul_split(mixing, solved_ref[g, here])
            growth = jnp.exp(cum_col) * jnp.where(first_rows, keep_first, keep_both)
            reach = growth * query.astype(F32) - own[:, :depth]
            part = own[:, depth:]
            if c:
                both = mul_split(reach, starts_ref[g, c - 1])
                reach = both[:, :depth]
                part = part + both[:, depth:]
            reach_ref[g, here] = reach.astype(BF16)
            part_ref[g, here] = part
            gate = gate_ref[h, here].astype(F32)
            gating_ref[g, here] = gain_ref[...] * silu(gate)


def partner(place, k, count):
    if count & (count - 1) == 0:
        return place ^ k
    return lax.rem(place + count - k, count)


def pairs_at(k, count):
    if count & (count - 1) == 0:
        return [(i, i ^ k) for i in range(count)]
    return [(i, (i + k) % count) for i in range(count)]


def join_kernel(count, place, *refs):
    maps = refs[:count]
    before_ref, state_ref, *trans_ref, ordered = refs[count:]
    heads, depth, _ = before_ref.shape
    me = place[0]
    for k in range(count):
        ordered[partner(me, k, count)] = maps[k][...]
    row, col = indices()
    eye = (row == col).astype(F32)
    states = [jnp.concatenate([eye, jnp.zeros((depth, depth), F32)], axis=1)] * heads
    for lap in range(count):

        @pl.when(lap == me)
        def _():
            for h in range(heads):
                before_ref[h] = states[h]

        for h in range(heads):
            step = ordered[lap, h]
            if lap:
                high, low = split(states[h])
                trans = step[:, :depth]
                joined = mul(trans, high) + mul(trans, low)
                states[h] = jnp.concatenate(
                    [joined[:, :depth], joined[:, depth:] + step[:, depth:].astype(F32)], axis=1
                )
            else:
                states[h] = step.astype(F32)
    for h in range(heads):
        state_ref[h] = states[h][:, depth:].astype(state_ref.dtype)
        for ref in trans_ref:
            ref[h] = states[h][:, :depth]


def outputs_kernel(base, arrived_ref, before_ref, reach_ref, part_ref, gating_ref, normed_ref):
    heads, depth, _ = arrived_ref.shape
    for g in range(heads):
        h = base + g
        before = before_ref[g]
        incoming = mul_split(before[:, :depth], arrived_ref[g].astype(F32)) + before[:, depth:]
        high, low = split(incoming)
        reach = reach_ref[h]
        reached = mul(reach, high) + mul(reach, low)
        for c in range(normed_ref.shape[0] // CHUNK):
            here = rows_of(c)
            core = part_ref[h, here] + reached[here]
            scale = lax.rsqrt(jnp.sum(core * core, axis=-1, keepdims=True) / depth + EPSILON)
            normed_ref[here, g * depth : (g + 1) * depth] = (
                core * scale * gating_ref[h, here]
            ).astype(BF16)


def last_kernel(section, total_ref, block_ref, weights_ref, out_ref, tiles, written):
    width = block_ref.shape[1]
    rows = pl.ds(pl.multiple_of(section[0] * width, width), width)
    copies = []
    for i in range(total_ref.shape[1] // TILE):
        here = slice(i * TILE, (i + 1) * TILE)
        term = mul(block_ref[...], weights_ref[rows, here])
        tiles[:, here] = (total_ref[:, here] + term).astype(BF16)
        columns = pl.ds(i * TILE, TILE)
        copies.append(
            pltpu.make_async_copy(tiles.at[:, columns], out_ref.at[:, columns], written.at[i])
        )
        copies[-1].start()
    for copy in copies:
        copy.wait()


def from_behind(value, axis, steps):
    count = lax.axis_size(axis)
    return lax.ppermute(value, axis, [(i, i + steps) for i in range(count - steps)])


def exchange(own_map, leaves):
    received = [lax.ppermute(own_map, "leaf", pairs_at(k, leaves)) for k in range(1, leaves)]
    return [own_map] + received


VMEM = pl.BlockSpec(memory_space=pltpu.VMEM)
SMEM = pl.BlockSpec(memory_space=pltpu.SMEM)
HBM = pl.BlockSpec(memory_space=pltpu.HBM)
PARAMS = pltpu.CompilerParams(vmem_limit_bytes=8 * 1024 * 1024)
LAST_PARAMS = pltpu.CompilerParams(vmem_limit_bytes=12 * 1024 * 1024)


def pack_rims(inputs):
    _, heads, depth = inputs[0].shape
    return pl.pallas_call(
        rims_kernel,
        out_shape=jax.ShapeDtypeStruct((len(inputs) * RIM, heads, depth), BF16),
        in_specs=[HBM] * len(inputs),
        out_specs=VMEM,
        scratch_shapes=[pltpu.SemaphoreType.DMA((len(inputs),))],
        compiler_params=pltpu.CompilerParams(vmem_limit_bytes=65_700_000),
        cost_estimate=pl.CostEstimate(flops=10**9, bytes_accessed=2**16, transcendentals=0),
    )(*inputs)


def filters_of(key, value, taps):
    heads, length, depth = key.shape
    per_token = jax.ShapeDtypeStruct((heads, length, depth), BF16)
    return pl.pallas_call(
        filters_kernel,
        out_shape=(per_token, per_token, jax.ShapeDtypeStruct((2, heads, AGAIN, depth), F32)),
        in_specs=[VMEM] * 3,
        out_specs=[VMEM] * 3,
        scratch_shapes=[pltpu.VMEM((2, heads, length + RIM, depth), F32)],
        compiler_params=PARAMS,
        cost_estimate=pl.CostEstimate(
            flops=3 * 10**9, bytes_accessed=4 * 2**20, transcendentals=10**6
        ),
    )(key, value, taps)


def maps_of(base, heads, resets, unit_in, value_in, first, rims, taps, decay, strength):
    _, length, depth = unit_in.shape
    chunks = length // CHUNK
    return pl.pallas_call(
        functools.partial(maps_kernel, base),
        out_shape=(
            jax.ShapeDtypeStruct((heads, length, depth), BF16),
            jax.ShapeDtypeStruct((heads, length, 2 * depth), F32),
            jax.ShapeDtypeStruct((heads, chunks - 1, depth, 2 * depth), F32),
            *[jax.ShapeDtypeStruct((heads // GROUPS, depth, 2 * depth), BF16)] * GROUPS,
        ),
        in_specs=[SMEM] + [VMEM] * 7,
        out_specs=[VMEM] * (3 + GROUPS),
        scratch_shapes=[
            pltpu.VMEM(rims.shape, F32),
            pltpu.VMEM((heads, 2, RIM + AGAIN, depth), F32),
            pltpu.VMEM((heads, CHUNK, depth), BF16),
            pltpu.VMEM((heads, chunks, depth, 2 * depth), F32),
        ],
        compiler_params=PARAMS,
        cost_estimate=pl.CostEstimate(
            flops=5 * 10**9, bytes_accessed=4 * 2**20, transcendentals=10**6
        ),
    )(resets, unit_in, value_in, first, rims, taps, decay, strength)


def reads_of(base, heads, resets, query, gate, gain, rims, taps, decay, strength, made):
    _, length, depth = query.shape
    per_token = jax.ShapeDtypeStruct((heads, length, depth), F32)
    return pl.pallas_call(
        functools.partial(reads_kernel, base),
        out_shape=(jax.ShapeDtypeStruct(per_token.shape, BF16), per_token, per_token),
        in_specs=[SMEM] + [VMEM] * 10,
        out_specs=[VMEM] * 3,
        scratch_shapes=[
            pltpu.VMEM(rims.shape, F32),
            pltpu.VMEM((heads, length + RIM, depth), F32),
        ],
        compiler_params=PARAMS,
        cost_estimate=pl.CostEstimate(
            flops=3 * 10**9, bytes_accessed=4 * 2**20, transcendentals=10**6
        ),
    )(resets, query, gate, gain, rims, taps, decay, strength, *made)


def join(place, maps, links):
    count = len(maps)
    heads, depth, _ = maps[0].shape
    pair = jax.ShapeDtypeStruct((heads, depth, 2 * depth), F32)
    square = (heads, depth, depth)
    if links == 1:
        totals = (jax.ShapeDtypeStruct(square, BF16),)
    else:
        totals = (jax.ShapeDtypeStruct(square, F32),) * 2
    return pl.pallas_call(
        functools.partial(join_kernel, count),
        out_shape=(pair, *totals),
        in_specs=[SMEM] + [VMEM] * count,
        out_specs=[VMEM] * (1 + len(totals)),
        scratch_shapes=[pltpu.VMEM((count, heads, depth, 2 * depth), BF16)],
        compiler_params=PARAMS,
    )(place, *maps)


def outputs_of(base, arrived, before, reads):
    heads, depth, _ = arrived.shape
    length = reads[0].shape[1]
    return pl.pallas_call(
        functools.partial(outputs_kernel, base),
        out_shape=jax.ShapeDtypeStruct((length, heads * depth), BF16),
        in_specs=[VMEM] * 5,
        out_specs=VMEM,
        compiler_params=PARAMS,
    )(arrived, before, *reads)


def last_projected(section, total, block, weights):
    length, columns = total.shape
    return pl.pallas_call(
        last_kernel,
        out_shape=jax.ShapeDtypeStruct((length, columns), BF16),
        in_specs=[SMEM] + [VMEM] * 3,
        out_specs=pl.BlockSpec(memory_space=pl.ANY),
        scratch_shapes=[
            pltpu.VMEM((length, columns), BF16),
            pltpu.SemaphoreType.DMA((columns // TILE,)),
        ],
        compiler_params=LAST_PARAMS,
    )(section.astype(jnp.int32).reshape(1), total, block, weights)


def after(first, *values):
    return lax.optimization_barrier((first, *values))[1:]


def on_device(
    query_in,
    key_in,
    value_in,
    gate_in,
    write_strength,
    log_decay,
    doc_resets,
    conv_weight,
    output_norm_gain,
    output_projection_weight,
):
    length, heads, depth = query_in.shape
    taps = conv_weight
    rims = from_behind(pack_rims((query_in, key_in, value_in)), ("chain", "leaf"), 1)
    key, value = (jnp.transpose(x, (1, 0, 2)) for x in (key_in, value_in))
    key, value, first = filters_of(key, value, taps)
    gain = output_norm_gain.reshape(1, depth)
    leaves = lax.axis_size("leaf")
    place = lax.axis_index("leaf").astype(jnp.int32).reshape(1)

    links = lax.axis_size("chain") - 1
    unit_key, solved, starts, *own_maps = maps_of(
        0, heads, doc_resets, key, value, first, rims, taps, log_decay, write_strength
    )
    query_in, gate_in = after(own_maps[-1], query_in, gate_in)
    query, gate = (jnp.transpose(x, (1, 0, 2)) for x in (query_in, gate_in))
    reads = reads_of(
        0, heads, doc_resets, query, gate, gain, rims, taps, log_decay, write_strength,
        (unit_key, solved, starts),
    )
    size = heads // GROUPS
    blocks = []
    exchanged = [exchange(own_maps[0], leaves)]
    for g in range(GROUPS):
        earlier = blocks[-1] if blocks else reads[0]
        maps = after(earlier, *exchanged[g])
        before, state, *trans = join(place, maps, links)
        if g + 1 < GROUPS:
            exchanged.append(exchange(*after(state, own_maps[g + 1]), leaves))
        arrived = from_behind(state.astype(BF16), "chain", 1)
        for _ in range(links - 1):
            passed = jnp.einsum(
                "hij,hjk->hik", trans[0], arrived.astype(F32), precision=lax.Precision.HIGHEST
            )
            arrived = from_behind((passed + state).astype(BF16), "chain", 1)
        blocks.append(outputs_of(g * size, arrived, before, reads))

    ring = lax.axis_size("head")
    mine = lax.axis_index("head")
    width = size * depth
    weights = output_projection_weight
    around = [(i, (i + 1) % ring) for i in range(ring)]
    sums = [None] * GROUPS
    for k in range(ring):
        owner = lax.rem(mine + ring - k, ring)
        last = k + 1 == ring
        following = blocks if last else [lax.ppermute(x, "head", around) for x in blocks]
        for g, block in enumerate(blocks):
            section = owner * GROUPS + g
            if last and g + 1 == GROUPS:
                return last_projected(section, sum(sums[1:], sums[0]), block, weights)
            rows = lax.dynamic_slice_in_dim(weights, section * width, width, 0)
            term = jnp.dot(block, rows, preferred_element_type=F32)
            sums[g] = term if sums[g] is None else sums[g] + term
        blocks = following


def solution(mesh):
    return jax.shard_map(
        on_device,
        mesh=mesh,
        in_specs=(
            P(("chain", "leaf"), "head", None),
            P(("chain", "leaf"), "head", None),
            P(("chain", "leaf"), "head", None),
            P(("chain", "leaf"), "head", None),
            P("head", ("chain", "leaf")),
            P("head", ("chain", "leaf")),
            P(("chain", "leaf")),
            P(None, None, "head", None),
            P(),
            P(None, "head"),
        ),
        out_specs=P(("chain", "leaf"), "head"),
        check_vma=False,
    )
```

```python
import functools

import jax
import jax.numpy as jnp
from jax import lax
from jax.experimental import pallas as pl
from jax.experimental.pallas import tpu as pltpu
from jax.sharding import PartitionSpec as P

BLOCK = 64
CHUNK = 128
GROUPS = 2
RIM = 8
EPSILON = 1e-06
FAR = -1e30
LARGE = 1e38
AGAIN = 16
TILE = 256
F32 = jnp.float32
BF16 = jnp.bfloat16
NN = (((1,), (0,)), ((), ()))
NT = (((1,), (1,)), ((), ()))
TN = (((0,), (0,)), ((), ()))


def split(a):
    high = a.astype(BF16)
    return high, (a - high.astype(F32)).astype(BF16)


def mul(a, b, dims=NN):
    return lax.dot_general(a, b, dims, preferred_element_type=F32)


def mul_split(a, b):
    a_high, a_low = split(a)
    b_high, b_low = split(b)
    return mul(a_high, b_high) + (mul(a_low, b_high) + mul(a_high, b_low))


def rows_of(c):
    return slice(c * CHUNK, (c + 1) * CHUNK)


def indices():
    shape = (CHUNK, CHUNK)
    return (
        lax.broadcasted_iota(jnp.int32, shape, 0),
        lax.broadcasted_iota(jnp.int32, shape, 1),
    )


def token_scalars(decay_ref, strength_ref, c):
    row, col = indices()
    cum = lax.dot_general(
        decay_ref[:, rows_of(c)],
        (row <= col).astype(F32),
        NN,
        precision=lax.Precision.HIGHEST,
        preferred_element_type=F32,
    )
    strength = strength_ref[:, rows_of(c)]
    stacked = [cum, strength]
    missing = 8 - 2 * cum.shape[0]
    if missing > 0:
        stacked.append(jnp.zeros((missing, CHUNK), F32))
    return cum, strength, jnp.transpose(jnp.concatenate(stacked, axis=0))


def silu(x):
    below = jnp.minimum(1.0 + jnp.exp(-x), LARGE)
    inverse = pl.reciprocal(below, approx=True)
    return x * (inverse * (2.0 - below * inverse))


def filtered(padded, taps, begin, length):
    first = begin + RIM + 1 - len(taps)
    total = taps[0] * padded[first : first + length]
    for j in range(1, len(taps)):
        total = total + taps[j] * padded[first + j : first + j + length]
    return silu(total)


def taps_of(taps_ref, which, head):
    return [taps_ref[which, j, pl.ds(head, 1), :] for j in range(taps_ref.shape[1])]


def unit(rows):
    return rows * lax.rsqrt(jnp.sum(rows * rows, axis=-1, keepdims=True) + EPSILON)


def same_document(second_resets, row, col):
    return ((row // BLOCK) - (col // BLOCK)) * second_resets == 0


def lower_inverse(lowers, row, col):
    differ = row ^ col
    eye = (row == col).astype(F32)
    in_block = (differ < 8).astype(F32)
    diagonal = [low * in_block for low in lowers]
    powers = [d.astype(BF16) for d in diagonal]
    squares = [mul(p, p).astype(BF16) for p in powers]
    inverse = [eye - d for d in diagonal]
    stacked = [
        mul(jnp.concatenate([s, x.astype(BF16)], axis=0), s) for x, s in zip(inverse, squares)
    ]
    fourths = [both[:CHUNK].astype(BF16) for both in stacked]
    inverse = [x + both[CHUNK:] for x, both in zip(inverse, stacked)]
    inverse = [x + mul(x.astype(BF16), s) for x, s in zip(inverse, fourths)]
    size = 8
    while size < CHUNK:
        joint = odd_blocks(((differ >= size) & (differ < 2 * size)).astype(F32), size)
        rounded = [x.astype(BF16) for x in inverse]
        inner = [
            mul((odd_blocks(low, size) * joint).astype(BF16), x)
            for low, x in zip(lowers, rounded)
        ]
        outer = [
            mul(odd_blocks(x, size).astype(BF16), with_even_zeros(i, size).astype(BF16))
            for x, i in zip(inverse, inner)
        ]
        inverse = [less_in_odd(x, o, size) for x, o in zip(inverse, outer)]
        size *= 2
    return inverse


def odd_blocks(a, size):
    return jnp.concatenate([a[b : b + size] for b in range(size, a.shape[0], 2 * size)], axis=0)


def with_even_zeros(odd, size):
    zeros = jnp.zeros((size, odd.shape[1]), odd.dtype)
    pieces = []
    for b in range(0, odd.shape[0], size):
        pieces += [zeros, odd[b : b + size]]
    return jnp.concatenate(pieces, axis=0)


def less_in_odd(a, odd, size):
    pieces = []
    for b in range(0, odd.shape[0], size):
        pieces.append(a[2 * b : 2 * b + size])
        pieces.append(a[2 * b + size : 2 * b + 2 * size] - odd[b : b + size])
    return jnp.concatenate(pieces, axis=0)


def rims_kernel(*refs):
    *inputs, packed_ref, arrived = refs
    copies = []
    for i, x_ref in enumerate(inputs):
        last = x_ref.at[pl.ds(x_ref.shape[0] - RIM, RIM)]
        here = packed_ref.at[pl.ds(i * RIM, RIM)]
        copies.append(pltpu.make_async_copy(last, here, arrived.at[i]))
    for copy in copies:
        copy.start()
    for copy in copies:
        copy.wait()


def filters_kernel(key_ref, value_ref, taps_ref, unit_ref, value_out_ref, first_ref, padded):
    heads, length, _ = key_ref.shape
    for i, x_ref in enumerate((key_ref, value_ref)):
        padded[i, :, RIM:] = x_ref[...].astype(F32)
        padded[i, :, 0:RIM] = jnp.zeros((heads, RIM, padded.shape[3]), F32)
    first_ref[...] = padded[:, :, RIM : RIM + AGAIN]

    def one_head(h, carry):
        for i in range(2):
            taps = taps_of(taps_ref, 1 + i, h)
            for c in range(length // CHUNK):
                rows = filtered(padded.at[i, h], taps, c * CHUNK, CHUNK)
                if i == 0:
                    unit_ref[h, rows_of(c)] = unit(rows).astype(BF16)
                else:
                    value_out_ref[h, rows_of(c)] = rows.astype(BF16)
        return carry

    lax.fori_loop(0, heads, one_head, 0)


def maps_kernel(
    base, resets, unit_in_ref, value_in_ref, first_ref, rim_ref, taps_ref, decay_ref, strength_ref,
    unit_ref, solved_ref, starts_ref, *refs,
):
    *map_refs, rims, padded, value_s, step_s = refs
    heads, length, depth = unit_ref.shape
    chunks = length // CHUNK
    size = heads // len(map_refs)
    total_heads = decay_ref.shape[0]
    row, col = indices()
    rims[...] = rim_ref[...].astype(F32)
    for g in range(heads):
        h = base + g
        for c in range(1, chunks):
            unit_ref[g, rows_of(c)] = unit_in_ref[h, rows_of(c)]
        unit_ref[g, AGAIN:CHUNK] = unit_in_ref[h, AGAIN:CHUNK]
        value_s[g, AGAIN:CHUNK] = value_in_ref[h, AGAIN:CHUNK]
        for i in range(2):
            padded[g, i, 0:RIM] = rims[(1 + i) * RIM : (2 + i) * RIM, h, :]
            padded[g, i, RIM : RIM + AGAIN] = first_ref[i, h]
            rows = filtered(padded.at[g, i], taps_of(taps_ref, 1 + i, h), 0, AGAIN)
            if i == 0:
                unit_ref[g, 0:AGAIN] = unit(rows).astype(BF16)
            else:
                value_s[g, 0:AGAIN] = rows.astype(BF16)

    parts = []
    lowers = []
    for c in range(chunks):
        cum, _, columns = token_scalars(decay_ref, strength_ref, c)
        first, second = resets[2 * c], resets[2 * c + 1]
        strictly = (row > col) & same_document(second, row, col)
        for g in range(heads):
            h = base + g
            cum_col = columns[:, h : h + 1]
            cum_row = cum[h : h + 1]
            key = unit_in_ref[h, rows_of(c)] if c else unit_ref[g, rows_of(c)]
            fading = jnp.exp(jnp.where(strictly, cum_col - cum_row, FAR))
            strength_col = columns[:, total_heads + h : total_heads + h + 1]
            lowers.append(strength_col * fading * mul(key, key, NT))
            parts.append((g, c, first, second, cum_col, cum_row, strength_col))
    inverses = lower_inverse(lowers, row, col)
    eye = (row == col).astype(F32)
    first_rows = lax.broadcasted_iota(jnp.int32, (CHUNK, 1), 0) < BLOCK
    for (g, c, first, second, cum_col, cum_row, strength_col), inverse in zip(parts, inverses):
        keep_first = (1 - first).astype(F32)
        keep_second = (1 - second).astype(F32)
        keep_both = keep_first * keep_second
        h = base + g
        key = unit_in_ref[h, rows_of(c)] if c else unit_ref[g, rows_of(c)]
        value = value_in_ref[h, rows_of(c)] if c else value_s[g]
        growth = jnp.exp(cum_col) * jnp.where(first_rows, keep_first, keep_both)
        targets = jnp.concatenate(
            [
                (strength_col * growth) * key.astype(F32),
                strength_col * value.astype(F32),
            ],
            axis=1,
        )
        solved = targets + mul((inverse - eye).astype(BF16), targets.astype(BF16))
        solved_ref[g, rows_of(c)] = solved
        end = cum_row[:, CHUNK - 1 : CHUNK]
        tail = jnp.exp(end - cum_col) * jnp.where(first_rows, keep_second, 1.0)
        product = mul(key, (tail * solved).astype(BF16), TN)
        passed = jnp.exp(end) * keep_both
        step_s[g, c, :, :depth] = jnp.where(row == col, passed, 0.0) - product[:, :depth]
        step_s[g, c, :, depth:] = product[:, depth:]

    def compose(later, earlier):
        high, low = split(earlier)
        trans = later[:, :depth].astype(BF16)
        joined = mul(trans, high) + mul(trans, low)
        return jnp.concatenate([joined[:, :depth], joined[:, depth:] + later[:, depth:]], axis=1)

    every = range(heads)
    states = [step_s[g, 0] for g in every]
    half = chunks // 2
    for c in range(1, half):
        for g in every:
            starts_ref[g, c - 1] = states[g]
        states = [compose(step_s[g, c], states[g]) for g in every]
    rest = [step_s[g, half] for g in every]
    for c in range(half + 1, chunks):
        rest = [compose(step_s[g, c], rest[g]) for g in every]
    for g in every:
        map_refs[g // size][g % size] = compose(rest[g], states[g]).astype(BF16)
    for c in range(half, chunks):
        for g in every:
            starts_ref[g, c - 1] = states[g]
        if c + 1 < chunks:
            states = [compose(step_s[g, c], states[g]) for g in every]


def reads_kernel(
    base, resets, query_ref, gate_ref, gain_ref, rim_ref, taps_ref, decay_ref, strength_ref,
    unit_ref, solved_ref, starts_ref,
    reach_ref, part_ref, gating_ref,
    rims, padded,
):
    heads, length, depth = unit_ref.shape
    chunks = length // CHUNK
    row, col = indices()
    first_rows = lax.broadcasted_iota(jnp.int32, (CHUNK, 1), 0) < BLOCK
    rims[...] = rim_ref[...].astype(F32)
    for g in range(heads):
        h = base + g
        padded[g, 0:RIM] = rims[0:RIM, h, :]
        padded[g, RIM : RIM + length] = query_ref[h].astype(F32)

    for c in range(chunks):
        here = rows_of(c)
        cum, _, columns = token_scalars(decay_ref, strength_ref, c)
        first, second = resets[2 * c], resets[2 * c + 1]
        keep_first = (1 - first).astype(F32)
        keep_both = keep_first * (1 - second).astype(F32)
        upto = (row >= col) & same_document(second, row, col)
        for g in range(heads):
            h = base + g
            cum_col = columns[:, h : h + 1]
            filtered_rows = filtered(padded.at[g], taps_of(taps_ref, 0, h), c * CHUNK, CHUNK)
            query = (unit(filtered_rows) * depth**-0.5).astype(BF16)
            fading = jnp.exp(jnp.where(upto, cum_col - cum[h : h + 1], FAR))
            mixing = fading * mul(query, unit_ref[g, here], NT)
            own = mul_split(mixing, solved_ref[g, here])
            growth = jnp.exp(cum_col) * jnp.where(first_rows, keep_first, keep_both)
            reach = growth * query.astype(F32) - own[:, :depth]
            part = own[:, depth:]
            if c:
                both = mul_split(reach, starts_ref[g, c - 1])
                reach = both[:, :depth]
                part = part + both[:, depth:]
            reach_ref[g, here] = reach.astype(BF16)
            part_ref[g, here] = part
            gate = gate_ref[h, here].astype(F32)
            gating_ref[g, here] = gain_ref[...] * silu(gate)


def partner(place, k, count):
    if count & (count - 1) == 0:
        return place ^ k
    return lax.rem(place + count - k, count)


def pairs_at(k, count):
    if count & (count - 1) == 0:
        return [(i, i ^ k) for i in range(count)]
    return [(i, (i + k) % count) for i in range(count)]


def join_kernel(count, place, *refs):
    maps = refs[:count]
    before_ref, state_ref, *trans_ref, ordered = refs[count:]
    heads, depth, _ = before_ref.shape
    me = place[0]
    for k in range(count):
        ordered[partner(me, k, count)] = maps[k][...]
    row, col = indices()
    eye = (row == col).astype(F32)
    states = [jnp.concatenate([eye, jnp.zeros((depth, depth), F32)], axis=1)] * heads
    for lap in range(count):

        @pl.when(lap == me)
        def _():
            for h in range(heads):
                before_ref[h] = states[h]

        for h in range(heads):
            step = ordered[lap, h]
            if lap:
                high, low = split(states[h])
                trans = step[:, :depth]
                joined = mul(trans, high) + mul(trans, low)
                states[h] = jnp.concatenate(
                    [joined[:, :depth], joined[:, depth:] + step[:, depth:].astype(F32)], axis=1
                )
            else:
                states[h] = step.astype(F32)
    for h in range(heads):
        state_ref[h] = states[h][:, depth:].astype(state_ref.dtype)
        for ref in trans_ref:
            ref[h] = states[h][:, :depth]


def outputs_kernel(base, arrived_ref, before_ref, reach_ref, part_ref, gating_ref, normed_ref):
    heads, depth, _ = arrived_ref.shape
    for g in range(heads):
        h = base + g
        before = before_ref[g]
        incoming = mul_split(before[:, :depth], arrived_ref[g].astype(F32)) + before[:, depth:]
        high, low = split(incoming)
        reach = reach_ref[h]
        reached = mul(reach, high) + mul(reach, low)
        for c in range(normed_ref.shape[0] // CHUNK):
            here = rows_of(c)
            core = part_ref[h, here] + reached[here]
            scale = lax.rsqrt(jnp.sum(core * core, axis=-1, keepdims=True) / depth + EPSILON)
            normed_ref[here, g * depth : (g + 1) * depth] = (
                core * scale * gating_ref[h, here]
            ).astype(BF16)


def last_kernel(begin, section, total_ref, block_ref, weights_ref, *refs):
    out_ref, tiles, written = refs[-3:]
    count, width = block_ref.shape
    rows = pl.ds(pl.multiple_of(section[0] * width, width), width)
    copies = []
    for i in range(total_ref.shape[1] // TILE):
        here = slice(i * TILE, (i + 1) * TILE)
        term = mul(block_ref[...], weights_ref[rows, here])
        tiles[:, here] = (total_ref[begin : begin + count, here] + term).astype(BF16)
        columns = pl.ds(i * TILE, TILE)
        target = out_ref.at[pl.ds(begin, count), columns]
        copies.append(pltpu.make_async_copy(tiles.at[:, columns], target, written.at[i]))
        copies[-1].start()
    for copy in copies:
        copy.wait()


def from_behind(value, axis, steps):
    count = lax.axis_size(axis)
    return lax.ppermute(value, axis, [(i, i + steps) for i in range(count - steps)])


def exchange(own_map, leaves):
    received = [lax.ppermute(own_map, "leaf", pairs_at(k, leaves)) for k in range(1, leaves)]
    return [own_map] + received


VMEM = pl.BlockSpec(memory_space=pltpu.VMEM)
SMEM = pl.BlockSpec(memory_space=pltpu.SMEM)
HBM = pl.BlockSpec(memory_space=pltpu.HBM)
PARAMS = pltpu.CompilerParams(vmem_limit_bytes=8 * 1024 * 1024)
LAST_PARAMS = pltpu.CompilerParams(vmem_limit_bytes=12 * 1024 * 1024)


def pack_rims(inputs):
    _, heads, depth = inputs[0].shape
    return pl.pallas_call(
        rims_kernel,
        out_shape=jax.ShapeDtypeStruct((len(inputs) * RIM, heads, depth), BF16),
        in_specs=[HBM] * len(inputs),
        out_specs=VMEM,
        scratch_shapes=[pltpu.SemaphoreType.DMA((len(inputs),))],
        compiler_params=pltpu.CompilerParams(vmem_limit_bytes=65_700_000),
        cost_estimate=pl.CostEstimate(flops=10**9, bytes_accessed=2**16, transcendentals=0),
    )(*inputs)


def filters_of(key, value, taps):
    heads, length, depth = key.shape
    per_token = jax.ShapeDtypeStruct((heads, length, depth), BF16)
    return pl.pallas_call(
        filters_kernel,
        out_shape=(per_token, per_token, jax.ShapeDtypeStruct((2, heads, AGAIN, depth), F32)),
        in_specs=[VMEM] * 3,
        out_specs=[VMEM] * 3,
        scratch_shapes=[pltpu.VMEM((2, heads, length + RIM, depth), F32)],
        compiler_params=PARAMS,
        cost_estimate=pl.CostEstimate(
            flops=3 * 10**9, bytes_accessed=4 * 2**20, transcendentals=10**6
        ),
    )(key, value, taps)


def maps_of(base, heads, resets, unit_in, value_in, first, rims, taps, decay, strength):
    _, length, depth = unit_in.shape
    chunks = length // CHUNK
    return pl.pallas_call(
        functools.partial(maps_kernel, base),
        out_shape=(
            jax.ShapeDtypeStruct((heads, length, depth), BF16),
            jax.ShapeDtypeStruct((heads, length, 2 * depth), F32),
            jax.ShapeDtypeStruct((heads, chunks - 1, depth, 2 * depth), F32),
            *[jax.ShapeDtypeStruct((heads // GROUPS, depth, 2 * depth), BF16)] * GROUPS,
        ),
        in_specs=[SMEM] + [VMEM] * 7,
        out_specs=[VMEM] * (3 + GROUPS),
        scratch_shapes=[
            pltpu.VMEM(rims.shape, F32),
            pltpu.VMEM((heads, 2, RIM + AGAIN, depth), F32),
            pltpu.VMEM((heads, CHUNK, depth), BF16),
            pltpu.VMEM((heads, chunks, depth, 2 * depth), F32),
        ],
        compiler_params=PARAMS,
        cost_estimate=pl.CostEstimate(
            flops=5 * 10**9, bytes_accessed=4 * 2**20, transcendentals=10**6
        ),
    )(resets, unit_in, value_in, first, rims, taps, decay, strength)


def reads_of(base, heads, resets, query, gate, gain, rims, taps, decay, strength, made):
    _, length, depth = query.shape
    per_token = jax.ShapeDtypeStruct((heads, length, depth), F32)
    return pl.pallas_call(
        functools.partial(reads_kernel, base),
        out_shape=(jax.ShapeDtypeStruct(per_token.shape, BF16), per_token, per_token),
        in_specs=[SMEM] + [VMEM] * 10,
        out_specs=[VMEM] * 3,
        scratch_shapes=[
            pltpu.VMEM(rims.shape, F32),
            pltpu.VMEM((heads, length + RIM, depth), F32),
        ],
        compiler_params=PARAMS,
        cost_estimate=pl.CostEstimate(
            flops=3 * 10**9, bytes_accessed=4 * 2**20, transcendentals=10**6
        ),
    )(resets, query, gate, gain, rims, taps, decay, strength, *made)


def join(place, maps, links):
    count = len(maps)
    heads, depth, _ = maps[0].shape
    pair = jax.ShapeDtypeStruct((heads, depth, 2 * depth), F32)
    square = (heads, depth, depth)
    if links == 1:
        totals = (jax.ShapeDtypeStruct(square, BF16),)
    else:
        totals = (jax.ShapeDtypeStruct(square, F32),) * 2
    return pl.pallas_call(
        functools.partial(join_kernel, count),
        out_shape=(pair, *totals),
        in_specs=[SMEM] + [VMEM] * count,
        out_specs=[VMEM] * (1 + len(totals)),
        scratch_shapes=[pltpu.VMEM((count, heads, depth, 2 * depth), BF16)],
        compiler_params=PARAMS,
    )(place, *maps)


def outputs_of(base, arrived, before, reads):
    heads, depth, _ = arrived.shape
    length = reads[0].shape[1]
    return pl.pallas_call(
        functools.partial(outputs_kernel, base),
        out_shape=jax.ShapeDtypeStruct((length, heads * depth), BF16),
        in_specs=[VMEM] * 5,
        out_specs=VMEM,
        compiler_params=PARAMS,
    )(arrived, before, *reads)


def last_projected(begin, section, total, block, weights, earlier):
    length, columns = total.shape
    whole = pl.BlockSpec(memory_space=pl.ANY)
    return pl.pallas_call(
        functools.partial(last_kernel, begin),
        out_shape=jax.ShapeDtypeStruct((length, columns), BF16),
        in_specs=[SMEM] + [VMEM] * 3 + [whole] * len(earlier),
        out_specs=whole,
        scratch_shapes=[
            pltpu.VMEM((block.shape[0], columns), BF16),
            pltpu.SemaphoreType.DMA((columns // TILE,)),
        ],
        input_output_aliases={4: 0} if earlier else {},
        compiler_params=LAST_PARAMS,
    )(section.astype(jnp.int32).reshape(1), total, block, weights, *earlier)


def after(first, *values):
    return lax.optimization_barrier((first, *values))[1:]


def on_device(
    query_in,
    key_in,
    value_in,
    gate_in,
    write_strength,
    log_decay,
    doc_resets,
    conv_weight,
    output_norm_gain,
    output_projection_weight,
):
    length, heads, depth = query_in.shape
    taps = conv_weight
    rims = from_behind(pack_rims((query_in, key_in, value_in)), ("chain", "leaf"), 1)
    key, value = (jnp.transpose(x, (1, 0, 2)) for x in (key_in, value_in))
    key, value, first = filters_of(key, value, taps)
    gain = output_norm_gain.reshape(1, depth)
    leaves = lax.axis_size("leaf")
    place = lax.axis_index("leaf").astype(jnp.int32).reshape(1)

    links = lax.axis_size("chain") - 1
    unit_key, solved, starts, *own_maps = maps_of(
        0, heads, doc_resets, key, value, first, rims, taps, log_decay, write_strength
    )
    query_in, gate_in = after(own_maps[-1], query_in, gate_in)
    query, gate = (jnp.transpose(x, (1, 0, 2)) for x in (query_in, gate_in))
    reads = reads_of(
        0, heads, doc_resets, query, gate, gain, rims, taps, log_decay, write_strength,
        (unit_key, solved, starts),
    )
    size = heads // GROUPS
    blocks = []
    exchanged = [exchange(own_maps[0], leaves)]
    for g in range(GROUPS):
        earlier = blocks[-1] if blocks else reads[0]
        maps = after(earlier, *exchanged[g])
        before, state, *trans = join(place, maps, links)
        if g + 1 < GROUPS:
            exchanged.append(exchange(*after(state, own_maps[g + 1]), leaves))
        arrived = from_behind(state.astype(BF16), "chain", 1)
        for _ in range(links - 1):
            passed = jnp.einsum(
                "hij,hjk->hik", trans[0], arrived.astype(F32), precision=lax.Precision.HIGHEST
            )
            arrived = from_behind((passed + state).astype(BF16), "chain", 1)
        blocks.append(outputs_of(g * size, arrived, before, reads))

    ring = lax.axis_size("head")
    mine = lax.axis_index("head")
    width = size * depth
    weights = output_projection_weight
    around = [(i, (i + 1) % ring) for i in range(ring)]
    sums = [None] * GROUPS
    for k in range(ring):
        owner = lax.rem(mine + ring - k, ring)
        last = k + 1 == ring
        following = blocks if last else [lax.ppermute(x, "head", around) for x in blocks[:-1]]
        if k + 2 == ring:
            count = length // 2
            following.append(
                [lax.ppermute(x, "head", around) for x in (blocks[-1][:count], blocks[-1][count:])]
            )
        elif not last:
            following.append(lax.ppermute(blocks[-1], "head", around))
        for g, block in enumerate(blocks):
            section = owner * GROUPS + g
            if last and g + 1 == GROUPS:
                total = sum(sums[1:], sums[0])
                result = []
                for i, half in enumerate(block):
                    result = [last_projected(i * count, section, total, half, weights, result)]
                return result[0]
            rows = lax.dynamic_slice_in_dim(weights, section * width, width, 0)
            term = jnp.dot(block, rows, preferred_element_type=F32)
            sums[g] = term if sums[g] is None else sums[g] + term
        blocks = following


def solution(mesh):
    return jax.shard_map(
        on_device,
        mesh=mesh,
        in_specs=(
            P(("chain", "leaf"), "head", None),
            P(("chain", "leaf"), "head", None),
            P(("chain", "leaf"), "head", None),
            P(("chain", "leaf"), "head", None),
            P("head", ("chain", "leaf")),
            P("head", ("chain", "leaf")),
            P(("chain", "leaf")),
            P(None, None, "head", None),
            P(),
            P(None, "head"),
        ),
        out_specs=P(("chain", "leaf"), "head"),
        check_vma=False,
    )
```

```python
import functools

import jax
import jax.numpy as jnp
from jax import lax
from jax.experimental import pallas as pl
from jax.experimental.pallas import tpu as pltpu
from jax.sharding import PartitionSpec as P

BLOCK = 64
CHUNK = 128
GROUPS = 2
RIM = 8
EPSILON = 1e-06
FAR = -1e30
LARGE = 1e38
AGAIN = 16
TILE = 256
F32 = jnp.float32
BF16 = jnp.bfloat16
NN = (((1,), (0,)), ((), ()))
NT = (((1,), (1,)), ((), ()))
TN = (((0,), (0,)), ((), ()))


def split(a):
    high = a.astype(BF16)
    return high, (a - high.astype(F32)).astype(BF16)


def mul(a, b, dims=NN):
    return lax.dot_general(a, b, dims, preferred_element_type=F32)


def mul_split(a, b):
    a_high, a_low = split(a)
    b_high, b_low = split(b)
    return mul(a_high, b_high) + (mul(a_low, b_high) + mul(a_high, b_low))


def rows_of(c):
    return slice(c * CHUNK, (c + 1) * CHUNK)


def indices():
    shape = (CHUNK, CHUNK)
    return (
        lax.broadcasted_iota(jnp.int32, shape, 0),
        lax.broadcasted_iota(jnp.int32, shape, 1),
    )


def token_scalars(decay_ref, strength_ref, c):
    row, col = indices()
    cum = lax.dot_general(
        decay_ref[:, rows_of(c)],
        (row <= col).astype(F32),
        NN,
        precision=lax.Precision.HIGHEST,
        preferred_element_type=F32,
    )
    strength = strength_ref[:, rows_of(c)]
    stacked = [cum, strength]
    missing = 8 - 2 * cum.shape[0]
    if missing > 0:
        stacked.append(jnp.zeros((missing, CHUNK), F32))
    return cum, strength, jnp.transpose(jnp.concatenate(stacked, axis=0))


def silu(x):
    below = jnp.minimum(1.0 + jnp.exp(-x), LARGE)
    inverse = pl.reciprocal(below, approx=True)
    return x * (inverse * (2.0 - below * inverse))


def filtered(padded, taps, begin, length):
    first = begin + RIM + 1 - len(taps)
    total = taps[0] * padded[first : first + length]
    for j in range(1, len(taps)):
        total = total + taps[j] * padded[first + j : first + j + length]
    return silu(total)


def taps_of(taps_ref, which, head):
    return [taps_ref[which, j, pl.ds(head, 1), :] for j in range(taps_ref.shape[1])]


def unit(rows):
    return rows * lax.rsqrt(jnp.sum(rows * rows, axis=-1, keepdims=True) + EPSILON)


def same_document(second_resets, row, col):
    return ((row // BLOCK) - (col // BLOCK)) * second_resets == 0


def lower_inverse(lowers, row, col):
    differ = row ^ col
    eye = (row == col).astype(F32)
    in_block = (differ < 8).astype(F32)
    diagonal = [low * in_block for low in lowers]
    powers = [d.astype(BF16) for d in diagonal]
    squares = [mul(p, p).astype(BF16) for p in powers]
    inverse = [eye - d for d in diagonal]
    stacked = [
        mul(jnp.concatenate([s, x.astype(BF16)], axis=0), s) for x, s in zip(inverse, squares)
    ]
    fourths = [both[:CHUNK].astype(BF16) for both in stacked]
    inverse = [x + both[CHUNK:] for x, both in zip(inverse, stacked)]
    inverse = [x + mul(x.astype(BF16), s) for x, s in zip(inverse, fourths)]
    size = 8
    while size < CHUNK:
        joint = odd_blocks(((differ >= size) & (differ < 2 * size)).astype(F32), size)
        rounded = [x.astype(BF16) for x in inverse]
        inner = [
            mul((odd_blocks(low, size) * joint).astype(BF16), x)
            for low, x in zip(lowers, rounded)
        ]
        outer = [
            mul(odd_blocks(x, size).astype(BF16), with_even_zeros(i, size).astype(BF16))
            for x, i in zip(inverse, inner)
        ]
        inverse = [less_in_odd(x, o, size) for x, o in zip(inverse, outer)]
        size *= 2
    return inverse


def odd_blocks(a, size):
    return jnp.concatenate([a[b : b + size] for b in range(size, a.shape[0], 2 * size)], axis=0)


def with_even_zeros(odd, size):
    zeros = jnp.zeros((size, odd.shape[1]), odd.dtype)
    pieces = []
    for b in range(0, odd.shape[0], size):
        pieces += [zeros, odd[b : b + size]]
    return jnp.concatenate(pieces, axis=0)


def less_in_odd(a, odd, size):
    pieces = []
    for b in range(0, odd.shape[0], size):
        pieces.append(a[2 * b : 2 * b + size])
        pieces.append(a[2 * b + size : 2 * b + 2 * size] - odd[b : b + size])
    return jnp.concatenate(pieces, axis=0)


def rims_kernel(*refs):
    *inputs, packed_ref, arrived = refs
    copies = []
    for i, x_ref in enumerate(inputs):
        last = x_ref.at[pl.ds(x_ref.shape[0] - RIM, RIM)]
        here = packed_ref.at[pl.ds(i * RIM, RIM)]
        copies.append(pltpu.make_async_copy(last, here, arrived.at[i]))
    for copy in copies:
        copy.start()
    for copy in copies:
        copy.wait()


def filters_kernel(key_ref, value_ref, taps_ref, unit_ref, value_out_ref, first_ref, padded):
    heads, length, _ = key_ref.shape
    for i, x_ref in enumerate((key_ref, value_ref)):
        padded[i, :, RIM:] = x_ref[...].astype(F32)
        padded[i, :, 0:RIM] = jnp.zeros((heads, RIM, padded.shape[3]), F32)
    first_ref[...] = padded[:, :, RIM : RIM + AGAIN]

    def one_head(h, carry):
        for i in range(2):
            taps = taps_of(taps_ref, 1 + i, h)
            for c in range(length // CHUNK):
                rows = filtered(padded.at[i, h], taps, c * CHUNK, CHUNK)
                if i == 0:
                    unit_ref[h, rows_of(c)] = unit(rows).astype(BF16)
                else:
                    value_out_ref[h, rows_of(c)] = rows.astype(BF16)
        return carry

    lax.fori_loop(0, heads, one_head, 0)


def maps_kernel(
    base, resets, unit_in_ref, value_in_ref, first_ref, rim_ref, taps_ref, decay_ref, strength_ref,
    unit_ref, solved_ref, starts_ref, *refs,
):
    *map_refs, rims, padded, value_s, step_s = refs
    heads, length, depth = unit_ref.shape
    chunks = length // CHUNK
    size = heads // len(map_refs)
    total_heads = decay_ref.shape[0]
    row, col = indices()
    rims[...] = rim_ref[...].astype(F32)
    for g in range(heads):
        h = base + g
        for c in range(1, chunks):
            unit_ref[g, rows_of(c)] = unit_in_ref[h, rows_of(c)]
        unit_ref[g, AGAIN:CHUNK] = unit_in_ref[h, AGAIN:CHUNK]
        value_s[g, AGAIN:CHUNK] = value_in_ref[h, AGAIN:CHUNK]
        for i in range(2):
            padded[g, i, 0:RIM] = rims[(1 + i) * RIM : (2 + i) * RIM, h, :]
            padded[g, i, RIM : RIM + AGAIN] = first_ref[i, h]
            rows = filtered(padded.at[g, i], taps_of(taps_ref, 1 + i, h), 0, AGAIN)
            if i == 0:
                unit_ref[g, 0:AGAIN] = unit(rows).astype(BF16)
            else:
                value_s[g, 0:AGAIN] = rows.astype(BF16)

    parts = []
    lowers = []
    for c in range(chunks):
        cum, _, columns = token_scalars(decay_ref, strength_ref, c)
        first, second = resets[2 * c], resets[2 * c + 1]
        strictly = (row > col) & same_document(second, row, col)
        for g in range(heads):
            h = base + g
            cum_col = columns[:, h : h + 1]
            cum_row = cum[h : h + 1]
            key = unit_in_ref[h, rows_of(c)] if c else unit_ref[g, rows_of(c)]
            fading = jnp.exp(jnp.where(strictly, cum_col - cum_row, FAR))
            strength_col = columns[:, total_heads + h : total_heads + h + 1]
            lowers.append(strength_col * fading * mul(key, key, NT))
            parts.append((g, c, first, second, cum_col, cum_row, strength_col))
    inverses = lower_inverse(lowers, row, col)
    eye = (row == col).astype(F32)
    first_rows = lax.broadcasted_iota(jnp.int32, (CHUNK, 1), 0) < BLOCK
    for (g, c, first, second, cum_col, cum_row, strength_col), inverse in zip(parts, inverses):
        keep_first = (1 - first).astype(F32)
        keep_second = (1 - second).astype(F32)
        keep_both = keep_first * keep_second
        h = base + g
        key = unit_in_ref[h, rows_of(c)] if c else unit_ref[g, rows_of(c)]
        value = value_in_ref[h, rows_of(c)] if c else value_s[g]
        growth = jnp.exp(cum_col) * jnp.where(first_rows, keep_first, keep_both)
        targets = jnp.concatenate(
            [
                (strength_col * growth) * key.astype(F32),
                strength_col * value.astype(F32),
            ],
            axis=1,
        )
        solved = targets + mul((inverse - eye).astype(BF16), targets.astype(BF16))
        solved_ref[g, rows_of(c)] = solved
        end = cum_row[:, CHUNK - 1 : CHUNK]
        tail = jnp.exp(end - cum_col) * jnp.where(first_rows, keep_second, 1.0)
        product = mul(key, (tail * solved).astype(BF16), TN)
        passed = jnp.exp(end) * keep_both
        step_s[g, c, :, :depth] = jnp.where(row == col, passed, 0.0) - product[:, :depth]
        step_s[g, c, :, depth:] = product[:, depth:]

    def compose(later, earlier):
        high, low = split(earlier)
        trans = later[:, :depth].astype(BF16)
        joined = mul(trans, high) + mul(trans, low)
        return jnp.concatenate([joined[:, :depth], joined[:, depth:] + later[:, depth:]], axis=1)

    every = range(heads)
    states = [step_s[g, 0] for g in every]
    half = chunks // 2
    for c in range(1, half):
        for g in every:
            starts_ref[g, c - 1] = states[g]
        states = [compose(step_s[g, c], states[g]) for g in every]
    rest = [step_s[g, half] for g in every]
    for c in range(half + 1, chunks):
        rest = [compose(step_s[g, c], rest[g]) for g in every]
    for g in every:
        map_refs[g // size][g % size] = compose(rest[g], states[g]).astype(BF16)
    for c in range(half, chunks):
        for g in every:
            starts_ref[g, c - 1] = states[g]
        if c + 1 < chunks:
            states = [compose(step_s[g, c], states[g]) for g in every]


def reads_kernel(
    base, resets, query_ref, gate_ref, gain_ref, rim_ref, taps_ref, decay_ref, strength_ref,
    unit_ref, solved_ref, starts_ref,
    reach_ref, part_ref, gating_ref,
    rims, padded,
):
    heads, length, depth = unit_ref.shape
    chunks = length // CHUNK
    row, col = indices()
    first_rows = lax.broadcasted_iota(jnp.int32, (CHUNK, 1), 0) < BLOCK
    rims[...] = rim_ref[...].astype(F32)
    for g in range(heads):
        h = base + g
        padded[g, 0:RIM] = rims[0:RIM, h, :]
        padded[g, RIM : RIM + length] = query_ref[h].astype(F32)

    for c in range(chunks):
        here = rows_of(c)
        cum, _, columns = token_scalars(decay_ref, strength_ref, c)
        first, second = resets[2 * c], resets[2 * c + 1]
        keep_first = (1 - first).astype(F32)
        keep_both = keep_first * (1 - second).astype(F32)
        upto = (row >= col) & same_document(second, row, col)
        for g in range(heads):
            h = base + g
            cum_col = columns[:, h : h + 1]
            filtered_rows = filtered(padded.at[g], taps_of(taps_ref, 0, h), c * CHUNK, CHUNK)
            query = (unit(filtered_rows) * depth**-0.5).astype(BF16)
            fading = jnp.exp(jnp.where(upto, cum_col - cum[h : h + 1], FAR))
            mixing = fading * mul(query, unit_ref[g, here], NT)
            own = mul_split(mixing, solved_ref[g, here])
            growth = jnp.exp(cum_col) * jnp.where(first_rows, keep_first, keep_both)
            reach = growth * query.astype(F32) - own[:, :depth]
            part = own[:, depth:]
            if c:
                both = mul_split(reach, starts_ref[g, c - 1])
                reach = both[:, :depth]
                part = part + both[:, depth:]
            reach_ref[g, here] = reach.astype(BF16)
            part_ref[g, here] = part
            gate = gate_ref[h, here].astype(F32)
            gating_ref[g, here] = gain_ref[...] * silu(gate)


def partner(place, k, count):
    if count & (count - 1) == 0:
        return place ^ k
    return lax.rem(place + count - k, count)


def pairs_at(k, count):
    if count & (count - 1) == 0:
        return [(i, i ^ k) for i in range(count)]
    return [(i, (i + k) % count) for i in range(count)]


def join_kernel(count, place, *refs):
    maps = refs[:count]
    before_ref, state_ref, *trans_ref, ordered = refs[count:]
    heads, depth, _ = before_ref.shape
    me = place[0]
    for k in range(count):
        ordered[partner(me, k, count)] = maps[k][...]
    row, col = indices()
    eye = (row == col).astype(F32)
    states = [jnp.concatenate([eye, jnp.zeros((depth, depth), F32)], axis=1)] * heads
    for lap in range(count):

        @pl.when(lap == me)
        def _():
            for h in range(heads):
                before_ref[h] = states[h]

        for h in range(heads):
            step = ordered[lap, h]
            if lap:
                high, low = split(states[h])
                trans = step[:, :depth]
                joined = mul(trans, high) + mul(trans, low)
                states[h] = jnp.concatenate(
                    [joined[:, :depth], joined[:, depth:] + step[:, depth:].astype(F32)], axis=1
                )
            else:
                states[h] = step.astype(F32)
    for h in range(heads):
        state_ref[h] = states[h][:, depth:].astype(state_ref.dtype)
        for ref in trans_ref:
            ref[h] = states[h][:, :depth]


def outputs_kernel(base, arrived_ref, before_ref, reach_ref, part_ref, gating_ref, normed_ref):
    heads, depth, _ = arrived_ref.shape
    for g in range(heads):
        h = base + g
        before = before_ref[g]
        arrived = arrived_ref[g]
        high, low = split(before[:, :depth])
        incoming = (mul(high, arrived) + mul(low, arrived)) + before[:, depth:]
        high, low = split(incoming)
        reach = reach_ref[h]
        reached = mul(reach, high) + mul(reach, low)
        for c in range(normed_ref.shape[0] // CHUNK):
            here = rows_of(c)
            core = part_ref[h, here] + reached[here]
            scale = lax.rsqrt(jnp.sum(core * core, axis=-1, keepdims=True) / depth + EPSILON)
            normed_ref[here, g * depth : (g + 1) * depth] = (
                core * scale * gating_ref[h, here]
            ).astype(BF16)


def last_kernel(section, total_ref, block_ref, weights_ref, out_ref, tiles, written):
    width = block_ref.shape[1]
    rows = pl.ds(pl.multiple_of(section[0] * width, width), width)
    copies = []
    for i in range(total_ref.shape[1] // TILE):
        here = slice(i * TILE, (i + 1) * TILE)
        term = mul(block_ref[...], weights_ref[rows, here])
        tiles[:, here] = (total_ref[:, here] + term).astype(BF16)
        columns = pl.ds(i * TILE, TILE)
        copies.append(
            pltpu.make_async_copy(tiles.at[:, columns], out_ref.at[:, columns], written.at[i])
        )
        copies[-1].start()
    for copy in copies:
        copy.wait()


def from_behind(value, axis, steps):
    count = lax.axis_size(axis)
    return lax.ppermute(value, axis, [(i, i + steps) for i in range(count - steps)])


def exchange(own_map, leaves):
    received = [lax.ppermute(own_map, "leaf", pairs_at(k, leaves)) for k in range(1, leaves)]
    return [own_map] + received


VMEM = pl.BlockSpec(memory_space=pltpu.VMEM)
SMEM = pl.BlockSpec(memory_space=pltpu.SMEM)
HBM = pl.BlockSpec(memory_space=pltpu.HBM)
PARAMS = pltpu.CompilerParams(vmem_limit_bytes=8 * 1024 * 1024)
LAST_PARAMS = pltpu.CompilerParams(vmem_limit_bytes=12 * 1024 * 1024)


def pack_rims(inputs):
    _, heads, depth = inputs[0].shape
    return pl.pallas_call(
        rims_kernel,
        out_shape=jax.ShapeDtypeStruct((len(inputs) * RIM, heads, depth), BF16),
        in_specs=[HBM] * len(inputs),
        out_specs=VMEM,
        scratch_shapes=[pltpu.SemaphoreType.DMA((len(inputs),))],
        compiler_params=pltpu.CompilerParams(vmem_limit_bytes=65_700_000),
        cost_estimate=pl.CostEstimate(flops=10**9, bytes_accessed=2**16, transcendentals=0),
    )(*inputs)


def filters_of(key, value, taps):
    heads, length, depth = key.shape
    per_token = jax.ShapeDtypeStruct((heads, length, depth), BF16)
    return pl.pallas_call(
        filters_kernel,
        out_shape=(per_token, per_token, jax.ShapeDtypeStruct((2, heads, AGAIN, depth), F32)),
        in_specs=[VMEM] * 3,
        out_specs=[VMEM] * 3,
        scratch_shapes=[pltpu.VMEM((2, heads, length + RIM, depth), F32)],
        compiler_params=PARAMS,
        cost_estimate=pl.CostEstimate(
            flops=3 * 10**9, bytes_accessed=4 * 2**20, transcendentals=10**6
        ),
    )(key, value, taps)


def maps_of(base, heads, resets, unit_in, value_in, first, rims, taps, decay, strength):
    _, length, depth = unit_in.shape
    chunks = length // CHUNK
    return pl.pallas_call(
        functools.partial(maps_kernel, base),
        out_shape=(
            jax.ShapeDtypeStruct((heads, length, depth), BF16),
            jax.ShapeDtypeStruct((heads, length, 2 * depth), F32),
            jax.ShapeDtypeStruct((heads, chunks - 1, depth, 2 * depth), F32),
            *[jax.ShapeDtypeStruct((heads // GROUPS, depth, 2 * depth), BF16)] * GROUPS,
        ),
        in_specs=[SMEM] + [VMEM] * 7,
        out_specs=[VMEM] * (3 + GROUPS),
        scratch_shapes=[
            pltpu.VMEM(rims.shape, F32),
            pltpu.VMEM((heads, 2, RIM + AGAIN, depth), F32),
            pltpu.VMEM((heads, CHUNK, depth), BF16),
            pltpu.VMEM((heads, chunks, depth, 2 * depth), F32),
        ],
        compiler_params=PARAMS,
        cost_estimate=pl.CostEstimate(
            flops=5 * 10**9, bytes_accessed=4 * 2**20, transcendentals=10**6
        ),
    )(resets, unit_in, value_in, first, rims, taps, decay, strength)


def reads_of(base, heads, resets, query, gate, gain, rims, taps, decay, strength, made):
    _, length, depth = query.shape
    per_token = jax.ShapeDtypeStruct((heads, length, depth), F32)
    return pl.pallas_call(
        functools.partial(reads_kernel, base),
        out_shape=(jax.ShapeDtypeStruct(per_token.shape, BF16), per_token, per_token),
        in_specs=[SMEM] + [VMEM] * 10,
        out_specs=[VMEM] * 3,
        scratch_shapes=[
            pltpu.VMEM(rims.shape, F32),
            pltpu.VMEM((heads, length + RIM, depth), F32),
        ],
        compiler_params=PARAMS,
        cost_estimate=pl.CostEstimate(
            flops=3 * 10**9, bytes_accessed=4 * 2**20, transcendentals=10**6
        ),
    )(resets, query, gate, gain, rims, taps, decay, strength, *made)


def join(place, maps, links):
    count = len(maps)
    heads, depth, _ = maps[0].shape
    pair = jax.ShapeDtypeStruct((heads, depth, 2 * depth), F32)
    square = (heads, depth, depth)
    if links == 1:
        totals = (jax.ShapeDtypeStruct(square, BF16),)
    else:
        totals = (jax.ShapeDtypeStruct(square, F32),) * 2
    return pl.pallas_call(
        functools.partial(join_kernel, count),
        out_shape=(pair, *totals),
        in_specs=[SMEM] + [VMEM] * count,
        out_specs=[VMEM] * (1 + len(totals)),
        scratch_shapes=[pltpu.VMEM((count, heads, depth, 2 * depth), BF16)],
        compiler_params=PARAMS,
    )(place, *maps)


def outputs_of(base, arrived, before, reads):
    heads, depth, _ = arrived.shape
    length = reads[0].shape[1]
    return pl.pallas_call(
        functools.partial(outputs_kernel, base),
        out_shape=jax.ShapeDtypeStruct((length, heads * depth), BF16),
        in_specs=[VMEM] * 5,
        out_specs=VMEM,
        compiler_params=PARAMS,
    )(arrived, before, *reads)


def last_projected(section, total, block, weights):
    length, columns = total.shape
    return pl.pallas_call(
        last_kernel,
        out_shape=jax.ShapeDtypeStruct((length, columns), BF16),
        in_specs=[SMEM] + [VMEM] * 3,
        out_specs=pl.BlockSpec(memory_space=pl.ANY),
        scratch_shapes=[
            pltpu.VMEM((length, columns), BF16),
            pltpu.SemaphoreType.DMA((columns // TILE,)),
        ],
        compiler_params=LAST_PARAMS,
    )(section.astype(jnp.int32).reshape(1), total, block, weights)


def after(first, *values):
    return lax.optimization_barrier((first, *values))[1:]


def on_device(
    query_in,
    key_in,
    value_in,
    gate_in,
    write_strength,
    log_decay,
    doc_resets,
    conv_weight,
    output_norm_gain,
    output_projection_weight,
):
    length, heads, depth = query_in.shape
    taps = conv_weight
    rims = from_behind(pack_rims((query_in, key_in, value_in)), ("chain", "leaf"), 1)
    key, value = (jnp.transpose(x, (1, 0, 2)) for x in (key_in, value_in))
    key, value, first = filters_of(key, value, taps)
    gain = output_norm_gain.reshape(1, depth)
    leaves = lax.axis_size("leaf")
    place = lax.axis_index("leaf").astype(jnp.int32).reshape(1)

    links = lax.axis_size("chain") - 1
    unit_key, solved, starts, *own_maps = maps_of(
        0, heads, doc_resets, key, value, first, rims, taps, log_decay, write_strength
    )
    query_in, gate_in = after(own_maps[-1], query_in, gate_in)
    query, gate = (jnp.transpose(x, (1, 0, 2)) for x in (query_in, gate_in))
    reads = reads_of(
        0, heads, doc_resets, query, gate, gain, rims, taps, log_decay, write_strength,
        (unit_key, solved, starts),
    )
    size = heads // GROUPS
    blocks = []
    exchanged = [exchange(own_maps[0], leaves)]
    for g in range(GROUPS):
        earlier = blocks[-1] if blocks else reads[0]
        maps = after(earlier, *exchanged[g])
        before, state, *trans = join(place, maps, links)
        if g + 1 < GROUPS:
            exchanged.append(exchange(*after(state, own_maps[g + 1]), leaves))
        arrived = from_behind(state.astype(BF16), "chain", 1)
        for _ in range(links - 1):
            passed = jnp.einsum(
                "hij,hjk->hik", trans[0], arrived.astype(F32), precision=lax.Precision.HIGHEST
            )
            arrived = from_behind((passed + state).astype(BF16), "chain", 1)
        blocks.append(outputs_of(g * size, arrived, before, reads))

    ring = lax.axis_size("head")
    mine = lax.axis_index("head")
    width = size * depth
    weights = output_projection_weight
    around = [(i, (i + 1) % ring) for i in range(ring)]
    sums = [None] * GROUPS
    for k in range(ring):
        owner = lax.rem(mine + ring - k, ring)
        last = k + 1 == ring
        following = blocks if last else [lax.ppermute(x, "head", around) for x in blocks]
        for g, block in enumerate(blocks):
            section = owner * GROUPS + g
            if last and g + 1 == GROUPS:
                return last_projected(section, sum(sums[1:], sums[0]), block, weights)
            rows = lax.dynamic_slice_in_dim(weights, section * width, width, 0)
            term = jnp.dot(block, rows, preferred_element_type=F32)
            sums[g] = term if sums[g] is None else sums[g] + term
        blocks = following


def solution(mesh):
    return jax.shard_map(
        on_device,
        mesh=mesh,
        in_specs=(
            P(("chain", "leaf"), "head", None),
            P(("chain", "leaf"), "head", None),
            P(("chain", "leaf"), "head", None),
            P(("chain", "leaf"), "head", None),
            P("head", ("chain", "leaf")),
            P("head", ("chain", "leaf")),
            P(("chain", "leaf")),
            P(None, None, "head", None),
            P(),
            P(None, "head"),
        ),
        out_specs=P(("chain", "leaf"), "head"),
        check_vma=False,
    )
```
